32 devices in a mesh: dp: 4 (over x, core), row: 4 (over z), col: 2 (over y).
Axes of the slice: x: 2, y: 2, z: 4, core: 2. Of those that a mesh axis runs over, the one named last changes fastest.
Arguments:
- tokens: bfloat16 [768, 4096], P('row', ('dp', 'col')), may hold values from -6 to 6
- lengths: int32 [4], replicated, may hold values from 1024 to 1024, as said below
- w_query: bfloat16 [768, 768], P('row', 'col'), may hold values from -0.21875 to 0.21875
- w_key: bfloat16 [768, 768], P('row', 'col'), may hold values from -0.21875 to 0.21875
- w_value: bfloat16 [768, 768], P('row', 'col'), may hold values from -0.21875 to 0.21875
- w_out: bfloat16 [768, 768], P('col', 'row'), may hold values from -3.5 to 3.5
- gain_one: float32 [768], P('row'), may hold values from 0.5 to 1.5
- bias_one: float32 [768], P('row'), may hold values from -3 to 3
- w_up: bfloat16 [768, 3072], P('row', 'col'), may hold values from -0.21875 to 0.21875
- w_down: bfloat16 [3072, 768], P('col', 'row'), may hold values from -0.109375 to 0.109375
- gain_two: float32 [768], P('row'), may hold values from 0.5 to 1.5
- bias_two: float32 [768], P('row'), may hold values from -3 to 3
- cotangent: bfloat16 [768, 4096], P('row', ('dp', 'col')), may hold values from -6 to 6
Outputs:
- output: bfloat16 [768, 4096], P('row', ('dp', 'col'))
- input_grad: float32 [768, 4096], P('row', ('dp', 'col'))
- grad_query: float32 [768, 768], P('row', 'col')
- grad_key: float32 [768, 768], P('row', 'col')
- grad_value: float32 [768, 768], P('row', 'col')
- grad_out: float32 [768, 768], P('col', 'row')
- grad_gain_one: float32 [768], P('row')
- grad_bias_one: float32 [768], P('row')
- grad_up: float32 [768, 3072], P('row', 'col')
- grad_down: float32 [3072, 768], P('col', 'row')
- grad_gain_two: float32 [768], P('row')
- grad_bias_two: float32 [768], P('row')
The draws below stay inside these ranges and needn't reach their ends.
Inputs may be any that keep to these rules, and one draw needn't show every extreme that they name: lengths counts the real tokens at the start of each sequence's 1024 slots; some sequence is full and some has 1024.
All inputs are finite; a program needn't handle non-finite values.
Results may differ from the reference program's by a relative error of at most 0.02.
Values may be sent and summed in bfloat16 or wider, within the bound.
No kernel may reach another device: no remote copies, remote signals or barrier semaphores. Data moves between devices by JAX's collectives and lax.ppermute only.
A program may use at most 192 MiB of HBM per device.

```python
import math
import jax
import jax.numpy as jnp
from jax import lax

D = 768
H = 12
HD = 64
FF = 3072
LEN_MIN = 1024
TOK_DEV = 128
SEQ_LEN = 1024
TOKENS = 4096
SEQS = 4


def draw_lengths(key, part):
    key_base, key_full, key_short = jax.random.split(key, 3)
    drawn = jax.random.randint(key_base, (SEQS,), LEN_MIN, SEQ_LEN + 1)
    full_idx = jax.random.randint(key_full, (), 0, SEQS)
    short_idx = (full_idx + jax.random.randint(key_short, (), 1, SEQS)) % SEQS
    indices = jnp.arange(SEQS)
    drawn = jnp.where(indices == full_idx, SEQ_LEN, drawn)
    drawn = jnp.where(indices == short_idx, LEN_MIN, drawn)
    return drawn.astype(jnp.int32)


def block_scale(rng, extent, cuts, low, top_value):
    level = 1.0
    for dim, shards_of in cuts:
        heights = jax.random.uniform(jax.random.fold_in(jax.random.fold_in(rng, 6), dim), (shards_of,), jnp.float32, low / len(cuts), top_value / len(cuts))
        level = level * jnp.repeat(jnp.exp(heights), extent[dim] // shards_of).reshape((-1,) + (1,) * (len(extent) - 1 - dim))
    return level


def noise(own_key, dims, spread, limit, cuts=(), held_as=jnp.bfloat16):
    array = spread * jax.random.normal(own_key, dims, jnp.float32)
    if cuts:
        array = array * block_scale(own_key, dims, cuts, -0.22, 0.18)
    return jnp.clip(array, -limit, limit).astype(held_as)


def setup_inputs(seed: int = 0) -> dict:
    keys = jax.random.split(jax.random.key(seed), 14)
    tokens = noise(keys[0], (D, TOKENS), 1.0, 6.0, ((0, 4), (1, 8)))
    lengths = draw_lengths(jax.random.fold_in(keys[13], 71), 0)
    w_query = noise(keys[2], (D, D), D ** -0.5, 0.21875, ((0, 4), (1, 2)))
    w_key = noise(keys[3], (D, D), D ** -0.5, 0.21875, ((0, 4), (1, 2)))
    w_value = noise(keys[4], (D, D), D ** -0.5, 0.21875, ((0, 4), (1, 2)))
    w_out = noise(keys[5], (D, D), (max(1, D // 256)) ** -0.5, 3.5, ((0, 2), (1, 4)))
    gain_one = jnp.clip(1.0 + 0.1 * jax.random.normal(keys[6], (D,), jnp.float32), 0.5, 1.5)
    bias_one = noise(keys[7], (D,), 0.5, 3.0, ((0, 4),), jnp.float32)
    w_up = noise(keys[8], (D, FF), D ** -0.5, 0.21875, ((0, 4), (1, 2)))
    w_down = noise(keys[9], (FF, D), FF ** -0.5, 0.109375, ((0, 2), (1, 4)))
    gain_two = jnp.clip(1.0 + 0.1 * jax.random.normal(keys[10], (D,), jnp.float32), 0.5, 1.5)
    bias_two = noise(keys[11], (D,), 0.5, 3.0, ((0, 4),), jnp.float32)
    cotangent = noise(keys[12], (D, TOKENS), 1.0, 6.0, ((0, 4), (1, 8)))
    return dict(tokens=tokens, lengths=lengths, w_query=w_query, w_key=w_key, w_value=w_value, w_out=w_out, gain_one=gain_one, bias_one=bias_one, w_up=w_up, w_down=w_down, gain_two=gain_two, bias_two=bias_two, cotangent=cotangent)


norm_eps = 1e-05
highest = lax.Precision.HIGHEST

@jax.custom_vjp
def low(v):
    return lax.optimization_barrier(v.astype(jnp.bfloat16)).astype(jnp.float32)

@jax.custom_vjp
def low_back(v):
    return v

def low_keep(v):
    return (low(v), None)

def low_pass(kept, grad):
    return (grad,)

def back_keep(v):
    return (v, None)

def back_low(kept, grad):
    return (low(grad),)
low.defvjp(low_keep, low_pass)
low_back.defvjp(back_keep, back_low)

def product(left, right):
    return jnp.dot(left, right, precision=highest, preferred_element_type=jnp.float32)

def layer_norm(hidden, scale_vec, shift_vec):
    row_mean = lax.optimization_barrier(jnp.mean(hidden, -1, keepdims=True))
    centered = hidden - row_mean
    variance = lax.optimization_barrier(jnp.mean(centered * centered, -1, keepdims=True))
    return centered * lax.rsqrt(variance + norm_eps) * scale_vec + shift_vec

def attend(queries, keys_in, values_in, cos_pos, sin_pos, present):
    blocks = SEQ_LEN // TOK_DEV
    block_shape = (blocks, TOK_DEV, H, HD)
    row_ids = jnp.arange(TOK_DEV, dtype=jnp.int32)
    causal = (row_ids[:, None] >= row_ids[None, :]).astype(jnp.float32)

    def advance(running, block_in):
        s_cos, s_sin, z_cos, z_sin = running
        query_b, key_b, value_b, cos_b, sin_b, mask_b = block_in
        q_pos = jnp.maximum(query_b, 0.0)
        k_pos = jnp.maximum(key_b, 0.0) * mask_b[:, None, None]
        scores = low_back(jnp.einsum('ihd,jhd->hij', q_pos, k_pos, precision=highest))
        reweight = (cos_b[:, None] * cos_b[None, :] + sin_b[:, None] * sin_b[None, :]) * causal
        weights = scores * reweight[None]
        q_cos = q_pos * cos_b[:, None, None]
        q_sin = q_pos * sin_b[:, None, None]
        numerator = jnp.einsum('hij,jhe->ihe', low(weights), value_b, precision=highest)
        numerator = numerator + jnp.einsum('ihd,hde->ihe', q_cos, s_cos, precision=highest)
        numerator = numerator + jnp.einsum('ihd,hde->ihe', q_sin, s_sin, precision=highest)
        denominator = 1.0 + lax.optimization_barrier(jnp.sum(weights, 2)).T
        denominator = denominator + jnp.einsum('ihd,hd->ih', q_cos, z_cos, precision=highest)
        denominator = denominator + jnp.einsum('ihd,hd->ih', q_sin, z_sin, precision=highest)
        numerator = low_back(numerator)
        k_cos = k_pos * cos_b[:, None, None]
        k_sin = k_pos * sin_b[:, None, None]
        updated = (s_cos + jnp.einsum('jhd,jhe->hde', k_cos, value_b, precision=highest), s_sin + jnp.einsum('jhd,jhe->hde', k_sin, value_b, precision=highest), z_cos + lax.optimization_barrier(jnp.sum(k_cos, 0)), z_sin + lax.optimization_barrier(jnp.sum(k_sin, 0)))
        return (updated, numerator / denominator[:, :, None])
    zero_state = (jnp.zeros((H, HD, HD), jnp.float32), jnp.zeros((H, HD, HD), jnp.float32), jnp.zeros((H, HD), jnp.float32), jnp.zeros((H, HD), jnp.float32))
    block_data = (queries.reshape(block_shape), keys_in.reshape(block_shape), values_in.reshape(block_shape), cos_pos.reshape(blocks, TOK_DEV), sin_pos.reshape(blocks, TOK_DEV), present.reshape(blocks, TOK_DEV))
    final_state, results = lax.scan(jax.checkpoint(advance), zero_state, block_data)
    return results.reshape(SEQ_LEN, H, HD)

def layer(hidden, params, cos_pos, sin_pos, present):
    w_query, w_key, w_value, w_out, gain_one, bias_one, w_up, w_down, gain_two, bias_two = params
    queries = low_back(low(product(hidden, w_query))).reshape(SEQ_LEN, H, HD)
    keys_in = low_back(low(product(hidden, w_key))).reshape(SEQ_LEN, H, HD)
    values_in = low_back(low(product(hidden, w_value))).reshape(SEQ_LEN, H, HD)
    mixed = attend(queries, keys_in, values_in, cos_pos, sin_pos, present).reshape(SEQ_LEN, D)
    mixed = low_back(low(mixed))
    branch = low_back(product(mixed, w_out))
    first = layer_norm(hidden + branch, gain_one, bias_one)
    pre = low_back(product(low(first), w_up))
    act = low(jax.nn.gelu(pre, approximate=False))
    ffn = low_back(product(act, w_down))
    return layer_norm(first + ffn, gain_two, bias_two)

def reference(tokens, lengths, w_query, w_key, w_value, w_out, gain_one, bias_one, w_up, w_down, gain_two, bias_two, cotangent):
    params = tuple((weight_arg.astype(jnp.float32) for weight_arg in (w_query, w_key, w_value, w_out, gain_one, bias_one, w_up, w_down, gain_two, bias_two)))
    positions = jnp.arange(SEQ_LEN, dtype=jnp.int32)
    angles = math.pi * positions.astype(jnp.float32) / (2.0 * SEQ_LEN)
    cos_pos = jnp.cos(angles)
    sin_pos = jnp.sin(angles)
    inputs_seq = tokens.astype(jnp.float32).T.reshape(SEQS, SEQ_LEN, D)
    cot_seq = cotangent.astype(jnp.float32).T.reshape(SEQS, SEQ_LEN, D)

    def one_sequence(grad_sums, seq_in):
        hidden_in, cot_in, length_in = seq_in
        present = (positions < length_in).astype(jnp.float32)

        def forward(hidden, *weights_in):
            return layer(hidden, weights_in, cos_pos, sin_pos, present)
        result, pull = jax.vjp(forward, hidden_in, *params)
        gradients = pull(cot_in * present[:, None])
        summed = tuple((prior_sum + next_grad for prior_sum, next_grad in zip(grad_sums, gradients[1:])))
        return (summed, (result, gradients[0]))
    zero_grads = tuple((jnp.zeros_like(weight_arg) for weight_arg in params))
    grad_sums, (results, input_grads) = lax.scan(one_sequence, zero_grads, (inputs_seq, cot_seq, lengths))
    output = results.reshape(TOKENS, D).T.astype(jnp.bfloat16)
    input_grad = input_grads.reshape(TOKENS, D).T
    return (output, input_grad, grad_sums[0], grad_sums[1], grad_sums[2], grad_sums[3], grad_sums[4], grad_sums[5], grad_sums[6], grad_sums[7], grad_sums[8], grad_sums[9])
```

```python
from functools import partial
import math

import jax
import jax.numpy as jnp
from jax import lax
from jax.sharding import PartitionSpec as P

D = 768
H = 12
HD = 64
SEQ_MAX = 4096
TOK_DEV = 128


norm_eps = 1e-05
highest = lax.Precision.HIGHEST


def carried_in(shard, axis, join, neutral, backward):
    count = lax.axis_size(axis)
    place = lax.axis_index(axis)
    ahead = count - 1 - place if backward else place
    gathered = jax.tree.map(
        lambda a, kind: lax.all_gather(a.astype(kind), axis),
        shard,
        jax.tree.map(lambda a: jnp.bfloat16 if a.dtype == jnp.float32 else a.dtype, shard),
    )
    state = jax.tree.map(lambda a, e: jnp.zeros_like(a) + jnp.asarray(e, a.dtype), shard, neutral)

    def one(turn, state):
        source = count - 1 - turn if backward else turn
        return join(
            state,
            jax.tree.map(
                lambda a, own: lax.dynamic_index_in_dim(a, source, 0, False).astype(own.dtype),
                gathered,
                shard,
            ),
        )

    return lax.fori_loop(0, ahead, one, state)


def gather_cols(operand):
    return lax.all_gather(operand, "col", axis=0, tiled=True)


def gather_rows(operand):
    return lax.all_gather(operand, "row", axis=0, tiled=True)


def summed_over_rows(gathered, matrix):
    out_rows = gathered.shape[0] // lax.axis_size("row")

    def term_rows(first_row, row_count):
        sliced = lax.dynamic_slice_in_dim(gathered, first_row, row_count, 0)
        return jnp.dot(sliced, matrix, preferred_element_type=jnp.float32)

    return lax.psum_scatter(
        term_rows(jnp.int32(0), out_rows * lax.axis_size("row")),
        "row",
        scatter_dimension=0,
        tiled=True,
    )


def summed_over_cols(gathered, matrix):
    out_rows = gathered.shape[0] // lax.axis_size("col")

    def term_rows(first_row, row_count):
        sliced = lax.dynamic_slice_in_dim(gathered, first_row, row_count, 0)
        return jnp.dot(sliced, matrix, preferred_element_type=jnp.float32)

    return lax.psum_scatter(
        term_rows(jnp.int32(0), out_rows * lax.axis_size("col")).astype(jnp.bfloat16),
        "col",
        scatter_dimension=0,
        tiled=True,
    ).astype(jnp.float32)


def to_heads(stacked):
    return lax.all_to_all(stacked, "col", split_axis=1, concat_axis=2, tiled=True)


def to_tokens(stacked):
    return lax.all_to_all(stacked, "col", split_axis=2, concat_axis=1, tiled=True)


def row_totals(first_part, second_part):
    return lax.psum((first_part, second_part), "row")


def norm_forward(hidden, scale_vec, shift_vec):
    sum_one, sum_two = row_totals(jnp.sum(hidden, 1), jnp.sum(hidden * hidden, 1))
    row_mean = sum_one / D
    variance = sum_two / D - row_mean * row_mean
    inv_std = lax.rsqrt(variance + norm_eps)
    normed = (hidden - row_mean[:, None]) * inv_std[:, None]
    return (normed * scale_vec + shift_vec, normed, inv_std)


def norm_backward(grad_in, normed, inv_std, scale_vec):
    grad_normed = grad_in * scale_vec
    total_one, total_two = row_totals(jnp.sum(grad_normed, 1), jnp.sum(grad_normed * normed, 1))
    grad_hidden = inv_std[:, None] * (
        grad_normed - total_one[:, None] / D - normed * (total_two[:, None] / D)
    )
    return (grad_hidden, jnp.sum(grad_in * normed, 0), jnp.sum(grad_in, 0))


def seq_lengths(lengths, seq_ids):
    matches = seq_ids[:, None] == jnp.arange(lengths.shape[0], dtype=jnp.int32)[None, :]
    return jnp.sum(jnp.where(matches, lengths[None, :], 0), 1)


def reset_combine(earlier, later):
    keep_prior = 1.0 - later[4]
    joined = tuple(
        (
            keep_prior * prior_part + next_part
            for prior_part, next_part in zip(earlier[:4], later[:4])
        )
    )
    return joined + (jnp.maximum(earlier[4], later[4]),)


def empty_state():
    return (
        jnp.zeros((H, HD, HD), jnp.float32),
        jnp.zeros((H, HD, HD), jnp.float32),
        jnp.zeros((H, HD), jnp.float32),
        jnp.zeros((H, HD), jnp.float32),
        jnp.zeros((), jnp.float32),
    )


def attend_forward(queries, keys_in, values_in, present, cos_flat, sin_flat, opens_seq):
    block_rows = queries.shape[0]
    cos_pos = cos_flat[:, None, None]
    sin_pos = sin_flat[:, None, None]
    q_pos = jnp.maximum(queries, 0)
    k_pos = jnp.maximum(keys_in, 0) * present[:, None, None].astype(jnp.bfloat16)
    q_cos = q_pos.astype(jnp.float32) * cos_pos
    q_sin = q_pos.astype(jnp.float32) * sin_pos
    k_cos = k_pos.astype(jnp.float32) * cos_pos
    k_sin = k_pos.astype(jnp.float32) * sin_pos
    values_wide = values_in.astype(jnp.float32)
    local_state = (
        jnp.einsum("jhd,jhe->hde", k_cos, values_wide, precision=highest),
        jnp.einsum("jhd,jhe->hde", k_sin, values_wide, precision=highest),
        jnp.sum(k_cos, 0),
        jnp.sum(k_sin, 0),
    )
    arrived = carried_in(
        local_state + (opens_seq,), ("row", "col"), reset_combine, empty_state(), False
    )
    s_cos, s_sin, z_cos, z_sin = tuple(
        (state_part * (1.0 - opens_seq) for state_part in arrived[:4])
    )
    row_ids = jnp.arange(block_rows, dtype=jnp.int32)
    causal = (row_ids[:, None] >= row_ids[None, :]).astype(jnp.float32)
    reweight = (
        cos_flat[:, None] * cos_flat[None, :] + sin_flat[:, None] * sin_flat[None, :]
    ) * causal
    scores = jnp.einsum("ihd,jhd->hij", q_pos, k_pos, preferred_element_type=jnp.float32)
    weights = scores * reweight[None]
    weights_low = weights.astype(jnp.bfloat16)
    numerator = jnp.einsum(
        "hij,jhe->ihe", weights_low, values_in, preferred_element_type=jnp.float32
    )
    numerator = numerator + jnp.einsum("ihd,hde->ihe", q_cos, s_cos, precision=highest)
    numerator = numerator + jnp.einsum("ihd,hde->ihe", q_sin, s_sin, precision=highest)
    denominator = 1.0 + jnp.sum(weights, 2).T
    denominator = denominator + jnp.einsum("ihd,hd->ih", q_cos, z_cos, precision=highest)
    denominator = denominator + jnp.einsum("ihd,hd->ih", q_sin, z_sin, precision=highest)
    mixed = (numerator / denominator[:, :, None]).astype(jnp.bfloat16).reshape(block_rows, D)
    kept = (
        queries,
        keys_in,
        values_in,
        q_pos,
        k_pos,
        q_cos,
        q_sin,
        k_cos,
        k_sin,
        values_wide,
        reweight,
        weights_low,
        numerator,
        denominator,
        s_cos,
        s_sin,
        z_cos,
        z_sin,
        present,
        cos_pos,
        sin_pos,
    )
    return (mixed, kept)


def attend_backward(grad_heads, kept, closes_seq):
    (
        queries,
        keys_in,
        values_in,
        q_pos,
        k_pos,
        q_cos,
        q_sin,
        k_cos,
        k_sin,
        values_wide,
        reweight,
        weights_low,
        numerator,
        denominator,
        s_cos,
        s_sin,
        z_cos,
        z_sin,
        present,
        cos_pos,
        sin_pos,
    ) = kept
    block_rows = queries.shape[0]
    grad_attn = grad_heads.astype(jnp.float32).reshape(block_rows, H, HD)
    grad_num_low = (grad_attn / denominator[:, :, None]).astype(jnp.bfloat16)
    grad_num = grad_num_low.astype(jnp.float32)
    grad_den = -jnp.sum(grad_attn * numerator, 2) / (denominator * denominator)
    grad_weights = jnp.einsum(
        "ihe,jhe->hij", grad_num_low, values_in, preferred_element_type=jnp.float32
    )
    grad_weights = grad_weights + grad_den.T[:, :, None]
    grad_scores = (grad_weights * reweight[None]).astype(jnp.bfloat16)
    local_grad = (
        jnp.einsum("ihd,ihe->hde", q_cos, grad_num, precision=highest),
        jnp.einsum("ihd,ihe->hde", q_sin, grad_num, precision=highest),
        jnp.einsum("ihd,ih->hd", q_cos, grad_den, precision=highest),
        jnp.einsum("ihd,ih->hd", q_sin, grad_den, precision=highest),
    )
    later_sum = carried_in(
        local_grad + (closes_seq,), ("row", "col"), reset_combine, empty_state(), True
    )
    g_cos, g_sin, gz_cos, gz_sin = tuple(
        (state_part * (1.0 - closes_seq) for state_part in later_sum[:4])
    )
    grad_qpos = jnp.einsum("hij,jhd->ihd", grad_scores, k_pos, preferred_element_type=jnp.float32)
    grad_qpos = grad_qpos + cos_pos * (
        jnp.einsum("ihe,hde->ihd", grad_num, s_cos, precision=highest)
        + grad_den[:, :, None] * z_cos[None]
    )
    grad_qpos = grad_qpos + sin_pos * (
        jnp.einsum("ihe,hde->ihd", grad_num, s_sin, precision=highest)
        + grad_den[:, :, None] * z_sin[None]
    )
    grad_kpos = jnp.einsum("hij,ihd->jhd", grad_scores, q_pos, preferred_element_type=jnp.float32)
    grad_kpos = grad_kpos + cos_pos * (
        jnp.einsum("jhe,hde->jhd", values_wide, g_cos, precision=highest) + gz_cos[None]
    )
    grad_kpos = grad_kpos + sin_pos * (
        jnp.einsum("jhe,hde->jhd", values_wide, g_sin, precision=highest) + gz_sin[None]
    )
    grad_values = jnp.einsum(
        "hij,ihe->jhe", weights_low, grad_num_low, preferred_element_type=jnp.float32
    )
    grad_values = grad_values + jnp.einsum("jhd,hde->jhe", k_cos, g_cos, precision=highest)
    grad_values = grad_values + jnp.einsum("jhd,hde->jhe", k_sin, g_sin, precision=highest)
    grad_q = (grad_qpos * (queries > 0).astype(jnp.float32)).astype(jnp.bfloat16)
    grad_k = (grad_kpos * (keys_in > 0).astype(jnp.float32) * present[:, None, None]).astype(
        jnp.bfloat16
    )
    grad_v = grad_values.astype(jnp.bfloat16)
    return (
        grad_q.reshape(block_rows, D),
        grad_k.reshape(block_rows, D),
        grad_v.reshape(block_rows, D),
    )


def on_device(
    tokens,
    lengths,
    w_query,
    w_key,
    w_value,
    w_out,
    gain_one,
    bias_one,
    w_up,
    w_down,
    gain_two,
    bias_two,
    cotangent,
):
    row_count = lax.axis_size("row")
    col_count = lax.axis_size("col")
    seq_len = min(SEQ_MAX, TOK_DEV * row_count * col_count)
    data_idx = lax.axis_index("dp")
    row_idx = lax.axis_index("row")
    col_idx = lax.axis_index("col")
    feat_rows = tokens.shape[0]
    group_idx = row_idx * col_count + col_idx
    global_idx = (data_idx * row_count * col_count + group_idx) * TOK_DEV + jnp.arange(
        TOK_DEV, dtype=jnp.int32
    )
    positions = global_idx % seq_len
    present = (positions < seq_lengths(lengths, global_idx // seq_len)).astype(jnp.float32)
    angles = math.pi * positions.astype(jnp.float32) / (2.0 * seq_len)
    cos_flat = jnp.cos(angles)
    sin_flat = jnp.sin(angles)
    opens_seq = (group_idx * TOK_DEV % seq_len == 0).astype(jnp.float32)
    closes_seq = ((group_idx + 1) * TOK_DEV % seq_len == 0).astype(jnp.float32)
    token_rows = tokens.T
    width_col = w_query.shape[1]
    w_cat = jnp.concatenate([w_query, w_key, w_value], 1)
    x_gathered = gather_cols(token_rows)
    qkv = summed_over_rows(x_gathered, w_cat).astype(jnp.bfloat16)
    stacked = jnp.stack(
        [qkv[:, :width_col], qkv[:, width_col : 2 * width_col], qkv[:, 2 * width_col :]], 0
    )
    head_rows = to_heads(stacked)
    mixed, kept = attend_forward(
        head_rows[0].reshape(TOK_DEV, H, HD),
        head_rows[1].reshape(TOK_DEV, H, HD),
        head_rows[2].reshape(TOK_DEV, H, HD),
        present,
        cos_flat,
        sin_flat,
        opens_seq,
    )
    mixed_two = to_tokens(mixed[None])[0]
    mixed_gathered = gather_rows(mixed_two)
    branch = summed_over_cols(mixed_gathered, w_out)
    first, normed_one, inv_one = norm_forward(
        token_rows.astype(jnp.float32) + branch, gain_one, bias_one
    )
    first_low = first.astype(jnp.bfloat16)
    first_gathered = gather_cols(first_low)
    pre = summed_over_rows(first_gathered, w_up)
    act, gelu_pull = jax.vjp(partial(jax.nn.gelu, approximate=False), pre)
    act_low = act.astype(jnp.bfloat16)
    act_gathered = gather_rows(act_low)
    ffn = summed_over_cols(act_gathered, w_down)
    result, normed_two, inv_two = norm_forward(first + ffn, gain_two, bias_two)
    rows_one = token_rows.shape[0]
    global_one = (data_idx * col_count + col_idx) * rows_one + jnp.arange(rows_one, dtype=jnp.int32)
    present_one = (global_one % seq_len < seq_lengths(lengths, global_one // seq_len)).astype(
        jnp.float32
    )
    grad_result = cotangent.T.astype(jnp.float32) * present_one[:, None]
    grad_second, grad_gain_two, grad_bias_two = norm_backward(
        grad_result, normed_two, inv_two, gain_two
    )
    grad_ffn_gathered = gather_cols(grad_second.astype(jnp.bfloat16))
    act_again = gather_rows(act_low)
    grad_down = jnp.einsum(
        "tf,td->fd", act_again, grad_ffn_gathered, preferred_element_type=jnp.float32
    )
    grad_act = summed_over_rows(grad_ffn_gathered, w_down.T)
    grad_pre = gelu_pull(grad_act)[0].astype(jnp.bfloat16)
    grad_pre_gathered = gather_rows(grad_pre)
    first_again = gather_cols(first_low)
    grad_up = jnp.einsum(
        "td,tf->df", first_again, grad_pre_gathered, preferred_element_type=jnp.float32
    )
    grad_first = summed_over_cols(grad_pre_gathered, w_up.T) + grad_second
    grad_hidden, grad_gain_one, grad_bias_one = norm_backward(
        grad_first, normed_one, inv_one, gain_one
    )
    branch_grad_gathered = gather_cols(grad_hidden.astype(jnp.bfloat16))
    mixed_again = gather_rows(mixed_two)
    grad_out = jnp.einsum(
        "tc,tr->cr", mixed_again, branch_grad_gathered, preferred_element_type=jnp.float32
    )
    grad_mixed = summed_over_rows(branch_grad_gathered, w_out.T).astype(jnp.bfloat16)
    grad_heads = to_heads(grad_mixed[None])[0]
    grad_q, grad_k, grad_v = attend_backward(grad_heads, kept, closes_seq)
    grad_rows = to_tokens(jnp.stack([grad_q, grad_k, grad_v], 0))
    grad_cat = jnp.concatenate([grad_rows[0], grad_rows[1], grad_rows[2]], 1)
    grad_cat_gathered = gather_rows(grad_cat)
    x_again = gather_cols(token_rows)
    grad_cat_w = jnp.einsum(
        "tr,tc->rc", x_again, grad_cat_gathered, preferred_element_type=jnp.float32
    )
    input_rows = summed_over_cols(grad_cat_gathered, w_cat.T) + grad_hidden
    gain_parts = jnp.stack([grad_gain_one, grad_bias_one, grad_gain_two, grad_bias_two], 0)
    gain_sums = lax.psum(gain_parts.reshape(4 * feat_rows), "col")
    grad_query = grad_cat_w[:, :width_col]
    grad_key = grad_cat_w[:, width_col : 2 * width_col]
    grad_value = grad_cat_w[:, 2 * width_col :]
    output = result.astype(jnp.bfloat16).T
    input_grad = input_rows.T
    sums = (
        lax.psum(grad_query.astype(jnp.bfloat16), "dp").astype(jnp.float32),
        lax.psum(grad_key.astype(jnp.bfloat16), "dp").astype(jnp.float32),
        lax.psum(grad_value.astype(jnp.bfloat16), "dp").astype(jnp.float32),
        lax.psum(grad_out.astype(jnp.bfloat16), "dp").astype(jnp.float32),
        lax.psum(grad_up.astype(jnp.bfloat16), "dp").astype(jnp.float32),
        lax.psum(grad_down.astype(jnp.bfloat16), "dp").astype(jnp.float32),
        lax.psum(gain_sums.astype(jnp.bfloat16), "dp").astype(jnp.float32),
    )
    gain_total = sums[6].reshape(4, feat_rows)
    return (
        output,
        input_grad,
        sums[0],
        sums[1],
        sums[2],
        sums[3],
        gain_total[0],
        gain_total[1],
        sums[4],
        sums[5],
        gain_total[2],
        gain_total[3],
    )


def paired_layout(mesh):
    rows, cols, dps = mesh.shape["row"], mesh.shape["col"], mesh.shape["dp"]
    return cols == 2 and dps == 4 and H % (2 * cols) == 0 and TOK_DEV * rows * cols <= SEQ_MAX


def swap_cols(operand):
    return lax.ppermute(operand, "col", [(0, 1), (1, 0)])


def swap_pair(operand):
    return lax.ppermute(operand, "dp", [(i, i ^ 1) for i in range(lax.axis_size("dp"))])


def swap_copies(operand):
    return lax.ppermute(operand, "dp", [(i, i ^ 2) for i in range(lax.axis_size("dp"))])


def shift_rows(operand, step):
    count = lax.axis_size("row")
    pairs = [(i, i + step) for i in range(count) if 0 <= i + step < count]
    return lax.ppermute(operand, "row", pairs)


def rotate_rows(operand, step):
    count = lax.axis_size("row")
    return lax.ppermute(operand, "row", [(i, (i + step) % count) for i in range(count)])


def by_col(own, other):
    first_col = lax.axis_index("col") == 0
    return (jnp.where(first_col, own, other), jnp.where(first_col, other, own))


def col_part(operand, axis, other=False):
    part = operand.shape[axis] // 2
    place = lax.axis_index("col")
    place = 1 - place if other else place
    return lax.dynamic_slice_in_dim(operand, place * part, part, axis)


def spread_tokens(block):
    rows = lax.axis_size("row")
    own = col_part(block, 0)
    other = swap_cols(col_part(block, 0, True))
    wide = jnp.concatenate(by_col(own, other), 1)
    some = lax.all_to_all(wide, "row", split_axis=1, concat_axis=0, tiled=True)
    part = own.shape[0]
    count = some.shape[1]
    rest = swap_cols(some)
    pair = by_col(some.reshape(rows, 1, part, count), rest.reshape(rows, 1, part, count))
    return jnp.concatenate(pair, 1).reshape(rows * 2 * part, count)


def gather_tokens(some):
    wide = lax.all_to_all(some, "row", split_axis=0, concat_axis=1, tiled=True)
    own = col_part(wide, 1)
    other = swap_cols(col_part(wide, 1, True))
    return jnp.concatenate(by_col(own, other), 0)


def half_features(full):
    rows = lax.axis_size("row")
    feats, count = full.shape
    cut = full.reshape(rows, 2, feats // rows // 2, count)
    first_col = lax.axis_index("col") == 0
    own = jnp.where(first_col, cut[:, 0], cut[:, 1]).reshape(feats // 2, count)
    other = jnp.where(first_col, cut[:, 1], cut[:, 0]).reshape(feats // 2, count)
    return own, other


def with_pair(own):
    return jnp.concatenate([own, swap_pair(own)], 1)


def pair_sum(partial_sum):
    count = partial_sum.shape[1] // 2
    return partial_sum[:, :count] + swap_pair(
        partial_sum[:, count:].astype(jnp.bfloat16)
    ).astype(jnp.float32)


def full_sum(partial_sum):
    half = pair_sum(partial_sum)
    return half + swap_cols(half.astype(jnp.bfloat16)).astype(jnp.float32)


def dot_tn(left, right):
    return lax.dot_general(
        left, right, (((0,), (0,)), ((), ())), preferred_element_type=jnp.float32
    )


def dot_nt(left, right):
    return lax.dot_general(
        left, right, (((1,), (1,)), ((), ())), preferred_element_type=jnp.float32
    )


def dot_nn(left, right):
    return jnp.dot(left, right, preferred_element_type=jnp.float32)


def norm_columns(hidden, scale_vec, shift_vec):
    mean = jnp.mean(hidden, 0, keepdims=True)
    centered = hidden - mean
    variance = jnp.mean(centered * centered, 0, keepdims=True)
    inv_std = lax.rsqrt(variance + norm_eps)
    normed = centered * inv_std
    return (normed * scale_vec[:, None] + shift_vec[:, None], normed, inv_std)


def norm_columns_back(grad_in, normed, inv_std, scale_vec):
    grad_normed = grad_in * scale_vec[:, None]
    mean_one = jnp.mean(grad_normed, 0, keepdims=True)
    mean_two = jnp.mean(grad_normed * normed, 0, keepdims=True)
    grad_hidden = inv_std * (grad_normed - mean_one - normed * mean_two)
    return grad_hidden


def batch_dot(spec, left, right):
    return jnp.einsum(spec, left, right, preferred_element_type=jnp.float32)


def reduce_copies(own):
    total = own.astype(jnp.float32) + swap_copies(own).astype(jnp.float32)
    low = total.astype(jnp.bfloat16)
    return low, swap_pair(low)


def in_pair_order(own, other, axis):
    first = lax.axis_index("dp") % 2 == 0
    return jnp.concatenate([jnp.where(first, own, other), jnp.where(first, other, own)], axis)


def on_device_paired(
    tokens,
    lengths,
    w_query,
    w_key,
    w_value,
    w_out,
    gain_one,
    bias_one,
    w_up,
    w_down,
    gain_two,
    bias_two,
    cotangent,
):
    rows = lax.axis_size("row")
    low = jnp.bfloat16
    seq_len = TOK_DEV * rows * 2
    span = TOK_DEV * 2
    heads = H // 4
    sets = 2 * heads
    row_idx = lax.axis_index("row")
    dp_idx = lax.axis_index("dp")
    core = dp_idx % 2
    feat_rows = tokens.shape[0]

    positions = row_idx * span + jnp.arange(span, dtype=jnp.int32)
    seq_pair = jnp.stack([dp_idx, dp_idx + 1 - 2 * core])
    present = (positions[None, :] < seq_lengths(lengths, seq_pair)[:, None]).astype(jnp.float32)
    angles = math.pi * positions.astype(jnp.float32) / (2.0 * seq_len)
    cos = jnp.cos(angles)
    sin = jnp.sin(angles)

    def core_part(operand, axis):
        part = operand.shape[axis] // 2
        return lax.dynamic_slice_in_dim(operand, core * part, part, axis)

    first_block = jnp.concatenate(
        [core_part(w_query, 1), core_part(w_key, 1), core_part(w_value, 1), core_part(w_out, 0).T],
        1,
    )
    width = H * HD // 4
    first_all = gather_rows(first_block)
    w_qkv = first_all[:, : 3 * width]
    w_out_t = first_all[:, 3 * width :]
    up_all = gather_rows(core_part(w_up, 1))
    down_t = gather_rows(core_part(w_down, 0).T)
    norm_vecs = jnp.stack([gain_one, bias_one, gain_two, bias_two], 0)
    vec_parts = [norm_vecs] + [rotate_rows(norm_vecs, step) for step in range(1, rows)]
    vec_stack = jnp.stack(vec_parts, 0)
    order = (row_idx - jnp.arange(rows)) % rows
    vecs = vec_stack[order].transpose(1, 0, 2).reshape(4, D)
    gain_1, bias_1, gain_2, bias_2 = (vecs[i] for i in range(4))

    x_own = spread_tokens(tokens)
    x_pair = with_pair(x_own)
    qkv = dot_tn(w_qkv, x_pair).astype(low)

    def by_set(flat):
        parts = flat.reshape(heads, HD, 2, span)
        return parts.transpose(2, 0, 1, 3).reshape(sets, HD, span)

    def from_set(parts):
        return parts.reshape(2, heads, HD, span).transpose(1, 2, 0, 3).reshape(width, 2 * span)

    q = by_set(qkv[:width])
    k = by_set(qkv[width : 2 * width])
    v = by_set(qkv[2 * width :])
    present_set = jnp.repeat(present, heads, 0)[:, None, :]
    q_pos = jnp.maximum(q, 0)
    k_pos = jnp.maximum(k, 0) * present_set.astype(low)
    turn = jnp.stack([cos, sin], 0)[None, :, None, :]

    def turned(parts):
        wide = parts.astype(jnp.float32)[:, None] * turn
        return wide.astype(low).reshape(sets, 2 * HD, span)

    q_turn = turned(q_pos)
    k_turn = turned(k_pos)
    ones = jnp.ones((sets, 1, span), low)
    zeros = jnp.zeros((sets, 15, span), low)
    v_ext = jnp.concatenate([v, ones, zeros], 1)
    state = batch_dot("bej,bdj->bed", v_ext, k_turn)
    state_low = state.astype(low)
    arrived = [shift_rows(state_low, step).astype(jnp.float32) for step in range(1, rows)]
    prior = sum(arrived[1:], arrived[0])
    prior_low = prior.astype(low)

    ids = jnp.arange(span, dtype=jnp.int32)
    causal = (ids[:, None] <= ids[None, :]).astype(jnp.float32)
    reweight = (cos[:, None] * cos[None, :] + sin[:, None] * sin[None, :]) * causal
    scores = batch_dot("bdj,bdi->bji", k_pos, q_pos)
    weights = scores * reweight[None]
    weights_low = weights.astype(low)
    numer = batch_dot("bej,bji->bei", v, weights_low) + batch_dot(
        "bed,bdi->bei", prior_low[:, :HD], q_turn
    )
    denom = (
        1.0
        + jnp.sum(weights, 1, keepdims=True)
        + batch_dot("bed,bdi->bei", prior_low[:, HD : HD + 1], q_turn)
    )
    attn_set = (numer / denom).astype(low)
    attn = from_set(attn_set)

    branch = full_sum(dot_nn(w_out_t, attn))
    first, normed_one, inv_one = norm_columns(x_own.astype(jnp.float32) + branch, gain_1, bias_1)
    first_pair = with_pair(first.astype(low))
    pre = dot_tn(up_all, first_pair)
    act, gelu_pull = jax.vjp(partial(jax.nn.gelu, approximate=False), pre)
    act_low = act.astype(low)
    ffn = full_sum(dot_nn(down_t, act_low))
    result, normed_two, inv_two = norm_columns(first + ffn, gain_2, bias_2)

    cot = spread_tokens(cotangent)
    grad_result = cot.astype(jnp.float32) * present[0][None, :]
    grad_second = norm_columns_back(grad_result, normed_two, inv_two, gain_2)
    grad_ffn = with_pair(grad_second.astype(low))
    grad_down_t = dot_nt(grad_ffn, act_low).astype(low)
    grad_act = dot_tn(down_t, grad_ffn)
    grad_pre = gelu_pull(grad_act)[0].astype(low)
    grad_up = dot_nt(first_pair, grad_pre).astype(low)
    grad_first = full_sum(dot_nn(up_all, grad_pre)) + grad_second
    grad_hidden = norm_columns_back(grad_first, normed_one, inv_one, gain_1)
    grad_branch = with_pair(grad_hidden.astype(low))
    grad_out_t = dot_nt(grad_branch, attn).astype(low)
    grad_attn = by_set(dot_tn(w_out_t, grad_branch).astype(low)).astype(jnp.float32)

    grad_num = (grad_attn / denom).astype(low)
    grad_den = -jnp.sum(grad_attn * numer, 1, keepdims=True) / (denom * denom)
    grad_ext = jnp.concatenate([grad_num, grad_den.astype(low), zeros], 1)
    grad_state = batch_dot("bei,bdi->bed", grad_ext, q_turn)
    grad_state_low = grad_state.astype(low)
    later = [shift_rows(grad_state_low, -step).astype(jnp.float32) for step in range(1, rows)]
    after = sum(later[1:], later[0])
    after_low = after.astype(low)

    grad_scores = (
        (batch_dot("bej,bei->bji", v, grad_num) + grad_den) * reweight[None]
    ).astype(low)

    def unturned(parts):
        wide = parts.reshape(sets, 2, HD, span)
        return jnp.sum(wide * turn, 1)

    grad_qp = batch_dot("bdj,bji->bdi", k_pos, grad_scores) + unturned(
        batch_dot("bed,bei->bdi", prior_low, grad_ext)
    )
    grad_kp = batch_dot("bdi,bji->bdj", q_pos, grad_scores) + unturned(
        batch_dot("bed,bej->bdj", after_low, v_ext)
    )
    grad_v = batch_dot("bei,bji->bej", grad_num, weights_low) + batch_dot(
        "bed,bdj->bej", after_low[:, :HD], k_turn
    )
    grad_q = (grad_qp * (q > 0).astype(jnp.float32)).astype(low)
    grad_k = (grad_kp * (k > 0).astype(jnp.float32) * present_set).astype(low)
    grad_qkv = jnp.concatenate(
        [from_set(grad_q), from_set(grad_k), from_set(grad_v.astype(low))], 0
    )
    grad_w_qkv = dot_nt(x_pair, grad_qkv).astype(low)
    grad_x = pair_sum(dot_nn(w_qkv, grad_qkv))
    own_x, other_x = half_features(grad_x)
    own_h, _ = half_features(grad_hidden)
    own_x = own_x + swap_cols(other_x.astype(low)).astype(jnp.float32) + own_h
    input_grad = gather_tokens(own_x.astype(low)).astype(jnp.float32)

    out_half, _ = half_features(result.astype(low))
    output = gather_tokens(out_half)

    half_span = span // 2
    col = lax.axis_index("col")
    mine = (ids // half_span == col).astype(jnp.float32)[None, :]
    vec_sums = jnp.stack(
        [
            jnp.sum(grad_first * normed_one * mine, 1),
            jnp.sum(grad_first * mine, 1),
            jnp.sum(grad_result * normed_two * mine, 1),
            jnp.sum(grad_result * mine, 1),
        ],
        0,
    )
    vec_sums = vec_sums + swap_pair(vec_sums)
    vec_sums = vec_sums + swap_cols(vec_sums)
    vec_sums = vec_sums + swap_copies(vec_sums)
    vec_rows = vec_sums.reshape(4, rows, feat_rows)

    def vec_part(place):
        return lax.dynamic_index_in_dim(vec_rows, place % rows, 1, False)

    vec_total = vec_part(row_idx)
    for step in range(1, rows):
        vec_total = vec_total + rotate_rows(vec_part(row_idx + step), step)

    def scatter_rows(partial_grad):
        return lax.psum_scatter(partial_grad, "row", scatter_dimension=0, tiled=True)

    down_own, down_other = reduce_copies(scatter_rows(grad_down_t))
    up_own, up_other = reduce_copies(scatter_rows(grad_up))
    last_own, last_other = reduce_copies(
        scatter_rows(jnp.concatenate([grad_w_qkv, grad_out_t], 1))
    )
    down_grad = in_pair_order(down_own, down_other, 1).T.astype(jnp.float32)
    up_grad = in_pair_order(up_own, up_other, 1).astype(jnp.float32)

    def piece(index):
        cut = slice(index * width, (index + 1) * width)
        return in_pair_order(last_own[:, cut], last_other[:, cut], 1)

    query_grad, key_grad, value_grad = (piece(i).astype(jnp.float32) for i in range(3))
    out_grad = piece(3).T.astype(jnp.float32)
    return (
        output,
        input_grad,
        query_grad,
        key_grad,
        value_grad,
        out_grad,
        vec_total[0],
        vec_total[1],
        up_grad,
        down_grad,
        vec_total[2],
        vec_total[3],
    )


def solution(mesh):
    placed = (
        P("row", ("dp", "col")),
        P(),
        P("row", "col"),
        P("row", "col"),
        P("row", "col"),
        P("col", "row"),
        P("row"),
        P("row"),
        P("row", "col"),
        P("col", "row"),
        P("row"),
        P("row"),
        P("row", ("dp", "col")),
    )
    return jax.shard_map(
        on_device_paired if paired_layout(mesh) else on_device,
        mesh=mesh,
        in_specs=placed,
        out_specs=(
            P("row", ("dp", "col")),
            P("row", ("dp", "col")),
            P("row", "col"),
            P("row", "col"),
            P("row", "col"),
            P("col", "row"),
            P("row"),
            P("row"),
            P("row", "col"),
            P("col", "row"),
            P("row"),
            P("row"),
        ),
        check_vma=False,
    )
```

```python
from functools import partial
import math

import jax
import jax.numpy as jnp
from jax import lax
from jax.experimental import pallas as pl
from jax.experimental.pallas import tpu as pltpu
from jax.sharding import PartitionSpec as P

D = 768
H = 12
HD = 64
SEQ_MAX = 4096
TOK_DEV = 128


norm_eps = 1e-05
highest = lax.Precision.HIGHEST


def carried_in(shard, axis, join, neutral, backward):
    count = lax.axis_size(axis)
    place = lax.axis_index(axis)
    ahead = count - 1 - place if backward else place
    gathered = jax.tree.map(
        lambda a, kind: lax.all_gather(a.astype(kind), axis),
        shard,
        jax.tree.map(lambda a: jnp.bfloat16 if a.dtype == jnp.float32 else a.dtype, shard),
    )
    state = jax.tree.map(lambda a, e: jnp.zeros_like(a) + jnp.asarray(e, a.dtype), shard, neutral)

    def one(turn, state):
        source = count - 1 - turn if backward else turn
        return join(
            state,
            jax.tree.map(
                lambda a, own: lax.dynamic_index_in_dim(a, source, 0, False).astype(own.dtype),
                gathered,
                shard,
            ),
        )

    return lax.fori_loop(0, ahead, one, state)


def gather_cols(operand):
    return lax.all_gather(operand, "col", axis=0, tiled=True)


def gather_rows(operand):
    return lax.all_gather(operand, "row", axis=0, tiled=True)


def summed_over_rows(gathered, matrix):
    out_rows = gathered.shape[0] // lax.axis_size("row")

    def term_rows(first_row, row_count):
        sliced = lax.dynamic_slice_in_dim(gathered, first_row, row_count, 0)
        return jnp.dot(sliced, matrix, preferred_element_type=jnp.float32)

    return lax.psum_scatter(
        term_rows(jnp.int32(0), out_rows * lax.axis_size("row")),
        "row",
        scatter_dimension=0,
        tiled=True,
    )


def summed_over_cols(gathered, matrix):
    out_rows = gathered.shape[0] // lax.axis_size("col")

    def term_rows(first_row, row_count):
        sliced = lax.dynamic_slice_in_dim(gathered, first_row, row_count, 0)
        return jnp.dot(sliced, matrix, preferred_element_type=jnp.float32)

    return lax.psum_scatter(
        term_rows(jnp.int32(0), out_rows * lax.axis_size("col")).astype(jnp.bfloat16),
        "col",
        scatter_dimension=0,
        tiled=True,
    ).astype(jnp.float32)


def to_heads(stacked):
    return lax.all_to_all(stacked, "col", split_axis=1, concat_axis=2, tiled=True)


def to_tokens(stacked):
    return lax.all_to_all(stacked, "col", split_axis=2, concat_axis=1, tiled=True)


def row_totals(first_part, second_part):
    return lax.psum((first_part, second_part), "row")


def norm_forward(hidden, scale_vec, shift_vec):
    sum_one, sum_two = row_totals(jnp.sum(hidden, 1), jnp.sum(hidden * hidden, 1))
    row_mean = sum_one / D
    variance = sum_two / D - row_mean * row_mean
    inv_std = lax.rsqrt(variance + norm_eps)
    normed = (hidden - row_mean[:, None]) * inv_std[:, None]
    return (normed * scale_vec + shift_vec, normed, inv_std)


def norm_backward(grad_in, normed, inv_std, scale_vec):
    grad_normed = grad_in * scale_vec
    total_one, total_two = row_totals(jnp.sum(grad_normed, 1), jnp.sum(grad_normed * normed, 1))
    grad_hidden = inv_std[:, None] * (
        grad_normed - total_one[:, None] / D - normed * (total_two[:, None] / D)
    )
    return (grad_hidden, jnp.sum(grad_in * normed, 0), jnp.sum(grad_in, 0))


def seq_lengths(lengths, seq_ids):
    matches = seq_ids[:, None] == jnp.arange(lengths.shape[0], dtype=jnp.int32)[None, :]
    return jnp.sum(jnp.where(matches, lengths[None, :], 0), 1)


def reset_combine(earlier, later):
    keep_prior = 1.0 - later[4]
    joined = tuple(
        (
            keep_prior * prior_part + next_part
            for prior_part, next_part in zip(earlier[:4], later[:4])
        )
    )
    return joined + (jnp.maximum(earlier[4], later[4]),)


def empty_state():
    return (
        jnp.zeros((H, HD, HD), jnp.float32),
        jnp.zeros((H, HD, HD), jnp.float32),
        jnp.zeros((H, HD), jnp.float32),
        jnp.zeros((H, HD), jnp.float32),
        jnp.zeros((), jnp.float32),
    )


def attend_forward(queries, keys_in, values_in, present, cos_flat, sin_flat, opens_seq):
    block_rows = queries.shape[0]
    cos_pos = cos_flat[:, None, None]
    sin_pos = sin_flat[:, None, None]
    q_pos = jnp.maximum(queries, 0)
    k_pos = jnp.maximum(keys_in, 0) * present[:, None, None].astype(jnp.bfloat16)
    q_cos = q_pos.astype(jnp.float32) * cos_pos
    q_sin = q_pos.astype(jnp.float32) * sin_pos
    k_cos = k_pos.astype(jnp.float32) * cos_pos
    k_sin = k_pos.astype(jnp.float32) * sin_pos
    values_wide = values_in.astype(jnp.float32)
    local_state = (
        jnp.einsum("jhd,jhe->hde", k_cos, values_wide, precision=highest),
        jnp.einsum("jhd,jhe->hde", k_sin, values_wide, precision=highest),
        jnp.sum(k_cos, 0),
        jnp.sum(k_sin, 0),
    )
    arrived = carried_in(
        local_state + (opens_seq,), ("row", "col"), reset_combine, empty_state(), False
    )
    s_cos, s_sin, z_cos, z_sin = tuple(
        (state_part * (1.0 - opens_seq) for state_part in arrived[:4])
    )
    row_ids = jnp.arange(block_rows, dtype=jnp.int32)
    causal = (row_ids[:, None] >= row_ids[None, :]).astype(jnp.float32)
    reweight = (
        cos_flat[:, None] * cos_flat[None, :] + sin_flat[:, None] * sin_flat[None, :]
    ) * causal
    scores = jnp.einsum("ihd,jhd->hij", q_pos, k_pos, preferred_element_type=jnp.float32)
    weights = scores * reweight[None]
    weights_low = weights.astype(jnp.bfloat16)
    numerator = jnp.einsum(
        "hij,jhe->ihe", weights_low, values_in, preferred_element_type=jnp.float32
    )
    numerator = numerator + jnp.einsum("ihd,hde->ihe", q_cos, s_cos, precision=highest)
    numerator = numerator + jnp.einsum("ihd,hde->ihe", q_sin, s_sin, precision=highest)
    denominator = 1.0 + jnp.sum(weights, 2).T
    denominator = denominator + jnp.einsum("ihd,hd->ih", q_cos, z_cos, precision=highest)
    denominator = denominator + jnp.einsum("ihd,hd->ih", q_sin, z_sin, precision=highest)
    mixed = (numerator / denominator[:, :, None]).astype(jnp.bfloat16).reshape(block_rows, D)
    kept = (
        queries,
        keys_in,
        values_in,
        q_pos,
        k_pos,
        q_cos,
        q_sin,
        k_cos,
        k_sin,
        values_wide,
        reweight,
        weights_low,
        numerator,
        denominator,
        s_cos,
        s_sin,
        z_cos,
        z_sin,
        present,
        cos_pos,
        sin_pos,
    )
    return (mixed, kept)


def attend_backward(grad_heads, kept, closes_seq):
    (
        queries,
        keys_in,
        values_in,
        q_pos,
        k_pos,
        q_cos,
        q_sin,
        k_cos,
        k_sin,
        values_wide,
        reweight,
        weights_low,
        numerator,
        denominator,
        s_cos,
        s_sin,
        z_cos,
        z_sin,
        present,
        cos_pos,
        sin_pos,
    ) = kept
    block_rows = queries.shape[0]
    grad_attn = grad_heads.astype(jnp.float32).reshape(block_rows, H, HD)
    grad_num_low = (grad_attn / denominator[:, :, None]).astype(jnp.bfloat16)
    grad_num = grad_num_low.astype(jnp.float32)
    grad_den = -jnp.sum(grad_attn * numerator, 2) / (denominator * denominator)
    grad_weights = jnp.einsum(
        "ihe,jhe->hij", grad_num_low, values_in, preferred_element_type=jnp.float32
    )
    grad_weights = grad_weights + grad_den.T[:, :, None]
    grad_scores = (grad_weights * reweight[None]).astype(jnp.bfloat16)
    local_grad = (
        jnp.einsum("ihd,ihe->hde", q_cos, grad_num, precision=highest),
        jnp.einsum("ihd,ihe->hde", q_sin, grad_num, precision=highest),
        jnp.einsum("ihd,ih->hd", q_cos, grad_den, precision=highest),
        jnp.einsum("ihd,ih->hd", q_sin, grad_den, precision=highest),
    )
    later_sum = carried_in(
        local_grad + (closes_seq,), ("row", "col"), reset_combine, empty_state(), True
    )
    g_cos, g_sin, gz_cos, gz_sin = tuple(
        (state_part * (1.0 - closes_seq) for state_part in later_sum[:4])
    )
    grad_qpos = jnp.einsum("hij,jhd->ihd", grad_scores, k_pos, preferred_element_type=jnp.float32)
    grad_qpos = grad_qpos + cos_pos * (
        jnp.einsum("ihe,hde->ihd", grad_num, s_cos, precision=highest)
        + grad_den[:, :, None] * z_cos[None]
    )
    grad_qpos = grad_qpos + sin_pos * (
        jnp.einsum("ihe,hde->ihd", grad_num, s_sin, precision=highest)
        + grad_den[:, :, None] * z_sin[None]
    )
    grad_kpos = jnp.einsum("hij,ihd->jhd", grad_scores, q_pos, preferred_element_type=jnp.float32)
    grad_kpos = grad_kpos + cos_pos * (
        jnp.einsum("jhe,hde->jhd", values_wide, g_cos, precision=highest) + gz_cos[None]
    )
    grad_kpos = grad_kpos + sin_pos * (
        jnp.einsum("jhe,hde->jhd", values_wide, g_sin, precision=highest) + gz_sin[None]
    )
    grad_values = jnp.einsum(
        "hij,ihe->jhe", weights_low, grad_num_low, preferred_element_type=jnp.float32
    )
    grad_values = grad_values + jnp.einsum("jhd,hde->jhe", k_cos, g_cos, precision=highest)
    grad_values = grad_values + jnp.einsum("jhd,hde->jhe", k_sin, g_sin, precision=highest)
    grad_q = (grad_qpos * (queries > 0).astype(jnp.float32)).astype(jnp.bfloat16)
    grad_k = (grad_kpos * (keys_in > 0).astype(jnp.float32) * present[:, None, None]).astype(
        jnp.bfloat16
    )
    grad_v = grad_values.astype(jnp.bfloat16)
    return (
        grad_q.reshape(block_rows, D),
        grad_k.reshape(block_rows, D),
        grad_v.reshape(block_rows, D),
    )


def on_device(
    tokens,
    lengths,
    w_query,
    w_key,
    w_value,
    w_out,
    gain_one,
    bias_one,
    w_up,
    w_down,
    gain_two,
    bias_two,
    cotangent,
):
    row_count = lax.axis_size("row")
    col_count = lax.axis_size("col")
    seq_len = min(SEQ_MAX, TOK_DEV * row_count * col_count)
    data_idx = lax.axis_index("dp")
    row_idx = lax.axis_index("row")
    col_idx = lax.axis_index("col")
    feat_rows = tokens.shape[0]
    group_idx = row_idx * col_count + col_idx
    global_idx = (data_idx * row_count * col_count + group_idx) * TOK_DEV + jnp.arange(
        TOK_DEV, dtype=jnp.int32
    )
    positions = global_idx % seq_len
    present = (positions < seq_lengths(lengths, global_idx // seq_len)).astype(jnp.float32)
    angles = math.pi * positions.astype(jnp.float32) / (2.0 * seq_len)
    cos_flat = jnp.cos(angles)
    sin_flat = jnp.sin(angles)
    opens_seq = (group_idx * TOK_DEV % seq_len == 0).astype(jnp.float32)
    closes_seq = ((group_idx + 1) * TOK_DEV % seq_len == 0).astype(jnp.float32)
    token_rows = tokens.T
    width_col = w_query.shape[1]
    w_cat = jnp.concatenate([w_query, w_key, w_value], 1)
    x_gathered = gather_cols(token_rows)
    qkv = summed_over_rows(x_gathered, w_cat).astype(jnp.bfloat16)
    stacked = jnp.stack(
        [qkv[:, :width_col], qkv[:, width_col : 2 * width_col], qkv[:, 2 * width_col :]], 0
    )
    head_rows = to_heads(stacked)
    mixed, kept = attend_forward(
        head_rows[0].reshape(TOK_DEV, H, HD),
        head_rows[1].reshape(TOK_DEV, H, HD),
        head_rows[2].reshape(TOK_DEV, H, HD),
        present,
        cos_flat,
        sin_flat,
        opens_seq,
    )
    mixed_two = to_tokens(mixed[None])[0]
    mixed_gathered = gather_rows(mixed_two)
    branch = summed_over_cols(mixed_gathered, w_out)
    first, normed_one, inv_one = norm_forward(
        token_rows.astype(jnp.float32) + branch, gain_one, bias_one
    )
    first_low = first.astype(jnp.bfloat16)
    first_gathered = gather_cols(first_low)
    pre = summed_over_rows(first_gathered, w_up)
    act, gelu_pull = jax.vjp(partial(jax.nn.gelu, approximate=False), pre)
    act_low = act.astype(jnp.bfloat16)
    act_gathered = gather_rows(act_low)
    ffn = summed_over_cols(act_gathered, w_down)
    result, normed_two, inv_two = norm_forward(first + ffn, gain_two, bias_two)
    rows_one = token_rows.shape[0]
    global_one = (data_idx * col_count + col_idx) * rows_one + jnp.arange(rows_one, dtype=jnp.int32)
    present_one = (global_one % seq_len < seq_lengths(lengths, global_one // seq_len)).astype(
        jnp.float32
    )
    grad_result = cotangent.T.astype(jnp.float32) * present_one[:, None]
    grad_second, grad_gain_two, grad_bias_two = norm_backward(
        grad_result, normed_two, inv_two, gain_two
    )
    grad_ffn_gathered = gather_cols(grad_second.astype(jnp.bfloat16))
    act_again = gather_rows(act_low)
    grad_down = jnp.einsum(
        "tf,td->fd", act_again, grad_ffn_gathered, preferred_element_type=jnp.float32
    )
    grad_act = summed_over_rows(grad_ffn_gathered, w_down.T)
    grad_pre = gelu_pull(grad_act)[0].astype(jnp.bfloat16)
    grad_pre_gathered = gather_rows(grad_pre)
    first_again = gather_cols(first_low)
    grad_up = jnp.einsum(
        "td,tf->df", first_again, grad_pre_gathered, preferred_element_type=jnp.float32
    )
    grad_first = summed_over_cols(grad_pre_gathered, w_up.T) + grad_second
    grad_hidden, grad_gain_one, grad_bias_one = norm_backward(
        grad_first, normed_one, inv_one, gain_one
    )
    branch_grad_gathered = gather_cols(grad_hidden.astype(jnp.bfloat16))
    mixed_again = gather_rows(mixed_two)
    grad_out = jnp.einsum(
        "tc,tr->cr", mixed_again, branch_grad_gathered, preferred_element_type=jnp.float32
    )
    grad_mixed = summed_over_rows(branch_grad_gathered, w_out.T).astype(jnp.bfloat16)
    grad_heads = to_heads(grad_mixed[None])[0]
    grad_q, grad_k, grad_v = attend_backward(grad_heads, kept, closes_seq)
    grad_rows = to_tokens(jnp.stack([grad_q, grad_k, grad_v], 0))
    grad_cat = jnp.concatenate([grad_rows[0], grad_rows[1], grad_rows[2]], 1)
    grad_cat_gathered = gather_rows(grad_cat)
    x_again = gather_cols(token_rows)
    grad_cat_w = jnp.einsum(
        "tr,tc->rc", x_again, grad_cat_gathered, preferred_element_type=jnp.float32
    )
    input_rows = summed_over_cols(grad_cat_gathered, w_cat.T) + grad_hidden
    gain_parts = jnp.stack([grad_gain_one, grad_bias_one, grad_gain_two, grad_bias_two], 0)
    gain_sums = lax.psum(gain_parts.reshape(4 * feat_rows), "col")
    grad_query = grad_cat_w[:, :width_col]
    grad_key = grad_cat_w[:, width_col : 2 * width_col]
    grad_value = grad_cat_w[:, 2 * width_col :]
    output = result.astype(jnp.bfloat16).T
    input_grad = input_rows.T
    sums = (
        lax.psum(grad_query.astype(jnp.bfloat16), "dp").astype(jnp.float32),
        lax.psum(grad_key.astype(jnp.bfloat16), "dp").astype(jnp.float32),
        lax.psum(grad_value.astype(jnp.bfloat16), "dp").astype(jnp.float32),
        lax.psum(grad_out.astype(jnp.bfloat16), "dp").astype(jnp.float32),
        lax.psum(grad_up.astype(jnp.bfloat16), "dp").astype(jnp.float32),
        lax.psum(grad_down.astype(jnp.bfloat16), "dp").astype(jnp.float32),
        lax.psum(gain_sums.astype(jnp.bfloat16), "dp").astype(jnp.float32),
    )
    gain_total = sums[6].reshape(4, feat_rows)
    return (
        output,
        input_grad,
        sums[0],
        sums[1],
        sums[2],
        sums[3],
        gain_total[0],
        gain_total[1],
        sums[4],
        sums[5],
        gain_total[2],
        gain_total[3],
    )


def paired_layout(mesh):
    rows, cols, dps = mesh.shape["row"], mesh.shape["col"], mesh.shape["dp"]
    return cols == 2 and dps == 4 and H % (2 * cols) == 0 and TOK_DEV * rows * cols <= SEQ_MAX


low = jnp.bfloat16
wide = jnp.float32
SPAN = 2 * TOK_DEV
HEADS = H // 4
WIDTH = HEADS * HD
STATE_ROWS = 2 * HEADS * HD
SUM_ROWS = 16
SUM_LANES = 64


def swap_cols(operand):
    return lax.ppermute(operand, "col", [(0, 1), (1, 0)])


def swap_pair(operand):
    return lax.ppermute(operand, "dp", [(i, i ^ 1) for i in range(lax.axis_size("dp"))])


def swap_copies(operand):
    return lax.ppermute(operand, "dp", [(i, i ^ 2) for i in range(lax.axis_size("dp"))])


def shift_rows(operand, step):
    count = lax.axis_size("row")
    pairs = [(i, i + step) for i in range(count) if 0 <= i + step < count]
    return lax.ppermute(operand, "row", pairs)


def rotate_rows(operand, step):
    count = lax.axis_size("row")
    return lax.ppermute(operand, "row", [(i, (i + step) % count) for i in range(count)])


def by_col(own, other):
    first_col = lax.axis_index("col") == 0
    return (jnp.where(first_col, own, other), jnp.where(first_col, other, own))


def col_halves(operand, axis):
    part = operand.shape[axis] // 2
    return by_col(
        lax.slice_in_dim(operand, 0, part, axis=axis),
        lax.slice_in_dim(operand, part, 2 * part, axis=axis),
    )


def spread_tokens(blocks, extra):
    rows = lax.axis_size("row")
    row_idx = lax.axis_index("row")
    count, feats, _ = blocks.shape
    own, other = col_halves(blocks, 1)
    whole = jnp.concatenate(by_col(own, swap_cols(other)), 2)
    part = feats // 2

    def piece(place):
        cut = lax.dynamic_slice_in_dim(whole, place % rows * SPAN, SPAN, 2)
        return jnp.concatenate([cut.reshape(count * part, SPAN), extra], 0)

    total = count * part + extra.shape[0]
    buf = jnp.zeros((rows, total, SPAN), low)
    for step in range(rows):
        sent = piece(row_idx + step)
        got = rotate_rows(sent, step) if step else sent
        buf = lax.dynamic_update_slice_in_dim(buf, got[None], (row_idx - step) % rows, 0)
    halves = [buf[:, i * part : (i + 1) * part] for i in range(count)]
    return halves, buf[:, count * part :]


def join_halves(half):
    pair = by_col(half, swap_cols(half))
    return jnp.stack(pair, 1).reshape(-1, half.shape[2])


def gather_tokens(halves):
    rows = lax.axis_size("row")
    row_idx = lax.axis_index("row")
    pieces = jnp.stack(halves, 1)
    _, count, part, _ = pieces.shape
    buf = jnp.zeros((count, part, rows * SPAN), low)
    for step in range(rows):
        sent = lax.dynamic_index_in_dim(pieces, (row_idx + step) % rows, 0, False)
        got = rotate_rows(sent, step) if step else sent
        buf = lax.dynamic_update_slice_in_dim(buf, got, (row_idx - step) % rows * SPAN, 2)
    own, other = col_halves(buf, 2)
    return jnp.concatenate(by_col(own, swap_cols(other)), 1)


def feature_halves(full):
    rows = lax.axis_size("row")
    feats, count = full.shape
    cut = full.reshape(rows, 2, feats // rows // 2, count)
    return by_col(cut[:, 0], cut[:, 1])


def column_parts(own_part, other_part):
    half = (own_part + swap_pair(other_part).astype(wide)).astype(low)
    return half, swap_cols(half)


def dot_tn(left, right):
    return lax.dot_general(left, right, (((0,), (0,)), ((), ())), preferred_element_type=wide)


def dot_nt(left, right):
    return lax.dot_general(left, right, (((1,), (1,)), ((), ())), preferred_element_type=wide)


def dot_nn(left, right):
    return jnp.dot(left, right, preferred_element_type=wide)


def norm_columns(hidden, scale, shift):
    mean = jnp.mean(hidden, 0, keepdims=True)
    centered = hidden - mean
    variance = jnp.mean(centered * centered, 0, keepdims=True)
    inv_std = lax.rsqrt(variance + norm_eps)
    normed = centered * inv_std
    return (normed * scale + shift, normed, inv_std)


def norm_columns_back(grad_in, normed, inv_std, scale):
    grad_normed = grad_in * scale
    mean_one = jnp.mean(grad_normed, 0, keepdims=True)
    mean_two = jnp.mean(grad_normed * normed, 0, keepdims=True)
    return inv_std * (grad_normed - mean_one - normed * mean_two)


def local_call(body, outs, name, *operands, scratch=()):
    return pl.pallas_call(
        body,
        out_shape=[jax.ShapeDtypeStruct(shape, kind) for shape, kind in outs],
        in_specs=[
            pl.BlockSpec(memory_space=pltpu.SMEM if operand.dtype == jnp.int32 else pltpu.VMEM)
            for operand in operands
        ],
        out_specs=[pl.BlockSpec(memory_space=pltpu.VMEM)] * len(outs),
        scratch_shapes=[pltpu.VMEM(shape, kind) for shape, kind in scratch],
        compiler_params=pltpu.CompilerParams(vmem_limit_bytes=24 * 2**20),
        name=name,
    )(*operands)


def head_sets():
    return [(seq, head, seq * HEADS + head) for seq in range(2) for head in range(HEADS)]


def set_row(place):
    ids = lax.broadcasted_iota(jnp.int32, (SUM_ROWS, SPAN), 0)
    return (ids == place).astype(wide)


def turned(parts, trig_ref):
    part_wide = parts.astype(wide)
    return jnp.concatenate(
        [(part_wide * trig_ref[0:1, :]).astype(low), (part_wide * trig_ref[1:2, :]).astype(low)], 0
    )


def unturned(pair, trig_ref):
    return pair[:HD] * trig_ref[0:1, :] + pair[HD:] * trig_ref[1:2, :]


def query_part(qkv_ref, seq, head):
    return qkv_ref[seq, head * HD : (head + 1) * HD, :]


def key_part(qkv_ref, seq, head):
    return qkv_ref[seq, WIDTH + head * HD : WIDTH + (head + 1) * HD, :]


def value_part(qkv_ref, seq, head):
    return qkv_ref[seq, 2 * WIDTH + head * HD : 2 * WIDTH + (head + 1) * HD, :]


def kept_keys(qkv_ref, trig_ref, seq, head):
    keys = jnp.maximum(key_part(qkv_ref, seq, head), 0)
    return (keys.astype(wide) * trig_ref[2 + seq : 3 + seq, :]).astype(low)


def state_slice(state, place):
    return state[place * HD : (place + 1) * HD]


def pack_first_body(flags_ref, query_ref, key_ref, value_ref, out_ref, packed_ref):
    first_core = flags_ref[0] == 0
    first_copy = flags_ref[1] == 0
    for place, (left_ref, right_ref) in enumerate(((query_ref, value_ref), (key_ref, out_ref))):
        left = jnp.where(first_core, left_ref[:, :WIDTH], left_ref[:, WIDTH:])
        right = jnp.where(first_core, right_ref[:, :WIDTH], right_ref[:, WIDTH:])
        packed_ref[:, place * WIDTH : (place + 1) * WIDTH] = jnp.where(first_copy, left, right)


def pack_hidden_body(flags_ref, up_ref, down_ref, packed_ref):
    part = packed_ref.shape[1] // 2
    start = pl.multiple_of((flags_ref[0] * 2 + flags_ref[1]) * part, 128)
    packed_ref[:, :part] = up_ref[:, pl.ds(start, part)]
    packed_ref[:, part:] = down_ref[:, pl.ds(start, part)]


def project_body(
    flags_ref, mine_ref, copy_ref, own_ref, other_ref, trig_ref, weight_ref, qkv_ref, state_ref
):
    first_copy = flags_ref[1] == 0
    part = mine_ref.shape[1]
    weight_ref[:, :part] = jnp.where(first_copy, mine_ref[...], copy_ref[...])
    weight_ref[:, part:] = jnp.where(first_copy, copy_ref[...], mine_ref[...])
    matrix = weight_ref[:, : 3 * WIDTH]
    for seq, x_ref in enumerate((own_ref, other_ref)):
        qkv_ref[seq] = dot_tn(matrix, x_ref[...]).astype(low)
    sums = jnp.zeros((SUM_ROWS, 2 * HD), wide)
    for seq, head, place in head_sets():
        turned_keys = turned(kept_keys(qkv_ref, trig_ref, seq, head), trig_ref)
        values = value_part(qkv_ref, seq, head)
        state_ref[place * HD : (place + 1) * HD, :] = dot_nt(values, turned_keys).astype(low)
        sums = sums + dot_nt(set_row(place).astype(low), turned_keys)
    state_ref[STATE_ROWS:, :] = sums.astype(low)


def block_body(qkv_ref, trig_ref, reweight_ref, weights_ref, numer_ref, denom_ref):
    denoms = jnp.zeros((SUM_ROWS, SPAN), wide)
    for seq, head, place in head_sets():
        queries = jnp.maximum(query_part(qkv_ref, seq, head), 0)
        keys = kept_keys(qkv_ref, trig_ref, seq, head)
        weights = dot_tn(keys, queries) * reweight_ref[...]
        weights_low = weights.astype(low)
        weights_ref[place] = weights_low
        numer_ref[place] = dot_nn(value_part(qkv_ref, seq, head), weights_low)
        denoms = denoms + set_row(place) * jnp.sum(weights, 0, keepdims=True)
    denom_ref[...] = denoms


def attend_body(
    qkv_ref,
    trig_ref,
    numer_ref,
    denom_ref,
    weight_ref,
    *refs,
):
    arrived = refs[:-6]
    prior_ref, attn_ref, attn_wide_ref, inverse_ref, own_ref, other_ref = refs[-6:]
    total = arrived[0][...].astype(wide)
    for ref in arrived[1:]:
        total = total + ref[...].astype(wide)
    prior_ref[...] = total.astype(low)
    matrix = weight_ref[:, 3 * WIDTH : 4 * WIDTH]
    prior_sums = prior_ref[STATE_ROWS:, :]
    inverses = jnp.zeros((SUM_ROWS, SPAN), wide)
    for seq, head, place in head_sets():
        queries = turned(jnp.maximum(query_part(qkv_ref, seq, head), 0), trig_ref)
        prior = prior_ref[place * HD : (place + 1) * HD, :]
        numer = numer_ref[place] + dot_nn(prior, queries)
        denoms = dot_nn(prior_sums, queries) + denom_ref[...]
        denom = 1.0 + jnp.sum(denoms * set_row(place), 0, keepdims=True)
        inverse = 1.0 / denom
        inverses = inverses + set_row(place) * inverse
        attended = numer * inverse
        attn_wide_ref[place] = attended
        attn_ref[seq, head * HD : (head + 1) * HD, :] = attended.astype(low)
    inverse_ref[...] = inverses
    own_ref[...] = dot_nn(matrix, attn_ref[0])
    other_ref[...] = dot_nn(matrix, attn_ref[1]).astype(low)


def grad_attend_body(
    own_ref,
    other_ref,
    weight_ref,
    attn_wide_ref,
    inverse_ref,
    qkv_ref,
    trig_ref,
    grad_num_ref,
    grad_den_ref,
    state_ref,
):
    matrix = weight_ref[:, 3 * WIDTH : 4 * WIDTH]
    sums = jnp.zeros((SUM_ROWS, 2 * HD), wide)
    dens = jnp.zeros((SUM_ROWS, SPAN), wide)
    for seq, grad_ref in enumerate((own_ref, other_ref)):
        grads = dot_tn(matrix, grad_ref[...]).astype(low).astype(wide)
        for head in range(HEADS):
            place = seq * HEADS + head
            inverse = jnp.sum(inverse_ref[...] * set_row(place), 0, keepdims=True)
            scaled = grads[head * HD : (head + 1) * HD] * inverse
            grad_num = scaled.astype(low)
            grad_num_ref[place] = grad_num
            grad_den = -jnp.sum(scaled * attn_wide_ref[place], 0, keepdims=True)
            den_row = set_row(place) * grad_den
            dens = dens + den_row
            queries = turned(jnp.maximum(query_part(qkv_ref, seq, head), 0), trig_ref)
            state_ref[place * HD : (place + 1) * HD, :] = dot_nt(grad_num, queries).astype(low)
            sums = sums + dot_nt(den_row.astype(low), queries)
    state_ref[STATE_ROWS:, :] = sums.astype(low)
    grad_den_ref[...] = dens


def grad_block_body(
    grad_num_ref,
    grad_den_ref,
    qkv_ref,
    trig_ref,
    reweight_ref,
    weights_ref,
    prior_ref,
    own_ref,
    other_ref,
    attn_ref,
    grad_query_ref,
    grad_key_ref,
    grad_value_ref,
    grad_out_ref,
):
    prior_sums = prior_ref[STATE_ROWS:, :]
    for seq, head, place in head_sets():
        query = query_part(qkv_ref, seq, head)
        queries = jnp.maximum(query, 0)
        keys = kept_keys(qkv_ref, trig_ref, seq, head)
        grad_num = grad_num_ref[place]
        den_rows = grad_den_ref[...] * set_row(place)
        grad_den = jnp.sum(den_rows, 0, keepdims=True)
        grad_scores = (
            (dot_tn(value_part(qkv_ref, seq, head), grad_num) + grad_den) * reweight_ref[...]
        ).astype(low)
        prior = jnp.concatenate([prior_ref[place * HD : (place + 1) * HD, :], prior_sums], 0)
        grads = jnp.concatenate([grad_num, den_rows.astype(low)], 0)
        grad_query = dot_nn(keys, grad_scores) + unturned(dot_tn(prior, grads), trig_ref)
        grad_query_ref[seq, head * HD : (head + 1) * HD, :] = jnp.where(
            query.astype(wide) > 0, grad_query, 0.0
        ).astype(low)
        grad_key_ref[place] = dot_nt(queries, grad_scores)
        grad_value_ref[place] = dot_nt(grad_num, weights_ref[place])
    grad_out_ref[...] = (
        dot_nt(own_ref[...], attn_ref[0]) + dot_nt(other_ref[...], attn_ref[1])
    ).astype(low)


def grad_project_body(
    grad_query_ref,
    grad_key_ref,
    grad_value_ref,
    qkv_ref,
    trig_ref,
    x_own_ref,
    x_other_ref,
    weight_ref,
    vec_ref,
    flags_ref,
    *refs,
):
    arrived = refs[:-6]
    kept_ref, sent_ref, own_ref, other_ref, after_ref, grad_ref = refs[-6:]
    total = arrived[0][...].astype(wide)
    for ref in arrived[1:]:
        total = total + ref[...].astype(wide)
    after_ref[...] = total.astype(low)
    after_sums = after_ref[STATE_ROWS:, :]
    for seq, head, place in head_sets():
        key = key_part(qkv_ref, seq, head)
        keys = turned(kept_keys(qkv_ref, trig_ref, seq, head), trig_ref)
        values = value_part(qkv_ref, seq, head)
        after = after_ref[place * HD : (place + 1) * HD, :]
        left = jnp.concatenate([after, after_sums], 0)
        right = jnp.concatenate([values, set_row(place).astype(low)], 0)
        grad_key = grad_key_ref[place] + unturned(dot_tn(left, right), trig_ref)
        grad_key = jnp.where(key.astype(wide) > 0, grad_key, 0.0) * trig_ref[2 + seq : 3 + seq, :]
        grad_value = grad_value_ref[place] + dot_nn(after, keys)
        rows = slice(head * HD, (head + 1) * HD)
        grad_ref[seq, rows, :] = grad_query_ref[seq, rows, :]
        rows = slice(WIDTH + head * HD, WIDTH + (head + 1) * HD)
        grad_ref[seq, rows, :] = grad_key.astype(low)
        rows = slice(2 * WIDTH + head * HD, 2 * WIDTH + (head + 1) * HD)
        grad_ref[seq, rows, :] = grad_value.astype(low)
    matrix = weight_ref[:, : 3 * WIDTH]
    grad_w = (
        dot_nt(x_own_ref[...], grad_ref[0]) + dot_nt(x_other_ref[...], grad_ref[1])
    ).astype(low)
    rows, part, _ = kept_ref.shape
    first_copy = flags_ref[1] == 0
    for row in range(rows):
        start = row * 2 * part
        whole = jnp.concatenate(
            [grad_w[start : start + 2 * part], vec_ref[start : start + 2 * part, : 2 * SUM_LANES]],
            1,
        )[:, : 3 * WIDTH + SUM_LANES]
        first, second = whole[:part], whole[part:]
        kept_ref[row] = jnp.where(first_copy, first, second)
        sent_ref[row] = jnp.where(first_copy, second, first)
    own_ref[...] = dot_nn(matrix, grad_ref[0])
    other_ref[...] = dot_nn(matrix, grad_ref[1]).astype(low)


def norm_body(x_ref, half_ref, recv_ref, vec_ref, first_ref, low_ref, normed_ref, inv_ref):
    hidden = x_ref[...].astype(wide) + (half_ref[...].astype(wide) + recv_ref[...].astype(wide))
    first, normed, inv_std = norm_columns(hidden, vec_ref[:, 0:1], vec_ref[:, 1:2])
    first_ref[...] = first
    low_ref[...] = first.astype(low)
    normed_ref[...] = normed
    inv_ref[...] = jnp.broadcast_to(inv_std, inv_ref.shape)


def lane_sums(columns, place):
    lanes = lax.broadcasted_iota(jnp.int32, (columns[0].shape[0], 2 * SUM_LANES), 1)
    total = jnp.zeros(lanes.shape, wide)
    for shift, column in enumerate(columns):
        total = jnp.where(lanes == place + shift, jnp.sum(column, 1, keepdims=True), total)
    return total


def second_norm_body(
    first_ref, half_ref, recv_ref, vec_ref, cot_ref, trig_ref, result_ref, grad_ref, low_ref, sum_ref
):
    hidden = first_ref[...] + (half_ref[...].astype(wide) + recv_ref[...].astype(wide))
    scale = vec_ref[:, 2:3]
    result, normed, inv_std = norm_columns(hidden, scale, vec_ref[:, 3:4])
    result_ref[...] = result.astype(low)
    grad_in = cot_ref[...].astype(wide) * trig_ref[2:3, :]
    grad = norm_columns_back(grad_in, normed, inv_std, scale)
    grad_ref[...] = grad
    low_ref[...] = grad.astype(low)
    sum_ref[...] = lane_sums((grad_in * normed, grad_in), 2)


def norm_back_body(
    grad_ref, half_ref, recv_ref, normed_ref, inv_ref, vec_ref, part_ref, hidden_ref, low_ref, sum_ref
):
    grad_in = grad_ref[...] + (half_ref[...].astype(wide) + recv_ref[...].astype(wide))
    normed = normed_ref[...]
    grad = norm_columns_back(grad_in, normed, inv_ref[0:1, :], vec_ref[:, 0:1])
    hidden_ref[...] = grad
    low_ref[...] = grad.astype(low)
    sum_ref[...] = (lane_sums((grad_in * normed, grad_in), 0) + part_ref[...]).astype(low)


def hidden_body(weight_ref, own_ref, other_ref, *refs):
    act_ref, slope_ref, part_own_ref, part_other_ref = refs[-4:]
    earlier = refs[:-4]
    part = act_ref.shape[0]
    up = weight_ref[:, :part]
    down = weight_ref[:, part:]
    for seq, (x_ref, part_ref) in enumerate(
        ((own_ref, part_own_ref), (other_ref, part_other_ref))
    ):
        cols = slice(seq * SPAN, (seq + 1) * SPAN)
        act, slope = gelu_and_slope(dot_tn(up, x_ref[...]))
        act_ref[:, cols] = act
        slope_ref[:, cols] = slope
        total = dot_nn(down, act)
        if earlier:
            total = total + earlier[seq][...]
        part_ref[...] = total.astype(part_ref.dtype)


def hidden_back_body(
    own_ref,
    other_ref,
    mine_ref,
    copy_ref,
    slope_mine_ref,
    slope_copy_ref,
    pre_mine_ref,
    pre_copy_ref,
    part_own_ref,
    part_other_ref,
):
    part = slope_mine_ref.shape[0]
    for seq, (x_ref, part_ref) in enumerate(
        ((own_ref, part_own_ref), (other_ref, part_other_ref))
    ):
        cols = slice(seq * SPAN, (seq + 1) * SPAN)
        total = None
        for weight_ref, slope_ref, pre_ref in (
            (mine_ref, slope_mine_ref, pre_mine_ref),
            (copy_ref, slope_copy_ref, pre_copy_ref),
        ):
            grad_pre = (dot_tn(weight_ref[:, part:], x_ref[...]) * slope_ref[:, cols]).astype(low)
            pre_ref[:, cols] = grad_pre
            term = dot_nn(weight_ref[:, :part], grad_pre)
            total = term if total is None else total + term
        part_ref[...] = total.astype(part_ref.dtype)


def pair_grad_body(own_ref, other_ref, mine_ref, copy_ref, kept_ref, sent_ref):
    for hidden_ref, out_ref in ((copy_ref, sent_ref), (mine_ref, kept_ref)):
        out_ref[...] = (
            dot_nt(own_ref[...], hidden_ref[:, :SPAN]) + dot_nt(other_ref[...], hidden_ref[:, SPAN:])
        ).astype(low)


def place_hidden(flags_ref, refs, out_ref):
    part = out_ref.shape[1] // 4
    core, copy = flags_ref[0], flags_ref[1]
    for ref, other_core, other_copy in zip(refs, (0, 0, 1, 1), (0, 1, 0, 1)):
        core_place = 1 - core if other_core else core
        copy_place = 1 - copy if other_copy else copy
        start = pl.multiple_of((core_place * 2 + copy_place) * part, 128)
        out_ref[:, pl.ds(start, part)] = ref[:, :part].astype(wide)


def place_down_body(flags_ref, *refs):
    place_hidden(flags_ref, refs[:4], refs[4])


def place_up_body(flags_ref, *refs):
    up_ref, out_ref = refs[4:]
    place_hidden(flags_ref, refs[:4], up_ref)
    part = up_ref.shape[1] // 4
    sums = [ref[:, part : part + WIDTH].astype(wide) for ref in refs[:4]]
    own, other = sums[0] + sums[1], sums[2] + sums[3]
    first_core = flags_ref[0] == 0
    out_ref[:, :WIDTH] = jnp.where(first_core, own, other)
    out_ref[:, WIDTH:] = jnp.where(first_core, other, own)


def place_last_body(flags_ref, *refs):
    outs, vec_ref = refs[4:7], refs[7]
    first_core = flags_ref[0] == 0
    part = refs[0].shape[0]
    for own_ref, other_ref, other_copy in ((refs[0], refs[2], 0), (refs[1], refs[3], 1)):
        copy = 1 - flags_ref[1] if other_copy else flags_ref[1]
        rows = pl.ds(pl.multiple_of(copy * part, 8), part)
        own, other = own_ref[...].astype(wide), other_ref[...].astype(wide)
        for place, out_ref in enumerate(outs):
            cols = slice(place * WIDTH, (place + 1) * WIDTH)
            out_ref[rows, :WIDTH] = jnp.where(first_core, own[:, cols], other[:, cols])
            out_ref[rows, WIDTH:] = jnp.where(first_core, other[:, cols], own[:, cols])
        vec_ref[rows, :] = own[:, 3 * WIDTH :] + other[:, 3 * WIDTH :]


def gelu_and_slope(pre):
    cdf = 0.5 * (1.0 + lax.erf(pre * math.sqrt(0.5)))
    density = jnp.exp(-0.5 * pre * pre) * (1.0 / math.sqrt(2.0 * math.pi))
    return (pre * cdf).astype(low), (cdf + pre * density)


def all_quarters(own):
    copied = swap_copies(own)
    return own, copied, swap_pair(own), swap_pair(copied)


def on_device_paired(
    tokens,
    lengths,
    w_query,
    w_key,
    w_value,
    w_out,
    gain_one,
    bias_one,
    w_up,
    w_down,
    gain_two,
    bias_two,
    cotangent,
):
    rows = lax.axis_size("row")
    seq_len = SPAN * rows
    row_idx = lax.axis_index("row")
    dp_idx = lax.axis_index("dp")
    core = dp_idx % 2
    feat_rows = tokens.shape[0]

    positions = row_idx * SPAN + jnp.arange(SPAN, dtype=jnp.int32)
    seq_pair = jnp.stack([dp_idx, dp_idx + 1 - 2 * core])
    present = (positions[None, :] < seq_lengths(lengths, seq_pair)[:, None]).astype(wide)
    angles = math.pi * positions.astype(wide) / (2.0 * seq_len)
    cos = jnp.cos(angles)
    sin = jnp.sin(angles)
    ids = jnp.arange(SPAN, dtype=jnp.int32)
    causal = (ids[:, None] <= ids[None, :]).astype(wide)
    reweight = (cos[:, None] * cos[None, :] + sin[:, None] * sin[None, :]) * causal
    trig = jnp.concatenate([jnp.stack([cos, sin], 0), present, jnp.zeros((4, SPAN), wide)], 0)

    flags = jnp.stack([core, dp_idx // 2])

    part = w_up.shape[1] // 4
    (first_packed,) = local_call(
        pack_first_body,
        [((feat_rows, 2 * WIDTH), low)],
        "pack_first",
        flags,
        w_query,
        w_key,
        w_value,
        w_out.T,
    )
    (hidden_packed,) = local_call(
        pack_hidden_body, [((feat_rows, 2 * part), low)], "pack_hidden", flags, w_up, w_down.T
    )
    first_mine = gather_rows(first_packed)
    hidden_mine = gather_rows(hidden_packed)
    first_copy = swap_copies(first_mine)
    hidden_copy = swap_copies(hidden_mine)

    vecs = jnp.stack([gain_one, bias_one, gain_two, bias_two], 0)
    vecs_high = vecs.astype(low)
    vecs_rest = (vecs - vecs_high.astype(wide)).astype(low)
    vec_rows = 8 * feat_rows // SPAN
    extra = jnp.concatenate(
        [
            jnp.stack([vecs_high, vecs_rest], 0).reshape(vec_rows, SPAN),
            jnp.zeros((-vec_rows % 16, SPAN), low),
        ],
        0,
    )
    (x_half, cot_half), got_vecs = spread_tokens(jnp.stack([tokens, cotangent], 0), extra)
    x_own = join_halves(x_half)
    x_other = swap_pair(x_own)
    cot = join_halves(cot_half)
    got_vecs = got_vecs[:, :vec_rows].reshape(rows, 2, 4, feat_rows).astype(wide)
    norm_vecs = (got_vecs[:, 0] + got_vecs[:, 1]).transpose(0, 2, 1).reshape(D, 4)

    state_shape = ((STATE_ROWS + SUM_ROWS, 2 * HD), low)
    sets = 2 * HEADS
    block_low = ((D, SPAN), low)
    block_wide = ((D, SPAN), wide)
    weight, qkv, state = local_call(
        project_body,
        [((D, 4 * WIDTH), low), ((2, 3 * WIDTH, SPAN), low), state_shape],
        "project",
        flags,
        first_mine,
        first_copy,
        x_own,
        x_other,
        trig,
    )
    arrived = [shift_rows(state, step) for step in range(1, rows)]
    weights, numer, denom = local_call(
        block_body,
        [((sets, SPAN, SPAN), low), ((sets, HD, SPAN), wide), ((SUM_ROWS, SPAN), wide)],
        "block",
        qkv,
        trig,
        reweight,
    )
    prior, attn, attn_wide, inverse, branch_own, branch_other = local_call(
        attend_body,
        [
            state_shape,
            ((2, WIDTH, SPAN), low),
            ((sets, HD, SPAN), wide),
            ((SUM_ROWS, SPAN), wide),
            block_wide,
            block_low,
        ],
        "attend",
        qkv,
        trig,
        numer,
        denom,
        weight,
        *arrived,
    )
    branch = column_parts(branch_own, branch_other)
    first, first_low, normed, inv_std = local_call(
        norm_body,
        [block_wide, block_low, block_wide, ((8, SPAN), wide)],
        "norm",
        x_own,
        *branch,
        norm_vecs,
    )
    first_other = swap_pair(first_low)
    half_hidden = [((part, 2 * SPAN), low), ((part, 2 * SPAN), wide)]
    act_mine, slope_mine, ffn_own, ffn_other = local_call(
        hidden_body,
        half_hidden + [block_wide, block_wide],
        "hidden_mine",
        hidden_mine,
        first_low,
        first_other,
    )
    act_copy, slope_copy, ffn_own, ffn_other = local_call(
        hidden_body,
        half_hidden + [block_wide, block_low],
        "hidden_copy",
        hidden_copy,
        first_low,
        first_other,
        ffn_own,
        ffn_other,
    )
    ffn = column_parts(ffn_own, ffn_other)
    result, grad_second, grad_ffn, sums_two = local_call(
        second_norm_body,
        [block_low, block_wide, block_low, ((D, 2 * SUM_LANES), wide)],
        "second_norm",
        first,
        *ffn,
        norm_vecs,
        cot,
        trig,
    )
    grad_ffn_other = swap_pair(grad_ffn)
    hidden_low = ((part, 2 * SPAN), low)
    pre_mine, pre_copy, first_own_part, first_other_part = local_call(
        hidden_back_body,
        [hidden_low, hidden_low, block_wide, block_low],
        "hidden_back",
        grad_ffn,
        grad_ffn_other,
        hidden_mine,
        hidden_copy,
        slope_mine,
        slope_copy,
    )
    first_sum = column_parts(first_own_part, first_other_part)

    def hidden_grad(own, other, mine, copied, name):
        kept, sent = local_call(
            pair_grad_body,
            [((D, part), low), ((D, part), low)],
            name,
            own,
            other,
            mine,
            copied,
        )
        return (kept.astype(wide) + swap_copies(sent).astype(wide)).astype(low)

    def scatter_rows(partial_grad):
        return lax.psum_scatter(partial_grad, "row", scatter_dimension=0, tiled=True)

    down_rows = scatter_rows(
        hidden_grad(grad_ffn, grad_ffn_other, act_mine, act_copy, "grad_down")
    )
    up_part = hidden_grad(first_low, first_other, pre_mine, pre_copy, "grad_up")
    grad_hidden, branch_grad, vec_sums = local_call(
        norm_back_body,
        [block_wide, block_low, ((D, 2 * SUM_LANES), low)],
        "norm_back",
        grad_second,
        *first_sum,
        normed,
        inv_std,
        norm_vecs,
        sums_two,
    )
    branch_grad_other = swap_pair(branch_grad)
    grad_num, grad_den, grad_state = local_call(
        grad_attend_body,
        [((sets, HD, SPAN), low), ((SUM_ROWS, SPAN), wide), state_shape],
        "grad_attend",
        branch_grad,
        branch_grad_other,
        weight,
        attn_wide,
        inverse,
        qkv,
        trig,
    )
    later = [shift_rows(grad_state, -step) for step in range(1, rows)]
    grad_query, grad_key, grad_value, grad_out = local_call(
        grad_block_body,
        [
            ((2, WIDTH, SPAN), low),
            ((sets, HD, SPAN), wide),
            ((sets, HD, SPAN), wide),
            ((D, WIDTH), low),
        ],
        "grad_block",
        grad_num,
        grad_den,
        qkv,
        trig,
        reweight,
        weights,
        prior,
        branch_grad,
        branch_grad_other,
        attn,
    )
    up_part, grad_out, down_rows = lax.optimization_barrier((up_part, grad_out, down_rows))
    up_rows = scatter_rows(jnp.concatenate([up_part, grad_out], 1))
    half_rows = ((rows, feat_rows // 2, 3 * WIDTH + SUM_LANES), low)
    kept_w, sent_w, x_grad_own, x_grad_other = local_call(
        grad_project_body,
        [half_rows, half_rows, block_wide, block_low],
        "grad_project",
        grad_query,
        grad_key,
        grad_value,
        qkv,
        trig,
        x_own,
        x_other,
        weight,
        vec_sums,
        flags,
        *later,
        scratch=[state_shape, ((2, 3 * WIDTH, SPAN), low)],
    )
    half_w = (kept_w.astype(wide) + swap_copies(sent_w).astype(wide)).astype(low)

    own_x, other_x = feature_halves(x_grad_own + swap_pair(x_grad_other).astype(wide))
    own_h, _ = feature_halves(grad_hidden)
    own_x = own_x + swap_cols(other_x.astype(low)).astype(wide) + own_h
    out_half, _ = feature_halves(result)
    placed_back = gather_tokens([own_x.astype(low), out_half])
    input_grad = placed_back[0].astype(wide)
    output = placed_back[1]

    last_rows = lax.dynamic_index_in_dim(half_w, row_idx, 0, False).astype(wide)
    for step in range(1, rows):
        sent = lax.dynamic_index_in_dim(half_w, (row_idx + step) % rows, 0, False)
        last_rows = last_rows + rotate_rows(sent, step).astype(wide)

    (down_t,) = local_call(
        place_down_body,
        [((feat_rows, 4 * part), wide)],
        "place_down",
        flags,
        *all_quarters(down_rows),
    )
    up_grad, out_t = local_call(
        place_up_body,
        [((feat_rows, 4 * part), wide), ((feat_rows, 2 * WIDTH), wide)],
        "place_up",
        flags,
        *all_quarters(up_rows),
    )
    query_grad, key_grad, value_grad, vec_total = local_call(
        place_last_body,
        [((feat_rows, 2 * WIDTH), wide)] * 3 + [((feat_rows, SUM_LANES), wide)],
        "place_last",
        flags,
        *all_quarters(last_rows.astype(low)),
    )
    return (
        output,
        input_grad,
        query_grad,
        key_grad,
        value_grad,
        out_t.T,
        vec_total[:, 0],
        vec_total[:, 1],
        up_grad,
        down_t.T,
        vec_total[:, 2],
        vec_total[:, 3],
    )


def solution(mesh):
    placed = (
        P("row", ("dp", "col")),
        P(),
        P("row", "col"),
        P("row", "col"),
        P("row", "col"),
        P("col", "row"),
        P("row"),
        P("row"),
        P("row", "col"),
        P("col", "row"),
        P("row"),
        P("row"),
        P("row", ("dp", "col")),
    )
    return jax.shard_map(
        on_device_paired if paired_layout(mesh) else on_device,
        mesh=mesh,
        in_specs=placed,
        out_specs=(
            P("row", ("dp", "col")),
            P("row", ("dp", "col")),
            P("row", "col"),
            P("row", "col"),
            P("row", "col"),
            P("col", "row"),
            P("row"),
            P("row"),
            P("row", "col"),
            P("col", "row"),
            P("row"),
            P("row"),
        ),
        check_vma=False,
    )
```

```python
from functools import partial
import math

import jax
import jax.numpy as jnp
from jax import lax
from jax.experimental import pallas as pl
from jax.experimental.pallas import tpu as pltpu
from jax.sharding import PartitionSpec as P

D = 768
H = 12
HD = 64
SEQ_MAX = 4096
TOK_DEV = 128


norm_eps = 1e-05
highest = lax.Precision.HIGHEST


def carried_in(shard, axis, join, neutral, backward):
    count = lax.axis_size(axis)
    place = lax.axis_index(axis)
    ahead = count - 1 - place if backward else place
    gathered = jax.tree.map(
        lambda a, kind: lax.all_gather(a.astype(kind), axis),
        shard,
        jax.tree.map(lambda a: jnp.bfloat16 if a.dtype == jnp.float32 else a.dtype, shard),
    )
    state = jax.tree.map(lambda a, e: jnp.zeros_like(a) + jnp.asarray(e, a.dtype), shard, neutral)

    def one(turn, state):
        source = count - 1 - turn if backward else turn
        return join(
            state,
            jax.tree.map(
                lambda a, own: lax.dynamic_index_in_dim(a, source, 0, False).astype(own.dtype),
                gathered,
                shard,
            ),
        )

    return lax.fori_loop(0, ahead, one, state)


def gather_cols(operand):
    return lax.all_gather(operand, "col", axis=0, tiled=True)


def gather_rows(operand):
    return lax.all_gather(operand, "row", axis=0, tiled=True)


def summed_over_rows(gathered, matrix):
    out_rows = gathered.shape[0] // lax.axis_size("row")

    def term_rows(first_row, row_count):
        sliced = lax.dynamic_slice_in_dim(gathered, first_row, row_count, 0)
        return jnp.dot(sliced, matrix, preferred_element_type=jnp.float32)

    return lax.psum_scatter(
        term_rows(jnp.int32(0), out_rows * lax.axis_size("row")),
        "row",
        scatter_dimension=0,
        tiled=True,
    )


def summed_over_cols(gathered, matrix):
    out_rows = gathered.shape[0] // lax.axis_size("col")

    def term_rows(first_row, row_count):
        sliced = lax.dynamic_slice_in_dim(gathered, first_row, row_count, 0)
        return jnp.dot(sliced, matrix, preferred_element_type=jnp.float32)

    return lax.psum_scatter(
        term_rows(jnp.int32(0), out_rows * lax.axis_size("col")).astype(jnp.bfloat16),
        "col",
        scatter_dimension=0,
        tiled=True,
    ).astype(jnp.float32)


def to_heads(stacked):
    return lax.all_to_all(stacked, "col", split_axis=1, concat_axis=2, tiled=True)


def to_tokens(stacked):
    return lax.all_to_all(stacked, "col", split_axis=2, concat_axis=1, tiled=True)


def row_totals(first_part, second_part):
    return lax.psum((first_part, second_part), "row")


def norm_forward(hidden, scale_vec, shift_vec):
    sum_one, sum_two = row_totals(jnp.sum(hidden, 1), jnp.sum(hidden * hidden, 1))
    row_mean = sum_one / D
    variance = sum_two / D - row_mean * row_mean
    inv_std = lax.rsqrt(variance + norm_eps)
    normed = (hidden - row_mean[:, None]) * inv_std[:, None]
    return (normed * scale_vec + shift_vec, normed, inv_std)


def norm_backward(grad_in, normed, inv_std, scale_vec):
    grad_normed = grad_in * scale_vec
    total_one, total_two = row_totals(jnp.sum(grad_normed, 1), jnp.sum(grad_normed * normed, 1))
    grad_hidden = inv_std[:, None] * (
        grad_normed - total_one[:, None] / D - normed * (total_two[:, None] / D)
    )
    return (grad_hidden, jnp.sum(grad_in * normed, 0), jnp.sum(grad_in, 0))


def seq_lengths(lengths, seq_ids):
    matches = seq_ids[:, None] == jnp.arange(lengths.shape[0], dtype=jnp.int32)[None, :]
    return jnp.sum(jnp.where(matches, lengths[None, :], 0), 1)


def reset_combine(earlier, later):
    keep_prior = 1.0 - later[4]
    joined = tuple(
        (
            keep_prior * prior_part + next_part
            for prior_part, next_part in zip(earlier[:4], later[:4])
        )
    )
    return joined + (jnp.maximum(earlier[4], later[4]),)


def empty_state():
    return (
        jnp.zeros((H, HD, HD), jnp.float32),
        jnp.zeros((H, HD, HD), jnp.float32),
        jnp.zeros((H, HD), jnp.float32),
        jnp.zeros((H, HD), jnp.float32),
        jnp.zeros((), jnp.float32),
    )


def attend_forward(queries, keys_in, values_in, present, cos_flat, sin_flat, opens_seq):
    block_rows = queries.shape[0]
    cos_pos = cos_flat[:, None, None]
    sin_pos = sin_flat[:, None, None]
    q_pos = jnp.maximum(queries, 0)
    k_pos = jnp.maximum(keys_in, 0) * present[:, None, None].astype(jnp.bfloat16)
    q_cos = q_pos.astype(jnp.float32) * cos_pos
    q_sin = q_pos.astype(jnp.float32) * sin_pos
    k_cos = k_pos.astype(jnp.float32) * cos_pos
    k_sin = k_pos.astype(jnp.float32) * sin_pos
    values_wide = values_in.astype(jnp.float32)
    local_state = (
        jnp.einsum("jhd,jhe->hde", k_cos, values_wide, precision=highest),
        jnp.einsum("jhd,jhe->hde", k_sin, values_wide, precision=highest),
        jnp.sum(k_cos, 0),
        jnp.sum(k_sin, 0),
    )
    arrived = carried_in(
        local_state + (opens_seq,), ("row", "col"), reset_combine, empty_state(), False
    )
    s_cos, s_sin, z_cos, z_sin = tuple(
        (state_part * (1.0 - opens_seq) for state_part in arrived[:4])
    )
    row_ids = jnp.arange(block_rows, dtype=jnp.int32)
    causal = (row_ids[:, None] >= row_ids[None, :]).astype(jnp.float32)
    reweight = (
        cos_flat[:, None] * cos_flat[None, :] + sin_flat[:, None] * sin_flat[None, :]
    ) * causal
    scores = jnp.einsum("ihd,jhd->hij", q_pos, k_pos, preferred_element_type=jnp.float32)
    weights = scores * reweight[None]
    weights_low = weights.astype(jnp.bfloat16)
    numerator = jnp.einsum(
        "hij,jhe->ihe", weights_low, values_in, preferred_element_type=jnp.float32
    )
    numerator = numerator + jnp.einsum("ihd,hde->ihe", q_cos, s_cos, precision=highest)
    numerator = numerator + jnp.einsum("ihd,hde->ihe", q_sin, s_sin, precision=highest)
    denominator = 1.0 + jnp.sum(weights, 2).T
    denominator = denominator + jnp.einsum("ihd,hd->ih", q_cos, z_cos, precision=highest)
    denominator = denominator + jnp.einsum("ihd,hd->ih", q_sin, z_sin, precision=highest)
    mixed = (numerator / denominator[:, :, None]).astype(jnp.bfloat16).reshape(block_rows, D)
    kept = (
        queries,
        keys_in,
        values_in,
        q_pos,
        k_pos,
        q_cos,
        q_sin,
        k_cos,
        k_sin,
        values_wide,
        reweight,
        weights_low,
        numerator,
        denominator,
        s_cos,
        s_sin,
        z_cos,
        z_sin,
        present,
        cos_pos,
        sin_pos,
    )
    return (mixed, kept)


def attend_backward(grad_heads, kept, closes_seq):
    (
        queries,
        keys_in,
        values_in,
        q_pos,
        k_pos,
        q_cos,
        q_sin,
        k_cos,
        k_sin,
        values_wide,
        reweight,
        weights_low,
        numerator,
        denominator,
        s_cos,
        s_sin,
        z_cos,
        z_sin,
        present,
        cos_pos,
        sin_pos,
    ) = kept
    block_rows = queries.shape[0]
    grad_attn = grad_heads.astype(jnp.float32).reshape(block_rows, H, HD)
    grad_num_low = (grad_attn / denominator[:, :, None]).astype(jnp.bfloat16)
    grad_num = grad_num_low.astype(jnp.float32)
    grad_den = -jnp.sum(grad_attn * numerator, 2) / (denominator * denominator)
    grad_weights = jnp.einsum(
        "ihe,jhe->hij", grad_num_low, values_in, preferred_element_type=jnp.float32
    )
    grad_weights = grad_weights + grad_den.T[:, :, None]
    grad_scores = (grad_weights * reweight[None]).astype(jnp.bfloat16)
    local_grad = (
        jnp.einsum("ihd,ihe->hde", q_cos, grad_num, precision=highest),
        jnp.einsum("ihd,ihe->hde", q_sin, grad_num, precision=highest),
        jnp.einsum("ihd,ih->hd", q_cos, grad_den, precision=highest),
        jnp.einsum("ihd,ih->hd", q_sin, grad_den, precision=highest),
    )
    later_sum = carried_in(
        local_grad + (closes_seq,), ("row", "col"), reset_combine, empty_state(), True
    )
    g_cos, g_sin, gz_cos, gz_sin = tuple(
        (state_part * (1.0 - closes_seq) for state_part in later_sum[:4])
    )
    grad_qpos = jnp.einsum("hij,jhd->ihd", grad_scores, k_pos, preferred_element_type=jnp.float32)
    grad_qpos = grad_qpos + cos_pos * (
        jnp.einsum("ihe,hde->ihd", grad_num, s_cos, precision=highest)
        + grad_den[:, :, None] * z_cos[None]
    )
    grad_qpos = grad_qpos + sin_pos * (
        jnp.einsum("ihe,hde->ihd", grad_num, s_sin, precision=highest)
        + grad_den[:, :, None] * z_sin[None]
    )
    grad_kpos = jnp.einsum("hij,ihd->jhd", grad_scores, q_pos, preferred_element_type=jnp.float32)
    grad_kpos = grad_kpos + cos_pos * (
        jnp.einsum("jhe,hde->jhd", values_wide, g_cos, precision=highest) + gz_cos[None]
    )
    grad_kpos = grad_kpos + sin_pos * (
        jnp.einsum("jhe,hde->jhd", values_wide, g_sin, precision=highest) + gz_sin[None]
    )
    grad_values = jnp.einsum(
        "hij,ihe->jhe", weights_low, grad_num_low, preferred_element_type=jnp.float32
    )
    grad_values = grad_values + jnp.einsum("jhd,hde->jhe", k_cos, g_cos, precision=highest)
    grad_values = grad_values + jnp.einsum("jhd,hde->jhe", k_sin, g_sin, precision=highest)
    grad_q = (grad_qpos * (queries > 0).astype(jnp.float32)).astype(jnp.bfloat16)
    grad_k = (grad_kpos * (keys_in > 0).astype(jnp.float32) * present[:, None, None]).astype(
        jnp.bfloat16
    )
    grad_v = grad_values.astype(jnp.bfloat16)
    return (
        grad_q.reshape(block_rows, D),
        grad_k.reshape(block_rows, D),
        grad_v.reshape(block_rows, D),
    )


def on_device(
    tokens,
    lengths,
    w_query,
    w_key,
    w_value,
    w_out,
    gain_one,
    bias_one,
    w_up,
    w_down,
    gain_two,
    bias_two,
    cotangent,
):
    row_count = lax.axis_size("row")
    col_count = lax.axis_size("col")
    seq_len = min(SEQ_MAX, TOK_DEV * row_count * col_count)
    data_idx = lax.axis_index("dp")
    row_idx = lax.axis_index("row")
    col_idx = lax.axis_index("col")
    feat_rows = tokens.shape[0]
    group_idx = row_idx * col_count + col_idx
    global_idx = (data_idx * row_count * col_count + group_idx) * TOK_DEV + jnp.arange(
        TOK_DEV, dtype=jnp.int32
    )
    positions = global_idx % seq_len
    present = (positions < seq_lengths(lengths, global_idx // seq_len)).astype(jnp.float32)
    angles = math.pi * positions.astype(jnp.float32) / (2.0 * seq_len)
    cos_flat = jnp.cos(angles)
    sin_flat = jnp.sin(angles)
    opens_seq = (group_idx * TOK_DEV % seq_len == 0).astype(jnp.float32)
    closes_seq = ((group_idx + 1) * TOK_DEV % seq_len == 0).astype(jnp.float32)
    token_rows = tokens.T
    width_col = w_query.shape[1]
    w_cat = jnp.concatenate([w_query, w_key, w_value], 1)
    x_gathered = gather_cols(token_rows)
    qkv = summed_over_rows(x_gathered, w_cat).astype(jnp.bfloat16)
    stacked = jnp.stack(
        [qkv[:, :width_col], qkv[:, width_col : 2 * width_col], qkv[:, 2 * width_col :]], 0
    )
    head_rows = to_heads(stacked)
    mixed, kept = attend_forward(
        head_rows[0].reshape(TOK_DEV, H, HD),
        head_rows[1].reshape(TOK_DEV, H, HD),
        head_rows[2].reshape(TOK_DEV, H, HD),
        present,
        cos_flat,
        sin_flat,
        opens_seq,
    )
    mixed_two = to_tokens(mixed[None])[0]
    mixed_gathered = gather_rows(mixed_two)
    branch = summed_over_cols(mixed_gathered, w_out)
    first, normed_one, inv_one = norm_forward(
        token_rows.astype(jnp.float32) + branch, gain_one, bias_one
    )
    first_low = first.astype(jnp.bfloat16)
    first_gathered = gather_cols(first_low)
    pre = summed_over_rows(first_gathered, w_up)
    act, gelu_pull = jax.vjp(partial(jax.nn.gelu, approximate=False), pre)
    act_low = act.astype(jnp.bfloat16)
    act_gathered = gather_rows(act_low)
    ffn = summed_over_cols(act_gathered, w_down)
    result, normed_two, inv_two = norm_forward(first + ffn, gain_two, bias_two)
    rows_one = token_rows.shape[0]
    global_one = (data_idx * col_count + col_idx) * rows_one + jnp.arange(rows_one, dtype=jnp.int32)
    present_one = (global_one % seq_len < seq_lengths(lengths, global_one // seq_len)).astype(
        jnp.float32
    )
    grad_result = cotangent.T.astype(jnp.float32) * present_one[:, None]
    grad_second, grad_gain_two, grad_bias_two = norm_backward(
        grad_result, normed_two, inv_two, gain_two
    )
    grad_ffn_gathered = gather_cols(grad_second.astype(jnp.bfloat16))
    act_again = gather_rows(act_low)
    grad_down = jnp.einsum(
        "tf,td->fd", act_again, grad_ffn_gathered, preferred_element_type=jnp.float32
    )
    grad_act = summed_over_rows(grad_ffn_gathered, w_down.T)
    grad_pre = gelu_pull(grad_act)[0].astype(jnp.bfloat16)
    grad_pre_gathered = gather_rows(grad_pre)
    first_again = gather_cols(first_low)
    grad_up = jnp.einsum(
        "td,tf->df", first_again, grad_pre_gathered, preferred_element_type=jnp.float32
    )
    grad_first = summed_over_cols(grad_pre_gathered, w_up.T) + grad_second
    grad_hidden, grad_gain_one, grad_bias_one = norm_backward(
        grad_first, normed_one, inv_one, gain_one
    )
    branch_grad_gathered = gather_cols(grad_hidden.astype(jnp.bfloat16))
    mixed_again = gather_rows(mixed_two)
    grad_out = jnp.einsum(
        "tc,tr->cr", mixed_again, branch_grad_gathered, preferred_element_type=jnp.float32
    )
    grad_mixed = summed_over_rows(branch_grad_gathered, w_out.T).astype(jnp.bfloat16)
    grad_heads = to_heads(grad_mixed[None])[0]
    grad_q, grad_k, grad_v = attend_backward(grad_heads, kept, closes_seq)
    grad_rows = to_tokens(jnp.stack([grad_q, grad_k, grad_v], 0))
    grad_cat = jnp.concatenate([grad_rows[0], grad_rows[1], grad_rows[2]], 1)
    grad_cat_gathered = gather_rows(grad_cat)
    x_again = gather_cols(token_rows)
    grad_cat_w = jnp.einsum(
        "tr,tc->rc", x_again, grad_cat_gathered, preferred_element_type=jnp.float32
    )
    input_rows = summed_over_cols(grad_cat_gathered, w_cat.T) + grad_hidden
    gain_parts = jnp.stack([grad_gain_one, grad_bias_one, grad_gain_two, grad_bias_two], 0)
    gain_sums = lax.psum(gain_parts.reshape(4 * feat_rows), "col")
    grad_query = grad_cat_w[:, :width_col]
    grad_key = grad_cat_w[:, width_col : 2 * width_col]
    grad_value = grad_cat_w[:, 2 * width_col :]
    output = result.astype(jnp.bfloat16).T
    input_grad = input_rows.T
    sums = (
        lax.psum(grad_query.astype(jnp.bfloat16), "dp").astype(jnp.float32),
        lax.psum(grad_key.astype(jnp.bfloat16), "dp").astype(jnp.float32),
        lax.psum(grad_value.astype(jnp.bfloat16), "dp").astype(jnp.float32),
        lax.psum(grad_out.astype(jnp.bfloat16), "dp").astype(jnp.float32),
        lax.psum(grad_up.astype(jnp.bfloat16), "dp").astype(jnp.float32),
        lax.psum(grad_down.astype(jnp.bfloat16), "dp").astype(jnp.float32),
        lax.psum(gain_sums.astype(jnp.bfloat16), "dp").astype(jnp.float32),
    )
    gain_total = sums[6].reshape(4, feat_rows)
    return (
        output,
        input_grad,
        sums[0],
        sums[1],
        sums[2],
        sums[3],
        gain_total[0],
        gain_total[1],
        sums[4],
        sums[5],
        gain_total[2],
        gain_total[3],
    )


def paired_layout(mesh):
    rows, cols, dps = mesh.shape["row"], mesh.shape["col"], mesh.shape["dp"]
    return rows == 4 and cols == 2 and dps == 4 and H % 4 == 0 and 8 * TOK_DEV <= SEQ_MAX


low = jnp.bfloat16
wide = jnp.float32
SPAN = 2 * TOK_DEV
HEADS = H // 4
WIDTH = HEADS * HD
STATE_ROWS = 2 * HEADS * HD
SUM_ROWS = 16
SUM_LANES = 64


def swap_cols(operand):
    return lax.ppermute(operand, "col", [(0, 1), (1, 0)])


def swap_pair(operand):
    return lax.ppermute(operand, "dp", [(i, i ^ 1) for i in range(lax.axis_size("dp"))])


def swap_copies(operand):
    return lax.ppermute(operand, "dp", [(i, i ^ 2) for i in range(lax.axis_size("dp"))])


def shift_rows(operand, step):
    count = lax.axis_size("row")
    pairs = [(i, i + step) for i in range(count) if 0 <= i + step < count]
    return lax.ppermute(operand, "row", pairs)


def swap_rows(operand, mask):
    return lax.ppermute(operand, "row", [(i, i ^ mask) for i in range(4)])


def rotate_rows(operand, step):
    count = lax.axis_size("row")
    return lax.ppermute(operand, "row", [(i, (i + step) % count) for i in range(count)])


def dot_tn(left, right):
    return lax.dot_general(left, right, (((0,), (0,)), ((), ())), preferred_element_type=wide)


def dot_nt(left, right):
    return lax.dot_general(left, right, (((1,), (1,)), ((), ())), preferred_element_type=wide)


def dot_nn(left, right):
    return jnp.dot(left, right, preferred_element_type=wide)


def norm_columns(hidden, scale, shift):
    mean = jnp.mean(hidden, 0, keepdims=True)
    centered = hidden - mean
    variance = jnp.mean(centered * centered, 0, keepdims=True)
    inv_std = lax.rsqrt(variance + norm_eps)
    normed = centered * inv_std
    return (normed * scale + shift, normed, inv_std)


def norm_columns_back(grad_in, normed, inv_std, scale):
    grad_normed = grad_in * scale
    mean_one = jnp.mean(grad_normed, 0, keepdims=True)
    mean_two = jnp.mean(grad_normed * normed, 0, keepdims=True)
    return inv_std * (grad_normed - mean_one - normed * mean_two)


def local_call(body, outs, name, *operands, scratch=(), space=None):
    shapes = [jax.ShapeDtypeStruct(shape, kind) for shape, kind in outs]
    return pl.pallas_call(
        body,
        out_shape=shapes,
        in_specs=[
            pl.BlockSpec(
                memory_space=pltpu.SMEM
                if operand.dtype == jnp.int32
                else space or pltpu.VMEM
            )
            for operand in operands
        ],
        out_specs=[pl.BlockSpec(memory_space=pltpu.VMEM)] * len(outs),
        scratch_shapes=[
            pltpu.VMEM(*kind) if isinstance(kind, tuple) else kind for kind in scratch
        ],
        compiler_params=pltpu.CompilerParams(vmem_limit_bytes=24 * 2**20),
        name=name,
    )(*operands)


CORE, COPY, ROW, COL, SEQ = range(5)


def low_outs(count, *shape):
    return [(shape, low)] * count


def turn_body(flags_ref, lengths_ref, trig_ref, reweight_ref, *, seq_len):
    start = flags_ref[ROW] * SPAN
    positions = start + lax.broadcasted_iota(jnp.int32, (8, SPAN), 1)
    lines = lax.broadcasted_iota(jnp.int32, (8, SPAN), 0)
    angles = math.pi * positions.astype(wide) / (2.0 * seq_len)
    turns = jnp.where(lines == 0, jnp.cos(angles), jnp.where(lines == 1, jnp.sin(angles), 0.0))
    own = lengths_ref[flags_ref[SEQ]]
    other = lengths_ref[flags_ref[SEQ] + 1 - 2 * flags_ref[CORE]]
    limits = jnp.where(lines == 2, own, other)
    present = jnp.where(positions < limits, 1.0, 0.0)
    trig_ref[...] = turns + jnp.where(lines == 2, present, jnp.where(lines == 3, present, 0.0))
    rows = lax.broadcasted_iota(jnp.int32, (SPAN, SPAN), 0)
    cols = lax.broadcasted_iota(jnp.int32, (SPAN, SPAN), 1)
    both = lax.dot_general(
        turns, turns, (((0,), (0,)), ((), ())), precision=highest, preferred_element_type=wide
    )
    reweight_ref[...] = jnp.where(rows <= cols, both, 0.0)


def token_piece(flags_ref, own_ref, recv_ref, step, rows):
    place = lax.rem(flags_ref[ROW] + step, rows)
    half = lax.div(place, rows // 2)
    cols = pl.ds(pl.multiple_of(lax.rem(place, rows // 2) * SPAN, SPAN), SPAN)
    return jnp.where(half == flags_ref[COL], own_ref[:, cols], recv_ref[:, cols])


def pieces_body(flags_ref, own_ref, cot_ref, recv_ref, *refs, rows):
    vec_ref, piece_refs = refs[0], refs[1:]
    part = own_ref.shape[0]
    lines = []
    for line in range(4):
        vec = vec_ref[line : line + 1, :]
        vec = jnp.concatenate([vec, jnp.zeros((1, SPAN - vec.shape[1]), wide)], 1)
        high = vec.astype(low).astype(wide)
        lines = lines + [high, vec - high]
    for step, ref in enumerate(piece_refs):
        ref[:part] = token_piece(flags_ref, own_ref, recv_ref.at[:part], step, rows)
        ref[part : 2 * part] = token_piece(flags_ref, cot_ref, recv_ref.at[part:], step, rows)
        ref[2 * part :] = jnp.concatenate(lines + [jnp.zeros((8, SPAN), wide)], 0).astype(low)


def came_from(flags_ref, step, rows):
    return lax.rem(flags_ref[ROW] + rows - step, rows)


def place_tokens_body(flags_ref, *refs, rows, part):
    pieces, (half_ref, cot_ref, vec_ref) = refs[:rows], refs[rows:]
    for step, ref in enumerate(pieces):
        row = came_from(flags_ref, step, rows)
        half_ref[pl.ds(pl.multiple_of(row * part, 16), part), :] = ref[:part]
        cot_ref[pl.ds(pl.multiple_of(row * part, 16), part), :] = ref[part : 2 * part]
        extra = ref[2 * part :].astype(wide)
        sums = [extra[2 * i : 2 * i + 1] + extra[2 * i + 1 : 2 * i + 2] for i in range(4)]
        columns = jnp.concatenate(sums + [jnp.zeros((4, SPAN), wide)], 0).T
        vec_ref[pl.ds(pl.multiple_of(row * 2 * part, 8), 2 * part), :] = columns[: 2 * part]


def join_halves_body(flags_ref, half_ref, recv_ref, full_ref, *, rows):
    part = half_ref.shape[0] // rows
    first_col = flags_ref[COL] == 0
    for row in range(rows):
        own = half_ref[row * part : (row + 1) * part]
        other = recv_ref[row * part : (row + 1) * part]
        full_ref[2 * row * part : (2 * row + 1) * part] = jnp.where(first_col, own, other)
        full_ref[(2 * row + 1) * part : (2 * row + 2) * part] = jnp.where(first_col, other, own)


def add_body(own_ref, recv_ref, half_ref):
    half_ref[...] = (own_ref[...] + recv_ref[...].astype(wide)).astype(low)


def feature_piece(flags_ref, source, step, rows):
    part = source.shape[0] // (2 * rows)
    start = (lax.rem(flags_ref[ROW] + step, rows) * 2 + flags_ref[COL]) * part
    return source[pl.ds(pl.multiple_of(start, 16), part), :]


def place_back(flags_ref, pieces, rows, own_ref, other_ref):
    half = len(pieces) // 2
    for row, piece in zip(rows, pieces):
        cols = pl.ds(pl.multiple_of(lax.rem(row, half) * SPAN, SPAN), SPAN)
        mine = lax.div(row, half) == flags_ref[COL]

        @pl.when(mine)
        def _(piece=piece, cols=cols):
            own_ref[:, cols] = piece[...]

        @pl.when(jnp.logical_not(mine))
        def _(piece=piece, cols=cols):
            other_ref[:, cols] = piece[...]


def sum_of(refs):
    total = refs[0][...].astype(wide)
    for ref in refs[1:]:
        total = total + ref[...].astype(wide)
    return total


def join_back_body(flags_ref, own_ref, recv_ref, out_ref):
    part = own_ref.shape[0]
    first_col = flags_ref[COL] == 0
    out_ref[:part] = jnp.where(first_col, own_ref[...], recv_ref[...]).astype(out_ref.dtype)
    out_ref[part:] = jnp.where(first_col, recv_ref[...], own_ref[...]).astype(out_ref.dtype)


def input_halves_body(flags_ref, own_ref, recv_ref, half_ref, sent_ref, sum_ref, *, rows):
    part = own_ref.shape[0] // (2 * rows)
    sum_ref[...] = own_ref[...] + recv_ref[...].astype(wide)
    for row in range(rows):
        rows_out = slice(row * part, (row + 1) * part)
        mine = pl.multiple_of((2 * row + flags_ref[COL]) * part, 16)
        theirs = pl.multiple_of((2 * row + 1 - flags_ref[COL]) * part, 16)
        half_ref[rows_out] = sum_ref[pl.ds(mine, part), :]
        sent_ref[rows_out] = sum_ref[pl.ds(theirs, part), :].astype(low)


def last_pieces_body(
    flags_ref, kept_ref, got_ref, half_ref, recv_ref, hidden_ref, held_ref, sent_ref
):
    rows = kept_ref.shape[0]
    part = half_ref.shape[0] // rows
    lanes = kept_ref.shape[2]
    for mask in range(rows):
        ref = sent_ref if mask % 2 else held_ref
        out = slice(mask // 2 * part, (mask // 2 + 1) * part)
        place = partner(flags_ref[ROW], mask)
        ref[out, :lanes] = (kept_ref[place].astype(wide) + got_ref[place].astype(wide)).astype(low)
        rows_in = pl.ds(pl.multiple_of(place * part, 16), part)
        total = half_ref[rows_in, :] + recv_ref[rows_in, :].astype(wide)
        start = pl.multiple_of((place * 2 + flags_ref[COL]) * part, 16)
        ref[out, lanes:] = (total + hidden_ref[pl.ds(start, part), :]).astype(low)


def last_pairs_body(held_ref, got_ref, sum_ref, sent_ref):
    part, lanes = sum_ref.shape
    sum_ref[...] = held_ref[:part, :lanes].astype(wide) + got_ref[:part, :lanes].astype(wide)
    pair = held_ref[part:, :lanes].astype(wide) + got_ref[part:, :lanes].astype(wide)
    sent_ref[:, :lanes] = pair.astype(low)
    sent_ref[:, lanes : lanes + SPAN] = held_ref[part:, lanes:]
    sent_ref[:, lanes + SPAN :] = got_ref[part:, lanes:]


def last_sums_body(
    flags_ref, part_ref, held_ref, got_ref, far_ref, sum_ref, own_ref, other_ref
):
    part, lanes = part_ref.shape
    sum_ref[...] = (part_ref[...] + far_ref[:, :lanes].astype(wide)).astype(low)
    pieces = (
        held_ref.at[:part, lanes:],
        got_ref.at[:part, lanes:],
        far_ref.at[:, lanes : lanes + SPAN],
        far_ref.at[:, lanes + SPAN :],
    )
    rows = [partner(flags_ref[ROW], mask) for mask in range(4)]
    place_back(flags_ref, pieces, rows, own_ref, other_ref)


def pair_pieces_body(flags_ref, kept_ref, got_ref, *refs):
    extras, (held_ref, sent_ref) = refs[:-2], refs[-2:]
    rows = 4
    feats, part = kept_ref.shape[0] // rows, kept_ref.shape[1]
    for mask in range(rows):
        ref = sent_ref if mask % 2 else held_ref
        out = slice(mask // 2 * feats, (mask // 2 + 1) * feats)
        place = partner(flags_ref[ROW], mask)
        rows_in = pl.ds(pl.multiple_of(place * feats, 16), feats)
        ref[out, :part] = (
            kept_ref[rows_in, :].astype(wide) + got_ref[rows_in, :].astype(wide)
        ).astype(low)
        for extra in extras:
            ref[out, part:] = extra[rows_in, :]


def pair_sums_body(held_ref, got_ref, sum_ref, sent_ref):
    feats = sum_ref.shape[0]
    sum_ref[...] = held_ref[:feats].astype(wide) + got_ref[:feats].astype(wide)
    sent_ref[...] = (held_ref[feats:].astype(wide) + got_ref[feats:].astype(wide)).astype(low)


def hidden_sums_body(down_ref, down_far_ref, up_ref, up_far_ref, sum_ref):
    part = down_ref.shape[1]
    sum_ref[:, :part] = (down_ref[...] + down_far_ref[...].astype(wide)).astype(low)
    sum_ref[:, part:] = (up_ref[...] + up_far_ref[...].astype(wide)).astype(low)


def out_pieces_body(flags_ref, result_ref, *refs):
    for step, ref in enumerate(refs):
        ref[...] = feature_piece(flags_ref, result_ref, step, len(refs))


def out_place_body(flags_ref, *refs):
    pieces = refs[:-2]
    rows = [came_from(flags_ref, step, len(pieces)) for step in range(len(pieces))]
    place_back(flags_ref, pieces, rows, *refs[-2:])


def head_sets():
    return [(seq, head, seq * HEADS + head) for seq in range(2) for head in range(HEADS)]


def set_row(place):
    ids = lax.broadcasted_iota(jnp.int32, (SUM_ROWS, SPAN), 0)
    return (ids == place).astype(wide)


def turned(parts, trig_ref):
    part_wide = parts.astype(wide)
    return jnp.concatenate(
        [(part_wide * trig_ref[0:1, :]).astype(low), (part_wide * trig_ref[1:2, :]).astype(low)], 0
    )


def unturned(pair, trig_ref):
    return pair[:HD] * trig_ref[0:1, :] + pair[HD:] * trig_ref[1:2, :]


def query_part(qkv_ref, seq, head):
    return qkv_ref[seq, head * HD : (head + 1) * HD, :]


def key_part(qkv_ref, seq, head):
    return qkv_ref[seq, WIDTH + head * HD : WIDTH + (head + 1) * HD, :]


def value_part(qkv_ref, seq, head):
    return qkv_ref[seq, 2 * WIDTH + head * HD : 2 * WIDTH + (head + 1) * HD, :]


def kept_keys(qkv_ref, trig_ref, seq, head):
    keys = jnp.maximum(key_part(qkv_ref, seq, head), 0)
    return (keys.astype(wide) * trig_ref[2 + seq : 3 + seq, :]).astype(low)


def state_slice(state, place):
    return state[place * HD : (place + 1) * HD]


def pack_hidden_body(flags_ref, up_ref, down_ref, mine_ref, copy_ref, sems):
    part = mine_ref.shape[1] // 2
    copies = []
    for half, packed_ref in enumerate((mine_ref, copy_ref)):
        copy = 1 - flags_ref[COPY] if half else flags_ref[COPY]
        start = pl.multiple_of((flags_ref[CORE] * 2 + copy) * part, 128)
        for place, ref in enumerate((up_ref, down_ref)):
            copies.append(
                pltpu.make_async_copy(
                    ref.at[:, pl.ds(start, part)],
                    packed_ref.at[:, pl.ds(place * part, part)],
                    sems.at[2 * half + place],
                )
            )
    for copy in copies:
        copy.start()
    for copy in copies:
        copy.wait()


def partner(row, mask):
    if mask == 0:
        return row
    if mask == 1:
        return row + 1 - 2 * lax.rem(row, 2)
    return lax.rem(row + 2, 4) if mask == 2 else 3 - row


def row_block(flags_ref, mask, feats):
    return pl.ds(pl.multiple_of(partner(flags_ref[ROW], mask) * feats, 16), feats)


def project_body(flags_ref, own_ref, other_ref, trig_ref, packed_ref, *refs):
    weight_ref, qkv_ref, state_ref = refs[-3:]
    blocks = refs[:-3]
    count = len(blocks) // 2
    first_copy = flags_ref[COPY] == 0
    feats = packed_ref.shape[0]
    part = packed_ref.shape[1] // 2

    def rows_of(mask):
        return row_block(flags_ref, mask, feats)

    weight_ref[rows_of(0), :] = packed_ref[...]
    for step in range(1, count + 1):
        mine, copied = blocks[step - 1][...], blocks[count + step - 1][...]
        weight_ref[rows_of(step), :part] = jnp.where(first_copy, mine, copied)
        weight_ref[rows_of(step), part:] = jnp.where(first_copy, copied, mine)
    matrix = weight_ref[:, : 3 * WIDTH]
    for seq, x_ref in enumerate((own_ref, other_ref)):
        qkv_ref[seq] = dot_tn(matrix, x_ref[...]).astype(low)
    sums = jnp.zeros((SUM_ROWS, 2 * HD), wide)
    for seq, head, place in head_sets():
        turned_keys = turned(kept_keys(qkv_ref, trig_ref, seq, head), trig_ref)
        values = value_part(qkv_ref, seq, head)
        state_ref[place * HD : (place + 1) * HD, :] = dot_nt(values, turned_keys).astype(low)
        sums = sums + dot_nt(set_row(place).astype(low), turned_keys)
    state_ref[STATE_ROWS:, :] = sums.astype(low)


def block_body(qkv_ref, trig_ref, reweight_ref, weights_ref, numer_ref, denom_ref):
    denoms = jnp.zeros((SUM_ROWS, SPAN), wide)
    for seq, head, place in head_sets():
        queries = jnp.maximum(query_part(qkv_ref, seq, head), 0)
        keys = kept_keys(qkv_ref, trig_ref, seq, head)
        weights = dot_tn(keys, queries) * reweight_ref[...]
        weights_low = weights.astype(low)
        weights_ref[place] = weights_low
        numer_ref[place] = dot_nn(value_part(qkv_ref, seq, head), weights_low)
        denoms = denoms + set_row(place) * jnp.sum(weights, 0, keepdims=True)
    denom_ref[...] = denoms


def attend_body(
    qkv_ref,
    trig_ref,
    numer_ref,
    denom_ref,
    weight_ref,
    *refs,
):
    arrived = refs[:-5]
    prior_ref, attn_wide_ref, own_ref, other_ref, attn_ref = refs[-5:]
    total = arrived[0][...].astype(wide)
    for ref in arrived[1:]:
        total = total + ref[...].astype(wide)
    prior_ref[...] = total.astype(low)
    matrix = weight_ref[:, 3 * WIDTH : 4 * WIDTH]
    prior_sums = prior_ref[STATE_ROWS:, :]
    inverses = jnp.zeros((SUM_ROWS, SPAN), wide)
    for seq, head, place in head_sets():
        queries = turned(jnp.maximum(query_part(qkv_ref, seq, head), 0), trig_ref)
        prior = prior_ref[place * HD : (place + 1) * HD, :]
        numer = numer_ref[place] + dot_nn(prior, queries)
        denoms = dot_nn(prior_sums, queries) + denom_ref[...]
        denom = 1.0 + jnp.sum(denoms * set_row(place), 0, keepdims=True)
        inverse = 1.0 / denom
        inverses = inverses + set_row(place) * inverse
        attended = numer * inverse
        attn_wide_ref[place * HD : (place + 1) * HD, :] = attended
        attn_ref[seq, head * HD : (head + 1) * HD, :] = attended.astype(low)
    attn_wide_ref[STATE_ROWS:, :] = inverses
    own_ref[...] = dot_nn(matrix, attn_ref[0])
    other_ref[...] = dot_nn(matrix, attn_ref[1]).astype(low)


def grad_attend_body(
    own_ref,
    other_ref,
    weight_ref,
    attn_wide_ref,
    qkv_ref,
    trig_ref,
    grad_num_ref,
    grad_den_ref,
    state_ref,
):
    matrix = weight_ref[:, 3 * WIDTH : 4 * WIDTH]
    sums = jnp.zeros((SUM_ROWS, 2 * HD), wide)
    dens = jnp.zeros((SUM_ROWS, SPAN), wide)
    for seq, grad_ref in enumerate((own_ref, other_ref)):
        grads = dot_tn(matrix, grad_ref[...]).astype(low).astype(wide)
        for head in range(HEADS):
            place = seq * HEADS + head
            inverse = jnp.sum(attn_wide_ref[STATE_ROWS:, :] * set_row(place), 0, keepdims=True)
            scaled = grads[head * HD : (head + 1) * HD] * inverse
            grad_num = scaled.astype(low)
            grad_num_ref[place] = grad_num
            grad_den = -jnp.sum(scaled * attn_wide_ref[place * HD : (place + 1) * HD, :], 0, keepdims=True)
            den_row = set_row(place) * grad_den
            dens = dens + den_row
            queries = turned(jnp.maximum(query_part(qkv_ref, seq, head), 0), trig_ref)
            state_ref[place * HD : (place + 1) * HD, :] = dot_nt(grad_num, queries).astype(low)
            sums = sums + dot_nt(den_row.astype(low), queries)
    state_ref[STATE_ROWS:, :] = sums.astype(low)
    grad_den_ref[...] = dens


def grad_block_body(
    grad_num_ref,
    grad_den_ref,
    qkv_ref,
    trig_ref,
    reweight_ref,
    weights_ref,
    prior_ref,
    grad_query_ref,
    grad_key_ref,
    grad_value_ref,
):
    prior_sums = prior_ref[STATE_ROWS:, :]
    for seq, head, place in head_sets():
        query = query_part(qkv_ref, seq, head)
        queries = jnp.maximum(query, 0)
        keys = kept_keys(qkv_ref, trig_ref, seq, head)
        grad_num = grad_num_ref[place]
        den_rows = grad_den_ref[...] * set_row(place)
        grad_den = jnp.sum(den_rows, 0, keepdims=True)
        grad_scores = (
            (dot_tn(value_part(qkv_ref, seq, head), grad_num) + grad_den) * reweight_ref[...]
        ).astype(low)
        prior = jnp.concatenate([prior_ref[place * HD : (place + 1) * HD, :], prior_sums], 0)
        grads = jnp.concatenate([grad_num, den_rows.astype(low)], 0)
        grad_query = dot_nn(keys, grad_scores) + unturned(dot_tn(prior, grads), trig_ref)
        grad_query_ref[seq, head * HD : (head + 1) * HD, :] = jnp.where(
            query.astype(wide) > 0, grad_query, 0.0
        ).astype(low)
        grad_key_ref[place] = dot_nt(queries, grad_scores)
        grad_value_ref[place] = dot_nt(grad_num, weights_ref[place])


def grad_project_body(
    grad_query_ref,
    grad_key_ref,
    grad_value_ref,
    qkv_ref,
    trig_ref,
    x_own_ref,
    x_other_ref,
    weight_ref,
    vec_ref,
    flags_ref,
    *refs,
):
    arrived = refs[:-6]
    kept_ref, sent_ref, own_ref, other_ref, after_ref, grad_ref = refs[-6:]
    total = arrived[0][...].astype(wide)
    for ref in arrived[1:]:
        total = total + ref[...].astype(wide)
    after_ref[...] = total.astype(low)
    after_sums = after_ref[STATE_ROWS:, :]
    for seq, head, place in head_sets():
        key = key_part(qkv_ref, seq, head)
        keys = turned(kept_keys(qkv_ref, trig_ref, seq, head), trig_ref)
        values = value_part(qkv_ref, seq, head)
        after = after_ref[place * HD : (place + 1) * HD, :]
        left = jnp.concatenate([after, after_sums], 0)
        right = jnp.concatenate([values, set_row(place).astype(low)], 0)
        grad_key = grad_key_ref[place] + unturned(dot_tn(left, right), trig_ref)
        grad_key = jnp.where(key.astype(wide) > 0, grad_key, 0.0) * trig_ref[2 + seq : 3 + seq, :]
        grad_value = grad_value_ref[place] + dot_nn(after, keys)
        rows = slice(head * HD, (head + 1) * HD)
        grad_ref[seq, rows, :] = grad_query_ref[seq, rows, :]
        rows = slice(WIDTH + head * HD, WIDTH + (head + 1) * HD)
        grad_ref[seq, rows, :] = grad_key.astype(low)
        rows = slice(2 * WIDTH + head * HD, 2 * WIDTH + (head + 1) * HD)
        grad_ref[seq, rows, :] = grad_value.astype(low)
    matrix = weight_ref[:, : 3 * WIDTH]
    grad_w = (
        dot_nt(x_own_ref[...], grad_ref[0]) + dot_nt(x_other_ref[...], grad_ref[1])
    ).astype(low)
    rows, part, _ = kept_ref.shape
    first_copy = flags_ref[COPY] == 0
    for row in range(rows):
        start = row * 2 * part
        whole = jnp.concatenate(
            [grad_w[start : start + 2 * part], vec_ref[start : start + 2 * part, : 2 * SUM_LANES]],
            1,
        )[:, : 3 * WIDTH + SUM_LANES]
        first, second = whole[:part], whole[part:]
        kept_ref[row] = jnp.where(first_copy, first, second)
        sent_ref[row] = jnp.where(first_copy, second, first)
    own_ref[...] = dot_nn(matrix, grad_ref[0])
    other_ref[...] = dot_nn(matrix, grad_ref[1]).astype(low)


def norm_body(x_ref, half_ref, recv_ref, vec_ref, first_ref, low_ref, normed_ref):
    hidden = x_ref[...].astype(wide) + (half_ref[...].astype(wide) + recv_ref[...].astype(wide))
    first, normed, inv_std = norm_columns(hidden, vec_ref[:, 0:1], vec_ref[:, 1:2])
    first_ref[...] = first
    low_ref[...] = first.astype(low)
    normed_ref[:D, :] = normed
    normed_ref[D:, :] = jnp.broadcast_to(inv_std, (8, SPAN))


def lane_sums(columns, place):
    lanes = lax.broadcasted_iota(jnp.int32, (columns[0].shape[0], 2 * SUM_LANES), 1)
    total = jnp.zeros(lanes.shape, wide)
    for shift, column in enumerate(columns):
        total = jnp.where(lanes == place + shift, jnp.sum(column, 1, keepdims=True), total)
    return total


def second_norm_body(
    first_ref, half_ref, recv_ref, vec_ref, cot_ref, trig_ref, result_ref, grad_ref, low_ref
):
    hidden = first_ref[...] + (half_ref[...].astype(wide) + recv_ref[...].astype(wide))
    scale = vec_ref[:, 2:3]
    result, normed, inv_std = norm_columns(hidden, scale, vec_ref[:, 3:4])
    result_ref[...] = result.astype(low)
    grad_in = cot_ref[...].astype(wide) * trig_ref[2:3, :]
    grad = norm_columns_back(grad_in, normed, inv_std, scale)
    grad_ref[:, :SPAN] = grad
    low_ref[...] = grad.astype(low)
    grad_ref[:, SPAN:] = lane_sums((grad_in * normed, grad_in), 2)


def norm_back_body(
    grad_ref, half_ref, recv_ref, normed_ref, vec_ref, hidden_ref, low_ref, sum_ref
):
    grad_in = grad_ref[:, :SPAN] + (half_ref[...].astype(wide) + recv_ref[...].astype(wide))
    normed = normed_ref[:D, :]
    grad = norm_columns_back(grad_in, normed, normed_ref[D : D + 1, :], vec_ref[:, 0:1])
    hidden_ref[...] = grad
    low_ref[...] = grad.astype(low)
    sum_ref[...] = (lane_sums((grad_in * normed, grad_in), 0) + grad_ref[:, SPAN:]).astype(low)


def hidden_body(flags_ref, own_ref, other_ref, *refs):
    weight_ref, act_ref, slope_ref, part_own_ref, part_other_ref = refs[-5:]
    blocks, earlier = refs[:4], refs[4:-5]
    part = act_ref.shape[0]
    for mask, ref in enumerate(blocks):
        weight_ref[row_block(flags_ref, mask, ref.shape[0]), :] = ref[...]
    up = weight_ref[:, :part]
    down = weight_ref[:, part:]
    for seq, (x_ref, part_ref) in enumerate(
        ((own_ref, part_own_ref), (other_ref, part_other_ref))
    ):
        cols = slice(seq * SPAN, (seq + 1) * SPAN)
        act, slope = gelu_and_slope(dot_tn(up, x_ref[...]))
        act_ref[:, cols] = act
        slope_ref[:, cols] = slope
        total = dot_nn(down, act)
        if earlier:
            total = total + earlier[seq][...]
        part_ref[...] = total.astype(part_ref.dtype)


def hidden_back_body(
    own_ref,
    other_ref,
    mine_ref,
    copy_ref,
    slope_mine_ref,
    slope_copy_ref,
    pre_mine_ref,
    pre_copy_ref,
    part_own_ref,
    part_other_ref,
):
    part = slope_mine_ref.shape[0]
    for seq, (x_ref, part_ref) in enumerate(
        ((own_ref, part_own_ref), (other_ref, part_other_ref))
    ):
        cols = slice(seq * SPAN, (seq + 1) * SPAN)
        total = None
        for weight_ref, slope_ref, pre_ref in (
            (mine_ref, slope_mine_ref, pre_mine_ref),
            (copy_ref, slope_copy_ref, pre_copy_ref),
        ):
            grad_pre = (dot_tn(weight_ref[:, part:], x_ref[...]) * slope_ref[:, cols]).astype(low)
            pre_ref[:, cols] = grad_pre
            term = dot_nn(weight_ref[:, :part], grad_pre)
            total = term if total is None else total + term
        part_ref[...] = total.astype(part_ref.dtype)


def half_grads_body(own_ref, other_ref, mine_ref, copy_ref, kept_ref, sent_ref):
    for pre_ref, out_ref in ((copy_ref, sent_ref), (mine_ref, kept_ref)):
        out_ref[...] = (
            dot_nt(own_ref[...], pre_ref[:, :SPAN]) + dot_nt(other_ref[...], pre_ref[:, SPAN:])
        ).astype(low)


def out_grad_body(own_ref, other_ref, attn_wide_ref, out_ref):
    out_ref[...] = (
        dot_nt(own_ref[...], attn_wide_ref[:WIDTH, :].astype(low))
        + dot_nt(other_ref[...], attn_wide_ref[WIDTH : 2 * WIDTH, :].astype(low))
    ).astype(low)


def quarters(flags_ref, refs):
    core, copy = flags_ref[CORE], flags_ref[COPY]
    for ref, other_core, other_copy in zip(refs, (0, 0, 1, 1), (0, 1, 0, 1)):
        core_place = 1 - core if other_core else core
        copy_place = 1 - copy if other_copy else copy
        yield core_place * 2 + copy_place, ref


def place_hidden_body(flags_ref, *refs):
    down_ref, up_ref, out_ref = refs[4:]
    part = up_ref.shape[1] // 4
    for place, ref in quarters(flags_ref, refs[:4]):
        cols = pl.ds(pl.multiple_of(place * part, 128), part)
        down_ref[:, cols] = ref[:, :part].astype(wide)
        up_ref[:, cols] = ref[:, part : 2 * part].astype(wide)
    sums = [ref[:, 2 * part :].astype(wide) for ref in refs[:4]]
    own, other = sums[0] + sums[1], sums[2] + sums[3]
    first_core = flags_ref[CORE] == 0
    out_ref[:, :WIDTH] = jnp.where(first_core, own, other)
    out_ref[:, WIDTH:] = jnp.where(first_core, other, own)


def place_last_body(flags_ref, *refs):
    outs, vec_ref = refs[4:7], refs[7]
    first_core = flags_ref[CORE] == 0
    part = refs[0].shape[0]
    for own_ref, other_ref, other_copy in ((refs[0], refs[2], 0), (refs[1], refs[3], 1)):
        copy = 1 - flags_ref[COPY] if other_copy else flags_ref[COPY]
        rows = pl.ds(pl.multiple_of(copy * part, 8), part)
        own, other = own_ref[...].astype(wide), other_ref[...].astype(wide)
        for place, out_ref in enumerate(outs):
            cols = slice(place * WIDTH, (place + 1) * WIDTH)
            out_ref[rows, :WIDTH] = jnp.where(first_core, own[:, cols], other[:, cols])
            out_ref[rows, WIDTH:] = jnp.where(first_core, other[:, cols], own[:, cols])
        vec_ref[rows, :] = own[:, 3 * WIDTH :] + other[:, 3 * WIDTH :]


def gelu_and_slope(pre):
    cdf = 0.5 * (1.0 + lax.erf(pre * math.sqrt(0.5)))
    density = jnp.exp(-0.5 * pre * pre) * (1.0 / math.sqrt(2.0 * math.pi))
    return (pre * cdf).astype(low), (cdf + pre * density)


def all_quarters(own):
    copied = swap_copies(own)
    return own, copied, swap_pair(own), swap_pair(copied)


def on_device_paired(
    tokens,
    lengths,
    w_query,
    w_key,
    w_value,
    w_out,
    gain_one,
    bias_one,
    w_up,
    w_down,
    gain_two,
    bias_two,
    cotangent,
):
    rows = lax.axis_size("row")
    seq_len = SPAN * rows
    dp_idx = lax.axis_index("dp")
    feat_rows = tokens.shape[0]
    half_feats = feat_rows // 2
    flags = jnp.stack(
        [dp_idx % 2, dp_idx // 2, lax.axis_index("row"), lax.axis_index("col"), dp_idx]
    )
    trig, reweight = local_call(
        partial(turn_body, seq_len=seq_len),
        [((8, SPAN), wide), ((SPAN, SPAN), wide)],
        "turn",
        flags,
        lengths,
    )

    def passed_on(pieces):
        return [pieces[0]] + [
            rotate_rows(piece, step) for step, piece in enumerate(pieces) if step
        ]

    def joined_halves(half, name):
        return local_call(
            partial(join_halves_body, rows=rows),
            [((D, SPAN), low)],
            name,
            flags,
            half,
            swap_cols(half),
        )[0]

    def cols_back(own, other, kind, name):
        return local_call(
            join_back_body,
            [((feat_rows, SPAN * rows // 2), kind)],
            name,
            flags,
            own,
            swap_cols(other),
        )[0]

    def column_parts(own_part, other_part, name):
        (half,) = local_call(add_body, low_outs(1, D, SPAN), name, own_part, swap_pair(other_part))
        return half, swap_cols(half)

    first_col = lax.axis_index("col") == 0

    def halved(block):
        top, bottom = block[:half_feats], block[half_feats:]
        return jnp.where(first_col, top, bottom), jnp.where(first_col, bottom, top)

    (token_own, token_sent), (cot_own, cot_sent) = halved(tokens), halved(cotangent)
    got = swap_cols(jnp.concatenate([token_sent, cot_sent], 0))

    part = w_up.shape[1] // 4
    first_core = dp_idx % 2 == 0

    def core_part(operand):
        return jnp.where(first_core, operand[:, :WIDTH], operand[:, WIDTH:])

    parts = [core_part(operand) for operand in (w_query, w_key, w_value, w_out.T)]
    first_packed = jnp.concatenate(parts, 1)
    first_mine = jnp.where(
        dp_idx < 2, jnp.concatenate(parts[:2], 1), jnp.concatenate(parts[2:], 1)
    )

    def row_blocks(block):
        return swap_rows(block, 1), swap_rows(block, 2)

    first_one, first_two = row_blocks(first_mine)
    first_one, got = lax.optimization_barrier((first_one, got))
    first_blocks = [first_one, first_two, swap_rows(first_two, 1)]
    first_blocks = first_blocks + [swap_copies(block) for block in first_blocks]
    hidden_packed = local_call(
        pack_hidden_body,
        low_outs(2, feat_rows, 2 * part),
        "pack_hidden",
        flags,
        w_up,
        w_down.T,
        scratch=[pltpu.SemaphoreType.DMA((4,))],
        space=pltpu.HBM,
    )
    vecs = jnp.stack([gain_one, bias_one, gain_two, bias_two], 0)
    token_pieces = local_call(
        partial(pieces_body, rows=rows),
        low_outs(rows, feat_rows + 16, SPAN),
        "token_pieces",
        flags,
        token_own,
        cot_own,
        got,
        vecs,
    )
    x_half, cot_half, norm_vecs = local_call(
        partial(place_tokens_body, rows=rows, part=half_feats),
        low_outs(2, D // 2, SPAN) + [((D, 8), wide)],
        "token_place",
        flags,
        *passed_on(token_pieces),
    )
    x_half, trig, reweight, hidden_packed = lax.optimization_barrier(
        (x_half, trig, reweight, hidden_packed)
    )
    hidden_one, hidden_two = row_blocks(hidden_packed[0])
    x_own = joined_halves(x_half, "token_join")
    cot = joined_halves(cot_half, "cot_join")
    x_own, first_blocks, hidden_one, hidden_two, cot = lax.optimization_barrier(
        (x_own, first_blocks, hidden_one, hidden_two, cot)
    )
    x_other = swap_pair(x_own)
    hidden_three = swap_rows(hidden_two, 1)
    copy_two = swap_copies(hidden_two)
    state_shape = ((STATE_ROWS + SUM_ROWS, 2 * HD), low)
    sets = 2 * HEADS
    block_low = ((D, SPAN), low)
    block_wide = ((D, SPAN), wide)
    weight, qkv, state = local_call(
        project_body,
        [((D, 4 * WIDTH), low), ((2, 3 * WIDTH, SPAN), low), state_shape],
        "project",
        flags,
        x_own,
        x_other,
        trig,
        first_packed,
        *first_blocks,
    )
    arrived = [shift_rows(state, step) for step in range(1, rows)]
    arrived, hidden_three, copy_two = lax.optimization_barrier(
        (arrived, hidden_three, copy_two)
    )
    weights, numer, denom = local_call(
        block_body,
        [((sets, SPAN, SPAN), low), ((sets, HD, SPAN), wide), ((SUM_ROWS, SPAN), wide)],
        "block",
        qkv,
        trig,
        reweight,
    )
    prior, attn_wide, branch_own, branch_other = local_call(
        attend_body,
        [
            state_shape,
            ((STATE_ROWS + SUM_ROWS, SPAN), wide),
            block_wide,
            block_low,
        ],
        "attend",
        qkv,
        trig,
        numer,
        denom,
        weight,
        *arrived,
        scratch=[((2, WIDTH, SPAN), low)],
    )
    branch = column_parts(branch_own, branch_other, "branch_half")
    copy_one, copy_three = swap_copies(hidden_one), swap_copies(hidden_three)
    branch, copy_one, copy_three = lax.optimization_barrier((branch, copy_one, copy_three))
    hidden_mine = [hidden_packed[0], hidden_one, hidden_two, hidden_three]
    hidden_copy = [hidden_packed[1], copy_one, copy_two, copy_three]
    first, first_low, normed = local_call(
        norm_body,
        [block_wide, block_low, ((D + 8, SPAN), wide)],
        "norm",
        x_own,
        *branch,
        norm_vecs,
    )
    first_other = swap_pair(first_low)
    half_hidden = [((part, 2 * SPAN), low), ((part, 2 * SPAN), wide)]
    hidden_weight = [((D, 2 * part), low)]
    hidden_mine, act_mine, slope_mine, ffn_own, ffn_other = local_call(
        hidden_body,
        hidden_weight + half_hidden + [block_wide, block_wide],
        "hidden_mine",
        flags,
        first_low,
        first_other,
        *hidden_mine,
    )
    hidden_copy, act_copy, slope_copy, ffn_own, ffn_other = local_call(
        hidden_body,
        hidden_weight + half_hidden + [block_wide, block_low],
        "hidden_copy",
        flags,
        first_low,
        first_other,
        *hidden_copy,
        ffn_own,
        ffn_other,
    )
    ffn = column_parts(ffn_own, ffn_other, "ffn_half")
    result, grad_second, grad_ffn = local_call(
        second_norm_body,
        [block_low, ((D, SPAN + 2 * SUM_LANES), wide), block_low],
        "second_norm",
        first,
        *ffn,
        norm_vecs,
        cot,
        trig,
    )
    grad_ffn_other = swap_pair(grad_ffn)
    pair_low = ((D, part), low)
    kept_down, sent_down = local_call(
        half_grads_body,
        [pair_low, pair_low],
        "down_grad",
        grad_ffn,
        grad_ffn_other,
        act_mine,
        act_copy,
    )
    got_down = swap_copies(sent_down)
    grad_ffn, grad_ffn_other, kept_down = lax.optimization_barrier(
        (grad_ffn, grad_ffn_other, kept_down)
    )
    hidden_low = ((part, 2 * SPAN), low)
    pre_mine, pre_copy, first_own_part, first_other_part = local_call(
        hidden_back_body,
        [hidden_low, hidden_low, block_wide, block_low],
        "hidden_back",
        grad_ffn,
        grad_ffn_other,
        hidden_mine,
        hidden_copy,
        slope_mine,
        slope_copy,
    )
    first_sum = column_parts(first_own_part, first_other_part, "first_half")

    kept_up, sent_up = local_call(
        half_grads_body,
        [pair_low, pair_low],
        "up_grad",
        first_low,
        first_other,
        pre_mine,
        pre_copy,
    )
    got_up = swap_copies(sent_up)
    out_pieces = local_call(
        out_pieces_body, low_outs(rows, half_feats, SPAN), "out_pieces", flags, result
    )
    out_wide = local_call(
        out_place_body,
        low_outs(2, half_feats, SPAN * rows // 2),
        "out_place",
        flags,
        *passed_on(out_pieces),
    )
    first_sum, kept_up, out_wide = lax.optimization_barrier((first_sum, kept_up, out_wide))
    output = cols_back(*out_wide, low, "out_join")
    grad_hidden, branch_grad, vec_sums = local_call(
        norm_back_body,
        [block_wide, block_low, ((D, 2 * SUM_LANES), low)],
        "norm_back",
        grad_second,
        *first_sum,
        normed,
        norm_vecs,
    )
    branch_grad_other = swap_pair(branch_grad)
    (grad_out,) = local_call(
        out_grad_body,
        [((D, WIDTH), low)],
        "out_grad",
        branch_grad,
        branch_grad_other,
        attn_wide,
    )
    grad_num, grad_den, grad_state = local_call(
        grad_attend_body,
        [((sets, HD, SPAN), low), ((SUM_ROWS, SPAN), wide), state_shape],
        "grad_attend",
        branch_grad,
        branch_grad_other,
        weight,
        attn_wide,
        qkv,
        trig,
    )
    later = [shift_rows(grad_state, -step) for step in range(1, rows)]
    grad_query, grad_key, grad_value = local_call(
        grad_block_body,
        [
            ((2, WIDTH, SPAN), low),
            ((sets, HD, SPAN), wide),
            ((sets, HD, SPAN), wide),
        ],
        "grad_block",
        grad_num,
        grad_den,
        qkv,
        trig,
        reweight,
        weights,
        prior,
    )
    down_held, down_sent = local_call(
        pair_pieces_body,
        low_outs(2, 2 * feat_rows, part),
        "down_pieces",
        flags,
        kept_down,
        got_down,
    )
    down_got = swap_rows(down_sent, 1)
    later, got_up, down_got = lax.optimization_barrier((later, got_up, down_got))

    def pair_sums(held, got, name):
        shape = (feat_rows, held.shape[1])
        mine, sent = local_call(pair_sums_body, [(shape, wide), (shape, low)], name, held, got)
        return mine, swap_rows(sent, 2)

    down_sums = pair_sums(down_held, down_got, "down_sums")
    up_held, up_sent = local_call(
        pair_pieces_body,
        low_outs(2, 2 * feat_rows, part + WIDTH),
        "up_pieces",
        flags,
        kept_up,
        got_up,
        grad_out,
    )
    up_sums = pair_sums(up_held, swap_rows(up_sent, 1), "up_sums")
    (hidden_sum,) = local_call(
        hidden_sums_body,
        low_outs(1, feat_rows, 2 * part + WIDTH),
        "hidden_sums",
        *down_sums,
        *up_sums,
    )
    half_rows = ((rows, feat_rows // 2, 3 * WIDTH + SUM_LANES), low)
    kept_w, sent_w, x_grad_own, x_grad_other = local_call(
        grad_project_body,
        [half_rows, half_rows, block_wide, block_low],
        "grad_project",
        grad_query,
        grad_key,
        grad_value,
        qkv,
        trig,
        x_own,
        x_other,
        weight,
        vec_sums,
        flags,
        *later,
        scratch=[state_shape, ((2, 3 * WIDTH, SPAN), low)],
    )
    got_w = swap_copies(sent_w)
    got_x = swap_pair(x_grad_other)
    x_grad_own, got_x, got_w = lax.optimization_barrier((x_grad_own, got_x, got_w))
    x_half_grad, x_half_sent = local_call(
        partial(input_halves_body, rows=rows),
        [((D // 2, SPAN), wide), ((D // 2, SPAN), low)],
        "input_halves",
        flags,
        x_grad_own,
        got_x,
        scratch=[block_wide],
    )
    last_lanes = 3 * WIDTH + SUM_LANES
    last_held, last_sent = local_call(
        last_pieces_body,
        low_outs(2, 2 * half_feats, last_lanes + SPAN),
        "last_pieces",
        flags,
        kept_w,
        got_w,
        x_half_grad,
        swap_cols(x_half_sent),
        grad_hidden,
    )
    last_got = swap_rows(last_sent, 1)
    last_part, last_far = local_call(
        last_pairs_body,
        [((half_feats, last_lanes), wide), ((half_feats, last_lanes + 2 * SPAN), low)],
        "last_pairs",
        last_held,
        last_got,
    )
    last_sum, *input_wide = local_call(
        last_sums_body,
        low_outs(1, half_feats, last_lanes) + low_outs(2, half_feats, SPAN * rows // 2),
        "last_sums",
        flags,
        last_part,
        last_held,
        last_got,
        swap_rows(last_far, 2),
    )
    input_grad = cols_back(*input_wide, wide, "input_join")
    down_t, up_grad, out_t = local_call(
        place_hidden_body,
        [((feat_rows, 4 * part), wide)] * 2 + [((feat_rows, 2 * WIDTH), wide)],
        "place_hidden",
        flags,
        *all_quarters(hidden_sum),
    )
    query_grad, key_grad, value_grad, vec_total = local_call(
        place_last_body,
        [((feat_rows, 2 * WIDTH), wide)] * 3 + [((feat_rows, SUM_LANES), wide)],
        "place_last",
        flags,
        *all_quarters(last_sum),
    )
    return (
        output,
        input_grad,
        query_grad,
        key_grad,
        value_grad,
        out_t.T,
        vec_total[:, 0],
        vec_total[:, 1],
        up_grad,
        down_t.T,
        vec_total[:, 2],
        vec_total[:, 3],
    )


def solution(mesh):
    placed = (
        P("row", ("dp", "col")),
        P(),
        P("row", "col"),
        P("row", "col"),
        P("row", "col"),
        P("col", "row"),
        P("row"),
        P("row"),
        P("row", "col"),
        P("col", "row"),
        P("row"),
        P("row"),
        P("row", ("dp", "col")),
    )
    return jax.shard_map(
        on_device_paired if paired_layout(mesh) else on_device,
        mesh=mesh,
        in_specs=placed,
        out_specs=(
            P("row", ("dp", "col")),
            P("row", ("dp", "col")),
            P("row", "col"),
            P("row", "col"),
            P("row", "col"),
            P("col", "row"),
            P("row"),
            P("row"),
            P("row", "col"),
            P("col", "row"),
            P("row"),
            P("row"),
        ),
        check_vma=False,
    )
```

```python
from functools import partial
import math

import jax
import jax.numpy as jnp
from jax import lax
from jax.experimental import pallas as pl
from jax.experimental.pallas import tpu as pltpu
from jax.sharding import PartitionSpec as P

D = 768
H = 12
HD = 64
SEQ_MAX = 4096
TOK_DEV = 128


norm_eps = 1e-05
highest = lax.Precision.HIGHEST


def carried_in(shard, axis, join, neutral, backward):
    count = lax.axis_size(axis)
    place = lax.axis_index(axis)
    ahead = count - 1 - place if backward else place
    gathered = jax.tree.map(
        lambda a, kind: lax.all_gather(a.astype(kind), axis),
        shard,
        jax.tree.map(lambda a: jnp.bfloat16 if a.dtype == jnp.float32 else a.dtype, shard),
    )
    state = jax.tree.map(lambda a, e: jnp.zeros_like(a) + jnp.asarray(e, a.dtype), shard, neutral)

    def one(turn, state):
        source = count - 1 - turn if backward else turn
        return join(
            state,
            jax.tree.map(
                lambda a, own: lax.dynamic_index_in_dim(a, source, 0, False).astype(own.dtype),
                gathered,
                shard,
            ),
        )

    return lax.fori_loop(0, ahead, one, state)


def gather_cols(operand):
    return lax.all_gather(operand, "col", axis=0, tiled=True)


def gather_rows(operand):
    return lax.all_gather(operand, "row", axis=0, tiled=True)


def summed_over_rows(gathered, matrix):
    out_rows = gathered.shape[0] // lax.axis_size("row")

    def term_rows(first_row, row_count):
        sliced = lax.dynamic_slice_in_dim(gathered, first_row, row_count, 0)
        return jnp.dot(sliced, matrix, preferred_element_type=jnp.float32)

    return lax.psum_scatter(
        term_rows(jnp.int32(0), out_rows * lax.axis_size("row")),
        "row",
        scatter_dimension=0,
        tiled=True,
    )


def summed_over_cols(gathered, matrix):
    out_rows = gathered.shape[0] // lax.axis_size("col")

    def term_rows(first_row, row_count):
        sliced = lax.dynamic_slice_in_dim(gathered, first_row, row_count, 0)
        return jnp.dot(sliced, matrix, preferred_element_type=jnp.float32)

    return lax.psum_scatter(
        term_rows(jnp.int32(0), out_rows * lax.axis_size("col")).astype(jnp.bfloat16),
        "col",
        scatter_dimension=0,
        tiled=True,
    ).astype(jnp.float32)


def to_heads(stacked):
    return lax.all_to_all(stacked, "col", split_axis=1, concat_axis=2, tiled=True)


def to_tokens(stacked):
    return lax.all_to_all(stacked, "col", split_axis=2, concat_axis=1, tiled=True)


def row_totals(first_part, second_part):
    return lax.psum((first_part, second_part), "row")


def norm_forward(hidden, scale_vec, shift_vec):
    sum_one, sum_two = row_totals(jnp.sum(hidden, 1), jnp.sum(hidden * hidden, 1))
    row_mean = sum_one / D
    variance = sum_two / D - row_mean * row_mean
    inv_std = lax.rsqrt(variance + norm_eps)
    normed = (hidden - row_mean[:, None]) * inv_std[:, None]
    return (normed * scale_vec + shift_vec, normed, inv_std)


def norm_backward(grad_in, normed, inv_std, scale_vec):
    grad_normed = grad_in * scale_vec
    total_one, total_two = row_totals(jnp.sum(grad_normed, 1), jnp.sum(grad_normed * normed, 1))
    grad_hidden = inv_std[:, None] * (
        grad_normed - total_one[:, None] / D - normed * (total_two[:, None] / D)
    )
    return (grad_hidden, jnp.sum(grad_in * normed, 0), jnp.sum(grad_in, 0))


def seq_lengths(lengths, seq_ids):
    matches = seq_ids[:, None] == jnp.arange(lengths.shape[0], dtype=jnp.int32)[None, :]
    return jnp.sum(jnp.where(matches, lengths[None, :], 0), 1)


def reset_combine(earlier, later):
    keep_prior = 1.0 - later[4]
    joined = tuple(
        (
            keep_prior * prior_part + next_part
            for prior_part, next_part in zip(earlier[:4], later[:4])
        )
    )
    return joined + (jnp.maximum(earlier[4], later[4]),)


def empty_state():
    return (
        jnp.zeros((H, HD, HD), jnp.float32),
        jnp.zeros((H, HD, HD), jnp.float32),
        jnp.zeros((H, HD), jnp.float32),
        jnp.zeros((H, HD), jnp.float32),
        jnp.zeros((), jnp.float32),
    )


def attend_forward(queries, keys_in, values_in, present, cos_flat, sin_flat, opens_seq):
    block_rows = queries.shape[0]
    cos_pos = cos_flat[:, None, None]
    sin_pos = sin_flat[:, None, None]
    q_pos = jnp.maximum(queries, 0)
    k_pos = jnp.maximum(keys_in, 0) * present[:, None, None].astype(jnp.bfloat16)
    q_cos = q_pos.astype(jnp.float32) * cos_pos
    q_sin = q_pos.astype(jnp.float32) * sin_pos
    k_cos = k_pos.astype(jnp.float32) * cos_pos
    k_sin = k_pos.astype(jnp.float32) * sin_pos
    values_wide = values_in.astype(jnp.float32)
    local_state = (
        jnp.einsum("jhd,jhe->hde", k_cos, values_wide, precision=highest),
        jnp.einsum("jhd,jhe->hde", k_sin, values_wide, precision=highest),
        jnp.sum(k_cos, 0),
        jnp.sum(k_sin, 0),
    )
    arrived = carried_in(
        local_state + (opens_seq,), ("row", "col"), reset_combine, empty_state(), False
    )
    s_cos, s_sin, z_cos, z_sin = tuple(
        (state_part * (1.0 - opens_seq) for state_part in arrived[:4])
    )
    row_ids = jnp.arange(block_rows, dtype=jnp.int32)
    causal = (row_ids[:, None] >= row_ids[None, :]).astype(jnp.float32)
    reweight = (
        cos_flat[:, None] * cos_flat[None, :] + sin_flat[:, None] * sin_flat[None, :]
    ) * causal
    scores = jnp.einsum("ihd,jhd->hij", q_pos, k_pos, preferred_element_type=jnp.float32)
    weights = scores * reweight[None]
    weights_low = weights.astype(jnp.bfloat16)
    numerator = jnp.einsum(
        "hij,jhe->ihe", weights_low, values_in, preferred_element_type=jnp.float32
    )
    numerator = numerator + jnp.einsum("ihd,hde->ihe", q_cos, s_cos, precision=highest)
    numerator = numerator + jnp.einsum("ihd,hde->ihe", q_sin, s_sin, precision=highest)
    denominator = 1.0 + jnp.sum(weights, 2).T
    denominator = denominator + jnp.einsum("ihd,hd->ih", q_cos, z_cos, precision=highest)
    denominator = denominator + jnp.einsum("ihd,hd->ih", q_sin, z_sin, precision=highest)
    mixed = (numerator / denominator[:, :, None]).astype(jnp.bfloat16).reshape(block_rows, D)
    kept = (
        queries,
        keys_in,
        values_in,
        q_pos,
        k_pos,
        q_cos,
        q_sin,
        k_cos,
        k_sin,
        values_wide,
        reweight,
        weights_low,
        numerator,
        denominator,
        s_cos,
        s_sin,
        z_cos,
        z_sin,
        present,
        cos_pos,
        sin_pos,
    )
    return (mixed, kept)


def attend_backward(grad_heads, kept, closes_seq):
    (
        queries,
        keys_in,
        values_in,
        q_pos,
        k_pos,
        q_cos,
        q_sin,
        k_cos,
        k_sin,
        values_wide,
        reweight,
        weights_low,
        numerator,
        denominator,
        s_cos,
        s_sin,
        z_cos,
        z_sin,
        present,
        cos_pos,
        sin_pos,
    ) = kept
    block_rows = queries.shape[0]
    grad_attn = grad_heads.astype(jnp.float32).reshape(block_rows, H, HD)
    grad_num_low = (grad_attn / denominator[:, :, None]).astype(jnp.bfloat16)
    grad_num = grad_num_low.astype(jnp.float32)
    grad_den = -jnp.sum(grad_attn * numerator, 2) / (denominator * denominator)
    grad_weights = jnp.einsum(
        "ihe,jhe->hij", grad_num_low, values_in, preferred_element_type=jnp.float32
    )
    grad_weights = grad_weights + grad_den.T[:, :, None]
    grad_scores = (grad_weights * reweight[None]).astype(jnp.bfloat16)
    local_grad = (
        jnp.einsum("ihd,ihe->hde", q_cos, grad_num, precision=highest),
        jnp.einsum("ihd,ihe->hde", q_sin, grad_num, precision=highest),
        jnp.einsum("ihd,ih->hd", q_cos, grad_den, precision=highest),
        jnp.einsum("ihd,ih->hd", q_sin, grad_den, precision=highest),
    )
    later_sum = carried_in(
        local_grad + (closes_seq,), ("row", "col"), reset_combine, empty_state(), True
    )
    g_cos, g_sin, gz_cos, gz_sin = tuple(
        (state_part * (1.0 - closes_seq) for state_part in later_sum[:4])
    )
    grad_qpos = jnp.einsum("hij,jhd->ihd", grad_scores, k_pos, preferred_element_type=jnp.float32)
    grad_qpos = grad_qpos + cos_pos * (
        jnp.einsum("ihe,hde->ihd", grad_num, s_cos, precision=highest)
        + grad_den[:, :, None] * z_cos[None]
    )
    grad_qpos = grad_qpos + sin_pos * (
        jnp.einsum("ihe,hde->ihd", grad_num, s_sin, precision=highest)
        + grad_den[:, :, None] * z_sin[None]
    )
    grad_kpos = jnp.einsum("hij,ihd->jhd", grad_scores, q_pos, preferred_element_type=jnp.float32)
    grad_kpos = grad_kpos + cos_pos * (
        jnp.einsum("jhe,hde->jhd", values_wide, g_cos, precision=highest) + gz_cos[None]
    )
    grad_kpos = grad_kpos + sin_pos * (
        jnp.einsum("jhe,hde->jhd", values_wide, g_sin, precision=highest) + gz_sin[None]
    )
    grad_values = jnp.einsum(
        "hij,ihe->jhe", weights_low, grad_num_low, preferred_element_type=jnp.float32
    )
    grad_values = grad_values + jnp.einsum("jhd,hde->jhe", k_cos, g_cos, precision=highest)
    grad_values = grad_values + jnp.einsum("jhd,hde->jhe", k_sin, g_sin, precision=highest)
    grad_q = (grad_qpos * (queries > 0).astype(jnp.float32)).astype(jnp.bfloat16)
    grad_k = (grad_kpos * (keys_in > 0).astype(jnp.float32) * present[:, None, None]).astype(
        jnp.bfloat16
    )
    grad_v = grad_values.astype(jnp.bfloat16)
    return (
        grad_q.reshape(block_rows, D),
        grad_k.reshape(block_rows, D),
        grad_v.reshape(block_rows, D),
    )


def on_device(
    tokens,
    lengths,
    w_query,
    w_key,
    w_value,
    w_out,
    gain_one,
    bias_one,
    w_up,
    w_down,
    gain_two,
    bias_two,
    cotangent,
):
    row_count = lax.axis_size("row")
    col_count = lax.axis_size("col")
    seq_len = min(SEQ_MAX, TOK_DEV * row_count * col_count)
    data_idx = lax.axis_index("dp")
    row_idx = lax.axis_index("row")
    col_idx = lax.axis_index("col")
    feat_rows = tokens.shape[0]
    group_idx = row_idx * col_count + col_idx
    global_idx = (data_idx * row_count * col_count + group_idx) * TOK_DEV + jnp.arange(
        TOK_DEV, dtype=jnp.int32
    )
    positions = global_idx % seq_len
    present = (positions < seq_lengths(lengths, global_idx // seq_len)).astype(jnp.float32)
    angles = math.pi * positions.astype(jnp.float32) / (2.0 * seq_len)
    cos_flat = jnp.cos(angles)
    sin_flat = jnp.sin(angles)
    opens_seq = (group_idx * TOK_DEV % seq_len == 0).astype(jnp.float32)
    closes_seq = ((group_idx + 1) * TOK_DEV % seq_len == 0).astype(jnp.float32)
    token_rows = tokens.T
    width_col = w_query.shape[1]
    w_cat = jnp.concatenate([w_query, w_key, w_value], 1)
    x_gathered = gather_cols(token_rows)
    qkv = summed_over_rows(x_gathered, w_cat).astype(jnp.bfloat16)
    stacked = jnp.stack(
        [qkv[:, :width_col], qkv[:, width_col : 2 * width_col], qkv[:, 2 * width_col :]], 0
    )
    head_rows = to_heads(stacked)
    mixed, kept = attend_forward(
        head_rows[0].reshape(TOK_DEV, H, HD),
        head_rows[1].reshape(TOK_DEV, H, HD),
        head_rows[2].reshape(TOK_DEV, H, HD),
        present,
        cos_flat,
        sin_flat,
        opens_seq,
    )
    mixed_two = to_tokens(mixed[None])[0]
    mixed_gathered = gather_rows(mixed_two)
    branch = summed_over_cols(mixed_gathered, w_out)
    first, normed_one, inv_one = norm_forward(
        token_rows.astype(jnp.float32) + branch, gain_one, bias_one
    )
    first_low = first.astype(jnp.bfloat16)
    first_gathered = gather_cols(first_low)
    pre = summed_over_rows(first_gathered, w_up)
    act, gelu_pull = jax.vjp(partial(jax.nn.gelu, approximate=False), pre)
    act_low = act.astype(jnp.bfloat16)
    act_gathered = gather_rows(act_low)
    ffn = summed_over_cols(act_gathered, w_down)
    result, normed_two, inv_two = norm_forward(first + ffn, gain_two, bias_two)
    rows_one = token_rows.shape[0]
    global_one = (data_idx * col_count + col_idx) * rows_one + jnp.arange(rows_one, dtype=jnp.int32)
    present_one = (global_one % seq_len < seq_lengths(lengths, global_one // seq_len)).astype(
        jnp.float32
    )
    grad_result = cotangent.T.astype(jnp.float32) * present_one[:, None]
    grad_second, grad_gain_two, grad_bias_two = norm_backward(
        grad_result, normed_two, inv_two, gain_two
    )
    grad_ffn_gathered = gather_cols(grad_second.astype(jnp.bfloat16))
    act_again = gather_rows(act_low)
    grad_down = jnp.einsum(
        "tf,td->fd", act_again, grad_ffn_gathered, preferred_element_type=jnp.float32
    )
    grad_act = summed_over_rows(grad_ffn_gathered, w_down.T)
    grad_pre = gelu_pull(grad_act)[0].astype(jnp.bfloat16)
    grad_pre_gathered = gather_rows(grad_pre)
    first_again = gather_cols(first_low)
    grad_up = jnp.einsum(
        "td,tf->df", first_again, grad_pre_gathered, preferred_element_type=jnp.float32
    )
    grad_first = summed_over_cols(grad_pre_gathered, w_up.T) + grad_second
    grad_hidden, grad_gain_one, grad_bias_one = norm_backward(
        grad_first, normed_one, inv_one, gain_one
    )
    branch_grad_gathered = gather_cols(grad_hidden.astype(jnp.bfloat16))
    mixed_again = gather_rows(mixed_two)
    grad_out = jnp.einsum(
        "tc,tr->cr", mixed_again, branch_grad_gathered, preferred_element_type=jnp.float32
    )
    grad_mixed = summed_over_rows(branch_grad_gathered, w_out.T).astype(jnp.bfloat16)
    grad_heads = to_heads(grad_mixed[None])[0]
    grad_q, grad_k, grad_v = attend_backward(grad_heads, kept, closes_seq)
    grad_rows = to_tokens(jnp.stack([grad_q, grad_k, grad_v], 0))
    grad_cat = jnp.concatenate([grad_rows[0], grad_rows[1], grad_rows[2]], 1)
    grad_cat_gathered = gather_rows(grad_cat)
    x_again = gather_cols(token_rows)
    grad_cat_w = jnp.einsum(
        "tr,tc->rc", x_again, grad_cat_gathered, preferred_element_type=jnp.float32
    )
    input_rows = summed_over_cols(grad_cat_gathered, w_cat.T) + grad_hidden
    gain_parts = jnp.stack([grad_gain_one, grad_bias_one, grad_gain_two, grad_bias_two], 0)
    gain_sums = lax.psum(gain_parts.reshape(4 * feat_rows), "col")
    grad_query = grad_cat_w[:, :width_col]
    grad_key = grad_cat_w[:, width_col : 2 * width_col]
    grad_value = grad_cat_w[:, 2 * width_col :]
    output = result.astype(jnp.bfloat16).T
    input_grad = input_rows.T
    sums = (
        lax.psum(grad_query.astype(jnp.bfloat16), "dp").astype(jnp.float32),
        lax.psum(grad_key.astype(jnp.bfloat16), "dp").astype(jnp.float32),
        lax.psum(grad_value.astype(jnp.bfloat16), "dp").astype(jnp.float32),
        lax.psum(grad_out.astype(jnp.bfloat16), "dp").astype(jnp.float32),
        lax.psum(grad_up.astype(jnp.bfloat16), "dp").astype(jnp.float32),
        lax.psum(grad_down.astype(jnp.bfloat16), "dp").astype(jnp.float32),
        lax.psum(gain_sums.astype(jnp.bfloat16), "dp").astype(jnp.float32),
    )
    gain_total = sums[6].reshape(4, feat_rows)
    return (
        output,
        input_grad,
        sums[0],
        sums[1],
        sums[2],
        sums[3],
        gain_total[0],
        gain_total[1],
        sums[4],
        sums[5],
        gain_total[2],
        gain_total[3],
    )


def paired_layout(mesh):
    rows, cols, dps = mesh.shape["row"], mesh.shape["col"], mesh.shape["dp"]
    return rows == 4 and cols == 2 and dps == 4 and H % 4 == 0 and 8 * TOK_DEV <= SEQ_MAX


low = jnp.bfloat16
wide = jnp.float32
SPAN = 2 * TOK_DEV
HEADS = H // 4
WIDTH = HEADS * HD
STATE_ROWS = 2 * HEADS * HD
SUM_ROWS = 16
SUM_LANES = 64


def swap_cols(operand):
    return lax.ppermute(operand, "col", [(0, 1), (1, 0)])


def swap_pair(operand):
    return lax.ppermute(operand, "dp", [(i, i ^ 1) for i in range(lax.axis_size("dp"))])


def swap_copies(operand):
    return lax.ppermute(operand, "dp", [(i, i ^ 2) for i in range(lax.axis_size("dp"))])


def shift_rows(operand, step):
    count = lax.axis_size("row")
    pairs = [(i, i + step) for i in range(count) if 0 <= i + step < count]
    return lax.ppermute(operand, "row", pairs)


def swap_rows(operand, mask):
    return lax.ppermute(operand, "row", [(i, i ^ mask) for i in range(4)])


def rotate_rows(operand, step):
    count = lax.axis_size("row")
    return lax.ppermute(operand, "row", [(i, (i + step) % count) for i in range(count)])


def dot_tn(left, right):
    return lax.dot_general(left, right, (((0,), (0,)), ((), ())), preferred_element_type=wide)


def dot_nt(left, right):
    return lax.dot_general(left, right, (((1,), (1,)), ((), ())), preferred_element_type=wide)


def dot_nn(left, right):
    return jnp.dot(left, right, preferred_element_type=wide)


def norm_columns(hidden, scale, shift):
    mean = jnp.mean(hidden, 0, keepdims=True)
    centered = hidden - mean
    variance = jnp.mean(centered * centered, 0, keepdims=True)
    inv_std = lax.rsqrt(variance + norm_eps)
    normed = centered * inv_std
    return (normed * scale + shift, normed, inv_std)


def norm_columns_back(grad_in, normed, inv_std, scale):
    grad_normed = grad_in * scale
    mean_one = jnp.mean(grad_normed, 0, keepdims=True)
    mean_two = jnp.mean(grad_normed * normed, 0, keepdims=True)
    return inv_std * (grad_normed - mean_one - normed * mean_two)


def local_call(body, outs, name, *operands, scratch=(), space=None):
    shapes = [jax.ShapeDtypeStruct(shape, kind) for shape, kind in outs]
    return pl.pallas_call(
        body,
        out_shape=shapes,
        in_specs=[
            pl.BlockSpec(
                memory_space=pltpu.SMEM
                if operand.dtype == jnp.int32
                else space or pltpu.VMEM
            )
            for operand in operands
        ],
        out_specs=[pl.BlockSpec(memory_space=pltpu.VMEM)] * len(outs),
        scratch_shapes=[
            pltpu.VMEM(*kind) if isinstance(kind, tuple) else kind for kind in scratch
        ],
        compiler_params=pltpu.CompilerParams(vmem_limit_bytes=24 * 2**20),
        name=name,
    )(*operands)


CORE, COPY, ROW, COL, SEQ = range(5)


def low_outs(count, *shape):
    return [(shape, low)] * count


def turn_body(flags_ref, lengths_ref, trig_ref, reweight_ref, *, seq_len):
    start = flags_ref[ROW] * SPAN
    positions = start + lax.broadcasted_iota(jnp.int32, (8, SPAN), 1)
    lines = lax.broadcasted_iota(jnp.int32, (8, SPAN), 0)
    angles = math.pi * positions.astype(wide) / (2.0 * seq_len)
    turns = jnp.where(lines == 0, jnp.cos(angles), jnp.where(lines == 1, jnp.sin(angles), 0.0))
    own = lengths_ref[flags_ref[SEQ]]
    other = lengths_ref[flags_ref[SEQ] + 1 - 2 * flags_ref[CORE]]
    limits = jnp.where(lines == 2, own, other)
    present = jnp.where(positions < limits, 1.0, 0.0)
    trig_ref[...] = turns + jnp.where(lines == 2, present, jnp.where(lines == 3, present, 0.0))
    rows = lax.broadcasted_iota(jnp.int32, (SPAN, SPAN), 0)
    cols = lax.broadcasted_iota(jnp.int32, (SPAN, SPAN), 1)
    both = lax.dot_general(
        turns, turns, (((0,), (0,)), ((), ())), precision=highest, preferred_element_type=wide
    )
    reweight_ref[...] = jnp.where(rows <= cols, both, 0.0)


def token_piece(flags_ref, own_ref, recv_ref, step, rows):
    place = lax.rem(flags_ref[ROW] + step, rows)
    half = lax.div(place, rows // 2)
    cols = pl.ds(pl.multiple_of(lax.rem(place, rows // 2) * SPAN, SPAN), SPAN)
    return jnp.where(half == flags_ref[COL], own_ref[:, cols], recv_ref[:, cols])


def pieces_body(flags_ref, own_ref, cot_ref, recv_ref, *refs, rows):
    vec_ref, piece_refs = refs[0], refs[1:]
    part = own_ref.shape[0]
    lines = []
    for line in range(4):
        vec = vec_ref[line : line + 1, :]
        vec = jnp.concatenate([vec, jnp.zeros((1, SPAN - vec.shape[1]), wide)], 1)
        high = vec.astype(low).astype(wide)
        lines = lines + [high, vec - high]
    for step, ref in enumerate(piece_refs):
        ref[:part] = token_piece(flags_ref, own_ref, recv_ref.at[:part], step, rows)
        ref[part : 2 * part] = token_piece(flags_ref, cot_ref, recv_ref.at[part:], step, rows)
        ref[2 * part :] = jnp.concatenate(lines + [jnp.zeros((8, SPAN), wide)], 0).astype(low)


def came_from(flags_ref, step, rows):
    return lax.rem(flags_ref[ROW] + rows - step, rows)


def place_tokens_body(flags_ref, *refs, rows, part):
    pieces, (half_ref, cot_ref, vec_ref) = refs[:rows], refs[rows:]
    for step, ref in enumerate(pieces):
        row = came_from(flags_ref, step, rows)
        half_ref[pl.ds(pl.multiple_of(row * part, 16), part), :] = ref[:part]
        cot_ref[pl.ds(pl.multiple_of(row * part, 16), part), :] = ref[part : 2 * part]
        extra = ref[2 * part :].astype(wide)
        sums = [extra[2 * i : 2 * i + 1] + extra[2 * i + 1 : 2 * i + 2] for i in range(4)]
        columns = jnp.concatenate(sums + [jnp.zeros((4, SPAN), wide)], 0).T
        vec_ref[pl.ds(pl.multiple_of(row * 2 * part, 8), 2 * part), :] = columns[: 2 * part]


def join_halves_body(flags_ref, half_ref, recv_ref, full_ref, *, rows):
    part = half_ref.shape[0] // rows
    first_col = flags_ref[COL] == 0
    for row in range(rows):
        own = half_ref[row * part : (row + 1) * part]
        other = recv_ref[row * part : (row + 1) * part]
        full_ref[2 * row * part : (2 * row + 1) * part] = jnp.where(first_col, own, other)
        full_ref[(2 * row + 1) * part : (2 * row + 2) * part] = jnp.where(first_col, other, own)


def add_body(own_ref, recv_ref, half_ref):
    half_ref[...] = (own_ref[...] + recv_ref[...].astype(wide)).astype(low)


def feature_piece(flags_ref, source, step, rows):
    part = source.shape[0] // (2 * rows)
    start = (lax.rem(flags_ref[ROW] + step, rows) * 2 + flags_ref[COL]) * part
    return source[pl.ds(pl.multiple_of(start, 16), part), :]


def place_back(flags_ref, pieces, rows, own_ref, other_ref):
    half = len(pieces) // 2
    for row, piece in zip(rows, pieces):
        cols = pl.ds(pl.multiple_of(lax.rem(row, half) * SPAN, SPAN), SPAN)
        mine = lax.div(row, half) == flags_ref[COL]

        @pl.when(mine)
        def _(piece=piece, cols=cols):
            own_ref[:, cols] = piece[...]

        @pl.when(jnp.logical_not(mine))
        def _(piece=piece, cols=cols):
            other_ref[:, cols] = piece[...]


def sum_of(refs):
    total = refs[0][...].astype(wide)
    for ref in refs[1:]:
        total = total + ref[...].astype(wide)
    return total


def join_back_body(flags_ref, own_ref, recv_ref, out_ref):
    part = own_ref.shape[0]
    first_col = flags_ref[COL] == 0
    out_ref[:part] = jnp.where(first_col, own_ref[...], recv_ref[...]).astype(out_ref.dtype)
    out_ref[part:] = jnp.where(first_col, recv_ref[...], own_ref[...]).astype(out_ref.dtype)


def input_halves_body(flags_ref, own_ref, recv_ref, half_ref, sent_ref, sum_ref, *, rows):
    part = own_ref.shape[0] // (2 * rows)
    sum_ref[...] = own_ref[...] + recv_ref[...].astype(wide)
    for row in range(rows):
        rows_out = slice(row * part, (row + 1) * part)
        mine = pl.multiple_of((2 * row + flags_ref[COL]) * part, 16)
        theirs = pl.multiple_of((2 * row + 1 - flags_ref[COL]) * part, 16)
        half_ref[rows_out] = sum_ref[pl.ds(mine, part), :]
        sent_ref[rows_out] = sum_ref[pl.ds(theirs, part), :].astype(low)


def last_pieces_body(
    flags_ref, kept_ref, got_ref, half_ref, recv_ref, hidden_ref, held_ref, sent_ref
):
    rows = kept_ref.shape[0]
    part = half_ref.shape[0] // rows
    lanes = kept_ref.shape[2]
    for mask in range(rows):
        ref = sent_ref if mask % 2 else held_ref
        out = slice(mask // 2 * part, (mask // 2 + 1) * part)
        place = partner(flags_ref[ROW], mask)
        ref[out, :lanes] = (kept_ref[place].astype(wide) + got_ref[place].astype(wide)).astype(low)
        rows_in = pl.ds(pl.multiple_of(place * part, 16), part)
        total = half_ref[rows_in, :] + recv_ref[rows_in, :].astype(wide)
        start = pl.multiple_of((place * 2 + flags_ref[COL]) * part, 16)
        ref[out, lanes:] = (total + hidden_ref[pl.ds(start, part), :]).astype(low)


def last_pairs_body(held_ref, got_ref, sum_ref, sent_ref):
    part, lanes = sum_ref.shape
    sum_ref[...] = held_ref[:part, :lanes].astype(wide) + got_ref[:part, :lanes].astype(wide)
    pair = held_ref[part:, :lanes].astype(wide) + got_ref[part:, :lanes].astype(wide)
    sent_ref[:, :lanes] = pair.astype(low)
    sent_ref[:, lanes : lanes + SPAN] = held_ref[part:, lanes:]
    sent_ref[:, lanes + SPAN :] = got_ref[part:, lanes:]


def last_sums_body(
    flags_ref, part_ref, held_ref, got_ref, far_ref, sum_ref, own_ref, other_ref
):
    part, lanes = part_ref.shape
    sum_ref[...] = (part_ref[...] + far_ref[:, :lanes].astype(wide)).astype(low)
    pieces = (
        held_ref.at[:part, lanes:],
        got_ref.at[:part, lanes:],
        far_ref.at[:, lanes : lanes + SPAN],
        far_ref.at[:, lanes + SPAN :],
    )
    rows = [partner(flags_ref[ROW], mask) for mask in range(4)]
    place_back(flags_ref, pieces, rows, own_ref, other_ref)


def pair_pieces_body(flags_ref, kept_ref, got_ref, *refs):
    extras, (held_ref, sent_ref) = refs[:-2], refs[-2:]
    rows = 4
    feats, part = kept_ref.shape[0] // rows, kept_ref.shape[1]
    for mask in range(rows):
        ref = sent_ref if mask % 2 else held_ref
        out = slice(mask // 2 * feats, (mask // 2 + 1) * feats)
        place = partner(flags_ref[ROW], mask)
        rows_in = pl.ds(pl.multiple_of(place * feats, 16), feats)
        ref[out, :part] = (
            kept_ref[rows_in, :].astype(wide) + got_ref[rows_in, :].astype(wide)
        ).astype(low)
        lane = part
        for extra in extras:
            width = min(extra.shape[1], ref.shape[1] - lane)
            ref[out, lane : lane + width] = extra[rows_in, :width]
            lane = lane + width


def pair_sums_body(held_ref, got_ref, sum_ref, sent_ref):
    feats = sum_ref.shape[0]
    sum_ref[...] = held_ref[:feats].astype(wide) + got_ref[:feats].astype(wide)
    sent_ref[...] = (held_ref[feats:].astype(wide) + got_ref[feats:].astype(wide)).astype(low)


def hidden_sums_body(down_ref, up_ref, up_far_ref, sum_ref):
    part = down_ref.shape[1]
    sum_ref[:, :part] = down_ref[...]
    sum_ref[:, part:] = (up_ref[...] + up_far_ref[...].astype(wide)).astype(low)


def down_pieces_body(flags_ref, kept_ref, got_ref, result_ref, held_ref, sent_ref):
    feats, part = kept_ref.shape[0] // 4, kept_ref.shape[1]
    half = feats // 2
    for mask in range(4):
        ref = sent_ref if mask % 2 else held_ref
        start = mask // 2 * feats
        place = partner(flags_ref[ROW], mask)
        rows_in = pl.ds(pl.multiple_of(place * feats, 16), feats)
        ref[start : start + feats, :part] = (
            kept_ref[rows_in, :].astype(wide) + got_ref[rows_in, :].astype(wide)
        ).astype(low)
        rows_in = pl.ds(pl.multiple_of((place * 2 + flags_ref[COL]) * half, 16), half)
        ref[start : start + half, part:] = result_ref[rows_in, : SPAN // 2]
        ref[start + half : start + feats, part:] = result_ref[rows_in, SPAN // 2 :]


def down_pairs_body(held_ref, got_ref, sum_ref, sent_ref):
    feats, part = sum_ref.shape
    lanes = SPAN // 2
    sum_ref[...] = held_ref[:feats, :part].astype(wide) + got_ref[:feats, :part].astype(wide)
    pair = held_ref[feats:, :part].astype(wide) + got_ref[feats:, :part].astype(wide)
    sent_ref[:, :part] = pair.astype(low)
    sent_ref[:, part : part + lanes] = held_ref[feats:, part:]
    sent_ref[:, part + lanes :] = got_ref[feats:, part:]


def down_sums_body(
    flags_ref, part_ref, held_ref, got_ref, far_ref, sum_ref, own_ref, other_ref, piece_ref
):
    feats, part = part_ref.shape
    lanes = SPAN // 2
    sum_ref[...] = (part_ref[...] + far_ref[:, :part].astype(wide)).astype(low)
    pieces = (
        held_ref[:feats, part:],
        got_ref[:feats, part:],
        far_ref[:, part : part + lanes],
        far_ref[:, part + lanes :],
    )
    for place, piece in enumerate(pieces):
        piece_ref[place, :, :lanes] = piece[: feats // 2]
        piece_ref[place, :, lanes:] = piece[feats // 2 :]
    rows = [partner(flags_ref[ROW], mask) for mask in range(4)]
    place_back(flags_ref, [piece_ref.at[i] for i in range(4)], rows, own_ref, other_ref)


def head_sets():
    return [(seq, head, seq * HEADS + head) for seq in range(2) for head in range(HEADS)]


def set_row(place):
    ids = lax.broadcasted_iota(jnp.int32, (SUM_ROWS, SPAN), 0)
    return (ids == place).astype(wide)


def turned(parts, trig_ref):
    part_wide = parts.astype(wide)
    return jnp.concatenate(
        [(part_wide * trig_ref[0:1, :]).astype(low), (part_wide * trig_ref[1:2, :]).astype(low)], 0
    )


def unturned(pair, trig_ref):
    return pair[:HD] * trig_ref[0:1, :] + pair[HD:] * trig_ref[1:2, :]


def query_part(qkv_ref, seq, head):
    return qkv_ref[seq, head * HD : (head + 1) * HD, :]


def key_part(qkv_ref, seq, head):
    return qkv_ref[seq, WIDTH + head * HD : WIDTH + (head + 1) * HD, :]


def value_part(qkv_ref, seq, head):
    return qkv_ref[seq, 2 * WIDTH + head * HD : 2 * WIDTH + (head + 1) * HD, :]


def kept_keys(qkv_ref, trig_ref, seq, head):
    keys = jnp.maximum(key_part(qkv_ref, seq, head), 0)
    return (keys.astype(wide) * trig_ref[2 + seq : 3 + seq, :]).astype(low)


def state_slice(state, place):
    return state[place * HD : (place + 1) * HD]


def pack_hidden_body(flags_ref, up_ref, down_ref, mine_ref, copy_ref, sems):
    part = mine_ref.shape[1] // 2
    copies = []
    for half, packed_ref in enumerate((mine_ref, copy_ref)):
        copy = 1 - flags_ref[COPY] if half else flags_ref[COPY]
        start = pl.multiple_of((flags_ref[CORE] * 2 + copy) * part, 128)
        for place, ref in enumerate((up_ref, down_ref)):
            copies.append(
                pltpu.make_async_copy(
                    ref.at[:, pl.ds(start, part)],
                    packed_ref.at[:, pl.ds(place * part, part)],
                    sems.at[2 * half + place],
                )
            )
    for copy in copies:
        copy.start()
    for copy in copies:
        copy.wait()


def partner(row, mask):
    if mask == 0:
        return row
    if mask == 1:
        return row + 1 - 2 * lax.rem(row, 2)
    return lax.rem(row + 2, 4) if mask == 2 else 3 - row


def row_block(flags_ref, mask, feats):
    return pl.ds(pl.multiple_of(partner(flags_ref[ROW], mask) * feats, 16), feats)


def project_body(flags_ref, own_ref, other_ref, trig_ref, packed_ref, *refs):
    weight_ref, qkv_ref, state_ref = refs[-3:]
    blocks = refs[:-3]
    count = len(blocks) // 2
    first_copy = flags_ref[COPY] == 0
    feats = packed_ref.shape[0]
    part = packed_ref.shape[1] // 2

    def rows_of(mask):
        return row_block(flags_ref, mask, feats)

    weight_ref[rows_of(0), :] = packed_ref[...]
    for step in range(1, count + 1):
        mine, copied = blocks[step - 1][...], blocks[count + step - 1][...]
        weight_ref[rows_of(step), :part] = jnp.where(first_copy, mine, copied)
        weight_ref[rows_of(step), part:] = jnp.where(first_copy, copied, mine)
    matrix = weight_ref[:, : 3 * WIDTH]
    for seq, x_ref in enumerate((own_ref, other_ref)):
        qkv_ref[seq] = dot_tn(matrix, x_ref[...]).astype(low)
    sums = jnp.zeros((SUM_ROWS, 2 * HD), wide)
    for seq, head, place in head_sets():
        turned_keys = turned(kept_keys(qkv_ref, trig_ref, seq, head), trig_ref)
        values = value_part(qkv_ref, seq, head)
        state_ref[place * HD : (place + 1) * HD, :] = dot_nt(values, turned_keys).astype(low)
        sums = sums + dot_nt(set_row(place).astype(low), turned_keys)
    state_ref[STATE_ROWS:, :] = sums.astype(low)


def block_body(qkv_ref, trig_ref, reweight_ref, weights_ref, numer_ref, denom_ref):
    denoms = jnp.zeros((SUM_ROWS, SPAN), wide)
    for seq, head, place in head_sets():
        queries = jnp.maximum(query_part(qkv_ref, seq, head), 0)
        keys = kept_keys(qkv_ref, trig_ref, seq, head)
        weights = dot_tn(keys, queries) * reweight_ref[...]
        weights_low = weights.astype(low)
        weights_ref[place] = weights_low
        numer_ref[place] = dot_nn(value_part(qkv_ref, seq, head), weights_low)
        denoms = denoms + set_row(place) * jnp.sum(weights, 0, keepdims=True)
    denom_ref[...] = denoms


def attend_body(
    qkv_ref,
    trig_ref,
    numer_ref,
    denom_ref,
    weight_ref,
    *refs,
):
    arrived = refs[:-5]
    prior_ref, attn_wide_ref, own_ref, other_ref, attn_ref = refs[-5:]
    total = arrived[0][...].astype(wide)
    for ref in arrived[1:]:
        total = total + ref[...].astype(wide)
    prior_ref[...] = total.astype(low)
    matrix = weight_ref[:, 3 * WIDTH : 4 * WIDTH]
    prior_sums = prior_ref[STATE_ROWS:, :]
    inverses = jnp.zeros((SUM_ROWS, SPAN), wide)
    for seq, head, place in head_sets():
        queries = turned(jnp.maximum(query_part(qkv_ref, seq, head), 0), trig_ref)
        prior = prior_ref[place * HD : (place + 1) * HD, :]
        numer = numer_ref[place] + dot_nn(prior, queries)
        denoms = dot_nn(prior_sums, queries) + denom_ref[...]
        denom = 1.0 + jnp.sum(denoms * set_row(place), 0, keepdims=True)
        inverse = 1.0 / denom
        inverses = inverses + set_row(place) * inverse
        attended = numer * inverse
        attn_wide_ref[place * HD : (place + 1) * HD, :] = attended
        attn_ref[seq, head * HD : (head + 1) * HD, :] = attended.astype(low)
    attn_wide_ref[STATE_ROWS:, :] = inverses
    own_ref[...] = dot_nn(matrix, attn_ref[0])
    other_ref[...] = dot_nn(matrix, attn_ref[1]).astype(low)


def grad_attend_body(
    own_ref,
    other_ref,
    weight_ref,
    attn_wide_ref,
    qkv_ref,
    trig_ref,
    grad_num_ref,
    grad_den_ref,
    state_ref,
):
    matrix = weight_ref[:, 3 * WIDTH : 4 * WIDTH]
    sums = jnp.zeros((SUM_ROWS, 2 * HD), wide)
    dens = jnp.zeros((SUM_ROWS, SPAN), wide)
    for seq, grad_ref in enumerate((own_ref, other_ref)):
        grads = dot_tn(matrix, grad_ref[...]).astype(low).astype(wide)
        for head in range(HEADS):
            place = seq * HEADS + head
            inverse = jnp.sum(attn_wide_ref[STATE_ROWS:, :] * set_row(place), 0, keepdims=True)
            scaled = grads[head * HD : (head + 1) * HD] * inverse
            grad_num = scaled.astype(low)
            grad_num_ref[place] = grad_num
            grad_den = -jnp.sum(scaled * attn_wide_ref[place * HD : (place + 1) * HD, :], 0, keepdims=True)
            den_row = set_row(place) * grad_den
            dens = dens + den_row
            queries = turned(jnp.maximum(query_part(qkv_ref, seq, head), 0), trig_ref)
            state_ref[place * HD : (place + 1) * HD, :] = dot_nt(grad_num, queries).astype(low)
            sums = sums + dot_nt(den_row.astype(low), queries)
    state_ref[STATE_ROWS:, :] = sums.astype(low)
    grad_den_ref[...] = dens


def grad_block_body(
    grad_num_ref,
    grad_den_ref,
    qkv_ref,
    trig_ref,
    reweight_ref,
    weights_ref,
    prior_ref,
    grad_query_ref,
    grad_key_ref,
    grad_value_ref,
):
    prior_sums = prior_ref[STATE_ROWS:, :]
    for seq, head, place in head_sets():
        query = query_part(qkv_ref, seq, head)
        queries = jnp.maximum(query, 0)
        keys = kept_keys(qkv_ref, trig_ref, seq, head)
        grad_num = grad_num_ref[place]
        den_rows = grad_den_ref[...] * set_row(place)
        grad_den = jnp.sum(den_rows, 0, keepdims=True)
        grad_scores = (
            (dot_tn(value_part(qkv_ref, seq, head), grad_num) + grad_den) * reweight_ref[...]
        ).astype(low)
        prior = jnp.concatenate([prior_ref[place * HD : (place + 1) * HD, :], prior_sums], 0)
        grads = jnp.concatenate([grad_num, den_rows.astype(low)], 0)
        grad_query = dot_nn(keys, grad_scores) + unturned(dot_tn(prior, grads), trig_ref)
        grad_query_ref[seq, head * HD : (head + 1) * HD, :] = jnp.where(
            query.astype(wide) > 0, grad_query, 0.0
        ).astype(low)
        grad_key_ref[place] = dot_nt(queries, grad_scores)
        grad_value_ref[place] = dot_nt(grad_num, weights_ref[place])


def grad_project_body(
    grad_query_ref,
    grad_key_ref,
    grad_value_ref,
    qkv_ref,
    trig_ref,
    x_own_ref,
    x_other_ref,
    weight_ref,
    flags_ref,
    *refs,
):
    arrived = refs[:-6]
    kept_ref, sent_ref, own_ref, other_ref, after_ref, grad_ref = refs[-6:]
    total = arrived[0][...].astype(wide)
    for ref in arrived[1:]:
        total = total + ref[...].astype(wide)
    after_ref[...] = total.astype(low)
    after_sums = after_ref[STATE_ROWS:, :]
    for seq, head, place in head_sets():
        key = key_part(qkv_ref, seq, head)
        keys = turned(kept_keys(qkv_ref, trig_ref, seq, head), trig_ref)
        values = value_part(qkv_ref, seq, head)
        after = after_ref[place * HD : (place + 1) * HD, :]
        left = jnp.concatenate([after, after_sums], 0)
        right = jnp.concatenate([values, set_row(place).astype(low)], 0)
        grad_key = grad_key_ref[place] + unturned(dot_tn(left, right), trig_ref)
        grad_key = jnp.where(key.astype(wide) > 0, grad_key, 0.0) * trig_ref[2 + seq : 3 + seq, :]
        grad_value = grad_value_ref[place] + dot_nn(after, keys)
        rows = slice(head * HD, (head + 1) * HD)
        grad_ref[seq, rows, :] = grad_query_ref[seq, rows, :]
        rows = slice(WIDTH + head * HD, WIDTH + (head + 1) * HD)
        grad_ref[seq, rows, :] = grad_key.astype(low)
        rows = slice(2 * WIDTH + head * HD, 2 * WIDTH + (head + 1) * HD)
        grad_ref[seq, rows, :] = grad_value.astype(low)
    matrix = weight_ref[:, : 3 * WIDTH]
    grad_w = (
        dot_nt(x_own_ref[...], grad_ref[0]) + dot_nt(x_other_ref[...], grad_ref[1])
    ).astype(low)
    rows, part, _ = kept_ref.shape
    first_copy = flags_ref[COPY] == 0
    for row in range(rows):
        start = row * 2 * part
        first, second = grad_w[start : start + part], grad_w[start + part : start + 2 * part]
        kept_ref[row] = jnp.where(first_copy, first, second)
        sent_ref[row] = jnp.where(first_copy, second, first)
    own_ref[...] = dot_nn(matrix, grad_ref[0])
    other_ref[...] = dot_nn(matrix, grad_ref[1]).astype(low)


def norm_body(x_ref, half_ref, recv_ref, vec_ref, first_ref, low_ref, normed_ref):
    hidden = x_ref[...].astype(wide) + (half_ref[...].astype(wide) + recv_ref[...].astype(wide))
    first, normed, inv_std = norm_columns(hidden, vec_ref[:, 0:1], vec_ref[:, 1:2])
    first_ref[...] = first
    low_ref[...] = first.astype(low)
    normed_ref[:D, :] = normed
    normed_ref[D:, :] = jnp.broadcast_to(inv_std, (8, SPAN))


def lane_sums(columns, place):
    lanes = lax.broadcasted_iota(jnp.int32, (columns[0].shape[0], 2 * SUM_LANES), 1)
    total = jnp.zeros(lanes.shape, wide)
    for shift, column in enumerate(columns):
        total = jnp.where(lanes == place + shift, jnp.sum(column, 1, keepdims=True), total)
    return total


def second_norm_body(
    first_ref, half_ref, recv_ref, vec_ref, cot_ref, trig_ref, result_ref, grad_ref, low_ref
):
    hidden = first_ref[...] + (half_ref[...].astype(wide) + recv_ref[...].astype(wide))
    scale = vec_ref[:, 2:3]
    result, normed, inv_std = norm_columns(hidden, scale, vec_ref[:, 3:4])
    result_ref[...] = result.astype(low)
    grad_in = cot_ref[...].astype(wide) * trig_ref[2:3, :]
    grad = norm_columns_back(grad_in, normed, inv_std, scale)
    grad_ref[:, :SPAN] = grad
    low_ref[...] = grad.astype(low)
    grad_ref[:, SPAN:] = lane_sums((grad_in * normed, grad_in), 2)


def norm_back_body(
    grad_ref, half_ref, recv_ref, normed_ref, vec_ref, hidden_ref, low_ref, sum_ref
):
    grad_in = grad_ref[:, :SPAN] + (half_ref[...].astype(wide) + recv_ref[...].astype(wide))
    normed = normed_ref[:D, :]
    grad = norm_columns_back(grad_in, normed, normed_ref[D : D + 1, :], vec_ref[:, 0:1])
    hidden_ref[...] = grad
    low_ref[...] = grad.astype(low)
    sum_ref[...] = (lane_sums((grad_in * normed, grad_in), 0) + grad_ref[:, SPAN:]).astype(low)


def hidden_body(flags_ref, own_ref, other_ref, *refs):
    weight_ref, act_ref, slope_ref, part_own_ref, part_other_ref = refs[-5:]
    blocks, earlier = refs[:4], refs[4:-5]
    part = act_ref.shape[0]
    for mask, ref in enumerate(blocks):
        weight_ref[row_block(flags_ref, mask, ref.shape[0]), :] = ref[...]
    up = weight_ref[:, :part]
    down = weight_ref[:, part:]
    for seq, (x_ref, part_ref) in enumerate(
        ((own_ref, part_own_ref), (other_ref, part_other_ref))
    ):
        cols = slice(seq * SPAN, (seq + 1) * SPAN)
        act, slope = gelu_and_slope(dot_tn(up, x_ref[...]))
        act_ref[:, cols] = act
        slope_ref[:, cols] = slope
        total = dot_nn(down, act)
        if earlier:
            total = total + earlier[seq][...]
        part_ref[...] = total.astype(part_ref.dtype)


def hidden_back_body(
    own_ref,
    other_ref,
    mine_ref,
    copy_ref,
    slope_mine_ref,
    slope_copy_ref,
    pre_mine_ref,
    pre_copy_ref,
    part_own_ref,
    part_other_ref,
):
    part = slope_mine_ref.shape[0]
    for seq, (x_ref, part_ref) in enumerate(
        ((own_ref, part_own_ref), (other_ref, part_other_ref))
    ):
        cols = slice(seq * SPAN, (seq + 1) * SPAN)
        total = None
        for weight_ref, slope_ref, pre_ref in (
            (mine_ref, slope_mine_ref, pre_mine_ref),
            (copy_ref, slope_copy_ref, pre_copy_ref),
        ):
            grad_pre = (dot_tn(weight_ref[:, part:], x_ref[...]) * slope_ref[:, cols]).astype(low)
            pre_ref[:, cols] = grad_pre
            term = dot_nn(weight_ref[:, :part], grad_pre)
            total = term if total is None else total + term
        part_ref[...] = total.astype(part_ref.dtype)


def half_grads_body(own_ref, other_ref, mine_ref, copy_ref, kept_ref, sent_ref):
    for pre_ref, out_ref in ((copy_ref, sent_ref), (mine_ref, kept_ref)):
        out_ref[...] = (
            dot_nt(own_ref[...], pre_ref[:, :SPAN]) + dot_nt(other_ref[...], pre_ref[:, SPAN:])
        ).astype(low)


def out_grad_body(own_ref, other_ref, attn_wide_ref, out_ref):
    out_ref[...] = (
        dot_nt(own_ref[...], attn_wide_ref[:WIDTH, :].astype(low))
        + dot_nt(other_ref[...], attn_wide_ref[WIDTH : 2 * WIDTH, :].astype(low))
    ).astype(low)


def quarters(flags_ref, refs):
    core, copy = flags_ref[CORE], flags_ref[COPY]
    for ref, other_core, other_copy in zip(refs, (0, 0, 1, 1), (0, 1, 0, 1)):
        core_place = 1 - core if other_core else core
        copy_place = 1 - copy if other_copy else copy
        yield core_place * 2 + copy_place, ref


def place_hidden_body(flags_ref, *refs):
    down_ref, up_ref, out_ref, vec_ref = refs[4:]
    part = up_ref.shape[1] // 4
    for place, ref in quarters(flags_ref, refs[:4]):
        cols = pl.ds(pl.multiple_of(place * part, 128), part)
        down_ref[:, cols] = ref[:, :part].astype(wide)
        up_ref[:, cols] = ref[:, part : 2 * part].astype(wide)
    sums = [ref[:, 2 * part :].astype(wide) for ref in refs[:4]]
    own, other = sums[0] + sums[1], sums[2] + sums[3]
    vec_ref[...] = own[:, WIDTH:] + other[:, WIDTH:]
    own, other = own[:, :WIDTH], other[:, :WIDTH]
    first_core = flags_ref[CORE] == 0
    out_ref[:, :WIDTH] = jnp.where(first_core, own, other)
    out_ref[:, WIDTH:] = jnp.where(first_core, other, own)


def place_last_body(flags_ref, *refs):
    outs = refs[4:]
    first_core = flags_ref[CORE] == 0
    part = refs[0].shape[0]
    for own_ref, other_ref, other_copy in ((refs[0], refs[2], 0), (refs[1], refs[3], 1)):
        copy = 1 - flags_ref[COPY] if other_copy else flags_ref[COPY]
        rows = pl.ds(pl.multiple_of(copy * part, 8), part)
        own, other = own_ref[...].astype(wide), other_ref[...].astype(wide)
        for place, out_ref in enumerate(outs):
            cols = slice(place * WIDTH, (place + 1) * WIDTH)
            out_ref[rows, :WIDTH] = jnp.where(first_core, own[:, cols], other[:, cols])
            out_ref[rows, WIDTH:] = jnp.where(first_core, other[:, cols], own[:, cols])


def gelu_and_slope(pre):
    cdf = 0.5 * (1.0 + lax.erf(pre * math.sqrt(0.5)))
    density = jnp.exp(-0.5 * pre * pre) * (1.0 / math.sqrt(2.0 * math.pi))
    return (pre * cdf).astype(low), (cdf + pre * density)


def all_quarters(own, direct=False):
    copied = swap_copies(own)
    if direct:
        pairs = [(i, i ^ 3) for i in range(lax.axis_size("dp"))]
        return own, copied, swap_pair(own), lax.ppermute(own, "dp", pairs)
    return own, copied, swap_pair(own), swap_pair(copied)


def on_device_paired(
    tokens,
    lengths,
    w_query,
    w_key,
    w_value,
    w_out,
    gain_one,
    bias_one,
    w_up,
    w_down,
    gain_two,
    bias_two,
    cotangent,
):
    rows = lax.axis_size("row")
    seq_len = SPAN * rows
    dp_idx = lax.axis_index("dp")
    feat_rows = tokens.shape[0]
    half_feats = feat_rows // 2
    flags = jnp.stack(
        [dp_idx % 2, dp_idx // 2, lax.axis_index("row"), lax.axis_index("col"), dp_idx]
    )
    trig, reweight = local_call(
        partial(turn_body, seq_len=seq_len),
        [((8, SPAN), wide), ((SPAN, SPAN), wide)],
        "turn",
        flags,
        lengths,
    )

    def passed_on(pieces):
        return [pieces[0]] + [
            rotate_rows(piece, step) for step, piece in enumerate(pieces) if step
        ]

    def joined_halves(half, got, name):
        return local_call(
            partial(join_halves_body, rows=rows), [((D, SPAN), low)], name, flags, half, got
        )[0]

    def cols_back(own, other, kind, name):
        return local_call(
            join_back_body,
            [((feat_rows, SPAN * rows // 2), kind)],
            name,
            flags,
            own,
            swap_cols(other),
        )[0]

    def column_parts(own_part, other_part, name):
        (half,) = local_call(add_body, low_outs(1, D, SPAN), name, own_part, swap_pair(other_part))
        return half, swap_cols(half)

    first_col = lax.axis_index("col") == 0

    def halved(block):
        top, bottom = block[:half_feats], block[half_feats:]
        return jnp.where(first_col, top, bottom), jnp.where(first_col, bottom, top)

    (token_own, token_sent), (cot_own, cot_sent) = halved(tokens), halved(cotangent)
    got = swap_cols(jnp.concatenate([token_sent, cot_sent], 0))

    part = w_up.shape[1] // 4
    first_core = dp_idx % 2 == 0

    def core_part(operand):
        return jnp.where(first_core, operand[:, :WIDTH], operand[:, WIDTH:])

    parts = [core_part(operand) for operand in (w_query, w_key, w_value, w_out.T)]
    first_packed = jnp.concatenate(parts, 1)
    first_mine = jnp.where(
        dp_idx < 2, jnp.concatenate(parts[:2], 1), jnp.concatenate(parts[2:], 1)
    )

    def row_blocks(block):
        return swap_rows(block, 1), swap_rows(block, 2)

    first_one, first_two = row_blocks(first_mine)
    first_one, got = lax.optimization_barrier((first_one, got))
    hidden_packed = local_call(
        pack_hidden_body,
        low_outs(2, feat_rows, 2 * part),
        "pack_hidden",
        flags,
        w_up,
        w_down.T,
        scratch=[pltpu.SemaphoreType.DMA((4,))],
        space=pltpu.HBM,
    )
    vecs = jnp.stack([gain_one, bias_one, gain_two, bias_two], 0)
    token_pieces = local_call(
        partial(pieces_body, rows=rows),
        low_outs(rows, feat_rows + 16, SPAN),
        "token_pieces",
        flags,
        token_own,
        cot_own,
        got,
        vecs,
    )
    def after(value, *others):
        return lax.optimization_barrier((value, others))[0]

    first_three = swap_rows(after(first_two, token_pieces[0]), 1)
    first_copies = [
        swap_copies(after(first_one, token_pieces[0])),
        swap_copies(first_two),
        swap_copies(first_three),
    ]
    token_pieces = passed_on(token_pieces)
    token_pieces, first_three, first_copies[0] = lax.optimization_barrier(
        (token_pieces, first_three, first_copies[0])
    )
    first_blocks = [first_one, first_two, first_three, *first_copies]
    x_half, cot_half, norm_vecs = local_call(
        partial(place_tokens_body, rows=rows, part=half_feats),
        low_outs(2, D // 2, SPAN) + [((D, 8), wide)],
        "token_place",
        flags,
        *token_pieces,
    )
    x_half, trig, reweight, hidden_packed = lax.optimization_barrier(
        (x_half, trig, reweight, hidden_packed)
    )
    hidden_one, hidden_two = row_blocks(hidden_packed[0])
    x_got, hidden_one = lax.optimization_barrier((swap_cols(x_half), hidden_one))
    x_own = joined_halves(x_half, x_got, "token_join")
    cot = joined_halves(cot_half, swap_cols(cot_half), "cot_join")
    x_own, first_blocks = lax.optimization_barrier((x_own, first_blocks))
    x_other = swap_pair(x_own)
    hidden_three = swap_rows(hidden_two, 1)
    copy_two = swap_copies(hidden_two)
    state_shape = ((STATE_ROWS + SUM_ROWS, 2 * HD), low)
    sets = 2 * HEADS
    block_low = ((D, SPAN), low)
    block_wide = ((D, SPAN), wide)
    weight, qkv, state = local_call(
        project_body,
        [((D, 4 * WIDTH), low), ((2, 3 * WIDTH, SPAN), low), state_shape],
        "project",
        flags,
        x_own,
        x_other,
        trig,
        first_packed,
        *first_blocks,
    )
    arrived = [shift_rows(state, step) for step in range(1, rows)]
    arrived, hidden_three, copy_two = lax.optimization_barrier(
        (arrived, hidden_three, copy_two)
    )
    weights, numer, denom = local_call(
        block_body,
        [((sets, SPAN, SPAN), low), ((sets, HD, SPAN), wide), ((SUM_ROWS, SPAN), wide)],
        "block",
        qkv,
        trig,
        reweight,
    )
    prior, attn_wide, branch_own, branch_other = local_call(
        attend_body,
        [
            state_shape,
            ((STATE_ROWS + SUM_ROWS, SPAN), wide),
            block_wide,
            block_low,
        ],
        "attend",
        qkv,
        trig,
        numer,
        denom,
        weight,
        *arrived,
        scratch=[((2, WIDTH, SPAN), low)],
    )
    copy_one = swap_copies(hidden_one)
    branch_own, branch_other, copy_one = lax.optimization_barrier(
        (branch_own, branch_other, copy_one)
    )
    branch = column_parts(branch_own, branch_other, "branch_half")
    copy_three = swap_copies(hidden_three)
    branch, copy_three = lax.optimization_barrier((branch, copy_three))
    hidden_mine = [hidden_packed[0], hidden_one, hidden_two, hidden_three]
    hidden_copy = [hidden_packed[1], copy_one, copy_two, copy_three]
    first, first_low, normed = local_call(
        norm_body,
        [block_wide, block_low, ((D + 8, SPAN), wide)],
        "norm",
        x_own,
        *branch,
        norm_vecs,
    )
    first_other = swap_pair(first_low)
    half_hidden = [((part, 2 * SPAN), low), ((part, 2 * SPAN), wide)]
    hidden_weight = [((D, 2 * part), low)]
    hidden_mine, act_mine, slope_mine, ffn_own, ffn_other = local_call(
        hidden_body,
        hidden_weight + half_hidden + [block_wide, block_wide],
        "hidden_mine",
        flags,
        first_low,
        first_other,
        *hidden_mine,
    )
    hidden_copy, act_copy, slope_copy, ffn_own, ffn_other = local_call(
        hidden_body,
        hidden_weight + half_hidden + [block_wide, block_low],
        "hidden_copy",
        flags,
        first_low,
        first_other,
        *hidden_copy,
        ffn_own,
        ffn_other,
    )
    ffn = column_parts(ffn_own, ffn_other, "ffn_half")
    result, grad_second, grad_ffn = local_call(
        second_norm_body,
        [block_low, ((D, SPAN + 2 * SUM_LANES), wide), block_low],
        "second_norm",
        first,
        *ffn,
        norm_vecs,
        cot,
        trig,
    )
    grad_ffn_other = swap_pair(grad_ffn)
    pair_low = ((D, part), low)
    kept_down, sent_down = local_call(
        half_grads_body,
        [pair_low, pair_low],
        "down_grad",
        grad_ffn,
        grad_ffn_other,
        act_mine,
        act_copy,
    )
    got_down = swap_copies(sent_down)
    grad_ffn, grad_ffn_other, kept_down = lax.optimization_barrier(
        (grad_ffn, grad_ffn_other, kept_down)
    )
    hidden_low = ((part, 2 * SPAN), low)
    pre_mine, pre_copy, first_own_part, first_other_part = local_call(
        hidden_back_body,
        [hidden_low, hidden_low, block_wide, block_low],
        "hidden_back",
        grad_ffn,
        grad_ffn_other,
        hidden_mine,
        hidden_copy,
        slope_mine,
        slope_copy,
    )
    first_sum = column_parts(first_own_part, first_other_part, "first_half")

    kept_up, sent_up = local_call(
        half_grads_body,
        [pair_low, pair_low],
        "up_grad",
        first_low,
        first_other,
        pre_mine,
        pre_copy,
    )
    got_up = swap_copies(sent_up)
    first_sum, kept_up = lax.optimization_barrier((first_sum, kept_up))
    grad_hidden, branch_grad, vec_sums = local_call(
        norm_back_body,
        [block_wide, block_low, ((D, 2 * SUM_LANES), low)],
        "norm_back",
        grad_second,
        *first_sum,
        normed,
        norm_vecs,
    )
    branch_grad_other = swap_pair(branch_grad)
    (grad_out,) = local_call(
        out_grad_body,
        [((D, WIDTH), low)],
        "out_grad",
        branch_grad,
        branch_grad_other,
        attn_wide,
    )
    grad_num, grad_den, grad_state = local_call(
        grad_attend_body,
        [((sets, HD, SPAN), low), ((SUM_ROWS, SPAN), wide), state_shape],
        "grad_attend",
        branch_grad,
        branch_grad_other,
        weight,
        attn_wide,
        qkv,
        trig,
    )
    later = [shift_rows(grad_state, -step) for step in range(1, rows)]
    grad_query, grad_key, grad_value = local_call(
        grad_block_body,
        [
            ((2, WIDTH, SPAN), low),
            ((sets, HD, SPAN), wide),
            ((sets, HD, SPAN), wide),
        ],
        "grad_block",
        grad_num,
        grad_den,
        qkv,
        trig,
        reweight,
        weights,
        prior,
    )
    down_held, down_sent = local_call(
        down_pieces_body,
        low_outs(2, 2 * feat_rows, part + SPAN // 2),
        "down_pieces",
        flags,
        kept_down,
        after(got_down, later[0]),
        result,
    )
    down_got = swap_rows(down_sent, 1)

    up_held, up_sent = local_call(
        pair_pieces_body,
        low_outs(2, 2 * feat_rows, part + WIDTH + SUM_LANES),
        "up_pieces",
        flags,
        kept_up,
        after(got_up, later[0]),
        grad_out,
        vec_sums,
    )
    up_got = swap_rows(up_sent, 1)
    later, up_held = lax.optimization_barrier((later, up_held))
    half_rows = ((rows, half_feats, 3 * WIDTH), low)
    kept_w, sent_w, x_grad_own, x_grad_other = local_call(
        grad_project_body,
        [half_rows, half_rows, block_wide, block_low],
        "grad_project",
        grad_query,
        grad_key,
        grad_value,
        qkv,
        trig,
        x_own,
        x_other,
        weight,
        flags,
        *later,
        scratch=[state_shape, ((2, 3 * WIDTH, SPAN), low)],
    )
    got_w = swap_copies(sent_w)
    got_x = swap_pair(x_grad_other)
    x_half_grad, x_half_sent = local_call(
        partial(input_halves_body, rows=rows),
        [((D // 2, SPAN), wide), ((D // 2, SPAN), low)],
        "input_halves",
        flags,
        x_grad_own,
        got_x,
        scratch=[block_wide],
    )
    got_half = swap_cols(x_half_sent)
    last_lanes = 3 * WIDTH
    last_held, last_sent = local_call(
        last_pieces_body,
        low_outs(2, 2 * half_feats, last_lanes + SPAN),
        "last_pieces",
        flags,
        kept_w,
        got_w,
        x_half_grad,
        got_half,
        grad_hidden,
    )
    def pair_sums(held, got, name):
        shape = (feat_rows, held.shape[1])
        mine, sent = local_call(pair_sums_body, [(shape, wide), (shape, low)], name, held, got)
        return mine, swap_rows(sent, 2)

    down_part, down_far = local_call(
        down_pairs_body,
        [((feat_rows, part), wide), ((feat_rows, part + SPAN), low)],
        "down_pairs",
        down_held,
        down_got,
    )
    down_far = swap_rows(down_far, 2)
    up_part, up_far = pair_sums(up_held, up_got, "up_sums")
    last_got = swap_rows(last_sent, 1)
    last_part, last_far = local_call(
        last_pairs_body,
        [((half_feats, last_lanes), wide), ((half_feats, last_lanes + 2 * SPAN), low)],
        "last_pairs",
        last_held,
        last_got,
    )
    down_sum, *out_wide = local_call(
        down_sums_body,
        low_outs(1, feat_rows, part) + low_outs(2, half_feats, SPAN * rows // 2),
        "down_sums",
        flags,
        down_part,
        down_held,
        down_got,
        down_far,
        scratch=[((4, half_feats, SPAN), low)],
    )
    (hidden_sum,) = local_call(
        hidden_sums_body,
        low_outs(1, feat_rows, 2 * part + WIDTH + SUM_LANES),
        "hidden_sums",
        down_sum,
        up_part,
        up_far,
    )
    last_sum, *input_wide = local_call(
        last_sums_body,
        low_outs(1, half_feats, last_lanes) + low_outs(2, half_feats, SPAN * rows // 2),
        "last_sums",
        flags,
        last_part,
        last_held,
        last_got,
        swap_rows(last_far, 2),
    )
    output = cols_back(*out_wide, low, "out_join")
    input_grad = cols_back(*input_wide, wide, "input_join")
    down_t, up_grad, out_t, vec_total = local_call(
        place_hidden_body,
        [((feat_rows, 4 * part), wide)] * 2
        + [((feat_rows, 2 * WIDTH), wide), ((feat_rows, SUM_LANES), wide)],
        "place_hidden",
        flags,
        *all_quarters(hidden_sum, True),
    )
    query_grad, key_grad, value_grad = local_call(
        place_last_body,
        [((feat_rows, 2 * WIDTH), wide)] * 3,
        "place_last",
        flags,
        *all_quarters(last_sum, True),
    )
    return (
        output,
        input_grad,
        query_grad,
        key_grad,
        value_grad,
        out_t.T,
        vec_total[:, 0],
        vec_total[:, 1],
        up_grad,
        down_t.T,
        vec_total[:, 2],
        vec_total[:, 3],
    )


def solution(mesh):
    placed = (
        P("row", ("dp", "col")),
        P(),
        P("row", "col"),
        P("row", "col"),
        P("row", "col"),
        P("col", "row"),
        P("row"),
        P("row"),
        P("row", "col"),
        P("col", "row"),
        P("row"),
        P("row"),
        P("row", ("dp", "col")),
    )
    return jax.shard_map(
        on_device_paired if paired_layout(mesh) else on_device,
        mesh=mesh,
        in_specs=placed,
        out_specs=(
            P("row", ("dp", "col")),
            P("row", ("dp", "col")),
            P("row", "col"),
            P("row", "col"),
            P("row", "col"),
            P("col", "row"),
            P("row"),
            P("row"),
            P("row", "col"),
            P("col", "row"),
            P("row"),
            P("row"),
        ),
        check_vma=False,
    )
```

```python
from functools import partial
import math

import jax
import jax.numpy as jnp
from jax import lax
from jax.experimental import pallas as pl
from jax.experimental.pallas import tpu as pltpu
from jax.sharding import PartitionSpec as P

D = 768
H = 12
HD = 64
SEQ_MAX = 4096
TOK_DEV = 128


norm_eps = 1e-05
highest = lax.Precision.HIGHEST


def carried_in(shard, axis, join, neutral, backward):
    count = lax.axis_size(axis)
    place = lax.axis_index(axis)
    ahead = count - 1 - place if backward else place
    gathered = jax.tree.map(
        lambda a, kind: lax.all_gather(a.astype(kind), axis),
        shard,
        jax.tree.map(lambda a: jnp.bfloat16 if a.dtype == jnp.float32 else a.dtype, shard),
    )
    state = jax.tree.map(lambda a, e: jnp.zeros_like(a) + jnp.asarray(e, a.dtype), shard, neutral)

    def one(turn, state):
        source = count - 1 - turn if backward else turn
        return join(
            state,
            jax.tree.map(
                lambda a, own: lax.dynamic_index_in_dim(a, source, 0, False).astype(own.dtype),
                gathered,
                shard,
            ),
        )

    return lax.fori_loop(0, ahead, one, state)


def gather_cols(operand):
    return lax.all_gather(operand, "col", axis=0, tiled=True)


def gather_rows(operand):
    return lax.all_gather(operand, "row", axis=0, tiled=True)


def summed_over_rows(gathered, matrix):
    out_rows = gathered.shape[0] // lax.axis_size("row")

    def term_rows(first_row, row_count):
        sliced = lax.dynamic_slice_in_dim(gathered, first_row, row_count, 0)
        return jnp.dot(sliced, matrix, preferred_element_type=jnp.float32)

    return lax.psum_scatter(
        term_rows(jnp.int32(0), out_rows * lax.axis_size("row")),
        "row",
        scatter_dimension=0,
        tiled=True,
    )


def summed_over_cols(gathered, matrix):
    out_rows = gathered.shape[0] // lax.axis_size("col")

    def term_rows(first_row, row_count):
        sliced = lax.dynamic_slice_in_dim(gathered, first_row, row_count, 0)
        return jnp.dot(sliced, matrix, preferred_element_type=jnp.float32)

    return lax.psum_scatter(
        term_rows(jnp.int32(0), out_rows * lax.axis_size("col")).astype(jnp.bfloat16),
        "col",
        scatter_dimension=0,
        tiled=True,
    ).astype(jnp.float32)


def to_heads(stacked):
    return lax.all_to_all(stacked, "col", split_axis=1, concat_axis=2, tiled=True)


def to_tokens(stacked):
    return lax.all_to_all(stacked, "col", split_axis=2, concat_axis=1, tiled=True)


def row_totals(first_part, second_part):
    return lax.psum((first_part, second_part), "row")


def norm_forward(hidden, scale_vec, shift_vec):
    sum_one, sum_two = row_totals(jnp.sum(hidden, 1), jnp.sum(hidden * hidden, 1))
    row_mean = sum_one / D
    variance = sum_two / D - row_mean * row_mean
    inv_std = lax.rsqrt(variance + norm_eps)
    normed = (hidden - row_mean[:, None]) * inv_std[:, None]
    return (normed * scale_vec + shift_vec, normed, inv_std)


def norm_backward(grad_in, normed, inv_std, scale_vec):
    grad_normed = grad_in * scale_vec
    total_one, total_two = row_totals(jnp.sum(grad_normed, 1), jnp.sum(grad_normed * normed, 1))
    grad_hidden = inv_std[:, None] * (
        grad_normed - total_one[:, None] / D - normed * (total_two[:, None] / D)
    )
    return (grad_hidden, jnp.sum(grad_in * normed, 0), jnp.sum(grad_in, 0))


def seq_lengths(lengths, seq_ids):
    matches = seq_ids[:, None] == jnp.arange(lengths.shape[0], dtype=jnp.int32)[None, :]
    return jnp.sum(jnp.where(matches, lengths[None, :], 0), 1)


def reset_combine(earlier, later):
    keep_prior = 1.0 - later[4]
    joined = tuple(
        (
            keep_prior * prior_part + next_part
            for prior_part, next_part in zip(earlier[:4], later[:4])
        )
    )
    return joined + (jnp.maximum(earlier[4], later[4]),)


def empty_state():
    return (
        jnp.zeros((H, HD, HD), jnp.float32),
        jnp.zeros((H, HD, HD), jnp.float32),
        jnp.zeros((H, HD), jnp.float32),
        jnp.zeros((H, HD), jnp.float32),
        jnp.zeros((), jnp.float32),
    )


def attend_forward(queries, keys_in, values_in, present, cos_flat, sin_flat, opens_seq):
    block_rows = queries.shape[0]
    cos_pos = cos_flat[:, None, None]
    sin_pos = sin_flat[:, None, None]
    q_pos = jnp.maximum(queries, 0)
    k_pos = jnp.maximum(keys_in, 0) * present[:, None, None].astype(jnp.bfloat16)
    q_cos = q_pos.astype(jnp.float32) * cos_pos
    q_sin = q_pos.astype(jnp.float32) * sin_pos
    k_cos = k_pos.astype(jnp.float32) * cos_pos
    k_sin = k_pos.astype(jnp.float32) * sin_pos
    values_wide = values_in.astype(jnp.float32)
    local_state = (
        jnp.einsum("jhd,jhe->hde", k_cos, values_wide, precision=highest),
        jnp.einsum("jhd,jhe->hde", k_sin, values_wide, precision=highest),
        jnp.sum(k_cos, 0),
        jnp.sum(k_sin, 0),
    )
    arrived = carried_in(
        local_state + (opens_seq,), ("row", "col"), reset_combine, empty_state(), False
    )
    s_cos, s_sin, z_cos, z_sin = tuple(
        (state_part * (1.0 - opens_seq) for state_part in arrived[:4])
    )
    row_ids = jnp.arange(block_rows, dtype=jnp.int32)
    causal = (row_ids[:, None] >= row_ids[None, :]).astype(jnp.float32)
    reweight = (
        cos_flat[:, None] * cos_flat[None, :] + sin_flat[:, None] * sin_flat[None, :]
    ) * causal
    scores = jnp.einsum("ihd,jhd->hij", q_pos, k_pos, preferred_element_type=jnp.float32)
    weights = scores * reweight[None]
    weights_low = weights.astype(jnp.bfloat16)
    numerator = jnp.einsum(
        "hij,jhe->ihe", weights_low, values_in, preferred_element_type=jnp.float32
    )
    numerator = numerator + jnp.einsum("ihd,hde->ihe", q_cos, s_cos, precision=highest)
    numerator = numerator + jnp.einsum("ihd,hde->ihe", q_sin, s_sin, precision=highest)
    denominator = 1.0 + jnp.sum(weights, 2).T
    denominator = denominator + jnp.einsum("ihd,hd->ih", q_cos, z_cos, precision=highest)
    denominator = denominator + jnp.einsum("ihd,hd->ih", q_sin, z_sin, precision=highest)
    mixed = (numerator / denominator[:, :, None]).astype(jnp.bfloat16).reshape(block_rows, D)
    kept = (
        queries,
        keys_in,
        values_in,
        q_pos,
        k_pos,
        q_cos,
        q_sin,
        k_cos,
        k_sin,
        values_wide,
        reweight,
        weights_low,
        numerator,
        denominator,
        s_cos,
        s_sin,
        z_cos,
        z_sin,
        present,
        cos_pos,
        sin_pos,
    )
    return (mixed, kept)


def attend_backward(grad_heads, kept, closes_seq):
    (
        queries,
        keys_in,
        values_in,
        q_pos,
        k_pos,
        q_cos,
        q_sin,
        k_cos,
        k_sin,
        values_wide,
        reweight,
        weights_low,
        numerator,
        denominator,
        s_cos,
        s_sin,
        z_cos,
        z_sin,
        present,
        cos_pos,
        sin_pos,
    ) = kept
    block_rows = queries.shape[0]
    grad_attn = grad_heads.astype(jnp.float32).reshape(block_rows, H, HD)
    grad_num_low = (grad_attn / denominator[:, :, None]).astype(jnp.bfloat16)
    grad_num = grad_num_low.astype(jnp.float32)
    grad_den = -jnp.sum(grad_attn * numerator, 2) / (denominator * denominator)
    grad_weights = jnp.einsum(
        "ihe,jhe->hij", grad_num_low, values_in, preferred_element_type=jnp.float32
    )
    grad_weights = grad_weights + grad_den.T[:, :, None]
    grad_scores = (grad_weights * reweight[None]).astype(jnp.bfloat16)
    local_grad = (
        jnp.einsum("ihd,ihe->hde", q_cos, grad_num, precision=highest),
        jnp.einsum("ihd,ihe->hde", q_sin, grad_num, precision=highest),
        jnp.einsum("ihd,ih->hd", q_cos, grad_den, precision=highest),
        jnp.einsum("ihd,ih->hd", q_sin, grad_den, precision=highest),
    )
    later_sum = carried_in(
        local_grad + (closes_seq,), ("row", "col"), reset_combine, empty_state(), True
    )
    g_cos, g_sin, gz_cos, gz_sin = tuple(
        (state_part * (1.0 - closes_seq) for state_part in later_sum[:4])
    )
    grad_qpos = jnp.einsum("hij,jhd->ihd", grad_scores, k_pos, preferred_element_type=jnp.float32)
    grad_qpos = grad_qpos + cos_pos * (
        jnp.einsum("ihe,hde->ihd", grad_num, s_cos, precision=highest)
        + grad_den[:, :, None] * z_cos[None]
    )
    grad_qpos = grad_qpos + sin_pos * (
        jnp.einsum("ihe,hde->ihd", grad_num, s_sin, precision=highest)
        + grad_den[:, :, None] * z_sin[None]
    )
    grad_kpos = jnp.einsum("hij,ihd->jhd", grad_scores, q_pos, preferred_element_type=jnp.float32)
    grad_kpos = grad_kpos + cos_pos * (
        jnp.einsum("jhe,hde->jhd", values_wide, g_cos, precision=highest) + gz_cos[None]
    )
    grad_kpos = grad_kpos + sin_pos * (
        jnp.einsum("jhe,hde->jhd", values_wide, g_sin, precision=highest) + gz_sin[None]
    )
    grad_values = jnp.einsum(
        "hij,ihe->jhe", weights_low, grad_num_low, preferred_element_type=jnp.float32
    )
    grad_values = grad_values + jnp.einsum("jhd,hde->jhe", k_cos, g_cos, precision=highest)
    grad_values = grad_values + jnp.einsum("jhd,hde->jhe", k_sin, g_sin, precision=highest)
    grad_q = (grad_qpos * (queries > 0).astype(jnp.float32)).astype(jnp.bfloat16)
    grad_k = (grad_kpos * (keys_in > 0).astype(jnp.float32) * present[:, None, None]).astype(
        jnp.bfloat16
    )
    grad_v = grad_values.astype(jnp.bfloat16)
    return (
        grad_q.reshape(block_rows, D),
        grad_k.reshape(block_rows, D),
        grad_v.reshape(block_rows, D),
    )


def on_device(
    tokens,
    lengths,
    w_query,
    w_key,
    w_value,
    w_out,
    gain_one,
    bias_one,
    w_up,
    w_down,
    gain_two,
    bias_two,
    cotangent,
):
    row_count = lax.axis_size("row")
    col_count = lax.axis_size("col")
    seq_len = min(SEQ_MAX, TOK_DEV * row_count * col_count)
    data_idx = lax.axis_index("dp")
    row_idx = lax.axis_index("row")
    col_idx = lax.axis_index("col")
    feat_rows = tokens.shape[0]
    group_idx = row_idx * col_count + col_idx
    global_idx = (data_idx * row_count * col_count + group_idx) * TOK_DEV + jnp.arange(
        TOK_DEV, dtype=jnp.int32
    )
    positions = global_idx % seq_len
    present = (positions < seq_lengths(lengths, global_idx // seq_len)).astype(jnp.float32)
    angles = math.pi * positions.astype(jnp.float32) / (2.0 * seq_len)
    cos_flat = jnp.cos(angles)
    sin_flat = jnp.sin(angles)
    opens_seq = (group_idx * TOK_DEV % seq_len == 0).astype(jnp.float32)
    closes_seq = ((group_idx + 1) * TOK_DEV % seq_len == 0).astype(jnp.float32)
    token_rows = tokens.T
    width_col = w_query.shape[1]
    w_cat = jnp.concatenate([w_query, w_key, w_value], 1)
    x_gathered = gather_cols(token_rows)
    qkv = summed_over_rows(x_gathered, w_cat).astype(jnp.bfloat16)
    stacked = jnp.stack(
        [qkv[:, :width_col], qkv[:, width_col : 2 * width_col], qkv[:, 2 * width_col :]], 0
    )
    head_rows = to_heads(stacked)
    mixed, kept = attend_forward(
        head_rows[0].reshape(TOK_DEV, H, HD),
        head_rows[1].reshape(TOK_DEV, H, HD),
        head_rows[2].reshape(TOK_DEV, H, HD),
        present,
        cos_flat,
        sin_flat,
        opens_seq,
    )
    mixed_two = to_tokens(mixed[None])[0]
    mixed_gathered = gather_rows(mixed_two)
    branch = summed_over_cols(mixed_gathered, w_out)
    first, normed_one, inv_one = norm_forward(
        token_rows.astype(jnp.float32) + branch, gain_one, bias_one
    )
    first_low = first.astype(jnp.bfloat16)
    first_gathered = gather_cols(first_low)
    pre = summed_over_rows(first_gathered, w_up)
    act, gelu_pull = jax.vjp(partial(jax.nn.gelu, approximate=False), pre)
    act_low = act.astype(jnp.bfloat16)
    act_gathered = gather_rows(act_low)
    ffn = summed_over_cols(act_gathered, w_down)
    result, normed_two, inv_two = norm_forward(first + ffn, gain_two, bias_two)
    rows_one = token_rows.shape[0]
    global_one = (data_idx * col_count + col_idx) * rows_one + jnp.arange(rows_one, dtype=jnp.int32)
    present_one = (global_one % seq_len < seq_lengths(lengths, global_one // seq_len)).astype(
        jnp.float32
    )
    grad_result = cotangent.T.astype(jnp.float32) * present_one[:, None]
    grad_second, grad_gain_two, grad_bias_two = norm_backward(
        grad_result, normed_two, inv_two, gain_two
    )
    grad_ffn_gathered = gather_cols(grad_second.astype(jnp.bfloat16))
    act_again = gather_rows(act_low)
    grad_down = jnp.einsum(
        "tf,td->fd", act_again, grad_ffn_gathered, preferred_element_type=jnp.float32
    )
    grad_act = summed_over_rows(grad_ffn_gathered, w_down.T)
    grad_pre = gelu_pull(grad_act)[0].astype(jnp.bfloat16)
    grad_pre_gathered = gather_rows(grad_pre)
    first_again = gather_cols(first_low)
    grad_up = jnp.einsum(
        "td,tf->df", first_again, grad_pre_gathered, preferred_element_type=jnp.float32
    )
    grad_first = summed_over_cols(grad_pre_gathered, w_up.T) + grad_second
    grad_hidden, grad_gain_one, grad_bias_one = norm_backward(
        grad_first, normed_one, inv_one, gain_one
    )
    branch_grad_gathered = gather_cols(grad_hidden.astype(jnp.bfloat16))
    mixed_again = gather_rows(mixed_two)
    grad_out = jnp.einsum(
        "tc,tr->cr", mixed_again, branch_grad_gathered, preferred_element_type=jnp.float32
    )
    grad_mixed = summed_over_rows(branch_grad_gathered, w_out.T).astype(jnp.bfloat16)
    grad_heads = to_heads(grad_mixed[None])[0]
    grad_q, grad_k, grad_v = attend_backward(grad_heads, kept, closes_seq)
    grad_rows = to_tokens(jnp.stack([grad_q, grad_k, grad_v], 0))
    grad_cat = jnp.concatenate([grad_rows[0], grad_rows[1], grad_rows[2]], 1)
    grad_cat_gathered = gather_rows(grad_cat)
    x_again = gather_cols(token_rows)
    grad_cat_w = jnp.einsum(
        "tr,tc->rc", x_again, grad_cat_gathered, preferred_element_type=jnp.float32
    )
    input_rows = summed_over_cols(grad_cat_gathered, w_cat.T) + grad_hidden
    gain_parts = jnp.stack([grad_gain_one, grad_bias_one, grad_gain_two, grad_bias_two], 0)
    gain_sums = lax.psum(gain_parts.reshape(4 * feat_rows), "col")
    grad_query = grad_cat_w[:, :width_col]
    grad_key = grad_cat_w[:, width_col : 2 * width_col]
    grad_value = grad_cat_w[:, 2 * width_col :]
    output = result.astype(jnp.bfloat16).T
    input_grad = input_rows.T
    sums = (
        lax.psum(grad_query.astype(jnp.bfloat16), "dp").astype(jnp.float32),
        lax.psum(grad_key.astype(jnp.bfloat16), "dp").astype(jnp.float32),
        lax.psum(grad_value.astype(jnp.bfloat16), "dp").astype(jnp.float32),
        lax.psum(grad_out.astype(jnp.bfloat16), "dp").astype(jnp.float32),
        lax.psum(grad_up.astype(jnp.bfloat16), "dp").astype(jnp.float32),
        lax.psum(grad_down.astype(jnp.bfloat16), "dp").astype(jnp.float32),
        lax.psum(gain_sums.astype(jnp.bfloat16), "dp").astype(jnp.float32),
    )
    gain_total = sums[6].reshape(4, feat_rows)
    return (
        output,
        input_grad,
        sums[0],
        sums[1],
        sums[2],
        sums[3],
        gain_total[0],
        gain_total[1],
        sums[4],
        sums[5],
        gain_total[2],
        gain_total[3],
    )


def paired_layout(mesh):
    rows, cols, dps = mesh.shape["row"], mesh.shape["col"], mesh.shape["dp"]
    return rows == 4 and cols == 2 and dps == 4 and H % 4 == 0 and 8 * TOK_DEV <= SEQ_MAX


low = jnp.bfloat16
wide = jnp.float32
SPAN = 2 * TOK_DEV
HEADS = H // 4
WIDTH = HEADS * HD
STATE_ROWS = 2 * HEADS * HD
SUM_ROWS = 16
SUM_LANES = 64


def swap_cols(operand):
    return lax.ppermute(operand, "col", [(0, 1), (1, 0)])


def swap_pair(operand):
    return lax.ppermute(operand, "dp", [(i, i ^ 1) for i in range(lax.axis_size("dp"))])


def swap_copies(operand):
    return lax.ppermute(operand, "dp", [(i, i ^ 2) for i in range(lax.axis_size("dp"))])


def shift_rows(operand, step):
    count = lax.axis_size("row")
    pairs = [(i, i + step) for i in range(count) if 0 <= i + step < count]
    return lax.ppermute(operand, "row", pairs)


def swap_rows(operand, mask):
    return lax.ppermute(operand, "row", [(i, i ^ mask) for i in range(4)])


def rotate_rows(operand, step):
    count = lax.axis_size("row")
    return lax.ppermute(operand, "row", [(i, (i + step) % count) for i in range(count)])


def dot_tn(left, right):
    return lax.dot_general(left, right, (((0,), (0,)), ((), ())), preferred_element_type=wide)


def dot_nt(left, right):
    return lax.dot_general(left, right, (((1,), (1,)), ((), ())), preferred_element_type=wide)


def dot_nn(left, right):
    return jnp.dot(left, right, preferred_element_type=wide)


def norm_columns(hidden, scale, shift):
    mean = jnp.mean(hidden, 0, keepdims=True)
    centered = hidden - mean
    variance = jnp.mean(centered * centered, 0, keepdims=True)
    inv_std = lax.rsqrt(variance + norm_eps)
    normed = centered * inv_std
    return (normed * scale + shift, normed, inv_std)


def norm_columns_back(grad_in, normed, inv_std, scale):
    grad_normed = grad_in * scale
    mean_one = jnp.mean(grad_normed, 0, keepdims=True)
    mean_two = jnp.mean(grad_normed * normed, 0, keepdims=True)
    return inv_std * (grad_normed - mean_one - normed * mean_two)


def local_call(body, outs, name, *operands, scratch=(), space=None):
    shapes = [jax.ShapeDtypeStruct(shape, kind) for shape, kind in outs]
    return pl.pallas_call(
        body,
        out_shape=shapes,
        in_specs=[
            pl.BlockSpec(
                memory_space=pltpu.SMEM
                if operand.dtype == jnp.int32
                else space or pltpu.VMEM
            )
            for operand in operands
        ],
        out_specs=[pl.BlockSpec(memory_space=pltpu.VMEM)] * len(outs),
        scratch_shapes=[
            pltpu.VMEM(*kind) if isinstance(kind, tuple) else kind for kind in scratch
        ],
        compiler_params=pltpu.CompilerParams(vmem_limit_bytes=24 * 2**20),
        name=name,
    )(*operands)


CORE, COPY, ROW, COL, SEQ = range(5)


def low_outs(count, *shape):
    return [(shape, low)] * count


def turn_body(flags_ref, lengths_ref, trig_ref, reweight_ref, *, seq_len):
    start = flags_ref[ROW] * SPAN
    positions = start + lax.broadcasted_iota(jnp.int32, (8, SPAN), 1)
    lines = lax.broadcasted_iota(jnp.int32, (8, SPAN), 0)
    angles = math.pi * positions.astype(wide) / (2.0 * seq_len)
    turns = jnp.where(lines == 0, jnp.cos(angles), jnp.where(lines == 1, jnp.sin(angles), 0.0))
    own = lengths_ref[flags_ref[SEQ]]
    other = lengths_ref[flags_ref[SEQ] + 1 - 2 * flags_ref[CORE]]
    limits = jnp.where(lines == 2, own, other)
    present = jnp.where(positions < limits, 1.0, 0.0)
    trig_ref[...] = turns + jnp.where(lines == 2, present, jnp.where(lines == 3, present, 0.0))
    rows = lax.broadcasted_iota(jnp.int32, (SPAN, SPAN), 0)
    cols = lax.broadcasted_iota(jnp.int32, (SPAN, SPAN), 1)
    both = lax.dot_general(
        turns, turns, (((0,), (0,)), ((), ())), precision=highest, preferred_element_type=wide
    )
    reweight_ref[...] = jnp.where(rows <= cols, both, 0.0)


def token_piece(flags_ref, own_ref, recv_ref, step, rows):
    place = lax.rem(flags_ref[ROW] + step, rows)
    half = lax.div(place, rows // 2)
    cols = pl.ds(pl.multiple_of(lax.rem(place, rows // 2) * SPAN, SPAN), SPAN)
    return jnp.where(half == flags_ref[COL], own_ref[:, cols], recv_ref[:, cols])


def pieces_body(flags_ref, own_ref, cot_ref, recv_ref, *refs, rows):
    vec_ref, piece_refs = refs[0], refs[1:]
    part = own_ref.shape[0]
    lines = []
    for line in range(4):
        vec = vec_ref[line : line + 1, :]
        vec = jnp.concatenate([vec, jnp.zeros((1, SPAN - vec.shape[1]), wide)], 1)
        high = vec.astype(low).astype(wide)
        lines = lines + [high, vec - high]
    for step, ref in enumerate(piece_refs):
        ref[:part] = token_piece(flags_ref, own_ref, recv_ref.at[:part], step, rows)
        ref[part : 2 * part] = token_piece(flags_ref, cot_ref, recv_ref.at[part:], step, rows)
        ref[2 * part :] = jnp.concatenate(lines + [jnp.zeros((8, SPAN), wide)], 0).astype(low)


def came_from(flags_ref, step, rows):
    return lax.rem(flags_ref[ROW] + rows - step, rows)


def place_tokens_body(flags_ref, *refs, rows, part):
    pieces, (half_ref, vec_ref) = refs[:rows], refs[rows:]
    below = half_ref.shape[0] // 2
    for step, ref in enumerate(pieces):
        row = came_from(flags_ref, step, rows)
        half_ref[pl.ds(pl.multiple_of(row * part, 16), part), :] = ref[:part]
        half_ref[pl.ds(pl.multiple_of(below + row * part, 16), part), :] = ref[part : 2 * part]
        extra = ref[2 * part :].astype(wide)
        sums = [extra[2 * i : 2 * i + 1] + extra[2 * i + 1 : 2 * i + 2] for i in range(4)]
        columns = jnp.concatenate(sums + [jnp.zeros((4, SPAN), wide)], 0).T
        vec_ref[pl.ds(pl.multiple_of(row * 2 * part, 8), 2 * part), :] = columns[: 2 * part]


def join_halves_body(flags_ref, half_ref, recv_ref, x_ref, cot_ref, *, rows):
    part = half_ref.shape[0] // (2 * rows)
    first_col = flags_ref[COL] == 0
    for place, full_ref in enumerate((x_ref, cot_ref)):
        for row in range(rows):
            source = (place * rows + row) * part
            own = half_ref[source : source + part]
            other = recv_ref[source : source + part]
            start = 2 * row * part
            full_ref[start : start + part] = jnp.where(first_col, own, other)
            full_ref[start + part : start + 2 * part] = jnp.where(first_col, other, own)


def add_body(own_ref, recv_ref, half_ref):
    half_ref[...] = (own_ref[...] + recv_ref[...].astype(wide)).astype(low)


def feature_piece(flags_ref, source, step, rows):
    part = source.shape[0] // (2 * rows)
    start = (lax.rem(flags_ref[ROW] + step, rows) * 2 + flags_ref[COL]) * part
    return source[pl.ds(pl.multiple_of(start, 16), part), :]


def place_back(flags_ref, pieces, rows, own_ref, other_ref):
    half = len(pieces) // 2
    for row, piece in zip(rows, pieces):
        cols = pl.ds(pl.multiple_of(lax.rem(row, half) * SPAN, SPAN), SPAN)
        mine = lax.div(row, half) == flags_ref[COL]

        @pl.when(mine)
        def _(piece=piece, cols=cols):
            own_ref[:, cols] = piece[...]

        @pl.when(jnp.logical_not(mine))
        def _(piece=piece, cols=cols):
            other_ref[:, cols] = piece[...]


def sum_of(refs):
    total = refs[0][...].astype(wide)
    for ref in refs[1:]:
        total = total + ref[...].astype(wide)
    return total


def join_back_body(flags_ref, own_ref, recv_ref, out_ref):
    part = own_ref.shape[0]
    first_col = flags_ref[COL] == 0
    out_ref[:part] = jnp.where(first_col, own_ref[...], recv_ref[...]).astype(out_ref.dtype)
    out_ref[part:] = jnp.where(first_col, recv_ref[...], own_ref[...]).astype(out_ref.dtype)


def input_halves_body(flags_ref, own_ref, recv_ref, half_ref, sent_ref, sum_ref, *, rows):
    part = own_ref.shape[0] // (2 * rows)
    sum_ref[...] = own_ref[...] + recv_ref[...].astype(wide)
    for row in range(rows):
        rows_out = slice(row * part, (row + 1) * part)
        mine = pl.multiple_of((2 * row + flags_ref[COL]) * part, 16)
        theirs = pl.multiple_of((2 * row + 1 - flags_ref[COL]) * part, 16)
        half_ref[rows_out] = sum_ref[pl.ds(mine, part), :]
        sent_ref[rows_out] = sum_ref[pl.ds(theirs, part), :].astype(low)


def last_pieces_body(
    flags_ref, kept_ref, got_ref, half_ref, recv_ref, hidden_ref, held_ref, sent_ref
):
    rows = kept_ref.shape[0]
    part = half_ref.shape[0] // rows
    lanes = kept_ref.shape[2]
    for mask in range(rows):
        ref = sent_ref if mask % 2 else held_ref
        out = slice(mask // 2 * part, (mask // 2 + 1) * part)
        place = partner(flags_ref[ROW], mask)
        ref[out, :lanes] = (kept_ref[place].astype(wide) + got_ref[place].astype(wide)).astype(low)
        rows_in = pl.ds(pl.multiple_of(place * part, 16), part)
        total = half_ref[rows_in, :] + recv_ref[rows_in, :].astype(wide)
        start = pl.multiple_of((place * 2 + flags_ref[COL]) * part, 16)
        ref[out, lanes:] = (total + hidden_ref[pl.ds(start, part), :]).astype(low)


def last_pairs_body(held_ref, got_ref, sum_ref, sent_ref):
    part, lanes = sum_ref.shape
    sum_ref[...] = held_ref[:part, :lanes].astype(wide) + got_ref[:part, :lanes].astype(wide)
    pair = held_ref[part:, :lanes].astype(wide) + got_ref[part:, :lanes].astype(wide)
    sent_ref[:, :lanes] = pair.astype(low)
    sent_ref[:, lanes : lanes + SPAN] = held_ref[part:, lanes:]
    sent_ref[:, lanes + SPAN :] = got_ref[part:, lanes:]


def last_sums_body(
    flags_ref, part_ref, held_ref, got_ref, far_ref, sum_ref, own_ref, other_ref
):
    part, lanes = part_ref.shape
    sum_ref[...] = (part_ref[...] + far_ref[:, :lanes].astype(wide)).astype(low)
    pieces = (
        held_ref.at[:part, lanes:],
        got_ref.at[:part, lanes:],
        far_ref.at[:, lanes : lanes + SPAN],
        far_ref.at[:, lanes + SPAN :],
    )
    rows = [partner(flags_ref[ROW], mask) for mask in range(4)]
    place_back(flags_ref, pieces, rows, own_ref, other_ref)


def down_grad_body(
    flags_ref, own_ref, other_ref, mine_ref, copy_ref, held_ref, sent_ref, grad_ref
):
    feats, part = held_ref.shape[0] // 2, mine_ref.shape[0]
    for act_ref, cols in ((mine_ref, slice(0, part)), (copy_ref, slice(part, 2 * part))):
        grad_ref[:, cols] = (
            dot_nt(own_ref[...], act_ref[:, :SPAN]) + dot_nt(other_ref[...], act_ref[:, SPAN:])
        ).astype(low)
    for mask in range(4):
        ref = sent_ref if mask % 2 else held_ref
        start = mask // 2 * feats
        place = partner(flags_ref[ROW], mask)
        rows_in = pl.ds(pl.multiple_of(place * feats, 16), feats)
        ref[start : start + feats, :] = grad_ref[rows_in, :]


def down_pairs_body(held_ref, got_ref, kept_ref, sent_ref):
    part = kept_ref.shape[1]
    kept_ref[...] = held_ref[:, :part].astype(wide) + got_ref[:, :part].astype(wide)
    sent_ref[...] = (held_ref[:, part:].astype(wide) + got_ref[:, part:].astype(wide)).astype(low)


def mix_body(
    flags_ref, own_ref, other_ref, attn_wide_ref, vec_ref, pair_ref, kept_ref, sent_ref, grad_ref
):
    grad_ref[:, :WIDTH] = (
        dot_nt(own_ref[...], attn_wide_ref[:WIDTH, :].astype(low))
        + dot_nt(other_ref[...], attn_wide_ref[WIDTH : 2 * WIDTH, :].astype(low))
    ).astype(low)
    grad_ref[:, WIDTH:] = vec_ref[:, :SUM_LANES]
    first_copy = flags_ref[COPY] == 0
    half = (WIDTH + SUM_LANES) // 2
    kept_ref[...] = jnp.where(first_copy, grad_ref[:, :half], grad_ref[:, half:])
    sent = jnp.where(first_copy, grad_ref[:, half:], grad_ref[:, :half])
    lines, part = pair_ref.shape
    sent_ref[:, :part] = pair_ref[...]
    sent_ref[:, part : part + half] = sent[:lines]
    sent_ref[:, part + half :] = sent[lines:]


def down_far_body(kept_ref, got_ref, sum_ref, sent_ref):
    feats, part = sum_ref.shape
    sum_ref[...] = kept_ref[:feats] + got_ref[:feats, :part].astype(wide)
    sent_ref[...] = (kept_ref[feats:] + got_ref[feats:, :part].astype(wide)).astype(low)


def up_pieces_body(
    flags_ref, result_ref, kept_ref, got_ref, mix_ref, mix_got_ref, held_ref, sent_ref, sum_ref
):
    feats, part = kept_ref.shape[0] // 4, kept_ref.shape[1]
    half, lanes = feats // 2, SPAN // 2
    lines, cols = mix_got_ref.shape[0], mix_ref.shape[1]
    sum_ref[:lines] = (
        mix_ref[:lines].astype(wide) + mix_got_ref[:, part : part + cols].astype(wide)
    ).astype(low)
    sum_ref[lines:] = (
        mix_ref[lines:].astype(wide) + mix_got_ref[:, part + cols :].astype(wide)
    ).astype(low)
    for mask in range(4):
        ref = sent_ref if mask % 2 else held_ref
        start = mask // 2 * feats
        out = slice(start, start + feats)
        place = partner(flags_ref[ROW], mask)
        rows_in = pl.ds(pl.multiple_of((place * 2 + flags_ref[COL]) * half, 16), half)
        ref[start : start + half, :lanes] = result_ref[rows_in, :lanes]
        ref[start + half : start + feats, :lanes] = result_ref[rows_in, lanes:]
        rows_in = pl.ds(pl.multiple_of(place * feats, 16), feats)
        ref[out, lanes : lanes + part] = (
            kept_ref[rows_in, :].astype(wide) + got_ref[rows_in, :].astype(wide)
        ).astype(low)
        ref[out, lanes + part :] = sum_ref[rows_in, :]


def up_pairs_body(held_ref, got_ref, sum_ref, sent_ref):
    feats, total = held_ref.shape[0] // 2, held_ref.shape[1]
    lanes = SPAN // 2
    sum_ref[...] = held_ref[:feats, lanes:].astype(wide) + got_ref[:feats, lanes:].astype(wide)
    pair = held_ref[feats:, lanes:].astype(wide) + got_ref[feats:, lanes:].astype(wide)
    sent_ref[:, :lanes] = held_ref[feats:, :lanes]
    sent_ref[:, lanes:total] = pair.astype(low)
    sent_ref[:, total:] = got_ref[feats:, :lanes]


def hidden_sums_body(
    flags_ref,
    down_ref,
    down_far_ref,
    up_ref,
    held_ref,
    got_ref,
    far_ref,
    sum_ref,
    own_ref,
    other_ref,
    piece_ref,
):
    feats, part = down_ref.shape
    lanes = SPAN // 2
    total = lanes + up_ref.shape[1]
    sum_ref[:, :part] = (down_ref[...] + down_far_ref[...].astype(wide)).astype(low)
    sum_ref[:, part:] = (up_ref[...] + far_ref[:, lanes:total].astype(wide)).astype(low)
    pieces = (
        held_ref[:feats, :lanes],
        got_ref[:feats, :lanes],
        far_ref[:, :lanes],
        far_ref[:, total:],
    )
    for place, piece in enumerate(pieces):
        piece_ref[place, :, :lanes] = piece[: feats // 2]
        piece_ref[place, :, lanes:] = piece[feats // 2 :]
    rows = [partner(flags_ref[ROW], mask) for mask in range(4)]
    place_back(flags_ref, [piece_ref.at[i] for i in range(4)], rows, own_ref, other_ref)


def head_sets():
    return [(seq, head, seq * HEADS + head) for seq in range(2) for head in range(HEADS)]


def set_row(place):
    ids = lax.broadcasted_iota(jnp.int32, (SUM_ROWS, SPAN), 0)
    return (ids == place).astype(wide)


def turned(parts, trig_ref):
    part_wide = parts.astype(wide)
    return jnp.concatenate(
        [(part_wide * trig_ref[0:1, :]).astype(low), (part_wide * trig_ref[1:2, :]).astype(low)], 0
    )


def unturned(pair, trig_ref):
    return pair[:HD] * trig_ref[0:1, :] + pair[HD:] * trig_ref[1:2, :]


def query_part(qkv_ref, seq, head):
    return qkv_ref[seq, head * HD : (head + 1) * HD, :]


def key_part(qkv_ref, seq, head):
    return qkv_ref[seq, WIDTH + head * HD : WIDTH + (head + 1) * HD, :]


def value_part(qkv_ref, seq, head):
    return qkv_ref[seq, 2 * WIDTH + head * HD : 2 * WIDTH + (head + 1) * HD, :]


def kept_keys(qkv_ref, trig_ref, seq, head):
    keys = jnp.maximum(key_part(qkv_ref, seq, head), 0)
    return (keys.astype(wide) * trig_ref[2 + seq : 3 + seq, :]).astype(low)


def state_slice(state, place):
    return state[place * HD : (place + 1) * HD]


def pack_hidden_body(flags_ref, up_ref, down_ref, mine_ref, copy_ref, sems):
    part = mine_ref.shape[1] // 2
    copies = []
    for half, packed_ref in enumerate((mine_ref, copy_ref)):
        copy = 1 - flags_ref[COPY] if half else flags_ref[COPY]
        start = pl.multiple_of((flags_ref[CORE] * 2 + copy) * part, 128)
        for place, ref in enumerate((up_ref, down_ref)):
            copies.append(
                pltpu.make_async_copy(
                    ref.at[:, pl.ds(start, part)],
                    packed_ref.at[:, pl.ds(place * part, part)],
                    sems.at[2 * half + place],
                )
            )
    for copy in copies:
        copy.start()
    for copy in copies:
        copy.wait()


def partner(row, mask):
    if mask == 0:
        return row
    if mask == 1:
        return row + 1 - 2 * lax.rem(row, 2)
    return lax.rem(row + 2, 4) if mask == 2 else 3 - row


def row_block(flags_ref, mask, feats):
    return pl.ds(pl.multiple_of(partner(flags_ref[ROW], mask) * feats, 16), feats)


def project_body(flags_ref, own_ref, other_ref, trig_ref, packed_ref, *refs):
    weight_ref, qkv_ref, state_ref = refs[-3:]
    blocks = refs[:-3]
    count = len(blocks) // 2
    first_copy = flags_ref[COPY] == 0
    feats = packed_ref.shape[0]
    part = packed_ref.shape[1] // 2

    def rows_of(mask):
        return row_block(flags_ref, mask, feats)

    weight_ref[rows_of(0), :] = packed_ref[...]
    for step in range(1, count + 1):
        mine, copied = blocks[step - 1][...], blocks[count + step - 1][...]
        weight_ref[rows_of(step), :part] = jnp.where(first_copy, mine, copied)
        weight_ref[rows_of(step), part:] = jnp.where(first_copy, copied, mine)
    matrix = weight_ref[:, : 3 * WIDTH]
    for seq, x_ref in enumerate((own_ref, other_ref)):
        qkv_ref[seq] = dot_tn(matrix, x_ref[...]).astype(low)
    sums = jnp.zeros((SUM_ROWS, 2 * HD), wide)
    for seq, head, place in head_sets():
        turned_keys = turned(kept_keys(qkv_ref, trig_ref, seq, head), trig_ref)
        values = value_part(qkv_ref, seq, head)
        state_ref[place * HD : (place + 1) * HD, :] = dot_nt(values, turned_keys).astype(low)
        sums = sums + dot_nt(set_row(place).astype(low), turned_keys)
    state_ref[STATE_ROWS:, :] = sums.astype(low)


def block_body(qkv_ref, trig_ref, reweight_ref, weights_ref, numer_ref, denom_ref):
    denoms = jnp.zeros((SUM_ROWS, SPAN), wide)
    for seq, head, place in head_sets():
        queries = jnp.maximum(query_part(qkv_ref, seq, head), 0)
        keys = kept_keys(qkv_ref, trig_ref, seq, head)
        weights = dot_tn(keys, queries) * reweight_ref[...]
        weights_low = weights.astype(low)
        weights_ref[place] = weights_low
        numer_ref[place] = dot_nn(value_part(qkv_ref, seq, head), weights_low)
        denoms = denoms + set_row(place) * jnp.sum(weights, 0, keepdims=True)
    denom_ref[...] = denoms


def attend_body(
    qkv_ref,
    trig_ref,
    numer_ref,
    denom_ref,
    weight_ref,
    *refs,
):
    arrived = refs[:-5]
    prior_ref, attn_wide_ref, own_ref, other_ref, attn_ref = refs[-5:]
    total = arrived[0][...].astype(wide)
    for ref in arrived[1:]:
        total = total + ref[...].astype(wide)
    prior_ref[...] = total.astype(low)
    matrix = weight_ref[:, 3 * WIDTH : 4 * WIDTH]
    prior_sums = prior_ref[STATE_ROWS:, :]
    inverses = jnp.zeros((SUM_ROWS, SPAN), wide)
    for seq, head, place in head_sets():
        queries = turned(jnp.maximum(query_part(qkv_ref, seq, head), 0), trig_ref)
        prior = prior_ref[place * HD : (place + 1) * HD, :]
        numer = numer_ref[place] + dot_nn(prior, queries)
        denoms = dot_nn(prior_sums, queries) + denom_ref[...]
        denom = 1.0 + jnp.sum(denoms * set_row(place), 0, keepdims=True)
        inverse = 1.0 / denom
        inverses = inverses + set_row(place) * inverse
        attended = numer * inverse
        attn_wide_ref[place * HD : (place + 1) * HD, :] = attended
        attn_ref[seq, head * HD : (head + 1) * HD, :] = attended.astype(low)
    attn_wide_ref[STATE_ROWS:, :] = inverses
    own_ref[...] = dot_nn(matrix, attn_ref[0])
    other_ref[...] = dot_nn(matrix, attn_ref[1]).astype(low)


def grad_attend_body(
    own_ref,
    other_ref,
    weight_ref,
    attn_wide_ref,
    qkv_ref,
    trig_ref,
    grad_num_ref,
    grad_den_ref,
    state_ref,
):
    matrix = weight_ref[:, 3 * WIDTH : 4 * WIDTH]
    sums = jnp.zeros((SUM_ROWS, 2 * HD), wide)
    dens = jnp.zeros((SUM_ROWS, SPAN), wide)
    for seq, grad_ref in enumerate((own_ref, other_ref)):
        grads = dot_tn(matrix, grad_ref[...]).astype(low).astype(wide)
        for head in range(HEADS):
            place = seq * HEADS + head
            inverse = jnp.sum(attn_wide_ref[STATE_ROWS:, :] * set_row(place), 0, keepdims=True)
            scaled = grads[head * HD : (head + 1) * HD] * inverse
            grad_num = scaled.astype(low)
            grad_num_ref[place] = grad_num
            grad_den = -jnp.sum(scaled * attn_wide_ref[place * HD : (place + 1) * HD, :], 0, keepdims=True)
            den_row = set_row(place) * grad_den
            dens = dens + den_row
            queries = turned(jnp.maximum(query_part(qkv_ref, seq, head), 0), trig_ref)
            state_ref[place * HD : (place + 1) * HD, :] = dot_nt(grad_num, queries).astype(low)
            sums = sums + dot_nt(den_row.astype(low), queries)
    state_ref[STATE_ROWS:, :] = sums.astype(low)
    grad_den_ref[...] = dens


def grad_block_body(
    grad_num_ref,
    grad_den_ref,
    qkv_ref,
    trig_ref,
    reweight_ref,
    weights_ref,
    prior_ref,
    grad_query_ref,
    grad_key_ref,
    grad_value_ref,
):
    prior_sums = prior_ref[STATE_ROWS:, :]
    for seq, head, place in head_sets():
        query = query_part(qkv_ref, seq, head)
        queries = jnp.maximum(query, 0)
        keys = kept_keys(qkv_ref, trig_ref, seq, head)
        grad_num = grad_num_ref[place]
        den_rows = grad_den_ref[...] * set_row(place)
        grad_den = jnp.sum(den_rows, 0, keepdims=True)
        grad_scores = (
            (dot_tn(value_part(qkv_ref, seq, head), grad_num) + grad_den) * reweight_ref[...]
        ).astype(low)
        prior = jnp.concatenate([prior_ref[place * HD : (place + 1) * HD, :], prior_sums], 0)
        grads = jnp.concatenate([grad_num, den_rows.astype(low)], 0)
        grad_query = dot_nn(keys, grad_scores) + unturned(dot_tn(prior, grads), trig_ref)
        grad_query_ref[seq, head * HD : (head + 1) * HD, :] = jnp.where(
            query.astype(wide) > 0, grad_query, 0.0
        ).astype(low)
        grad_key_ref[place] = dot_nt(queries, grad_scores)
        grad_value_ref[place] = dot_nt(grad_num, weights_ref[place])


def grad_project_body(
    grad_query_ref,
    grad_key_ref,
    grad_value_ref,
    qkv_ref,
    trig_ref,
    x_own_ref,
    x_other_ref,
    weight_ref,
    flags_ref,
    *refs,
):
    arrived = refs[:-6]
    kept_ref, sent_ref, own_ref, other_ref, after_ref, grad_ref = refs[-6:]
    total = arrived[0][...].astype(wide)
    for ref in arrived[1:]:
        total = total + ref[...].astype(wide)
    after_ref[...] = total.astype(low)
    after_sums = after_ref[STATE_ROWS:, :]
    for seq, head, place in head_sets():
        key = key_part(qkv_ref, seq, head)
        keys = turned(kept_keys(qkv_ref, trig_ref, seq, head), trig_ref)
        values = value_part(qkv_ref, seq, head)
        after = after_ref[place * HD : (place + 1) * HD, :]
        left = jnp.concatenate([after, after_sums], 0)
        right = jnp.concatenate([values, set_row(place).astype(low)], 0)
        grad_key = grad_key_ref[place] + unturned(dot_tn(left, right), trig_ref)
        grad_key = jnp.where(key.astype(wide) > 0, grad_key, 0.0) * trig_ref[2 + seq : 3 + seq, :]
        grad_value = grad_value_ref[place] + dot_nn(after, keys)
        rows = slice(head * HD, (head + 1) * HD)
        grad_ref[seq, rows, :] = grad_query_ref[seq, rows, :]
        rows = slice(WIDTH + head * HD, WIDTH + (head + 1) * HD)
        grad_ref[seq, rows, :] = grad_key.astype(low)
        rows = slice(2 * WIDTH + head * HD, 2 * WIDTH + (head + 1) * HD)
        grad_ref[seq, rows, :] = grad_value.astype(low)
    matrix = weight_ref[:, : 3 * WIDTH]
    grad_w = (
        dot_nt(x_own_ref[...], grad_ref[0]) + dot_nt(x_other_ref[...], grad_ref[1])
    ).astype(low)
    rows, part, _ = kept_ref.shape
    first_copy = flags_ref[COPY] == 0
    for row in range(rows):
        start = row * 2 * part
        first, second = grad_w[start : start + part], grad_w[start + part : start + 2 * part]
        kept_ref[row] = jnp.where(first_copy, first, second)
        sent_ref[row] = jnp.where(first_copy, second, first)
    own_ref[...] = dot_nn(matrix, grad_ref[0])
    other_ref[...] = dot_nn(matrix, grad_ref[1]).astype(low)


def norm_body(x_ref, half_ref, recv_ref, vec_ref, first_ref, low_ref, normed_ref):
    hidden = x_ref[...].astype(wide) + (half_ref[...].astype(wide) + recv_ref[...].astype(wide))
    first, normed, inv_std = norm_columns(hidden, vec_ref[:, 0:1], vec_ref[:, 1:2])
    first_ref[...] = first
    low_ref[...] = first.astype(low)
    normed_ref[:D, :] = normed
    normed_ref[D:, :] = jnp.broadcast_to(inv_std, (8, SPAN))


def lane_sums(columns, place):
    lanes = lax.broadcasted_iota(jnp.int32, (columns[0].shape[0], 2 * SUM_LANES), 1)
    total = jnp.zeros(lanes.shape, wide)
    for shift, column in enumerate(columns):
        total = jnp.where(lanes == place + shift, jnp.sum(column, 1, keepdims=True), total)
    return total


def second_norm_body(
    first_ref, half_ref, recv_ref, vec_ref, cot_ref, trig_ref, result_ref, grad_ref, low_ref
):
    hidden = first_ref[...] + (half_ref[...].astype(wide) + recv_ref[...].astype(wide))
    scale = vec_ref[:, 2:3]
    result, normed, inv_std = norm_columns(hidden, scale, vec_ref[:, 3:4])
    result_ref[...] = result.astype(low)
    grad_in = cot_ref[...].astype(wide) * trig_ref[2:3, :]
    grad = norm_columns_back(grad_in, normed, inv_std, scale)
    grad_ref[:, :SPAN] = grad
    low_ref[...] = grad.astype(low)
    grad_ref[:, SPAN:] = lane_sums((grad_in * normed, grad_in), 2)


def norm_back_body(
    grad_ref, half_ref, recv_ref, normed_ref, vec_ref, hidden_ref, low_ref, sum_ref
):
    grad_in = grad_ref[:, :SPAN] + (half_ref[...].astype(wide) + recv_ref[...].astype(wide))
    normed = normed_ref[:D, :]
    grad = norm_columns_back(grad_in, normed, normed_ref[D : D + 1, :], vec_ref[:, 0:1])
    hidden_ref[...] = grad
    low_ref[...] = grad.astype(low)
    sum_ref[...] = (lane_sums((grad_in * normed, grad_in), 0) + grad_ref[:, SPAN:]).astype(low)


def hidden_weights_body(flags_ref, *refs):
    blocks, outs = refs[:-2], refs[-2:]
    for half, weight_ref in enumerate(outs):
        for mask, ref in enumerate(blocks[4 * half : 4 * half + 4]):
            weight_ref[row_block(flags_ref, mask, ref.shape[0]), :] = ref[...]


def hidden_body(own_ref, other_ref, mine_ref, copy_ref, *refs):
    acts, slopes, parts = refs[:2], refs[2:4], refs[4:]
    part = acts[0].shape[0]
    for seq, (x_ref, part_ref) in enumerate(zip((own_ref, other_ref), parts)):
        cols = slice(seq * SPAN, (seq + 1) * SPAN)
        total = None
        for weight_ref, act_ref, slope_ref in zip((mine_ref, copy_ref), acts, slopes):
            act, slope = gelu_and_slope(dot_tn(weight_ref[:, :part], x_ref[...]))
            act_ref[:, cols] = act
            slope_ref[:, cols] = slope
            term = dot_nn(weight_ref[:, part:], act)
            total = term if total is None else total + term
        part_ref[...] = total.astype(part_ref.dtype)


def hidden_back_body(
    own_ref,
    other_ref,
    mine_ref,
    copy_ref,
    slope_mine_ref,
    slope_copy_ref,
    pre_mine_ref,
    pre_copy_ref,
    part_own_ref,
    part_other_ref,
):
    part = slope_mine_ref.shape[0]
    for seq, (x_ref, part_ref) in enumerate(
        ((own_ref, part_own_ref), (other_ref, part_other_ref))
    ):
        cols = slice(seq * SPAN, (seq + 1) * SPAN)
        total = None
        for weight_ref, slope_ref, pre_ref in (
            (mine_ref, slope_mine_ref, pre_mine_ref),
            (copy_ref, slope_copy_ref, pre_copy_ref),
        ):
            grad_pre = (dot_tn(weight_ref[:, part:], x_ref[...]) * slope_ref[:, cols]).astype(low)
            pre_ref[:, cols] = grad_pre
            term = dot_nn(weight_ref[:, :part], grad_pre)
            total = term if total is None else total + term
        part_ref[...] = total.astype(part_ref.dtype)


def half_grads_body(own_ref, other_ref, mine_ref, copy_ref, kept_ref, sent_ref):
    for pre_ref, out_ref in ((copy_ref, sent_ref), (mine_ref, kept_ref)):
        out_ref[...] = (
            dot_nt(own_ref[...], pre_ref[:, :SPAN]) + dot_nt(other_ref[...], pre_ref[:, SPAN:])
        ).astype(low)


def quarters(flags_ref, refs):
    core, copy = flags_ref[CORE], flags_ref[COPY]
    for ref, other_core, other_copy in zip(refs, (0, 0, 1, 1), (0, 1, 0, 1)):
        core_place = 1 - core if other_core else core
        copy_place = 1 - copy if other_copy else copy
        yield core_place * 2 + copy_place, ref


def place_hidden_body(flags_ref, *refs):
    down_ref, up_ref, out_ref, vec_ref = refs[4:]
    part = up_ref.shape[1] // 4
    for place, ref in quarters(flags_ref, refs[:4]):
        cols = pl.ds(pl.multiple_of(place * part, 128), part)
        down_ref[:, cols] = ref[:, :part].astype(wide)
        up_ref[:, cols] = ref[:, part : 2 * part].astype(wide)
    half = (WIDTH + SUM_LANES) // 2
    first_core, first_copy = flags_ref[CORE] == 0, flags_ref[COPY] == 0
    sums = []
    for own_ref, copy_ref in (refs[:2], refs[2:4]):
        own, copied = own_ref[:, 2 * part :].astype(wide), copy_ref[:, 2 * part :].astype(wide)
        sums.append((jnp.where(first_copy, own, copied), jnp.where(first_copy, copied, own)))
    first = [jnp.where(first_core, sums[0][i], sums[1][i]) for i in (0, 1)]
    second = [jnp.where(first_core, sums[1][i], sums[0][i]) for i in (0, 1)]
    for parts, start in ((first, 0), (second, WIDTH)):
        out_ref[:, start : start + half] = parts[0]
        out_ref[:, start + half : start + WIDTH] = parts[1][:, : WIDTH - half]
    vec_ref[...] = first[1][:, WIDTH - half :] + second[1][:, WIDTH - half :]


def place_last_body(flags_ref, *refs):
    outs = refs[4:]
    first_core = flags_ref[CORE] == 0
    part = refs[0].shape[0]
    for own_ref, other_ref, other_copy in ((refs[0], refs[2], 0), (refs[1], refs[3], 1)):
        copy = 1 - flags_ref[COPY] if other_copy else flags_ref[COPY]
        rows = pl.ds(pl.multiple_of(copy * part, 8), part)
        own, other = own_ref[...].astype(wide), other_ref[...].astype(wide)
        for place, out_ref in enumerate(outs):
            cols = slice(place * WIDTH, (place + 1) * WIDTH)
            out_ref[rows, :WIDTH] = jnp.where(first_core, own[:, cols], other[:, cols])
            out_ref[rows, WIDTH:] = jnp.where(first_core, other[:, cols], own[:, cols])


def gelu_and_slope(pre):
    cdf = 0.5 * (1.0 + lax.erf(pre * math.sqrt(0.5)))
    density = jnp.exp(-0.5 * pre * pre) * (1.0 / math.sqrt(2.0 * math.pi))
    return (pre * cdf).astype(low), (cdf + pre * density)


def all_quarters(own, direct=False):
    copied = swap_copies(own)
    if direct:
        pairs = [(i, i ^ 3) for i in range(lax.axis_size("dp"))]
        return own, copied, swap_pair(own), lax.ppermute(own, "dp", pairs)
    return own, copied, swap_pair(own), swap_pair(copied)


def on_device_paired(
    tokens,
    lengths,
    w_query,
    w_key,
    w_value,
    w_out,
    gain_one,
    bias_one,
    w_up,
    w_down,
    gain_two,
    bias_two,
    cotangent,
):
    rows = lax.axis_size("row")
    seq_len = SPAN * rows
    dp_idx = lax.axis_index("dp")
    feat_rows = tokens.shape[0]
    half_feats = feat_rows // 2
    flags = jnp.stack(
        [dp_idx % 2, dp_idx // 2, lax.axis_index("row"), lax.axis_index("col"), dp_idx]
    )
    trig, reweight = local_call(
        partial(turn_body, seq_len=seq_len),
        [((8, SPAN), wide), ((SPAN, SPAN), wide)],
        "turn",
        flags,
        lengths,
    )

    def passed_on(pieces):
        return [pieces[0]] + [
            rotate_rows(piece, step) for step, piece in enumerate(pieces) if step
        ]

    def cols_back(own, other, kind, name):
        return local_call(
            join_back_body,
            [((feat_rows, SPAN * rows // 2), kind)],
            name,
            flags,
            own,
            swap_cols(other),
        )[0]

    def column_parts(own_part, other_part, name):
        (half,) = local_call(add_body, low_outs(1, D, SPAN), name, own_part, swap_pair(other_part))
        return half, swap_cols(half)

    first_col = lax.axis_index("col") == 0

    def halved(block):
        top, bottom = block[:half_feats], block[half_feats:]
        return jnp.where(first_col, top, bottom), jnp.where(first_col, bottom, top)

    (token_own, token_sent), (cot_own, cot_sent) = halved(tokens), halved(cotangent)
    got = swap_cols(jnp.concatenate([token_sent, cot_sent], 0))

    part = w_up.shape[1] // 4
    first_core = dp_idx % 2 == 0

    def core_part(operand):
        return jnp.where(first_core, operand[:, :WIDTH], operand[:, WIDTH:])

    parts = [core_part(operand) for operand in (w_query, w_key, w_value, w_out.T)]
    first_packed = jnp.concatenate(parts, 1)
    first_mine = jnp.where(
        dp_idx < 2, jnp.concatenate(parts[:2], 1), jnp.concatenate(parts[2:], 1)
    )

    def row_blocks(block):
        return swap_rows(block, 1), swap_rows(block, 2)

    first_one, first_two = row_blocks(first_mine)
    first_one, got = lax.optimization_barrier((first_one, got))
    hidden_packed = local_call(
        pack_hidden_body,
        low_outs(2, feat_rows, 2 * part),
        "pack_hidden",
        flags,
        w_up,
        w_down.T,
        scratch=[pltpu.SemaphoreType.DMA((4,))],
        space=pltpu.HBM,
    )
    vecs = jnp.stack([gain_one, bias_one, gain_two, bias_two], 0)
    token_pieces = local_call(
        partial(pieces_body, rows=rows),
        low_outs(rows, feat_rows + 16, SPAN),
        "token_pieces",
        flags,
        token_own,
        cot_own,
        got,
        vecs,
    )
    def after(value, *others):
        return lax.optimization_barrier((value, others))[0]

    first_three = swap_rows(after(first_two, token_pieces[0]), 1)
    first_copies = [
        swap_copies(after(first_one, token_pieces[0])),
        swap_copies(first_two),
        swap_copies(first_three),
    ]
    token_pieces = passed_on(token_pieces)
    token_pieces, first_three, first_copies[0] = lax.optimization_barrier(
        (token_pieces, first_three, first_copies[0])
    )
    first_blocks = [first_one, first_two, first_three, *first_copies]
    x_half, norm_vecs = local_call(
        partial(place_tokens_body, rows=rows, part=half_feats),
        low_outs(1, D, SPAN) + [((D, 8), wide)],
        "token_place",
        flags,
        *token_pieces,
    )
    x_half, trig, reweight = lax.optimization_barrier((x_half, trig, reweight))
    hidden_one, hidden_two = row_blocks(hidden_packed[0])
    x_got, hidden_one = lax.optimization_barrier((swap_cols(x_half), hidden_one))
    x_own, cot = local_call(
        partial(join_halves_body, rows=rows),
        low_outs(2, D, SPAN),
        "token_join",
        flags,
        x_half,
        x_got,
    )
    x_own, first_blocks = lax.optimization_barrier((x_own, first_blocks))
    x_other = swap_pair(x_own)
    state_shape = ((STATE_ROWS + SUM_ROWS, 2 * HD), low)
    sets = 2 * HEADS
    block_low = ((D, SPAN), low)
    block_wide = ((D, SPAN), wide)
    weight, qkv, state = local_call(
        project_body,
        [((D, 4 * WIDTH), low), ((2, 3 * WIDTH, SPAN), low), state_shape],
        "project",
        flags,
        x_own,
        x_other,
        trig,
        first_packed,
        *first_blocks,
    )
    hidden_three = swap_rows(hidden_two, 1)
    copy_two = swap_copies(hidden_two)
    arrived = [shift_rows(state, step) for step in range(1, rows)]
    arrived, hidden_three, copy_two = lax.optimization_barrier(
        (arrived, hidden_three, copy_two)
    )
    weights, numer, denom = local_call(
        block_body,
        [((sets, SPAN, SPAN), low), ((sets, HD, SPAN), wide), ((SUM_ROWS, SPAN), wide)],
        "block",
        qkv,
        trig,
        reweight,
    )
    prior, attn_wide, branch_own, branch_other = local_call(
        attend_body,
        [
            state_shape,
            ((STATE_ROWS + SUM_ROWS, SPAN), wide),
            block_wide,
            block_low,
        ],
        "attend",
        qkv,
        trig,
        numer,
        denom,
        weight,
        *arrived,
        scratch=[((2, WIDTH, SPAN), low)],
    )
    copy_one = swap_copies(hidden_one)
    branch_own, branch_other, copy_one = lax.optimization_barrier(
        (branch_own, branch_other, copy_one)
    )
    branch = column_parts(branch_own, branch_other, "branch_half")
    copy_three = swap_copies(hidden_three)
    branch, copy_three = lax.optimization_barrier((branch, copy_three))
    hidden_mine, hidden_copy = local_call(
        hidden_weights_body,
        low_outs(2, D, 2 * part),
        "hidden_weights",
        flags,
        hidden_packed[0],
        hidden_one,
        hidden_two,
        hidden_three,
        hidden_packed[1],
        copy_one,
        copy_two,
        copy_three,
    )
    branch, hidden_mine = lax.optimization_barrier((branch, hidden_mine))
    first, first_low, normed = local_call(
        norm_body,
        [block_wide, block_low, ((D + 8, SPAN), wide)],
        "norm",
        x_own,
        *branch,
        norm_vecs,
    )
    first_other = swap_pair(first_low)
    hidden_acts = [((part, 2 * SPAN), low)] * 2 + [((part, 2 * SPAN), wide)] * 2
    act_mine, act_copy, slope_mine, slope_copy, ffn_own, ffn_other = local_call(
        hidden_body,
        hidden_acts + [block_wide, block_low],
        "hidden",
        first_low,
        first_other,
        hidden_mine,
        hidden_copy,
    )
    ffn = column_parts(ffn_own, ffn_other, "ffn_half")
    result, grad_second, grad_ffn = local_call(
        second_norm_body,
        [block_low, ((D, SPAN + 2 * SUM_LANES), wide), block_low],
        "second_norm",
        first,
        *ffn,
        norm_vecs,
        cot,
        trig,
    )
    grad_ffn_other = swap_pair(grad_ffn)
    pair_low = ((D, part), low)
    down_held, down_sent = local_call(
        down_grad_body,
        low_outs(2, 2 * feat_rows, 2 * part),
        "down_grad",
        flags,
        grad_ffn,
        grad_ffn_other,
        act_mine,
        act_copy,
        scratch=[((D, 2 * part), low)],
    )
    down_got = swap_rows(down_sent, 1)
    grad_ffn, grad_ffn_other, down_held = lax.optimization_barrier(
        (grad_ffn, grad_ffn_other, down_held)
    )
    hidden_low = ((part, 2 * SPAN), low)
    pre_mine, pre_copy, first_own_part, first_other_part = local_call(
        hidden_back_body,
        [hidden_low, hidden_low, block_wide, block_low],
        "hidden_back",
        grad_ffn,
        grad_ffn_other,
        hidden_mine,
        hidden_copy,
        slope_mine,
        slope_copy,
    )
    first_sum = column_parts(first_own_part, first_other_part, "first_half")

    kept_up, sent_up = local_call(
        half_grads_body,
        [pair_low, pair_low],
        "up_grad",
        first_low,
        first_other,
        pre_mine,
        pre_copy,
    )
    got_up = swap_copies(sent_up)
    down_kept, down_pair = local_call(
        down_pairs_body,
        [((2 * feat_rows, part), wide), ((2 * feat_rows, part), low)],
        "down_pairs",
        down_held,
        down_got,
    )
    first_sum, kept_up, down_kept = lax.optimization_barrier((first_sum, kept_up, down_kept))
    grad_hidden, branch_grad, vec_sums = local_call(
        norm_back_body,
        [block_wide, block_low, ((D, 2 * SUM_LANES), low)],
        "norm_back",
        grad_second,
        *first_sum,
        normed,
        norm_vecs,
    )
    branch_grad_other = swap_pair(branch_grad)
    grad_num, grad_den, grad_state = local_call(
        grad_attend_body,
        [((sets, HD, SPAN), low), ((SUM_ROWS, SPAN), wide), state_shape],
        "grad_attend",
        branch_grad,
        branch_grad_other,
        weight,
        attn_wide,
        qkv,
        trig,
    )
    later = [shift_rows(grad_state, -step) for step in range(1, rows)]
    half_lanes = (WIDTH + SUM_LANES) // 2
    mix_kept, mix_sent = local_call(
        mix_body,
        [((D, half_lanes), low), ((2 * feat_rows, part + 2 * half_lanes), low)],
        "mix",
        flags,
        branch_grad,
        branch_grad_other,
        attn_wide,
        vec_sums,
        after(down_pair, grad_num),
        scratch=[((D, WIDTH + SUM_LANES), low)],
    )
    grad_query, grad_key, grad_value = local_call(
        grad_block_body,
        [
            ((2, WIDTH, SPAN), low),
            ((sets, HD, SPAN), wide),
            ((sets, HD, SPAN), wide),
        ],
        "grad_block",
        grad_num,
        grad_den,
        qkv,
        trig,
        reweight,
        weights,
        prior,
    )
    mix_got = swap_copies(after(mix_sent, got_up))
    up_lanes = SPAN // 2 + part + half_lanes
    down_part, down_far = local_call(
        down_far_body,
        [((feat_rows, part), wide), ((feat_rows, part), low)],
        "down_far",
        down_kept,
        mix_got,
    )
    down_far = swap_rows(down_far, 2)
    up_held, up_sent = local_call(
        up_pieces_body,
        low_outs(2, 2 * feat_rows, up_lanes),
        "up_pieces",
        flags,
        result,
        kept_up,
        after(got_up, grad_query),
        mix_kept,
        mix_got,
        scratch=[((D, half_lanes), low)],
    )
    up_got = swap_rows(up_sent, 1)
    later, up_held = lax.optimization_barrier((later, up_held))
    half_rows = ((rows, half_feats, 3 * WIDTH), low)
    kept_w, sent_w, x_grad_own, x_grad_other = local_call(
        grad_project_body,
        [half_rows, half_rows, block_wide, block_low],
        "grad_project",
        grad_query,
        grad_key,
        grad_value,
        qkv,
        trig,
        x_own,
        x_other,
        weight,
        flags,
        *later,
        scratch=[state_shape, ((2, 3 * WIDTH, SPAN), low)],
    )
    got_w = swap_copies(sent_w)
    got_x = swap_pair(x_grad_other)
    x_half_grad, x_half_sent = local_call(
        partial(input_halves_body, rows=rows),
        [((D // 2, SPAN), wide), ((D // 2, SPAN), low)],
        "input_halves",
        flags,
        x_grad_own,
        got_x,
        scratch=[block_wide],
    )
    got_half = swap_cols(x_half_sent)
    last_lanes = 3 * WIDTH
    last_held, last_sent = local_call(
        last_pieces_body,
        low_outs(2, 2 * half_feats, last_lanes + SPAN),
        "last_pieces",
        flags,
        kept_w,
        got_w,
        x_half_grad,
        got_half,
        grad_hidden,
    )
    up_part, up_far = local_call(
        up_pairs_body,
        [((feat_rows, up_lanes - SPAN // 2), wide), ((feat_rows, up_lanes + SPAN // 2), low)],
        "up_pairs",
        up_held,
        up_got,
    )
    up_far = swap_rows(up_far, 2)
    last_got = swap_rows(last_sent, 1)
    last_part, last_far = local_call(
        last_pairs_body,
        [((half_feats, last_lanes), wide), ((half_feats, last_lanes + 2 * SPAN), low)],
        "last_pairs",
        last_held,
        last_got,
    )
    hidden_sum, *out_wide = local_call(
        hidden_sums_body,
        low_outs(1, feat_rows, 2 * part + half_lanes)
        + low_outs(2, half_feats, SPAN * rows // 2),
        "hidden_sums",
        flags,
        down_part,
        down_far,
        up_part,
        up_held,
        up_got,
        up_far,
        scratch=[((4, half_feats, SPAN), low)],
    )
    last_sum, *input_wide = local_call(
        last_sums_body,
        low_outs(1, half_feats, last_lanes) + low_outs(2, half_feats, SPAN * rows // 2),
        "last_sums",
        flags,
        last_part,
        last_held,
        last_got,
        swap_rows(last_far, 2),
    )
    output = cols_back(*out_wide, low, "out_join")
    input_grad = cols_back(*input_wide, wide, "input_join")
    down_t, up_grad, out_t, vec_total = local_call(
        place_hidden_body,
        [((feat_rows, 4 * part), wide)] * 2
        + [((feat_rows, 2 * WIDTH), wide), ((feat_rows, SUM_LANES), wide)],
        "place_hidden",
        flags,
        *all_quarters(hidden_sum, True),
    )
    query_grad, key_grad, value_grad = local_call(
        place_last_body,
        [((feat_rows, 2 * WIDTH), wide)] * 3,
        "place_last",
        flags,
        *all_quarters(last_sum, True),
    )
    return (
        output,
        input_grad,
        query_grad,
        key_grad,
        value_grad,
        out_t.T,
        vec_total[:, 0],
        vec_total[:, 1],
        up_grad,
        down_t.T,
        vec_total[:, 2],
        vec_total[:, 3],
    )


def solution(mesh):
    placed = (
        P("row", ("dp", "col")),
        P(),
        P("row", "col"),
        P("row", "col"),
        P("row", "col"),
        P("col", "row"),
        P("row"),
        P("row"),
        P("row", "col"),
        P("col", "row"),
        P("row"),
        P("row"),
        P("row", ("dp", "col")),
    )
    return jax.shard_map(
        on_device_paired if paired_layout(mesh) else on_device,
        mesh=mesh,
        in_specs=placed,
        out_specs=(
            P("row", ("dp", "col")),
            P("row", ("dp", "col")),
            P("row", "col"),
            P("row", "col"),
            P("row", "col"),
            P("col", "row"),
            P("row"),
            P("row"),
            P("row", "col"),
            P("col", "row"),
            P("row"),
            P("row"),
        ),
        check_vma=False,
    )
```

```python
from functools import partial
import math

import jax
import jax.numpy as jnp
from jax import lax
from jax.experimental import pallas as pl
from jax.experimental.pallas import tpu as pltpu
from jax.sharding import PartitionSpec as P

D = 768
H = 12
HD = 64
SEQ_MAX = 4096
TOK_DEV = 128


norm_eps = 1e-05
highest = lax.Precision.HIGHEST


def carried_in(shard, axis, join, neutral, backward):
    count = lax.axis_size(axis)
    place = lax.axis_index(axis)
    ahead = count - 1 - place if backward else place
    gathered = jax.tree.map(
        lambda a, kind: lax.all_gather(a.astype(kind), axis),
        shard,
        jax.tree.map(lambda a: jnp.bfloat16 if a.dtype == jnp.float32 else a.dtype, shard),
    )
    state = jax.tree.map(lambda a, e: jnp.zeros_like(a) + jnp.asarray(e, a.dtype), shard, neutral)

    def one(turn, state):
        source = count - 1 - turn if backward else turn
        return join(
            state,
            jax.tree.map(
                lambda a, own: lax.dynamic_index_in_dim(a, source, 0, False).astype(own.dtype),
                gathered,
                shard,
            ),
        )

    return lax.fori_loop(0, ahead, one, state)


def gather_cols(operand):
    return lax.all_gather(operand, "col", axis=0, tiled=True)


def gather_rows(operand):
    return lax.all_gather(operand, "row", axis=0, tiled=True)


def summed_over_rows(gathered, matrix):
    out_rows = gathered.shape[0] // lax.axis_size("row")

    def term_rows(first_row, row_count):
        sliced = lax.dynamic_slice_in_dim(gathered, first_row, row_count, 0)
        return jnp.dot(sliced, matrix, preferred_element_type=jnp.float32)

    return lax.psum_scatter(
        term_rows(jnp.int32(0), out_rows * lax.axis_size("row")),
        "row",
        scatter_dimension=0,
        tiled=True,
    )


def summed_over_cols(gathered, matrix):
    out_rows = gathered.shape[0] // lax.axis_size("col")

    def term_rows(first_row, row_count):
        sliced = lax.dynamic_slice_in_dim(gathered, first_row, row_count, 0)
        return jnp.dot(sliced, matrix, preferred_element_type=jnp.float32)

    return lax.psum_scatter(
        term_rows(jnp.int32(0), out_rows * lax.axis_size("col")).astype(jnp.bfloat16),
        "col",
        scatter_dimension=0,
        tiled=True,
    ).astype(jnp.float32)


def to_heads(stacked):
    return lax.all_to_all(stacked, "col", split_axis=1, concat_axis=2, tiled=True)


def to_tokens(stacked):
    return lax.all_to_all(stacked, "col", split_axis=2, concat_axis=1, tiled=True)


def row_totals(first_part, second_part):
    return lax.psum((first_part, second_part), "row")


def norm_forward(hidden, scale_vec, shift_vec):
    sum_one, sum_two = row_totals(jnp.sum(hidden, 1), jnp.sum(hidden * hidden, 1))
    row_mean = sum_one / D
    variance = sum_two / D - row_mean * row_mean
    inv_std = lax.rsqrt(variance + norm_eps)
    normed = (hidden - row_mean[:, None]) * inv_std[:, None]
    return (normed * scale_vec + shift_vec, normed, inv_std)


def norm_backward(grad_in, normed, inv_std, scale_vec):
    grad_normed = grad_in * scale_vec
    total_one, total_two = row_totals(jnp.sum(grad_normed, 1), jnp.sum(grad_normed * normed, 1))
    grad_hidden = inv_std[:, None] * (
        grad_normed - total_one[:, None] / D - normed * (total_two[:, None] / D)
    )
    return (grad_hidden, jnp.sum(grad_in * normed, 0), jnp.sum(grad_in, 0))


def seq_lengths(lengths, seq_ids):
    matches = seq_ids[:, None] == jnp.arange(lengths.shape[0], dtype=jnp.int32)[None, :]
    return jnp.sum(jnp.where(matches, lengths[None, :], 0), 1)


def reset_combine(earlier, later):
    keep_prior = 1.0 - later[4]
    joined = tuple(
        (
            keep_prior * prior_part + next_part
            for prior_part, next_part in zip(earlier[:4], later[:4])
        )
    )
    return joined + (jnp.maximum(earlier[4], later[4]),)


def empty_state():
    return (
        jnp.zeros((H, HD, HD), jnp.float32),
        jnp.zeros((H, HD, HD), jnp.float32),
        jnp.zeros((H, HD), jnp.float32),
        jnp.zeros((H, HD), jnp.float32),
        jnp.zeros((), jnp.float32),
    )


def attend_forward(queries, keys_in, values_in, present, cos_flat, sin_flat, opens_seq):
    block_rows = queries.shape[0]
    cos_pos = cos_flat[:, None, None]
    sin_pos = sin_flat[:, None, None]
    q_pos = jnp.maximum(queries, 0)
    k_pos = jnp.maximum(keys_in, 0) * present[:, None, None].astype(jnp.bfloat16)
    q_cos = q_pos.astype(jnp.float32) * cos_pos
    q_sin = q_pos.astype(jnp.float32) * sin_pos
    k_cos = k_pos.astype(jnp.float32) * cos_pos
    k_sin = k_pos.astype(jnp.float32) * sin_pos
    values_wide = values_in.astype(jnp.float32)
    local_state = (
        jnp.einsum("jhd,jhe->hde", k_cos, values_wide, precision=highest),
        jnp.einsum("jhd,jhe->hde", k_sin, values_wide, precision=highest),
        jnp.sum(k_cos, 0),
        jnp.sum(k_sin, 0),
    )
    arrived = carried_in(
        local_state + (opens_seq,), ("row", "col"), reset_combine, empty_state(), False
    )
    s_cos, s_sin, z_cos, z_sin = tuple(
        (state_part * (1.0 - opens_seq) for state_part in arrived[:4])
    )
    row_ids = jnp.arange(block_rows, dtype=jnp.int32)
    causal = (row_ids[:, None] >= row_ids[None, :]).astype(jnp.float32)
    reweight = (
        cos_flat[:, None] * cos_flat[None, :] + sin_flat[:, None] * sin_flat[None, :]
    ) * causal
    scores = jnp.einsum("ihd,jhd->hij", q_pos, k_pos, preferred_element_type=jnp.float32)
    weights = scores * reweight[None]
    weights_low = weights.astype(jnp.bfloat16)
    numerator = jnp.einsum(
        "hij,jhe->ihe", weights_low, values_in, preferred_element_type=jnp.float32
    )
    numerator = numerator + jnp.einsum("ihd,hde->ihe", q_cos, s_cos, precision=highest)
    numerator = numerator + jnp.einsum("ihd,hde->ihe", q_sin, s_sin, precision=highest)
    denominator = 1.0 + jnp.sum(weights, 2).T
    denominator = denominator + jnp.einsum("ihd,hd->ih", q_cos, z_cos, precision=highest)
    denominator = denominator + jnp.einsum("ihd,hd->ih", q_sin, z_sin, precision=highest)
    mixed = (numerator / denominator[:, :, None]).astype(jnp.bfloat16).reshape(block_rows, D)
    kept = (
        queries,
        keys_in,
        values_in,
        q_pos,
        k_pos,
        q_cos,
        q_sin,
        k_cos,
        k_sin,
        values_wide,
        reweight,
        weights_low,
        numerator,
        denominator,
        s_cos,
        s_sin,
        z_cos,
        z_sin,
        present,
        cos_pos,
        sin_pos,
    )
    return (mixed, kept)


def attend_backward(grad_heads, kept, closes_seq):
    (
        queries,
        keys_in,
        values_in,
        q_pos,
        k_pos,
        q_cos,
        q_sin,
        k_cos,
        k_sin,
        values_wide,
        reweight,
        weights_low,
        numerator,
        denominator,
        s_cos,
        s_sin,
        z_cos,
        z_sin,
        present,
        cos_pos,
        sin_pos,
    ) = kept
    block_rows = queries.shape[0]
    grad_attn = grad_heads.astype(jnp.float32).reshape(block_rows, H, HD)
    grad_num_low = (grad_attn / denominator[:, :, None]).astype(jnp.bfloat16)
    grad_num = grad_num_low.astype(jnp.float32)
    grad_den = -jnp.sum(grad_attn * numerator, 2) / (denominator * denominator)
    grad_weights = jnp.einsum(
        "ihe,jhe->hij", grad_num_low, values_in, preferred_element_type=jnp.float32
    )
    grad_weights = grad_weights + grad_den.T[:, :, None]
    grad_scores = (grad_weights * reweight[None]).astype(jnp.bfloat16)
    local_grad = (
        jnp.einsum("ihd,ihe->hde", q_cos, grad_num, precision=highest),
        jnp.einsum("ihd,ihe->hde", q_sin, grad_num, precision=highest),
        jnp.einsum("ihd,ih->hd", q_cos, grad_den, precision=highest),
        jnp.einsum("ihd,ih->hd", q_sin, grad_den, precision=highest),
    )
    later_sum = carried_in(
        local_grad + (closes_seq,), ("row", "col"), reset_combine, empty_state(), True
    )
    g_cos, g_sin, gz_cos, gz_sin = tuple(
        (state_part * (1.0 - closes_seq) for state_part in later_sum[:4])
    )
    grad_qpos = jnp.einsum("hij,jhd->ihd", grad_scores, k_pos, preferred_element_type=jnp.float32)
    grad_qpos = grad_qpos + cos_pos * (
        jnp.einsum("ihe,hde->ihd", grad_num, s_cos, precision=highest)
        + grad_den[:, :, None] * z_cos[None]
    )
    grad_qpos = grad_qpos + sin_pos * (
        jnp.einsum("ihe,hde->ihd", grad_num, s_sin, precision=highest)
        + grad_den[:, :, None] * z_sin[None]
    )
    grad_kpos = jnp.einsum("hij,ihd->jhd", grad_scores, q_pos, preferred_element_type=jnp.float32)
    grad_kpos = grad_kpos + cos_pos * (
        jnp.einsum("jhe,hde->jhd", values_wide, g_cos, precision=highest) + gz_cos[None]
    )
    grad_kpos = grad_kpos + sin_pos * (
        jnp.einsum("jhe,hde->jhd", values_wide, g_sin, precision=highest) + gz_sin[None]
    )
    grad_values = jnp.einsum(
        "hij,ihe->jhe", weights_low, grad_num_low, preferred_element_type=jnp.float32
    )
    grad_values = grad_values + jnp.einsum("jhd,hde->jhe", k_cos, g_cos, precision=highest)
    grad_values = grad_values + jnp.einsum("jhd,hde->jhe", k_sin, g_sin, precision=highest)
    grad_q = (grad_qpos * (queries > 0).astype(jnp.float32)).astype(jnp.bfloat16)
    grad_k = (grad_kpos * (keys_in > 0).astype(jnp.float32) * present[:, None, None]).astype(
        jnp.bfloat16
    )
    grad_v = grad_values.astype(jnp.bfloat16)
    return (
        grad_q.reshape(block_rows, D),
        grad_k.reshape(block_rows, D),
        grad_v.reshape(block_rows, D),
    )


def on_device(
    tokens,
    lengths,
    w_query,
    w_key,
    w_value,
    w_out,
    gain_one,
    bias_one,
    w_up,
    w_down,
    gain_two,
    bias_two,
    cotangent,
):
    row_count = lax.axis_size("row")
    col_count = lax.axis_size("col")
    seq_len = min(SEQ_MAX, TOK_DEV * row_count * col_count)
    data_idx = lax.axis_index("dp")
    row_idx = lax.axis_index("row")
    col_idx = lax.axis_index("col")
    feat_rows = tokens.shape[0]
    group_idx = row_idx * col_count + col_idx
    global_idx = (data_idx * row_count * col_count + group_idx) * TOK_DEV + jnp.arange(
        TOK_DEV, dtype=jnp.int32
    )
    positions = global_idx % seq_len
    present = (positions < seq_lengths(lengths, global_idx // seq_len)).astype(jnp.float32)
    angles = math.pi * positions.astype(jnp.float32) / (2.0 * seq_len)
    cos_flat = jnp.cos(angles)
    sin_flat = jnp.sin(angles)
    opens_seq = (group_idx * TOK_DEV % seq_len == 0).astype(jnp.float32)
    closes_seq = ((group_idx + 1) * TOK_DEV % seq_len == 0).astype(jnp.float32)
    token_rows = tokens.T
    width_col = w_query.shape[1]
    w_cat = jnp.concatenate([w_query, w_key, w_value], 1)
    x_gathered = gather_cols(token_rows)
    qkv = summed_over_rows(x_gathered, w_cat).astype(jnp.bfloat16)
    stacked = jnp.stack(
        [qkv[:, :width_col], qkv[:, width_col : 2 * width_col], qkv[:, 2 * width_col :]], 0
    )
    head_rows = to_heads(stacked)
    mixed, kept = attend_forward(
        head_rows[0].reshape(TOK_DEV, H, HD),
        head_rows[1].reshape(TOK_DEV, H, HD),
        head_rows[2].reshape(TOK_DEV, H, HD),
        present,
        cos_flat,
        sin_flat,
        opens_seq,
    )
    mixed_two = to_tokens(mixed[None])[0]
    mixed_gathered = gather_rows(mixed_two)
    branch = summed_over_cols(mixed_gathered, w_out)
    first, normed_one, inv_one = norm_forward(
        token_rows.astype(jnp.float32) + branch, gain_one, bias_one
    )
    first_low = first.astype(jnp.bfloat16)
    first_gathered = gather_cols(first_low)
    pre = summed_over_rows(first_gathered, w_up)
    act, gelu_pull = jax.vjp(partial(jax.nn.gelu, approximate=False), pre)
    act_low = act.astype(jnp.bfloat16)
    act_gathered = gather_rows(act_low)
    ffn = summed_over_cols(act_gathered, w_down)
    result, normed_two, inv_two = norm_forward(first + ffn, gain_two, bias_two)
    rows_one = token_rows.shape[0]
    global_one = (data_idx * col_count + col_idx) * rows_one + jnp.arange(rows_one, dtype=jnp.int32)
    present_one = (global_one % seq_len < seq_lengths(lengths, global_one // seq_len)).astype(
        jnp.float32
    )
    grad_result = cotangent.T.astype(jnp.float32) * present_one[:, None]
    grad_second, grad_gain_two, grad_bias_two = norm_backward(
        grad_result, normed_two, inv_two, gain_two
    )
    grad_ffn_gathered = gather_cols(grad_second.astype(jnp.bfloat16))
    act_again = gather_rows(act_low)
    grad_down = jnp.einsum(
        "tf,td->fd", act_again, grad_ffn_gathered, preferred_element_type=jnp.float32
    )
    grad_act = summed_over_rows(grad_ffn_gathered, w_down.T)
    grad_pre = gelu_pull(grad_act)[0].astype(jnp.bfloat16)
    grad_pre_gathered = gather_rows(grad_pre)
    first_again = gather_cols(first_low)
    grad_up = jnp.einsum(
        "td,tf->df", first_again, grad_pre_gathered, preferred_element_type=jnp.float32
    )
    grad_first = summed_over_cols(grad_pre_gathered, w_up.T) + grad_second
    grad_hidden, grad_gain_one, grad_bias_one = norm_backward(
        grad_first, normed_one, inv_one, gain_one
    )
    branch_grad_gathered = gather_cols(grad_hidden.astype(jnp.bfloat16))
    mixed_again = gather_rows(mixed_two)
    grad_out = jnp.einsum(
        "tc,tr->cr", mixed_again, branch_grad_gathered, preferred_element_type=jnp.float32
    )
    grad_mixed = summed_over_rows(branch_grad_gathered, w_out.T).astype(jnp.bfloat16)
    grad_heads = to_heads(grad_mixed[None])[0]
    grad_q, grad_k, grad_v = attend_backward(grad_heads, kept, closes_seq)
    grad_rows = to_tokens(jnp.stack([grad_q, grad_k, grad_v], 0))
    grad_cat = jnp.concatenate([grad_rows[0], grad_rows[1], grad_rows[2]], 1)
    grad_cat_gathered = gather_rows(grad_cat)
    x_again = gather_cols(token_rows)
    grad_cat_w = jnp.einsum(
        "tr,tc->rc", x_again, grad_cat_gathered, preferred_element_type=jnp.float32
    )
    input_rows = summed_over_cols(grad_cat_gathered, w_cat.T) + grad_hidden
    gain_parts = jnp.stack([grad_gain_one, grad_bias_one, grad_gain_two, grad_bias_two], 0)
    gain_sums = lax.psum(gain_parts.reshape(4 * feat_rows), "col")
    grad_query = grad_cat_w[:, :width_col]
    grad_key = grad_cat_w[:, width_col : 2 * width_col]
    grad_value = grad_cat_w[:, 2 * width_col :]
    output = result.astype(jnp.bfloat16).T
    input_grad = input_rows.T
    sums = (
        lax.psum(grad_query.astype(jnp.bfloat16), "dp").astype(jnp.float32),
        lax.psum(grad_key.astype(jnp.bfloat16), "dp").astype(jnp.float32),
        lax.psum(grad_value.astype(jnp.bfloat16), "dp").astype(jnp.float32),
        lax.psum(grad_out.astype(jnp.bfloat16), "dp").astype(jnp.float32),
        lax.psum(grad_up.astype(jnp.bfloat16), "dp").astype(jnp.float32),
        lax.psum(grad_down.astype(jnp.bfloat16), "dp").astype(jnp.float32),
        lax.psum(gain_sums.astype(jnp.bfloat16), "dp").astype(jnp.float32),
    )
    gain_total = sums[6].reshape(4, feat_rows)
    return (
        output,
        input_grad,
        sums[0],
        sums[1],
        sums[2],
        sums[3],
        gain_total[0],
        gain_total[1],
        sums[4],
        sums[5],
        gain_total[2],
        gain_total[3],
    )


def paired_layout(mesh):
    rows, cols, dps = mesh.shape["row"], mesh.shape["col"], mesh.shape["dp"]
    return rows == 4 and cols == 2 and dps == 4 and H % 4 == 0 and 8 * TOK_DEV <= SEQ_MAX


low = jnp.bfloat16
wide = jnp.float32
SPAN = 2 * TOK_DEV
HEADS = H // 4
WIDTH = HEADS * HD
STATE_ROWS = 2 * HEADS * HD
SUM_ROWS = 16
SUM_LANES = 64


def swap_cols(operand):
    return lax.ppermute(operand, "col", [(0, 1), (1, 0)])


def swap_pair(operand):
    return lax.ppermute(operand, "dp", [(i, i ^ 1) for i in range(lax.axis_size("dp"))])


def swap_copies(operand):
    return lax.ppermute(operand, "dp", [(i, i ^ 2) for i in range(lax.axis_size("dp"))])


def shift_rows(operand, step):
    count = lax.axis_size("row")
    pairs = [(i, i + step) for i in range(count) if 0 <= i + step < count]
    return lax.ppermute(operand, "row", pairs)


def swap_rows(operand, mask):
    return lax.ppermute(operand, "row", [(i, i ^ mask) for i in range(4)])


def rotate_rows(operand, step):
    count = lax.axis_size("row")
    return lax.ppermute(operand, "row", [(i, (i + step) % count) for i in range(count)])


def dot_tn(left, right):
    return lax.dot_general(left, right, (((0,), (0,)), ((), ())), preferred_element_type=wide)


def dot_nt(left, right):
    return lax.dot_general(left, right, (((1,), (1,)), ((), ())), preferred_element_type=wide)


def dot_nn(left, right):
    return jnp.dot(left, right, preferred_element_type=wide)


def norm_columns(hidden, scale, shift):
    mean = jnp.mean(hidden, 0, keepdims=True)
    centered = hidden - mean
    variance = jnp.mean(centered * centered, 0, keepdims=True)
    inv_std = lax.rsqrt(variance + norm_eps)
    normed = centered * inv_std
    return (normed * scale + shift, normed, inv_std)


def norm_columns_back(grad_in, normed, inv_std, scale):
    grad_normed = grad_in * scale
    mean_one = jnp.mean(grad_normed, 0, keepdims=True)
    mean_two = jnp.mean(grad_normed * normed, 0, keepdims=True)
    return inv_std * (grad_normed - mean_one - normed * mean_two)


def local_call(body, outs, name, *operands, scratch=(), space=None):
    shapes = [jax.ShapeDtypeStruct(shape, kind) for shape, kind in outs]
    return pl.pallas_call(
        body,
        out_shape=shapes,
        in_specs=[
            pl.BlockSpec(
                memory_space=pltpu.SMEM
                if operand.dtype == jnp.int32
                else space or pltpu.VMEM
            )
            for operand in operands
        ],
        out_specs=[pl.BlockSpec(memory_space=pltpu.VMEM)] * len(outs),
        scratch_shapes=[
            pltpu.VMEM(*kind) if isinstance(kind, tuple) else kind for kind in scratch
        ],
        compiler_params=pltpu.CompilerParams(vmem_limit_bytes=24 * 2**20),
        name=name,
    )(*operands)


CORE, COPY, ROW, COL, SEQ = range(5)


def low_outs(count, *shape):
    return [(shape, low)] * count


def turn_body(flags_ref, lengths_ref, trig_ref, reweight_ref, *, seq_len):
    start = flags_ref[ROW] * SPAN
    positions = start + lax.broadcasted_iota(jnp.int32, (8, SPAN), 1)
    lines = lax.broadcasted_iota(jnp.int32, (8, SPAN), 0)
    angles = math.pi * positions.astype(wide) / (2.0 * seq_len)
    turns = jnp.where(lines == 0, jnp.cos(angles), jnp.where(lines == 1, jnp.sin(angles), 0.0))
    own = lengths_ref[flags_ref[SEQ]]
    other = lengths_ref[flags_ref[SEQ] + 1 - 2 * flags_ref[CORE]]
    limits = jnp.where(lines == 2, own, other)
    present = jnp.where(positions < limits, 1.0, 0.0)
    trig_ref[...] = turns + jnp.where(lines == 2, present, jnp.where(lines == 3, present, 0.0))
    rows = lax.broadcasted_iota(jnp.int32, (SPAN, SPAN), 0)
    cols = lax.broadcasted_iota(jnp.int32, (SPAN, SPAN), 1)
    both = lax.dot_general(
        turns, turns, (((0,), (0,)), ((), ())), precision=highest, preferred_element_type=wide
    )
    reweight_ref[...] = jnp.where(rows <= cols, both, 0.0)


def token_piece(flags_ref, own_ref, recv_ref, step, rows):
    place = lax.rem(flags_ref[ROW] + step, rows)
    half = lax.div(place, rows // 2)
    cols = pl.ds(pl.multiple_of(lax.rem(place, rows // 2) * SPAN, SPAN), SPAN)
    return jnp.where(half == flags_ref[COL], own_ref[:, cols], recv_ref[:, cols])


def pieces_body(flags_ref, own_ref, cot_ref, recv_ref, *refs, rows):
    vec_ref, piece_refs = refs[0], refs[1:]
    part = own_ref.shape[0]
    lines = []
    for line in range(4):
        vec = vec_ref[line : line + 1, :]
        vec = jnp.concatenate([vec, jnp.zeros((1, SPAN - vec.shape[1]), wide)], 1)
        high = vec.astype(low).astype(wide)
        lines = lines + [high, vec - high]
    for step, ref in enumerate(piece_refs):
        ref[:part] = token_piece(flags_ref, own_ref, recv_ref.at[:part], step, rows)
        ref[part : 2 * part] = token_piece(flags_ref, cot_ref, recv_ref.at[part:], step, rows)
        ref[2 * part :] = jnp.concatenate(lines + [jnp.zeros((8, SPAN), wide)], 0).astype(low)


def came_from(flags_ref, step, rows):
    return lax.rem(flags_ref[ROW] + rows - step, rows)


def place_tokens_body(flags_ref, *refs, rows, part):
    pieces, (half_ref, vec_ref) = refs[:rows], refs[rows:]
    below = half_ref.shape[0] // 2
    for step, ref in enumerate(pieces):
        row = came_from(flags_ref, step, rows)
        half_ref[pl.ds(pl.multiple_of(row * part, 16), part), :] = ref[:part]
        half_ref[pl.ds(pl.multiple_of(below + row * part, 16), part), :] = ref[part : 2 * part]
        extra = ref[2 * part :].astype(wide)
        sums = [extra[2 * i : 2 * i + 1] + extra[2 * i + 1 : 2 * i + 2] for i in range(4)]
        columns = jnp.concatenate(sums + [jnp.zeros((4, SPAN), wide)], 0).T
        vec_ref[pl.ds(pl.multiple_of(row * 2 * part, 8), 2 * part), :] = columns[: 2 * part]


def join_halves_body(flags_ref, half_ref, recv_ref, x_ref, cot_ref, *, rows):
    part = half_ref.shape[0] // (2 * rows)
    first_col = flags_ref[COL] == 0
    for place, full_ref in enumerate((x_ref, cot_ref)):
        for row in range(rows):
            source = (place * rows + row) * part
            own = half_ref[source : source + part]
            other = recv_ref[source : source + part]
            start = 2 * row * part
            full_ref[start : start + part] = jnp.where(first_col, own, other)
            full_ref[start + part : start + 2 * part] = jnp.where(first_col, other, own)


def add_body(own_ref, recv_ref, half_ref):
    half_ref[...] = (own_ref[...] + recv_ref[...].astype(wide)).astype(low)


def feature_piece(flags_ref, source, step, rows):
    part = source.shape[0] // (2 * rows)
    start = (lax.rem(flags_ref[ROW] + step, rows) * 2 + flags_ref[COL]) * part
    return source[pl.ds(pl.multiple_of(start, 16), part), :]


def place_back(flags_ref, pieces, rows, own_ref, other_ref):
    half = len(pieces) // 2
    for row, piece in zip(rows, pieces):
        cols = pl.ds(pl.multiple_of(lax.rem(row, half) * SPAN, SPAN), SPAN)
        mine = lax.div(row, half) == flags_ref[COL]

        @pl.when(mine)
        def _(piece=piece, cols=cols):
            own_ref[:, cols] = piece[...]

        @pl.when(jnp.logical_not(mine))
        def _(piece=piece, cols=cols):
            other_ref[:, cols] = piece[...]


def sum_of(refs):
    total = refs[0][...].astype(wide)
    for ref in refs[1:]:
        total = total + ref[...].astype(wide)
    return total


def join_back_body(flags_ref, own_ref, recv_ref, out_ref):
    part = own_ref.shape[0]
    first_col = flags_ref[COL] == 0
    out_ref[:part] = jnp.where(first_col, own_ref[...], recv_ref[...]).astype(out_ref.dtype)
    out_ref[part:] = jnp.where(first_col, recv_ref[...], own_ref[...]).astype(out_ref.dtype)


def input_halves_body(flags_ref, own_ref, recv_ref, half_ref, sent_ref, sum_ref, *, rows):
    part = own_ref.shape[0] // (2 * rows)
    sum_ref[...] = own_ref[...] + recv_ref[...].astype(wide)
    for row in range(rows):
        rows_out = slice(row * part, (row + 1) * part)
        mine = pl.multiple_of((2 * row + flags_ref[COL]) * part, 16)
        theirs = pl.multiple_of((2 * row + 1 - flags_ref[COL]) * part, 16)
        half_ref[rows_out] = sum_ref[pl.ds(mine, part), :]
        sent_ref[rows_out] = sum_ref[pl.ds(theirs, part), :].astype(low)


def last_pieces_body(
    flags_ref, kept_ref, got_ref, half_ref, recv_ref, hidden_ref, held_ref, sent_ref
):
    rows = kept_ref.shape[0]
    part = half_ref.shape[0] // rows
    lanes = kept_ref.shape[2]
    for mask in range(rows):
        ref = sent_ref if mask % 2 else held_ref
        out = slice(mask // 2 * part, (mask // 2 + 1) * part)
        place = partner(flags_ref[ROW], mask)
        ref[out, :lanes] = (kept_ref[place].astype(wide) + got_ref[place].astype(wide)).astype(low)
        rows_in = pl.ds(pl.multiple_of(place * part, 16), part)
        total = half_ref[rows_in, :] + recv_ref[rows_in, :].astype(wide)
        start = pl.multiple_of((place * 2 + flags_ref[COL]) * part, 16)
        ref[out, lanes:] = (total + hidden_ref[pl.ds(start, part), :]).astype(low)


def last_pairs_body(held_ref, got_ref, sum_ref, sent_ref):
    part, lanes = sum_ref.shape
    sum_ref[...] = held_ref[:part, :lanes].astype(wide) + got_ref[:part, :lanes].astype(wide)
    pair = held_ref[part:, :lanes].astype(wide) + got_ref[part:, :lanes].astype(wide)
    sent_ref[:, :lanes] = pair.astype(low)
    sent_ref[:, lanes : lanes + SPAN] = held_ref[part:, lanes:]
    sent_ref[:, lanes + SPAN :] = got_ref[part:, lanes:]


def last_sums_body(
    flags_ref, part_ref, held_ref, got_ref, far_ref, sum_ref, own_ref, other_ref
):
    part, lanes = part_ref.shape
    sum_ref[...] = (part_ref[...] + far_ref[:, :lanes].astype(wide)).astype(low)
    pieces = (
        held_ref.at[:part, lanes:],
        got_ref.at[:part, lanes:],
        far_ref.at[:, lanes : lanes + SPAN],
        far_ref.at[:, lanes + SPAN :],
    )
    rows = [partner(flags_ref[ROW], mask) for mask in range(4)]
    place_back(flags_ref, pieces, rows, own_ref, other_ref)


def down_grad_body(
    flags_ref, own_ref, other_ref, mine_ref, copy_ref, held_ref, sent_ref, grad_ref
):
    feats, part = held_ref.shape[0] // 2, mine_ref.shape[0]
    for act_ref, cols in ((mine_ref, slice(0, part)), (copy_ref, slice(part, 2 * part))):
        grad_ref[:, cols] = (
            dot_nt(own_ref[...], act_ref[:, :SPAN]) + dot_nt(other_ref[...], act_ref[:, SPAN:])
        ).astype(low)
    for mask in range(4):
        ref = sent_ref if mask % 2 else held_ref
        start = mask // 2 * feats
        place = partner(flags_ref[ROW], mask)
        rows_in = pl.ds(pl.multiple_of(place * feats, 16), feats)
        ref[start : start + feats, :] = grad_ref[rows_in, :]


def down_pairs_body(held_ref, got_ref, kept_ref, sent_ref):
    part = kept_ref.shape[1]
    kept_ref[...] = held_ref[:, :part].astype(wide) + got_ref[:, :part].astype(wide)
    sent_ref[...] = (held_ref[:, part:].astype(wide) + got_ref[:, part:].astype(wide)).astype(low)


def mix_body(
    flags_ref, own_ref, other_ref, attn_wide_ref, vec_ref, pair_ref, kept_ref, sent_ref, grad_ref
):
    grad_ref[:, :WIDTH] = (
        dot_nt(own_ref[...], attn_wide_ref[:WIDTH, :].astype(low))
        + dot_nt(other_ref[...], attn_wide_ref[WIDTH : 2 * WIDTH, :].astype(low))
    ).astype(low)
    grad_ref[:, WIDTH:] = vec_ref[:, :SUM_LANES]
    first_copy = flags_ref[COPY] == 0
    half = (WIDTH + SUM_LANES) // 2
    kept_ref[...] = jnp.where(first_copy, grad_ref[:, :half], grad_ref[:, half:])
    sent = jnp.where(first_copy, grad_ref[:, half:], grad_ref[:, :half])
    lines, part = pair_ref.shape
    sent_ref[:, :part] = pair_ref[...]
    sent_ref[:, part : part + half] = sent[:lines]
    sent_ref[:, part + half :] = sent[lines:]


def down_far_body(kept_ref, got_ref, sum_ref, sent_ref):
    feats, part = sum_ref.shape
    sum_ref[...] = kept_ref[:feats] + got_ref[:feats, :part].astype(wide)
    sent_ref[...] = (kept_ref[feats:] + got_ref[feats:, :part].astype(wide)).astype(low)


def up_pieces_body(
    flags_ref, result_ref, kept_ref, got_ref, mix_ref, mix_got_ref, held_ref, sent_ref, sum_ref
):
    feats, part = kept_ref.shape[0] // 4, kept_ref.shape[1]
    half, lanes = feats // 2, SPAN // 2
    lines, cols = mix_got_ref.shape[0], mix_ref.shape[1]
    sum_ref[:lines] = (
        mix_ref[:lines].astype(wide) + mix_got_ref[:, part : part + cols].astype(wide)
    ).astype(low)
    sum_ref[lines:] = (
        mix_ref[lines:].astype(wide) + mix_got_ref[:, part + cols :].astype(wide)
    ).astype(low)
    for mask in range(4):
        ref = sent_ref if mask % 2 else held_ref
        start = mask // 2 * feats
        out = slice(start, start + feats)
        place = partner(flags_ref[ROW], mask)
        rows_in = pl.ds(pl.multiple_of((place * 2 + flags_ref[COL]) * half, 16), half)
        ref[start : start + half, :lanes] = result_ref[rows_in, :lanes]
        ref[start + half : start + feats, :lanes] = result_ref[rows_in, lanes:]
        rows_in = pl.ds(pl.multiple_of(place * feats, 16), feats)
        ref[out, lanes : lanes + part] = (
            kept_ref[rows_in, :].astype(wide) + got_ref[rows_in, :].astype(wide)
        ).astype(low)
        ref[out, lanes + part :] = sum_ref[rows_in, :]


def up_pairs_body(held_ref, got_ref, sum_ref, sent_ref):
    feats, total = held_ref.shape[0] // 2, held_ref.shape[1]
    lanes = SPAN // 2
    sum_ref[...] = held_ref[:feats, lanes:].astype(wide) + got_ref[:feats, lanes:].astype(wide)
    pair = held_ref[feats:, lanes:].astype(wide) + got_ref[feats:, lanes:].astype(wide)
    sent_ref[:, :lanes] = held_ref[feats:, :lanes]
    sent_ref[:, lanes:total] = pair.astype(low)
    sent_ref[:, total:] = got_ref[feats:, :lanes]


def hidden_sums_body(
    flags_ref,
    down_ref,
    down_far_ref,
    up_ref,
    held_ref,
    got_ref,
    far_ref,
    sum_ref,
    own_ref,
    other_ref,
    piece_ref,
):
    feats, part = down_ref.shape
    lanes = SPAN // 2
    total = lanes + up_ref.shape[1]
    sum_ref[:, :part] = (down_ref[...] + down_far_ref[...].astype(wide)).astype(low)
    sum_ref[:, part:] = (up_ref[...] + far_ref[:, lanes:total].astype(wide)).astype(low)
    pieces = (
        held_ref[:feats, :lanes],
        got_ref[:feats, :lanes],
        far_ref[:, :lanes],
        far_ref[:, total:],
    )
    for place, piece in enumerate(pieces):
        piece_ref[place, :, :lanes] = piece[: feats // 2]
        piece_ref[place, :, lanes:] = piece[feats // 2 :]
    rows = [partner(flags_ref[ROW], mask) for mask in range(4)]
    place_back(flags_ref, [piece_ref.at[i] for i in range(4)], rows, own_ref, other_ref)


def head_sets():
    return [(seq, head, seq * HEADS + head) for seq in range(2) for head in range(HEADS)]


def set_row(place):
    ids = lax.broadcasted_iota(jnp.int32, (SUM_ROWS, SPAN), 0)
    return (ids == place).astype(wide)


def turned(parts, trig_ref):
    part_wide = parts.astype(wide)
    return jnp.concatenate(
        [(part_wide * trig_ref[0:1, :]).astype(low), (part_wide * trig_ref[1:2, :]).astype(low)], 0
    )


def unturned(pair, trig_ref):
    return pair[:HD] * trig_ref[0:1, :] + pair[HD:] * trig_ref[1:2, :]


def query_part(qkv_ref, seq, head):
    return qkv_ref[seq, head * HD : (head + 1) * HD, :]


def key_part(qkv_ref, seq, head):
    return qkv_ref[seq, WIDTH + head * HD : WIDTH + (head + 1) * HD, :]


def value_part(qkv_ref, seq, head):
    return qkv_ref[seq, 2 * WIDTH + head * HD : 2 * WIDTH + (head + 1) * HD, :]


def kept_keys(qkv_ref, trig_ref, seq, head):
    keys = jnp.maximum(key_part(qkv_ref, seq, head), 0)
    return (keys.astype(wide) * trig_ref[2 + seq : 3 + seq, :]).astype(low)


def state_slice(state, place):
    return state[place * HD : (place + 1) * HD]


def pack_hidden_body(flags_ref, up_ref, down_ref, mine_ref, copy_ref, sems):
    part = mine_ref.shape[1] // 2
    copies = []
    for half, packed_ref in enumerate((mine_ref, copy_ref)):
        copy = 1 - flags_ref[COPY] if half else flags_ref[COPY]
        start = pl.multiple_of((flags_ref[CORE] * 2 + copy) * part, 128)
        for place, ref in enumerate((up_ref, down_ref)):
            copies.append(
                pltpu.make_async_copy(
                    ref.at[:, pl.ds(start, part)],
                    packed_ref.at[:, pl.ds(place * part, part)],
                    sems.at[2 * half + place],
                )
            )
    for copy in copies:
        copy.start()
    for copy in copies:
        copy.wait()


def partner(row, mask):
    if mask == 0:
        return row
    if mask == 1:
        return row + 1 - 2 * lax.rem(row, 2)
    return lax.rem(row + 2, 4) if mask == 2 else 3 - row


def row_block(flags_ref, mask, feats):
    return pl.ds(pl.multiple_of(partner(flags_ref[ROW], mask) * feats, 16), feats)


def project_body(flags_ref, own_ref, other_ref, trig_ref, packed_ref, *refs):
    weight_ref, qkv_ref, state_ref = refs[-3:]
    blocks = refs[:-3]
    count = len(blocks) // 2
    first_copy = flags_ref[COPY] == 0
    feats = packed_ref.shape[0]
    part = packed_ref.shape[1] // 2

    def rows_of(mask):
        return row_block(flags_ref, mask, feats)

    weight_ref[rows_of(0), :] = packed_ref[...]
    for step in range(1, count + 1):
        mine, copied = blocks[step - 1][...], blocks[count + step - 1][...]
        weight_ref[rows_of(step), :part] = jnp.where(first_copy, mine, copied)
        weight_ref[rows_of(step), part:] = jnp.where(first_copy, copied, mine)
    matrix = weight_ref[:, : 3 * WIDTH]
    for seq, x_ref in enumerate((own_ref, other_ref)):
        qkv_ref[seq] = dot_tn(matrix, x_ref[...]).astype(low)
    sums = jnp.zeros((SUM_ROWS, 2 * HD), wide)
    for seq, head, place in head_sets():
        turned_keys = turned(kept_keys(qkv_ref, trig_ref, seq, head), trig_ref)
        values = value_part(qkv_ref, seq, head)
        state_ref[place * HD : (place + 1) * HD, :] = dot_nt(values, turned_keys).astype(low)
        sums = sums + dot_nt(set_row(place).astype(low), turned_keys)
    state_ref[STATE_ROWS:, :] = sums.astype(low)


def block_body(qkv_ref, trig_ref, reweight_ref, weights_ref, numer_ref, denom_ref):
    denoms = jnp.zeros((SUM_ROWS, SPAN), wide)
    for seq, head, place in head_sets():
        queries = jnp.maximum(query_part(qkv_ref, seq, head), 0)
        keys = kept_keys(qkv_ref, trig_ref, seq, head)
        weights = dot_tn(keys, queries) * reweight_ref[...]
        weights_low = weights.astype(low)
        weights_ref[place] = weights_low
        numer_ref[place] = dot_nn(value_part(qkv_ref, seq, head), weights_low)
        denoms = denoms + set_row(place) * jnp.sum(weights, 0, keepdims=True)
    denom_ref[...] = denoms


def attend_body(
    qkv_ref,
    trig_ref,
    numer_ref,
    denom_ref,
    weight_ref,
    *refs,
):
    arrived = refs[:-5]
    prior_ref, attn_wide_ref, own_ref, other_ref, attn_ref = refs[-5:]
    total = arrived[0][...].astype(wide)
    for ref in arrived[1:]:
        total = total + ref[...].astype(wide)
    prior_ref[...] = total.astype(low)
    matrix = weight_ref[:, 3 * WIDTH : 4 * WIDTH]
    prior_sums = prior_ref[STATE_ROWS:, :]
    inverses = jnp.zeros((SUM_ROWS, SPAN), wide)
    for seq, head, place in head_sets():
        queries = turned(jnp.maximum(query_part(qkv_ref, seq, head), 0), trig_ref)
        prior = prior_ref[place * HD : (place + 1) * HD, :]
        numer = numer_ref[place] + dot_nn(prior, queries)
        denoms = dot_nn(prior_sums, queries) + denom_ref[...]
        denom = 1.0 + jnp.sum(denoms * set_row(place), 0, keepdims=True)
        inverse = 1.0 / denom
        inverses = inverses + set_row(place) * inverse
        attended = numer * inverse
        attn_wide_ref[place * HD : (place + 1) * HD, :] = attended
        attn_ref[seq, head * HD : (head + 1) * HD, :] = attended.astype(low)
    attn_wide_ref[STATE_ROWS:, :] = inverses
    own_ref[...] = dot_nn(matrix, attn_ref[0])
    other_ref[...] = dot_nn(matrix, attn_ref[1]).astype(low)


def grad_attend_body(
    own_ref,
    other_ref,
    weight_ref,
    attn_wide_ref,
    qkv_ref,
    trig_ref,
    grad_num_ref,
    grad_den_ref,
    state_ref,
):
    matrix = weight_ref[:, 3 * WIDTH : 4 * WIDTH]
    sums = jnp.zeros((SUM_ROWS, 2 * HD), wide)
    dens = jnp.zeros((SUM_ROWS, SPAN), wide)
    for seq, grad_ref in enumerate((own_ref, other_ref)):
        grads = dot_tn(matrix, grad_ref[...]).astype(low).astype(wide)
        for head in range(HEADS):
            place = seq * HEADS + head
            inverse = jnp.sum(attn_wide_ref[STATE_ROWS:, :] * set_row(place), 0, keepdims=True)
            scaled = grads[head * HD : (head + 1) * HD] * inverse
            grad_num = scaled.astype(low)
            grad_num_ref[place] = grad_num
            grad_den = -jnp.sum(scaled * attn_wide_ref[place * HD : (place + 1) * HD, :], 0, keepdims=True)
            den_row = set_row(place) * grad_den
            dens = dens + den_row
            queries = turned(jnp.maximum(query_part(qkv_ref, seq, head), 0), trig_ref)
            state_ref[place * HD : (place + 1) * HD, :] = dot_nt(grad_num, queries).astype(low)
            sums = sums + dot_nt(den_row.astype(low), queries)
    state_ref[STATE_ROWS:, :] = sums.astype(low)
    grad_den_ref[...] = dens


def grad_block_body(
    grad_num_ref,
    grad_den_ref,
    qkv_ref,
    trig_ref,
    reweight_ref,
    weights_ref,
    prior_ref,
    grad_query_ref,
    grad_key_ref,
    grad_value_ref,
):
    prior_sums = prior_ref[STATE_ROWS:, :]
    for seq, head, place in head_sets():
        query = query_part(qkv_ref, seq, head)
        queries = jnp.maximum(query, 0)
        keys = kept_keys(qkv_ref, trig_ref, seq, head)
        grad_num = grad_num_ref[place]
        den_rows = grad_den_ref[...] * set_row(place)
        grad_den = jnp.sum(den_rows, 0, keepdims=True)
        grad_scores = (
            (dot_tn(value_part(qkv_ref, seq, head), grad_num) + grad_den) * reweight_ref[...]
        ).astype(low)
        prior = jnp.concatenate([prior_ref[place * HD : (place + 1) * HD, :], prior_sums], 0)
        grads = jnp.concatenate([grad_num, den_rows.astype(low)], 0)
        grad_query = dot_nn(keys, grad_scores) + unturned(dot_tn(prior, grads), trig_ref)
        grad_query_ref[seq, head * HD : (head + 1) * HD, :] = jnp.where(
            query.astype(wide) > 0, grad_query, 0.0
        ).astype(low)
        grad_key_ref[place] = dot_nt(queries, grad_scores)
        grad_value_ref[place] = dot_nt(grad_num, weights_ref[place])


def grad_project_body(
    grad_query_ref,
    grad_key_ref,
    grad_value_ref,
    qkv_ref,
    trig_ref,
    x_own_ref,
    x_other_ref,
    weight_ref,
    flags_ref,
    *refs,
):
    arrived = refs[:-6]
    kept_ref, sent_ref, own_ref, other_ref, after_ref, grad_ref = refs[-6:]
    total = arrived[0][...].astype(wide)
    for ref in arrived[1:]:
        total = total + ref[...].astype(wide)
    after_ref[...] = total.astype(low)
    after_sums = after_ref[STATE_ROWS:, :]
    for seq, head, place in head_sets():
        key = key_part(qkv_ref, seq, head)
        keys = turned(kept_keys(qkv_ref, trig_ref, seq, head), trig_ref)
        values = value_part(qkv_ref, seq, head)
        after = after_ref[place * HD : (place + 1) * HD, :]
        left = jnp.concatenate([after, after_sums], 0)
        right = jnp.concatenate([values, set_row(place).astype(low)], 0)
        grad_key = grad_key_ref[place] + unturned(dot_tn(left, right), trig_ref)
        grad_key = jnp.where(key.astype(wide) > 0, grad_key, 0.0) * trig_ref[2 + seq : 3 + seq, :]
        grad_value = grad_value_ref[place] + dot_nn(after, keys)
        rows = slice(head * HD, (head + 1) * HD)
        grad_ref[seq, rows, :] = grad_query_ref[seq, rows, :]
        rows = slice(WIDTH + head * HD, WIDTH + (head + 1) * HD)
        grad_ref[seq, rows, :] = grad_key.astype(low)
        rows = slice(2 * WIDTH + head * HD, 2 * WIDTH + (head + 1) * HD)
        grad_ref[seq, rows, :] = grad_value.astype(low)
    matrix = weight_ref[:, : 3 * WIDTH]
    grad_w = (
        dot_nt(x_own_ref[...], grad_ref[0]) + dot_nt(x_other_ref[...], grad_ref[1])
    ).astype(low)
    rows, part, _ = kept_ref.shape
    first_copy = flags_ref[COPY] == 0
    for row in range(rows):
        start = row * 2 * part
        first, second = grad_w[start : start + part], grad_w[start + part : start + 2 * part]
        kept_ref[row] = jnp.where(first_copy, first, second)
        sent_ref[row] = jnp.where(first_copy, second, first)
    own_ref[...] = dot_nn(matrix, grad_ref[0])
    other_ref[...] = dot_nn(matrix, grad_ref[1]).astype(low)


def norm_body(x_ref, half_ref, recv_ref, vec_ref, first_ref, low_ref, normed_ref):
    hidden = x_ref[...].astype(wide) + (half_ref[...].astype(wide) + recv_ref[...].astype(wide))
    first, normed, inv_std = norm_columns(hidden, vec_ref[:, 0:1], vec_ref[:, 1:2])
    first_ref[...] = first
    low_ref[...] = first.astype(low)
    normed_ref[:D, :] = normed
    normed_ref[D:, :] = jnp.broadcast_to(inv_std, (8, SPAN))


def lane_sums(columns, place):
    lanes = lax.broadcasted_iota(jnp.int32, (columns[0].shape[0], 2 * SUM_LANES), 1)
    total = jnp.zeros(lanes.shape, wide)
    for shift, column in enumerate(columns):
        total = jnp.where(lanes == place + shift, jnp.sum(column, 1, keepdims=True), total)
    return total


def second_norm_body(
    first_ref, half_ref, recv_ref, vec_ref, cot_ref, trig_ref, result_ref, grad_ref, low_ref
):
    hidden = first_ref[...] + (half_ref[...].astype(wide) + recv_ref[...].astype(wide))
    scale = vec_ref[:, 2:3]
    result, normed, inv_std = norm_columns(hidden, scale, vec_ref[:, 3:4])
    result_ref[...] = result.astype(low)
    grad_in = cot_ref[...].astype(wide) * trig_ref[2:3, :]
    grad = norm_columns_back(grad_in, normed, inv_std, scale)
    grad_ref[:, :SPAN] = grad
    low_ref[...] = grad.astype(low)
    grad_ref[:, SPAN:] = lane_sums((grad_in * normed, grad_in), 2)


def norm_back_body(
    grad_ref, half_ref, recv_ref, normed_ref, vec_ref, hidden_ref, low_ref, sum_ref
):
    grad_in = grad_ref[:, :SPAN] + (half_ref[...].astype(wide) + recv_ref[...].astype(wide))
    normed = normed_ref[:D, :]
    grad = norm_columns_back(grad_in, normed, normed_ref[D : D + 1, :], vec_ref[:, 0:1])
    hidden_ref[...] = grad
    low_ref[...] = grad.astype(low)
    sum_ref[...] = (lane_sums((grad_in * normed, grad_in), 0) + grad_ref[:, SPAN:]).astype(low)


def hidden_weights_body(flags_ref, *refs):
    blocks, outs = refs[:-2], refs[-2:]
    for half, weight_ref in enumerate(outs):
        for mask, ref in enumerate(blocks[4 * half : 4 * half + 4]):
            weight_ref[row_block(flags_ref, mask, ref.shape[0]), :] = ref[...]


def hidden_body(own_ref, other_ref, mine_ref, copy_ref, *refs):
    acts, slopes, parts = refs[:2], refs[2:4], refs[4:]
    part = acts[0].shape[0]
    for seq, (x_ref, part_ref) in enumerate(zip((own_ref, other_ref), parts)):
        cols = slice(seq * SPAN, (seq + 1) * SPAN)
        total = None
        for weight_ref, act_ref, slope_ref in zip((mine_ref, copy_ref), acts, slopes):
            act, slope = gelu_and_slope(dot_tn(weight_ref[:, :part], x_ref[...]))
            act_ref[:, cols] = act
            slope_ref[:, cols] = slope
            term = dot_nn(weight_ref[:, part:], act)
            total = term if total is None else total + term
        part_ref[...] = total.astype(part_ref.dtype)


def hidden_back_body(
    own_ref,
    other_ref,
    mine_ref,
    copy_ref,
    slope_mine_ref,
    slope_copy_ref,
    pre_mine_ref,
    pre_copy_ref,
    part_own_ref,
    part_other_ref,
):
    part = slope_mine_ref.shape[0]
    for seq, (x_ref, part_ref) in enumerate(
        ((own_ref, part_own_ref), (other_ref, part_other_ref))
    ):
        cols = slice(seq * SPAN, (seq + 1) * SPAN)
        total = None
        for weight_ref, slope_ref, pre_ref in (
            (mine_ref, slope_mine_ref, pre_mine_ref),
            (copy_ref, slope_copy_ref, pre_copy_ref),
        ):
            grad_pre = (dot_tn(weight_ref[:, part:], x_ref[...]) * slope_ref[:, cols]).astype(low)
            pre_ref[:, cols] = grad_pre
            term = dot_nn(weight_ref[:, :part], grad_pre)
            total = term if total is None else total + term
        part_ref[...] = total.astype(part_ref.dtype)


def half_grads_body(own_ref, other_ref, mine_ref, copy_ref, kept_ref, sent_ref):
    for pre_ref, out_ref in ((copy_ref, sent_ref), (mine_ref, kept_ref)):
        out_ref[...] = (
            dot_nt(own_ref[...], pre_ref[:, :SPAN]) + dot_nt(other_ref[...], pre_ref[:, SPAN:])
        ).astype(low)


def quarters(flags_ref, refs):
    core, copy = flags_ref[CORE], flags_ref[COPY]
    for ref, other_core, other_copy in zip(refs, (0, 0, 1, 1), (0, 1, 0, 1)):
        core_place = 1 - core if other_core else core
        copy_place = 1 - copy if other_copy else copy
        yield core_place * 2 + copy_place, ref


def place_hidden_body(flags_ref, *refs):
    down_ref, up_ref, out_ref, vec_ref = refs[4:]
    part = up_ref.shape[1] // 4
    for place, ref in quarters(flags_ref, refs[:4]):
        cols = pl.ds(pl.multiple_of(place * part, 128), part)
        down_ref[:, cols] = ref[:, :part].astype(wide)
        up_ref[:, cols] = ref[:, part : 2 * part].astype(wide)
    half = (WIDTH + SUM_LANES) // 2
    first_core, first_copy = flags_ref[CORE] == 0, flags_ref[COPY] == 0
    sums = []
    for own_ref, copy_ref in (refs[:2], refs[2:4]):
        own, copied = own_ref[:, 2 * part :].astype(wide), copy_ref[:, 2 * part :].astype(wide)
        sums.append((jnp.where(first_copy, own, copied), jnp.where(first_copy, copied, own)))
    first = [jnp.where(first_core, sums[0][i], sums[1][i]) for i in (0, 1)]
    second = [jnp.where(first_core, sums[1][i], sums[0][i]) for i in (0, 1)]
    for parts, start in ((first, 0), (second, WIDTH)):
        out_ref[:, start : start + half] = parts[0]
        out_ref[:, start + half : start + WIDTH] = parts[1][:, : WIDTH - half]
    vec_ref[...] = first[1][:, WIDTH - half :] + second[1][:, WIDTH - half :]


def place_last_body(flags_ref, *refs):
    join_back_body(flags_ref, refs[4], refs[5], refs[6])
    outs = refs[7:]
    first_core = flags_ref[CORE] == 0
    part = refs[0].shape[0]
    for own_ref, other_ref, other_copy in ((refs[0], refs[2], 0), (refs[1], refs[3], 1)):
        copy = 1 - flags_ref[COPY] if other_copy else flags_ref[COPY]
        rows = pl.ds(pl.multiple_of(copy * part, 8), part)
        own, other = own_ref[...].astype(wide), other_ref[...].astype(wide)
        for place, out_ref in enumerate(outs):
            cols = slice(place * WIDTH, (place + 1) * WIDTH)
            out_ref[rows, :WIDTH] = jnp.where(first_core, own[:, cols], other[:, cols])
            out_ref[rows, WIDTH:] = jnp.where(first_core, other[:, cols], own[:, cols])


def gelu_and_slope(pre):
    cdf = 0.5 * (1.0 + lax.erf(pre * math.sqrt(0.5)))
    density = jnp.exp(-0.5 * pre * pre) * (1.0 / math.sqrt(2.0 * math.pi))
    return (pre * cdf).astype(low), (cdf + pre * density)


def all_quarters(own, direct=False):
    copied = swap_copies(own)
    if direct:
        pairs = [(i, i ^ 3) for i in range(lax.axis_size("dp"))]
        return own, copied, swap_pair(own), lax.ppermute(own, "dp", pairs)
    return own, copied, swap_pair(own), swap_pair(copied)


def on_device_paired(
    tokens,
    lengths,
    w_query,
    w_key,
    w_value,
    w_out,
    gain_one,
    bias_one,
    w_up,
    w_down,
    gain_two,
    bias_two,
    cotangent,
):
    rows = lax.axis_size("row")
    seq_len = SPAN * rows
    dp_idx = lax.axis_index("dp")
    feat_rows = tokens.shape[0]
    half_feats = feat_rows // 2
    flags = jnp.stack(
        [dp_idx % 2, dp_idx // 2, lax.axis_index("row"), lax.axis_index("col"), dp_idx]
    )
    trig, reweight = local_call(
        partial(turn_body, seq_len=seq_len),
        [((8, SPAN), wide), ((SPAN, SPAN), wide)],
        "turn",
        flags,
        lengths,
    )

    def passed_on(pieces):
        return [pieces[0]] + [
            rotate_rows(piece, step) for step, piece in enumerate(pieces) if step
        ]

    def cols_back(own, other, kind, name):
        return local_call(
            join_back_body,
            [((feat_rows, SPAN * rows // 2), kind)],
            name,
            flags,
            own,
            swap_cols(other),
        )[0]

    def column_parts(own_part, other_part, name):
        (half,) = local_call(add_body, low_outs(1, D, SPAN), name, own_part, swap_pair(other_part))
        return half, swap_cols(half)

    first_col = lax.axis_index("col") == 0

    def halved(block):
        top, bottom = block[:half_feats], block[half_feats:]
        return jnp.where(first_col, top, bottom), jnp.where(first_col, bottom, top)

    (token_own, token_sent), (cot_own, cot_sent) = halved(tokens), halved(cotangent)
    got = swap_cols(jnp.concatenate([token_sent, cot_sent], 0))

    part = w_up.shape[1] // 4
    first_core = dp_idx % 2 == 0

    def core_part(operand):
        return jnp.where(first_core, operand[:, :WIDTH], operand[:, WIDTH:])

    parts = [core_part(operand) for operand in (w_query, w_key, w_value, w_out.T)]
    first_packed = jnp.concatenate(parts, 1)
    first_mine = jnp.where(
        dp_idx < 2, jnp.concatenate(parts[:2], 1), jnp.concatenate(parts[2:], 1)
    )

    def row_blocks(block):
        return swap_rows(block, 1), swap_rows(block, 2)

    first_one, first_two = row_blocks(first_mine)
    first_one, got = lax.optimization_barrier((first_one, got))
    hidden_packed = local_call(
        pack_hidden_body,
        low_outs(2, feat_rows, 2 * part),
        "pack_hidden",
        flags,
        w_up,
        w_down.T,
        scratch=[pltpu.SemaphoreType.DMA((4,))],
        space=pltpu.HBM,
    )
    vecs = jnp.stack([gain_one, bias_one, gain_two, bias_two], 0)
    token_pieces = local_call(
        partial(pieces_body, rows=rows),
        low_outs(rows, feat_rows + 16, SPAN),
        "token_pieces",
        flags,
        token_own,
        cot_own,
        got,
        vecs,
    )
    def after(value, *others):
        return lax.optimization_barrier((value, others))[0]

    first_three = swap_rows(after(first_two, token_pieces[0]), 1)
    first_copies = [
        swap_copies(after(first_one, token_pieces[0])),
        swap_copies(first_two),
        swap_copies(first_three),
    ]
    token_pieces = passed_on(token_pieces)
    token_pieces, first_three, first_copies[0] = lax.optimization_barrier(
        (token_pieces, first_three, first_copies[0])
    )
    first_blocks = [first_one, first_two, first_three, *first_copies]
    x_half, norm_vecs = local_call(
        partial(place_tokens_body, rows=rows, part=half_feats),
        low_outs(1, D, SPAN) + [((D, 8), wide)],
        "token_place",
        flags,
        *token_pieces,
    )
    x_half, trig, reweight = lax.optimization_barrier((x_half, trig, reweight))
    hidden_one, hidden_two = row_blocks(hidden_packed[0])
    x_got, hidden_one = lax.optimization_barrier((swap_cols(x_half), hidden_one))
    x_own, cot = local_call(
        partial(join_halves_body, rows=rows),
        low_outs(2, D, SPAN),
        "token_join",
        flags,
        x_half,
        x_got,
    )
    x_own, first_blocks = lax.optimization_barrier((x_own, first_blocks))
    x_other = swap_pair(x_own)
    state_shape = ((STATE_ROWS + SUM_ROWS, 2 * HD), low)
    sets = 2 * HEADS
    block_low = ((D, SPAN), low)
    block_wide = ((D, SPAN), wide)
    weight, qkv, state = local_call(
        project_body,
        [((D, 4 * WIDTH), low), ((2, 3 * WIDTH, SPAN), low), state_shape],
        "project",
        flags,
        x_own,
        x_other,
        trig,
        first_packed,
        *first_blocks,
    )
    hidden_three = swap_rows(hidden_two, 1)
    copy_two = swap_copies(hidden_two)
    arrived = [shift_rows(state, step) for step in range(1, rows)]
    arrived, hidden_three, copy_two = lax.optimization_barrier(
        (arrived, hidden_three, copy_two)
    )
    weights, numer, denom = local_call(
        block_body,
        [((sets, SPAN, SPAN), low), ((sets, HD, SPAN), wide), ((SUM_ROWS, SPAN), wide)],
        "block",
        qkv,
        trig,
        reweight,
    )
    prior, attn_wide, branch_own, branch_other = local_call(
        attend_body,
        [
            state_shape,
            ((STATE_ROWS + SUM_ROWS, SPAN), wide),
            block_wide,
            block_low,
        ],
        "attend",
        qkv,
        trig,
        numer,
        denom,
        weight,
        *arrived,
        scratch=[((2, WIDTH, SPAN), low)],
    )
    copy_one = swap_copies(hidden_one)
    branch_own, branch_other, copy_one = lax.optimization_barrier(
        (branch_own, branch_other, copy_one)
    )
    branch = column_parts(branch_own, branch_other, "branch_half")
    copy_three = swap_copies(hidden_three)
    branch, copy_three = lax.optimization_barrier((branch, copy_three))
    hidden_mine, hidden_copy = local_call(
        hidden_weights_body,
        low_outs(2, D, 2 * part),
        "hidden_weights",
        flags,
        hidden_packed[0],
        hidden_one,
        hidden_two,
        hidden_three,
        hidden_packed[1],
        copy_one,
        copy_two,
        copy_three,
    )
    branch, hidden_mine = lax.optimization_barrier((branch, hidden_mine))
    first, first_low, normed = local_call(
        norm_body,
        [block_wide, block_low, ((D + 8, SPAN), wide)],
        "norm",
        x_own,
        *branch,
        norm_vecs,
    )
    first_other = swap_pair(first_low)
    hidden_acts = [((part, 2 * SPAN), low)] * 2 + [((part, 2 * SPAN), wide)] * 2
    act_mine, act_copy, slope_mine, slope_copy, ffn_own, ffn_other = local_call(
        hidden_body,
        hidden_acts + [block_wide, block_low],
        "hidden",
        first_low,
        first_other,
        hidden_mine,
        hidden_copy,
    )
    ffn = column_parts(ffn_own, ffn_other, "ffn_half")
    result, grad_second, grad_ffn = local_call(
        second_norm_body,
        [block_low, ((D, SPAN + 2 * SUM_LANES), wide), block_low],
        "second_norm",
        first,
        *ffn,
        norm_vecs,
        cot,
        trig,
    )
    grad_ffn_other = swap_pair(grad_ffn)
    pair_low = ((D, part), low)
    down_held, down_sent = local_call(
        down_grad_body,
        low_outs(2, 2 * feat_rows, 2 * part),
        "down_grad",
        flags,
        grad_ffn,
        grad_ffn_other,
        act_mine,
        act_copy,
        scratch=[((D, 2 * part), low)],
    )
    down_got = swap_rows(down_sent, 1)
    grad_ffn, grad_ffn_other, down_held = lax.optimization_barrier(
        (grad_ffn, grad_ffn_other, down_held)
    )
    hidden_low = ((part, 2 * SPAN), low)
    pre_mine, pre_copy, first_own_part, first_other_part = local_call(
        hidden_back_body,
        [hidden_low, hidden_low, block_wide, block_low],
        "hidden_back",
        grad_ffn,
        grad_ffn_other,
        hidden_mine,
        hidden_copy,
        slope_mine,
        slope_copy,
    )
    first_sum = column_parts(first_own_part, first_other_part, "first_half")

    kept_up, sent_up = local_call(
        half_grads_body,
        [pair_low, pair_low],
        "up_grad",
        first_low,
        first_other,
        pre_mine,
        pre_copy,
    )
    got_up = swap_copies(sent_up)
    down_kept, down_pair = local_call(
        down_pairs_body,
        [((2 * feat_rows, part), wide), ((2 * feat_rows, part), low)],
        "down_pairs",
        down_held,
        down_got,
    )
    first_sum, kept_up, down_kept = lax.optimization_barrier((first_sum, kept_up, down_kept))
    grad_hidden, branch_grad, vec_sums = local_call(
        norm_back_body,
        [block_wide, block_low, ((D, 2 * SUM_LANES), low)],
        "norm_back",
        grad_second,
        *first_sum,
        normed,
        norm_vecs,
    )
    branch_grad_other = swap_pair(branch_grad)
    grad_num, grad_den, grad_state = local_call(
        grad_attend_body,
        [((sets, HD, SPAN), low), ((SUM_ROWS, SPAN), wide), state_shape],
        "grad_attend",
        branch_grad,
        branch_grad_other,
        weight,
        attn_wide,
        qkv,
        trig,
    )
    later = [shift_rows(grad_state, -step) for step in range(1, rows)]
    half_lanes = (WIDTH + SUM_LANES) // 2
    mix_kept, mix_sent = local_call(
        mix_body,
        [((D, half_lanes), low), ((2 * feat_rows, part + 2 * half_lanes), low)],
        "mix",
        flags,
        branch_grad,
        branch_grad_other,
        attn_wide,
        vec_sums,
        after(down_pair, grad_num),
        scratch=[((D, WIDTH + SUM_LANES), low)],
    )
    grad_query, grad_key, grad_value = local_call(
        grad_block_body,
        [
            ((2, WIDTH, SPAN), low),
            ((sets, HD, SPAN), wide),
            ((sets, HD, SPAN), wide),
        ],
        "grad_block",
        grad_num,
        grad_den,
        qkv,
        trig,
        reweight,
        weights,
        prior,
    )
    mix_got = swap_copies(after(mix_sent, got_up, grad_den))
    up_lanes = SPAN // 2 + part + half_lanes
    down_part, down_far = local_call(
        down_far_body,
        [((feat_rows, part), wide), ((feat_rows, part), low)],
        "down_far",
        down_kept,
        mix_got,
    )
    down_far = swap_rows(down_far, 2)
    up_held, up_sent = local_call(
        up_pieces_body,
        low_outs(2, 2 * feat_rows, up_lanes),
        "up_pieces",
        flags,
        result,
        kept_up,
        after(got_up, grad_query),
        mix_kept,
        mix_got,
        scratch=[((D, half_lanes), low)],
    )
    up_got = swap_rows(up_sent, 1)
    later, up_held = lax.optimization_barrier((later, up_held))
    half_rows = ((rows, half_feats, 3 * WIDTH), low)
    kept_w, sent_w, x_grad_own, x_grad_other = local_call(
        grad_project_body,
        [half_rows, half_rows, block_wide, block_low],
        "grad_project",
        grad_query,
        grad_key,
        grad_value,
        qkv,
        trig,
        x_own,
        x_other,
        weight,
        flags,
        *later,
        scratch=[state_shape, ((2, 3 * WIDTH, SPAN), low)],
    )
    got_w = swap_copies(sent_w)
    got_w = after(got_w, down_part)
    got_x = swap_pair(x_grad_other)
    x_half_grad, x_half_sent = local_call(
        partial(input_halves_body, rows=rows),
        [((D // 2, SPAN), wide), ((D // 2, SPAN), low)],
        "input_halves",
        flags,
        x_grad_own,
        got_x,
        scratch=[block_wide],
    )
    got_half = swap_cols(x_half_sent)
    last_lanes = 3 * WIDTH
    last_held, last_sent = local_call(
        last_pieces_body,
        low_outs(2, 2 * half_feats, last_lanes + SPAN),
        "last_pieces",
        flags,
        kept_w,
        got_w,
        x_half_grad,
        got_half,
        grad_hidden,
    )
    up_part, up_far = local_call(
        up_pairs_body,
        [((feat_rows, up_lanes - SPAN // 2), wide), ((feat_rows, up_lanes + SPAN // 2), low)],
        "up_pairs",
        up_held,
        up_got,
    )
    up_far = swap_rows(up_far, 2)
    last_got = swap_rows(last_sent, 1)
    last_part, last_far = local_call(
        last_pairs_body,
        [((half_feats, last_lanes), wide), ((half_feats, last_lanes + 2 * SPAN), low)],
        "last_pairs",
        last_held,
        last_got,
    )
    hidden_sum, *out_wide = local_call(
        hidden_sums_body,
        low_outs(1, feat_rows, 2 * part + half_lanes)
        + low_outs(2, half_feats, SPAN * rows // 2),
        "hidden_sums",
        flags,
        down_part,
        down_far,
        up_part,
        up_held,
        up_got,
        up_far,
        scratch=[((4, half_feats, SPAN), low)],
    )
    last_sum, *input_wide = local_call(
        last_sums_body,
        low_outs(1, half_feats, last_lanes) + low_outs(2, half_feats, SPAN * rows // 2),
        "last_sums",
        flags,
        last_part,
        last_held,
        last_got,
        swap_rows(last_far, 2),
    )
    output = cols_back(*out_wide, low, "out_join")
    down_t, up_grad, out_t, vec_total = local_call(
        place_hidden_body,
        [((feat_rows, 4 * part), wide)] * 2
        + [((feat_rows, 2 * WIDTH), wide), ((feat_rows, SUM_LANES), wide)],
        "place_hidden",
        flags,
        *all_quarters(hidden_sum, True),
    )
    last_parts = all_quarters(last_sum, True)
    last_parts = (after(last_parts[0], up_grad), *last_parts[1:])
    input_grad, query_grad, key_grad, value_grad = local_call(
        place_last_body,
        [((feat_rows, SPAN * rows // 2), wide)] + [((feat_rows, 2 * WIDTH), wide)] * 3,
        "place_last",
        flags,
        *last_parts,
        input_wide[0],
        swap_cols(input_wide[1]),
    )
    return (
        output,
        input_grad,
        query_grad,
        key_grad,
        value_grad,
        out_t.T,
        vec_total[:, 0],
        vec_total[:, 1],
        up_grad,
        down_t.T,
        vec_total[:, 2],
        vec_total[:, 3],
    )


def solution(mesh):
    placed = (
        P("row", ("dp", "col")),
        P(),
        P("row", "col"),
        P("row", "col"),
        P("row", "col"),
        P("col", "row"),
        P("row"),
        P("row"),
        P("row", "col"),
        P("col", "row"),
        P("row"),
        P("row"),
        P("row", ("dp", "col")),
    )
    return jax.shard_map(
        on_device_paired if paired_layout(mesh) else on_device,
        mesh=mesh,
        in_specs=placed,
        out_specs=(
            P("row", ("dp", "col")),
            P("row", ("dp", "col")),
            P("row", "col"),
            P("row", "col"),
            P("row", "col"),
            P("col", "row"),
            P("row"),
            P("row"),
            P("row", "col"),
            P("col", "row"),
            P("row"),
            P("row"),
        ),
        check_vma=False,
    )
```

```python
from functools import partial
import math

import jax
import jax.numpy as jnp
from jax import lax
from jax.experimental import pallas as pl
from jax.experimental.pallas import tpu as pltpu
from jax.sharding import PartitionSpec as P

D = 768
H = 12
HD = 64
SEQ_MAX = 4096
TOK_DEV = 128


norm_eps = 1e-05
highest = lax.Precision.HIGHEST


def carried_in(shard, axis, join, neutral, backward):
    count = lax.axis_size(axis)
    place = lax.axis_index(axis)
    ahead = count - 1 - place if backward else place
    gathered = jax.tree.map(
        lambda a, kind: lax.all_gather(a.astype(kind), axis),
        shard,
        jax.tree.map(lambda a: jnp.bfloat16 if a.dtype == jnp.float32 else a.dtype, shard),
    )
    state = jax.tree.map(lambda a, e: jnp.zeros_like(a) + jnp.asarray(e, a.dtype), shard, neutral)

    def one(turn, state):
        source = count - 1 - turn if backward else turn
        return join(
            state,
            jax.tree.map(
                lambda a, own: lax.dynamic_index_in_dim(a, source, 0, False).astype(own.dtype),
                gathered,
                shard,
            ),
        )

    return lax.fori_loop(0, ahead, one, state)


def gather_cols(operand):
    return lax.all_gather(operand, "col", axis=0, tiled=True)


def gather_rows(operand):
    return lax.all_gather(operand, "row", axis=0, tiled=True)


def summed_over_rows(gathered, matrix):
    out_rows = gathered.shape[0] // lax.axis_size("row")

    def term_rows(first_row, row_count):
        sliced = lax.dynamic_slice_in_dim(gathered, first_row, row_count, 0)
        return jnp.dot(sliced, matrix, preferred_element_type=jnp.float32)

    return lax.psum_scatter(
        term_rows(jnp.int32(0), out_rows * lax.axis_size("row")),
        "row",
        scatter_dimension=0,
        tiled=True,
    )


def summed_over_cols(gathered, matrix):
    out_rows = gathered.shape[0] // lax.axis_size("col")

    def term_rows(first_row, row_count):
        sliced = lax.dynamic_slice_in_dim(gathered, first_row, row_count, 0)
        return jnp.dot(sliced, matrix, preferred_element_type=jnp.float32)

    return lax.psum_scatter(
        term_rows(jnp.int32(0), out_rows * lax.axis_size("col")).astype(jnp.bfloat16),
        "col",
        scatter_dimension=0,
        tiled=True,
    ).astype(jnp.float32)


def to_heads(stacked):
    return lax.all_to_all(stacked, "col", split_axis=1, concat_axis=2, tiled=True)


def to_tokens(stacked):
    return lax.all_to_all(stacked, "col", split_axis=2, concat_axis=1, tiled=True)


def row_totals(first_part, second_part):
    return lax.psum((first_part, second_part), "row")


def norm_forward(hidden, scale_vec, shift_vec):
    sum_one, sum_two = row_totals(jnp.sum(hidden, 1), jnp.sum(hidden * hidden, 1))
    row_mean = sum_one / D
    variance = sum_two / D - row_mean * row_mean
    inv_std = lax.rsqrt(variance + norm_eps)
    normed = (hidden - row_mean[:, None]) * inv_std[:, None]
    return (normed * scale_vec + shift_vec, normed, inv_std)


def norm_backward(grad_in, normed, inv_std, scale_vec):
    grad_normed = grad_in * scale_vec
    total_one, total_two = row_totals(jnp.sum(grad_normed, 1), jnp.sum(grad_normed * normed, 1))
    grad_hidden = inv_std[:, None] * (
        grad_normed - total_one[:, None] / D - normed * (total_two[:, None] / D)
    )
    return (grad_hidden, jnp.sum(grad_in * normed, 0), jnp.sum(grad_in, 0))


def seq_lengths(lengths, seq_ids):
    matches = seq_ids[:, None] == jnp.arange(lengths.shape[0], dtype=jnp.int32)[None, :]
    return jnp.sum(jnp.where(matches, lengths[None, :], 0), 1)


def reset_combine(earlier, later):
    keep_prior = 1.0 - later[4]
    joined = tuple(
        (
            keep_prior * prior_part + next_part
            for prior_part, next_part in zip(earlier[:4], later[:4])
        )
    )
    return joined + (jnp.maximum(earlier[4], later[4]),)


def empty_state():
    return (
        jnp.zeros((H, HD, HD), jnp.float32),
        jnp.zeros((H, HD, HD), jnp.float32),
        jnp.zeros((H, HD), jnp.float32),
        jnp.zeros((H, HD), jnp.float32),
        jnp.zeros((), jnp.float32),
    )


def attend_forward(queries, keys_in, values_in, present, cos_flat, sin_flat, opens_seq):
    block_rows = queries.shape[0]
    cos_pos = cos_flat[:, None, None]
    sin_pos = sin_flat[:, None, None]
    q_pos = jnp.maximum(queries, 0)
    k_pos = jnp.maximum(keys_in, 0) * present[:, None, None].astype(jnp.bfloat16)
    q_cos = q_pos.astype(jnp.float32) * cos_pos
    q_sin = q_pos.astype(jnp.float32) * sin_pos
    k_cos = k_pos.astype(jnp.float32) * cos_pos
    k_sin = k_pos.astype(jnp.float32) * sin_pos
    values_wide = values_in.astype(jnp.float32)
    local_state = (
        jnp.einsum("jhd,jhe->hde", k_cos, values_wide, precision=highest),
        jnp.einsum("jhd,jhe->hde", k_sin, values_wide, precision=highest),
        jnp.sum(k_cos, 0),
        jnp.sum(k_sin, 0),
    )
    arrived = carried_in(
        local_state + (opens_seq,), ("row", "col"), reset_combine, empty_state(), False
    )
    s_cos, s_sin, z_cos, z_sin = tuple(
        (state_part * (1.0 - opens_seq) for state_part in arrived[:4])
    )
    row_ids = jnp.arange(block_rows, dtype=jnp.int32)
    causal = (row_ids[:, None] >= row_ids[None, :]).astype(jnp.float32)
    reweight = (
        cos_flat[:, None] * cos_flat[None, :] + sin_flat[:, None] * sin_flat[None, :]
    ) * causal
    scores = jnp.einsum("ihd,jhd->hij", q_pos, k_pos, preferred_element_type=jnp.float32)
    weights = scores * reweight[None]
    weights_low = weights.astype(jnp.bfloat16)
    numerator = jnp.einsum(
        "hij,jhe->ihe", weights_low, values_in, preferred_element_type=jnp.float32
    )
    numerator = numerator + jnp.einsum("ihd,hde->ihe", q_cos, s_cos, precision=highest)
    numerator = numerator + jnp.einsum("ihd,hde->ihe", q_sin, s_sin, precision=highest)
    denominator = 1.0 + jnp.sum(weights, 2).T
    denominator = denominator + jnp.einsum("ihd,hd->ih", q_cos, z_cos, precision=highest)
    denominator = denominator + jnp.einsum("ihd,hd->ih", q_sin, z_sin, precision=highest)
    mixed = (numerator / denominator[:, :, None]).astype(jnp.bfloat16).reshape(block_rows, D)
    kept = (
        queries,
        keys_in,
        values_in,
        q_pos,
        k_pos,
        q_cos,
        q_sin,
        k_cos,
        k_sin,
        values_wide,
        reweight,
        weights_low,
        numerator,
        denominator,
        s_cos,
        s_sin,
        z_cos,
        z_sin,
        present,
        cos_pos,
        sin_pos,
    )
    return (mixed, kept)


def attend_backward(grad_heads, kept, closes_seq):
    (
        queries,
        keys_in,
        values_in,
        q_pos,
        k_pos,
        q_cos,
        q_sin,
        k_cos,
        k_sin,
        values_wide,
        reweight,
        weights_low,
        numerator,
        denominator,
        s_cos,
        s_sin,
        z_cos,
        z_sin,
        present,
        cos_pos,
        sin_pos,
    ) = kept
    block_rows = queries.shape[0]
    grad_attn = grad_heads.astype(jnp.float32).reshape(block_rows, H, HD)
    grad_num_low = (grad_attn / denominator[:, :, None]).astype(jnp.bfloat16)
    grad_num = grad_num_low.astype(jnp.float32)
    grad_den = -jnp.sum(grad_attn * numerator, 2) / (denominator * denominator)
    grad_weights = jnp.einsum(
        "ihe,jhe->hij", grad_num_low, values_in, preferred_element_type=jnp.float32
    )
    grad_weights = grad_weights + grad_den.T[:, :, None]
    grad_scores = (grad_weights * reweight[None]).astype(jnp.bfloat16)
    local_grad = (
        jnp.einsum("ihd,ihe->hde", q_cos, grad_num, precision=highest),
        jnp.einsum("ihd,ihe->hde", q_sin, grad_num, precision=highest),
        jnp.einsum("ihd,ih->hd", q_cos, grad_den, precision=highest),
        jnp.einsum("ihd,ih->hd", q_sin, grad_den, precision=highest),
    )
    later_sum = carried_in(
        local_grad + (closes_seq,), ("row", "col"), reset_combine, empty_state(), True
    )
    g_cos, g_sin, gz_cos, gz_sin = tuple(
        (state_part * (1.0 - closes_seq) for state_part in later_sum[:4])
    )
    grad_qpos = jnp.einsum("hij,jhd->ihd", grad_scores, k_pos, preferred_element_type=jnp.float32)
    grad_qpos = grad_qpos + cos_pos * (
        jnp.einsum("ihe,hde->ihd", grad_num, s_cos, precision=highest)
        + grad_den[:, :, None] * z_cos[None]
    )
    grad_qpos = grad_qpos + sin_pos * (
        jnp.einsum("ihe,hde->ihd", grad_num, s_sin, precision=highest)
        + grad_den[:, :, None] * z_sin[None]
    )
    grad_kpos = jnp.einsum("hij,ihd->jhd", grad_scores, q_pos, preferred_element_type=jnp.float32)
    grad_kpos = grad_kpos + cos_pos * (
        jnp.einsum("jhe,hde->jhd", values_wide, g_cos, precision=highest) + gz_cos[None]
    )
    grad_kpos = grad_kpos + sin_pos * (
        jnp.einsum("jhe,hde->jhd", values_wide, g_sin, precision=highest) + gz_sin[None]
    )
    grad_values = jnp.einsum(
        "hij,ihe->jhe", weights_low, grad_num_low, preferred_element_type=jnp.float32
    )
    grad_values = grad_values + jnp.einsum("jhd,hde->jhe", k_cos, g_cos, precision=highest)
    grad_values = grad_values + jnp.einsum("jhd,hde->jhe", k_sin, g_sin, precision=highest)
    grad_q = (grad_qpos * (queries > 0).astype(jnp.float32)).astype(jnp.bfloat16)
    grad_k = (grad_kpos * (keys_in > 0).astype(jnp.float32) * present[:, None, None]).astype(
        jnp.bfloat16
    )
    grad_v = grad_values.astype(jnp.bfloat16)
    return (
        grad_q.reshape(block_rows, D),
        grad_k.reshape(block_rows, D),
        grad_v.reshape(block_rows, D),
    )


def on_device(
    tokens,
    lengths,
    w_query,
    w_key,
    w_value,
    w_out,
    gain_one,
    bias_one,
    w_up,
    w_down,
    gain_two,
    bias_two,
    cotangent,
):
    row_count = lax.axis_size("row")
    col_count = lax.axis_size("col")
    seq_len = min(SEQ_MAX, TOK_DEV * row_count * col_count)
    data_idx = lax.axis_index("dp")
    row_idx = lax.axis_index("row")
    col_idx = lax.axis_index("col")
    feat_rows = tokens.shape[0]
    group_idx = row_idx * col_count + col_idx
    global_idx = (data_idx * row_count * col_count + group_idx) * TOK_DEV + jnp.arange(
        TOK_DEV, dtype=jnp.int32
    )
    positions = global_idx % seq_len
    present = (positions < seq_lengths(lengths, global_idx // seq_len)).astype(jnp.float32)
    angles = math.pi * positions.astype(jnp.float32) / (2.0 * seq_len)
    cos_flat = jnp.cos(angles)
    sin_flat = jnp.sin(angles)
    opens_seq = (group_idx * TOK_DEV % seq_len == 0).astype(jnp.float32)
    closes_seq = ((group_idx + 1) * TOK_DEV % seq_len == 0).astype(jnp.float32)
    token_rows = tokens.T
    width_col = w_query.shape[1]
    w_cat = jnp.concatenate([w_query, w_key, w_value], 1)
    x_gathered = gather_cols(token_rows)
    qkv = summed_over_rows(x_gathered, w_cat).astype(jnp.bfloat16)
    stacked = jnp.stack(
        [qkv[:, :width_col], qkv[:, width_col : 2 * width_col], qkv[:, 2 * width_col :]], 0
    )
    head_rows = to_heads(stacked)
    mixed, kept = attend_forward(
        head_rows[0].reshape(TOK_DEV, H, HD),
        head_rows[1].reshape(TOK_DEV, H, HD),
        head_rows[2].reshape(TOK_DEV, H, HD),
        present,
        cos_flat,
        sin_flat,
        opens_seq,
    )
    mixed_two = to_tokens(mixed[None])[0]
    mixed_gathered = gather_rows(mixed_two)
    branch = summed_over_cols(mixed_gathered, w_out)
    first, normed_one, inv_one = norm_forward(
        token_rows.astype(jnp.float32) + branch, gain_one, bias_one
    )
    first_low = first.astype(jnp.bfloat16)
    first_gathered = gather_cols(first_low)
    pre = summed_over_rows(first_gathered, w_up)
    act, gelu_pull = jax.vjp(partial(jax.nn.gelu, approximate=False), pre)
    act_low = act.astype(jnp.bfloat16)
    act_gathered = gather_rows(act_low)
    ffn = summed_over_cols(act_gathered, w_down)
    result, normed_two, inv_two = norm_forward(first + ffn, gain_two, bias_two)
    rows_one = token_rows.shape[0]
    global_one = (data_idx * col_count + col_idx) * rows_one + jnp.arange(rows_one, dtype=jnp.int32)
    present_one = (global_one % seq_len < seq_lengths(lengths, global_one // seq_len)).astype(
        jnp.float32
    )
    grad_result = cotangent.T.astype(jnp.float32) * present_one[:, None]
    grad_second, grad_gain_two, grad_bias_two = norm_backward(
        grad_result, normed_two, inv_two, gain_two
    )
    grad_ffn_gathered = gather_cols(grad_second.astype(jnp.bfloat16))
    act_again = gather_rows(act_low)
    grad_down = jnp.einsum(
        "tf,td->fd", act_again, grad_ffn_gathered, preferred_element_type=jnp.float32
    )
    grad_act = summed_over_rows(grad_ffn_gathered, w_down.T)
    grad_pre = gelu_pull(grad_act)[0].astype(jnp.bfloat16)
    grad_pre_gathered = gather_rows(grad_pre)
    first_again = gather_cols(first_low)
    grad_up = jnp.einsum(
        "td,tf->df", first_again, grad_pre_gathered, preferred_element_type=jnp.float32
    )
    grad_first = summed_over_cols(grad_pre_gathered, w_up.T) + grad_second
    grad_hidden, grad_gain_one, grad_bias_one = norm_backward(
        grad_first, normed_one, inv_one, gain_one
    )
    branch_grad_gathered = gather_cols(grad_hidden.astype(jnp.bfloat16))
    mixed_again = gather_rows(mixed_two)
    grad_out = jnp.einsum(
        "tc,tr->cr", mixed_again, branch_grad_gathered, preferred_element_type=jnp.float32
    )
    grad_mixed = summed_over_rows(branch_grad_gathered, w_out.T).astype(jnp.bfloat16)
    grad_heads = to_heads(grad_mixed[None])[0]
    grad_q, grad_k, grad_v = attend_backward(grad_heads, kept, closes_seq)
    grad_rows = to_tokens(jnp.stack([grad_q, grad_k, grad_v], 0))
    grad_cat = jnp.concatenate([grad_rows[0], grad_rows[1], grad_rows[2]], 1)
    grad_cat_gathered = gather_rows(grad_cat)
    x_again = gather_cols(token_rows)
    grad_cat_w = jnp.einsum(
        "tr,tc->rc", x_again, grad_cat_gathered, preferred_element_type=jnp.float32
    )
    input_rows = summed_over_cols(grad_cat_gathered, w_cat.T) + grad_hidden
    gain_parts = jnp.stack([grad_gain_one, grad_bias_one, grad_gain_two, grad_bias_two], 0)
    gain_sums = lax.psum(gain_parts.reshape(4 * feat_rows), "col")
    grad_query = grad_cat_w[:, :width_col]
    grad_key = grad_cat_w[:, width_col : 2 * width_col]
    grad_value = grad_cat_w[:, 2 * width_col :]
    output = result.astype(jnp.bfloat16).T
    input_grad = input_rows.T
    sums = (
        lax.psum(grad_query.astype(jnp.bfloat16), "dp").astype(jnp.float32),
        lax.psum(grad_key.astype(jnp.bfloat16), "dp").astype(jnp.float32),
        lax.psum(grad_value.astype(jnp.bfloat16), "dp").astype(jnp.float32),
        lax.psum(grad_out.astype(jnp.bfloat16), "dp").astype(jnp.float32),
        lax.psum(grad_up.astype(jnp.bfloat16), "dp").astype(jnp.float32),
        lax.psum(grad_down.astype(jnp.bfloat16), "dp").astype(jnp.float32),
        lax.psum(gain_sums.astype(jnp.bfloat16), "dp").astype(jnp.float32),
    )
    gain_total = sums[6].reshape(4, feat_rows)
    return (
        output,
        input_grad,
        sums[0],
        sums[1],
        sums[2],
        sums[3],
        gain_total[0],
        gain_total[1],
        sums[4],
        sums[5],
        gain_total[2],
        gain_total[3],
    )


def paired_layout(mesh):
    rows, cols, dps = mesh.shape["row"], mesh.shape["col"], mesh.shape["dp"]
    return rows == 4 and cols == 2 and dps == 4 and H % 4 == 0 and 8 * TOK_DEV <= SEQ_MAX


low = jnp.bfloat16
wide = jnp.float32
SPAN = 2 * TOK_DEV
HEADS = H // 4
WIDTH = HEADS * HD
STATE_ROWS = 2 * HEADS * HD
SUM_ROWS = 16
SUM_LANES = 64


def swap_cols(operand):
    return lax.ppermute(operand, "col", [(0, 1), (1, 0)])


def swap_pair(operand):
    return lax.ppermute(operand, "dp", [(i, i ^ 1) for i in range(lax.axis_size("dp"))])


def swap_copies(operand):
    return lax.ppermute(operand, "dp", [(i, i ^ 2) for i in range(lax.axis_size("dp"))])


def shift_rows(operand, step):
    count = lax.axis_size("row")
    pairs = [(i, i + step) for i in range(count) if 0 <= i + step < count]
    return lax.ppermute(operand, "row", pairs)


def swap_rows(operand, mask):
    return lax.ppermute(operand, "row", [(i, i ^ mask) for i in range(4)])


def rotate_rows(operand, step):
    count = lax.axis_size("row")
    return lax.ppermute(operand, "row", [(i, (i + step) % count) for i in range(count)])


def dot_tn(left, right):
    return lax.dot_general(left, right, (((0,), (0,)), ((), ())), preferred_element_type=wide)


def dot_nt(left, right):
    return lax.dot_general(left, right, (((1,), (1,)), ((), ())), preferred_element_type=wide)


def dot_nn(left, right):
    return jnp.dot(left, right, preferred_element_type=wide)


def norm_columns(hidden, scale, shift):
    mean = jnp.mean(hidden, 0, keepdims=True)
    centered = hidden - mean
    variance = jnp.mean(centered * centered, 0, keepdims=True)
    inv_std = lax.rsqrt(variance + norm_eps)
    normed = centered * inv_std
    return (normed * scale + shift, normed, inv_std)


def norm_columns_back(grad_in, normed, inv_std, scale):
    grad_normed = grad_in * scale
    mean_one = jnp.mean(grad_normed, 0, keepdims=True)
    mean_two = jnp.mean(grad_normed * normed, 0, keepdims=True)
    return inv_std * (grad_normed - mean_one - normed * mean_two)


def local_call(body, outs, name, *operands, scratch=(), space=None):
    shapes = [jax.ShapeDtypeStruct(shape, kind) for shape, kind in outs]
    return pl.pallas_call(
        body,
        out_shape=shapes,
        in_specs=[
            pl.BlockSpec(
                memory_space=pltpu.SMEM
                if operand.dtype == jnp.int32
                else space or pltpu.VMEM
            )
            for operand in operands
        ],
        out_specs=[pl.BlockSpec(memory_space=pltpu.VMEM)] * len(outs),
        scratch_shapes=[
            pltpu.VMEM(*kind) if isinstance(kind, tuple) else kind for kind in scratch
        ],
        compiler_params=pltpu.CompilerParams(vmem_limit_bytes=24 * 2**20),
        name=name,
    )(*operands)


CORE, COPY, ROW, COL, SEQ = range(5)


def low_outs(count, *shape):
    return [(shape, low)] * count


def turn_body(flags_ref, lengths_ref, trig_ref, reweight_ref, *, seq_len):
    start = flags_ref[ROW] * SPAN
    positions = start + lax.broadcasted_iota(jnp.int32, (8, SPAN), 1)
    lines = lax.broadcasted_iota(jnp.int32, (8, SPAN), 0)
    angles = math.pi * positions.astype(wide) / (2.0 * seq_len)
    turns = jnp.where(lines == 0, jnp.cos(angles), jnp.where(lines == 1, jnp.sin(angles), 0.0))
    own = lengths_ref[flags_ref[SEQ]]
    other = lengths_ref[flags_ref[SEQ] + 1 - 2 * flags_ref[CORE]]
    limits = jnp.where(lines == 2, own, other)
    present = jnp.where(positions < limits, 1.0, 0.0)
    trig_ref[...] = turns + jnp.where(lines == 2, present, jnp.where(lines == 3, present, 0.0))
    rows = lax.broadcasted_iota(jnp.int32, (SPAN, SPAN), 0)
    cols = lax.broadcasted_iota(jnp.int32, (SPAN, SPAN), 1)
    both = lax.dot_general(
        turns, turns, (((0,), (0,)), ((), ())), precision=highest, preferred_element_type=wide
    )
    reweight_ref[...] = jnp.where(rows <= cols, both, 0.0)


def token_piece(flags_ref, own_ref, recv_ref, step, rows):
    place = lax.rem(flags_ref[ROW] + step, rows)
    half = lax.div(place, rows // 2)
    cols = pl.ds(pl.multiple_of(lax.rem(place, rows // 2) * SPAN, SPAN), SPAN)
    return jnp.where(half == flags_ref[COL], own_ref[:, cols], recv_ref[:, cols])


def pieces_body(flags_ref, own_ref, cot_ref, recv_ref, *refs, rows):
    vec_ref, piece_refs = refs[0], refs[1:]
    part = own_ref.shape[0]
    lines = []
    for line in range(4):
        vec = vec_ref[line : line + 1, :]
        vec = jnp.concatenate([vec, jnp.zeros((1, SPAN - vec.shape[1]), wide)], 1)
        high = vec.astype(low).astype(wide)
        lines = lines + [high, vec - high]
    for step, ref in enumerate(piece_refs):
        ref[:part] = token_piece(flags_ref, own_ref, recv_ref.at[:part], step, rows)
        ref[part : 2 * part] = token_piece(flags_ref, cot_ref, recv_ref.at[part:], step, rows)
        ref[2 * part :] = jnp.concatenate(lines + [jnp.zeros((8, SPAN), wide)], 0).astype(low)


def came_from(flags_ref, step, rows):
    return lax.rem(flags_ref[ROW] + rows - step, rows)


def place_tokens_body(flags_ref, *refs, rows, part):
    pieces, (half_ref, vec_ref) = refs[:rows], refs[rows:]
    below = half_ref.shape[0] // 2
    for step, ref in enumerate(pieces):
        row = came_from(flags_ref, step, rows)
        half_ref[pl.ds(pl.multiple_of(row * part, 16), part), :] = ref[:part]
        half_ref[pl.ds(pl.multiple_of(below + row * part, 16), part), :] = ref[part : 2 * part]
        extra = ref[2 * part :].astype(wide)
        sums = [extra[2 * i : 2 * i + 1] + extra[2 * i + 1 : 2 * i + 2] for i in range(4)]
        columns = jnp.concatenate(sums + [jnp.zeros((4, SPAN), wide)], 0).T
        vec_ref[pl.ds(pl.multiple_of(row * 2 * part, 8), 2 * part), :] = columns[: 2 * part]


def join_halves_body(flags_ref, half_ref, recv_ref, x_ref, cot_ref, *, rows):
    part = half_ref.shape[0] // (2 * rows)
    first_col = flags_ref[COL] == 0
    for place, full_ref in enumerate((x_ref, cot_ref)):
        for row in range(rows):
            source = (place * rows + row) * part
            own = half_ref[source : source + part]
            other = recv_ref[source : source + part]
            start = 2 * row * part
            full_ref[start : start + part] = jnp.where(first_col, own, other)
            full_ref[start + part : start + 2 * part] = jnp.where(first_col, other, own)


def add_body(own_ref, recv_ref, half_ref):
    half_ref[...] = (own_ref[...] + recv_ref[...].astype(wide)).astype(low)


def feature_piece(flags_ref, source, step, rows):
    part = source.shape[0] // (2 * rows)
    start = (lax.rem(flags_ref[ROW] + step, rows) * 2 + flags_ref[COL]) * part
    return source[pl.ds(pl.multiple_of(start, 16), part), :]


def place_back(flags_ref, pieces, rows, own_ref, other_ref):
    half = len(pieces) // 2
    for row, piece in zip(rows, pieces):
        cols = pl.ds(pl.multiple_of(lax.rem(row, half) * SPAN, SPAN), SPAN)
        mine = lax.div(row, half) == flags_ref[COL]

        @pl.when(mine)
        def _(piece=piece, cols=cols):
            own_ref[:, cols] = piece[...]

        @pl.when(jnp.logical_not(mine))
        def _(piece=piece, cols=cols):
            other_ref[:, cols] = piece[...]


def sum_of(refs):
    total = refs[0][...].astype(wide)
    for ref in refs[1:]:
        total = total + ref[...].astype(wide)
    return total


def join_back_body(flags_ref, own_ref, recv_ref, out_ref):
    part = own_ref.shape[0]
    first_col = flags_ref[COL] == 0
    out_ref[:part] = jnp.where(first_col, own_ref[...], recv_ref[...]).astype(out_ref.dtype)
    out_ref[part:] = jnp.where(first_col, recv_ref[...], own_ref[...]).astype(out_ref.dtype)


def input_halves_body(flags_ref, own_ref, recv_ref, half_ref, sent_ref, sum_ref, *, rows):
    part = own_ref.shape[0] // (2 * rows)
    sum_ref[...] = own_ref[...] + recv_ref[...].astype(wide)
    for row in range(rows):
        rows_out = slice(row * part, (row + 1) * part)
        mine = pl.multiple_of((2 * row + flags_ref[COL]) * part, 16)
        theirs = pl.multiple_of((2 * row + 1 - flags_ref[COL]) * part, 16)
        half_ref[rows_out] = sum_ref[pl.ds(mine, part), :]
        sent_ref[rows_out] = sum_ref[pl.ds(theirs, part), :].astype(low)


def last_pieces_body(
    flags_ref, kept_ref, got_ref, half_ref, recv_ref, hidden_ref, held_ref, sent_ref
):
    rows = kept_ref.shape[0]
    part = half_ref.shape[0] // rows
    lanes = kept_ref.shape[2]
    for mask in range(rows):
        ref = sent_ref if mask % 2 else held_ref
        out = slice(mask // 2 * part, (mask // 2 + 1) * part)
        place = partner(flags_ref[ROW], mask)
        ref[out, :lanes] = (kept_ref[place].astype(wide) + got_ref[place].astype(wide)).astype(low)
        rows_in = pl.ds(pl.multiple_of(place * part, 16), part)
        total = half_ref[rows_in, :] + recv_ref[rows_in, :].astype(wide)
        start = pl.multiple_of((place * 2 + flags_ref[COL]) * part, 16)
        ref[out, lanes:] = (total + hidden_ref[pl.ds(start, part), :]).astype(low)


def last_pairs_body(held_ref, got_ref, sum_ref, sent_ref):
    part, lanes = sum_ref.shape
    sum_ref[...] = held_ref[:part, :lanes].astype(wide) + got_ref[:part, :lanes].astype(wide)
    pair = held_ref[part:, :lanes].astype(wide) + got_ref[part:, :lanes].astype(wide)
    sent_ref[:, :lanes] = pair.astype(low)
    sent_ref[:, lanes : lanes + SPAN] = held_ref[part:, lanes:]
    sent_ref[:, lanes + SPAN :] = got_ref[part:, lanes:]


def last_sums_body(
    flags_ref, part_ref, held_ref, got_ref, far_ref, sum_ref, own_ref, other_ref
):
    part, lanes = part_ref.shape
    sum_ref[...] = (part_ref[...] + far_ref[:, :lanes].astype(wide)).astype(low)
    pieces = (
        held_ref.at[:part, lanes:],
        got_ref.at[:part, lanes:],
        far_ref.at[:, lanes : lanes + SPAN],
        far_ref.at[:, lanes + SPAN :],
    )
    rows = [partner(flags_ref[ROW], mask) for mask in range(4)]
    place_back(flags_ref, pieces, rows, own_ref, other_ref)


def down_grad_body(
    flags_ref, own_ref, other_ref, mine_ref, copy_ref, held_ref, sent_ref, grad_ref
):
    feats, part = held_ref.shape[0] // 2, mine_ref.shape[0]
    for act_ref, cols in ((mine_ref, slice(0, part)), (copy_ref, slice(part, 2 * part))):
        grad_ref[:, cols] = (
            dot_nt(own_ref[...], act_ref[:, :SPAN]) + dot_nt(other_ref[...], act_ref[:, SPAN:])
        ).astype(low)
    for mask in range(4):
        ref = sent_ref if mask % 2 else held_ref
        start = mask // 2 * feats
        place = partner(flags_ref[ROW], mask)
        rows_in = pl.ds(pl.multiple_of(place * feats, 16), feats)
        ref[start : start + feats, :] = grad_ref[rows_in, :]


def down_pairs_body(held_ref, got_ref, kept_ref, sent_ref):
    part = kept_ref.shape[1]
    kept_ref[...] = held_ref[:, :part].astype(wide) + got_ref[:, :part].astype(wide)
    sent_ref[...] = (held_ref[:, part:].astype(wide) + got_ref[:, part:].astype(wide)).astype(low)


def mix_body(
    flags_ref, own_ref, other_ref, attn_wide_ref, vec_ref, pair_ref, kept_ref, sent_ref, grad_ref
):
    grad_ref[:, :WIDTH] = (
        dot_nt(own_ref[...], attn_wide_ref[:WIDTH, :].astype(low))
        + dot_nt(other_ref[...], attn_wide_ref[WIDTH : 2 * WIDTH, :].astype(low))
    ).astype(low)
    grad_ref[:, WIDTH:] = vec_ref[:, :SUM_LANES]
    first_copy = flags_ref[COPY] == 0
    half = (WIDTH + SUM_LANES) // 2
    kept_ref[...] = jnp.where(first_copy, grad_ref[:, :half], grad_ref[:, half:])
    sent = jnp.where(first_copy, grad_ref[:, half:], grad_ref[:, :half])
    lines, part = pair_ref.shape
    sent_ref[:, :part] = pair_ref[...]
    sent_ref[:, part : part + half] = sent[:lines]
    sent_ref[:, part + half :] = sent[lines:]


def down_far_body(kept_ref, got_ref, sum_ref, sent_ref):
    feats, part = sum_ref.shape
    sum_ref[...] = kept_ref[:feats] + got_ref[:feats, :part].astype(wide)
    sent_ref[...] = (kept_ref[feats:] + got_ref[feats:, :part].astype(wide)).astype(low)


def up_pieces_body(
    flags_ref, result_ref, kept_ref, got_ref, mix_ref, mix_got_ref, held_ref, sent_ref, sum_ref
):
    feats, part = kept_ref.shape[0] // 4, kept_ref.shape[1]
    half, lanes = feats // 2, SPAN // 2
    lines, cols = mix_got_ref.shape[0], mix_ref.shape[1]
    sum_ref[:lines] = (
        mix_ref[:lines].astype(wide) + mix_got_ref[:, part : part + cols].astype(wide)
    ).astype(low)
    sum_ref[lines:] = (
        mix_ref[lines:].astype(wide) + mix_got_ref[:, part + cols :].astype(wide)
    ).astype(low)
    for mask in range(4):
        ref = sent_ref if mask % 2 else held_ref
        start = mask // 2 * feats
        out = slice(start, start + feats)
        place = partner(flags_ref[ROW], mask)
        rows_in = pl.ds(pl.multiple_of((place * 2 + flags_ref[COL]) * half, 16), half)
        ref[start : start + half, :lanes] = result_ref[rows_in, :lanes]
        ref[start + half : start + feats, :lanes] = result_ref[rows_in, lanes:]
        rows_in = pl.ds(pl.multiple_of(place * feats, 16), feats)
        ref[out, lanes : lanes + part] = (
            kept_ref[rows_in, :].astype(wide) + got_ref[rows_in, :].astype(wide)
        ).astype(low)
        ref[out, lanes + part :] = sum_ref[rows_in, :]


def up_pairs_body(held_ref, got_ref, sum_ref, sent_ref):
    feats, total = held_ref.shape[0] // 2, held_ref.shape[1]
    lanes = SPAN // 2
    sum_ref[...] = held_ref[:feats, lanes:].astype(wide) + got_ref[:feats, lanes:].astype(wide)
    pair = held_ref[feats:, lanes:].astype(wide) + got_ref[feats:, lanes:].astype(wide)
    sent_ref[:, :lanes] = held_ref[feats:, :lanes]
    sent_ref[:, lanes:total] = pair.astype(low)
    sent_ref[:, total:] = got_ref[feats:, :lanes]


def hidden_sums_body(
    flags_ref,
    down_ref,
    down_far_ref,
    up_ref,
    held_ref,
    got_ref,
    far_ref,
    sum_ref,
    own_ref,
    other_ref,
    piece_ref,
):
    feats, part = down_ref.shape
    lanes = SPAN // 2
    total = lanes + up_ref.shape[1]
    sum_ref[:, :part] = (down_ref[...] + down_far_ref[...].astype(wide)).astype(low)
    sum_ref[:, part:] = (up_ref[...] + far_ref[:, lanes:total].astype(wide)).astype(low)
    pieces = (
        held_ref[:feats, :lanes],
        got_ref[:feats, :lanes],
        far_ref[:, :lanes],
        far_ref[:, total:],
    )
    for place, piece in enumerate(pieces):
        piece_ref[place, :, :lanes] = piece[: feats // 2]
        piece_ref[place, :, lanes:] = piece[feats // 2 :]
    rows = [partner(flags_ref[ROW], mask) for mask in range(4)]
    place_back(flags_ref, [piece_ref.at[i] for i in range(4)], rows, own_ref, other_ref)


def head_sets():
    return [(seq, head, seq * HEADS + head) for seq in range(2) for head in range(HEADS)]


def set_row(place):
    ids = lax.broadcasted_iota(jnp.int32, (SUM_ROWS, SPAN), 0)
    return (ids == place).astype(wide)


def turned(parts, trig_ref):
    part_wide = parts.astype(wide)
    return jnp.concatenate(
        [(part_wide * trig_ref[0:1, :]).astype(low), (part_wide * trig_ref[1:2, :]).astype(low)], 0
    )


def unturned(pair, trig_ref):
    return pair[:HD] * trig_ref[0:1, :] + pair[HD:] * trig_ref[1:2, :]


def query_part(qkv_ref, seq, head):
    return qkv_ref[seq, head * HD : (head + 1) * HD, :]


def key_part(qkv_ref, seq, head):
    return qkv_ref[seq, WIDTH + head * HD : WIDTH + (head + 1) * HD, :]


def value_part(qkv_ref, seq, head):
    return qkv_ref[seq, 2 * WIDTH + head * HD : 2 * WIDTH + (head + 1) * HD, :]


def kept_keys(qkv_ref, trig_ref, seq, head):
    keys = jnp.maximum(key_part(qkv_ref, seq, head), 0)
    return (keys.astype(wide) * trig_ref[2 + seq : 3 + seq, :]).astype(low)


def state_slice(state, place):
    return state[place * HD : (place + 1) * HD]


def pack_hidden_body(flags_ref, up_ref, down_ref, mine_ref, copy_ref, sems):
    part = mine_ref.shape[1] // 2
    copies = []
    for half, packed_ref in enumerate((mine_ref, copy_ref)):
        copy = 1 - flags_ref[COPY] if half else flags_ref[COPY]
        start = pl.multiple_of((flags_ref[CORE] * 2 + copy) * part, 128)
        for place, ref in enumerate((up_ref, down_ref)):
            copies.append(
                pltpu.make_async_copy(
                    ref.at[:, pl.ds(start, part)],
                    packed_ref.at[:, pl.ds(place * part, part)],
                    sems.at[2 * half + place],
                )
            )
    for copy in copies:
        copy.start()
    for copy in copies:
        copy.wait()


def partner(row, mask):
    if mask == 0:
        return row
    if mask == 1:
        return row + 1 - 2 * lax.rem(row, 2)
    return lax.rem(row + 2, 4) if mask == 2 else 3 - row


def row_block(flags_ref, mask, feats):
    return pl.ds(pl.multiple_of(partner(flags_ref[ROW], mask) * feats, 16), feats)


def project_body(flags_ref, own_ref, other_ref, trig_ref, packed_ref, *refs):
    weight_ref, qkv_ref, state_ref = refs[-3:]
    blocks = refs[:-3]
    count = len(blocks) // 2
    first_copy = flags_ref[COPY] == 0
    feats = packed_ref.shape[0]
    part = packed_ref.shape[1] // 2

    def rows_of(mask):
        return row_block(flags_ref, mask, feats)

    weight_ref[rows_of(0), :] = packed_ref[...]
    for step in range(1, count + 1):
        mine, copied = blocks[step - 1][...], blocks[count + step - 1][...]
        weight_ref[rows_of(step), :part] = jnp.where(first_copy, mine, copied)
        weight_ref[rows_of(step), part:] = jnp.where(first_copy, copied, mine)
    matrix = weight_ref[:, : 3 * WIDTH]
    for seq, x_ref in enumerate((own_ref, other_ref)):
        qkv_ref[seq] = dot_tn(matrix, x_ref[...]).astype(low)
    sums = jnp.zeros((SUM_ROWS, 2 * HD), wide)
    for seq, head, place in head_sets():
        turned_keys = turned(kept_keys(qkv_ref, trig_ref, seq, head), trig_ref)
        values = value_part(qkv_ref, seq, head)
        state_ref[place * HD : (place + 1) * HD, :] = dot_nt(values, turned_keys).astype(low)
        sums = sums + dot_nt(set_row(place).astype(low), turned_keys)
    state_ref[STATE_ROWS:, :] = sums.astype(low)


def block_body(qkv_ref, trig_ref, reweight_ref, weights_ref, numer_ref, denom_ref):
    denoms = jnp.zeros((SUM_ROWS, SPAN), wide)
    for seq, head, place in head_sets():
        queries = jnp.maximum(query_part(qkv_ref, seq, head), 0)
        keys = kept_keys(qkv_ref, trig_ref, seq, head)
        weights = dot_tn(keys, queries) * reweight_ref[...]
        weights_low = weights.astype(low)
        weights_ref[place] = weights_low
        numer_ref[place] = dot_nn(value_part(qkv_ref, seq, head), weights_low)
        denoms = denoms + set_row(place) * jnp.sum(weights, 0, keepdims=True)
    denom_ref[...] = denoms


def attend_body(
    qkv_ref,
    trig_ref,
    numer_ref,
    denom_ref,
    weight_ref,
    *refs,
):
    arrived = refs[:-5]
    prior_ref, attn_wide_ref, own_ref, other_ref, attn_ref = refs[-5:]
    total = arrived[0][...].astype(wide)
    for ref in arrived[1:]:
        total = total + ref[...].astype(wide)
    prior_ref[...] = total.astype(low)
    matrix = weight_ref[:, 3 * WIDTH : 4 * WIDTH]
    prior_sums = prior_ref[STATE_ROWS:, :]
    inverses = jnp.zeros((SUM_ROWS, SPAN), wide)
    for seq, head, place in head_sets():
        queries = turned(jnp.maximum(query_part(qkv_ref, seq, head), 0), trig_ref)
        prior = prior_ref[place * HD : (place + 1) * HD, :]
        numer = numer_ref[place] + dot_nn(prior, queries)
        denoms = dot_nn(prior_sums, queries) + denom_ref[...]
        denom = 1.0 + jnp.sum(denoms * set_row(place), 0, keepdims=True)
        inverse = 1.0 / denom
        inverses = inverses + set_row(place) * inverse
        attended = numer * inverse
        attn_wide_ref[place * HD : (place + 1) * HD, :] = attended
        attn_ref[seq, head * HD : (head + 1) * HD, :] = attended.astype(low)
    attn_wide_ref[STATE_ROWS:, :] = inverses
    own_ref[...] = dot_nn(matrix, attn_ref[0])
    other_ref[...] = dot_nn(matrix, attn_ref[1]).astype(low)


def grad_attend_body(
    own_ref,
    other_ref,
    weight_ref,
    attn_wide_ref,
    qkv_ref,
    trig_ref,
    grad_num_ref,
    grad_den_ref,
    state_ref,
):
    matrix = weight_ref[:, 3 * WIDTH : 4 * WIDTH]
    sums = jnp.zeros((SUM_ROWS, 2 * HD), wide)
    dens = jnp.zeros((SUM_ROWS, SPAN), wide)
    for seq, grad_ref in enumerate((own_ref, other_ref)):
        grads = dot_tn(matrix, grad_ref[...]).astype(low).astype(wide)
        for head in range(HEADS):
            place = seq * HEADS + head
            inverse = jnp.sum(attn_wide_ref[STATE_ROWS:, :] * set_row(place), 0, keepdims=True)
            scaled = grads[head * HD : (head + 1) * HD] * inverse
            grad_num = scaled.astype(low)
            grad_num_ref[place] = grad_num
            grad_den = -jnp.sum(scaled * attn_wide_ref[place * HD : (place + 1) * HD, :], 0, keepdims=True)
            den_row = set_row(place) * grad_den
            dens = dens + den_row
            queries = turned(jnp.maximum(query_part(qkv_ref, seq, head), 0), trig_ref)
            state_ref[place * HD : (place + 1) * HD, :] = dot_nt(grad_num, queries).astype(low)
            sums = sums + dot_nt(den_row.astype(low), queries)
    state_ref[STATE_ROWS:, :] = sums.astype(low)
    grad_den_ref[...] = dens


def grad_block_body(
    grad_num_ref,
    grad_den_ref,
    qkv_ref,
    trig_ref,
    reweight_ref,
    weights_ref,
    prior_ref,
    grad_query_ref,
    grad_key_ref,
    grad_value_ref,
):
    prior_sums = prior_ref[STATE_ROWS:, :]
    for seq, head, place in head_sets():
        query = query_part(qkv_ref, seq, head)
        queries = jnp.maximum(query, 0)
        keys = kept_keys(qkv_ref, trig_ref, seq, head)
        grad_num = grad_num_ref[place]
        den_rows = grad_den_ref[...] * set_row(place)
        grad_den = jnp.sum(den_rows, 0, keepdims=True)
        grad_scores = (
            (dot_tn(value_part(qkv_ref, seq, head), grad_num) + grad_den) * reweight_ref[...]
        ).astype(low)
        prior = jnp.concatenate([prior_ref[place * HD : (place + 1) * HD, :], prior_sums], 0)
        grads = jnp.concatenate([grad_num, den_rows.astype(low)], 0)
        grad_query = dot_nn(keys, grad_scores) + unturned(dot_tn(prior, grads), trig_ref)
        grad_query_ref[seq, head * HD : (head + 1) * HD, :] = jnp.where(
            query.astype(wide) > 0, grad_query, 0.0
        ).astype(low)
        grad_key_ref[place] = dot_nt(queries, grad_scores)
        grad_value_ref[place] = dot_nt(grad_num, weights_ref[place])


def grad_project_body(
    grad_query_ref,
    grad_key_ref,
    grad_value_ref,
    qkv_ref,
    trig_ref,
    x_own_ref,
    x_other_ref,
    weight_ref,
    flags_ref,
    *refs,
):
    arrived = refs[:-6]
    kept_ref, sent_ref, own_ref, other_ref, after_ref, grad_ref = refs[-6:]
    total = arrived[0][...].astype(wide)
    for ref in arrived[1:]:
        total = total + ref[...].astype(wide)
    after_ref[...] = total.astype(low)
    after_sums = after_ref[STATE_ROWS:, :]
    for seq, head, place in head_sets():
        key = key_part(qkv_ref, seq, head)
        keys = turned(kept_keys(qkv_ref, trig_ref, seq, head), trig_ref)
        values = value_part(qkv_ref, seq, head)
        after = after_ref[place * HD : (place + 1) * HD, :]
        left = jnp.concatenate([after, after_sums], 0)
        right = jnp.concatenate([values, set_row(place).astype(low)], 0)
        grad_key = grad_key_ref[place] + unturned(dot_tn(left, right), trig_ref)
        grad_key = jnp.where(key.astype(wide) > 0, grad_key, 0.0) * trig_ref[2 + seq : 3 + seq, :]
        grad_value = grad_value_ref[place] + dot_nn(after, keys)
        rows = slice(head * HD, (head + 1) * HD)
        grad_ref[seq, rows, :] = grad_query_ref[seq, rows, :]
        rows = slice(WIDTH + head * HD, WIDTH + (head + 1) * HD)
        grad_ref[seq, rows, :] = grad_key.astype(low)
        rows = slice(2 * WIDTH + head * HD, 2 * WIDTH + (head + 1) * HD)
        grad_ref[seq, rows, :] = grad_value.astype(low)
    matrix = weight_ref[:, : 3 * WIDTH]
    grad_w = (
        dot_nt(x_own_ref[...], grad_ref[0]) + dot_nt(x_other_ref[...], grad_ref[1])
    ).astype(low)
    rows, part, _ = kept_ref.shape
    first_copy = flags_ref[COPY] == 0
    for row in range(rows):
        start = row * 2 * part
        first, second = grad_w[start : start + part], grad_w[start + part : start + 2 * part]
        kept_ref[row] = jnp.where(first_copy, first, second)
        sent_ref[row] = jnp.where(first_copy, second, first)
    own_ref[...] = dot_nn(matrix, grad_ref[0])
    other_ref[...] = dot_nn(matrix, grad_ref[1]).astype(low)


def norm_body(x_ref, half_ref, recv_ref, vec_ref, first_ref, low_ref, normed_ref):
    hidden = x_ref[...].astype(wide) + (half_ref[...].astype(wide) + recv_ref[...].astype(wide))
    first, normed, inv_std = norm_columns(hidden, vec_ref[:, 0:1], vec_ref[:, 1:2])
    first_ref[...] = first
    low_ref[...] = first.astype(low)
    normed_ref[:D, :] = normed
    normed_ref[D:, :] = jnp.broadcast_to(inv_std, (8, SPAN))


def lane_sums(columns, place):
    lanes = lax.broadcasted_iota(jnp.int32, (columns[0].shape[0], 2 * SUM_LANES), 1)
    total = jnp.zeros(lanes.shape, wide)
    for shift, column in enumerate(columns):
        total = jnp.where(lanes == place + shift, jnp.sum(column, 1, keepdims=True), total)
    return total


def second_norm_body(
    first_ref, half_ref, recv_ref, vec_ref, cot_ref, trig_ref, result_ref, grad_ref, low_ref
):
    hidden = first_ref[...] + (half_ref[...].astype(wide) + recv_ref[...].astype(wide))
    scale = vec_ref[:, 2:3]
    result, normed, inv_std = norm_columns(hidden, scale, vec_ref[:, 3:4])
    result_ref[...] = result.astype(low)
    grad_in = cot_ref[...].astype(wide) * trig_ref[2:3, :]
    grad = norm_columns_back(grad_in, normed, inv_std, scale)
    grad_ref[:, :SPAN] = grad
    low_ref[...] = grad.astype(low)
    grad_ref[:, SPAN:] = lane_sums((grad_in * normed, grad_in), 2)


def norm_back_body(
    grad_ref, half_ref, recv_ref, normed_ref, vec_ref, hidden_ref, low_ref, sum_ref
):
    grad_in = grad_ref[:, :SPAN] + (half_ref[...].astype(wide) + recv_ref[...].astype(wide))
    normed = normed_ref[:D, :]
    grad = norm_columns_back(grad_in, normed, normed_ref[D : D + 1, :], vec_ref[:, 0:1])
    hidden_ref[...] = grad
    low_ref[...] = grad.astype(low)
    sum_ref[...] = (lane_sums((grad_in * normed, grad_in), 0) + grad_ref[:, SPAN:]).astype(low)


def hidden_weights_body(flags_ref, *refs):
    blocks, outs = refs[:-2], refs[-2:]
    for half, weight_ref in enumerate(outs):
        for mask, ref in enumerate(blocks[4 * half : 4 * half + 4]):
            weight_ref[row_block(flags_ref, mask, ref.shape[0]), :] = ref[...]


def hidden_body(own_ref, other_ref, mine_ref, copy_ref, *refs):
    acts, slopes, parts = refs[:2], refs[2:4], refs[4:]
    part = acts[0].shape[0]
    for seq, (x_ref, part_ref) in enumerate(zip((own_ref, other_ref), parts)):
        cols = slice(seq * SPAN, (seq + 1) * SPAN)
        total = None
        for weight_ref, act_ref, slope_ref in zip((mine_ref, copy_ref), acts, slopes):
            act, slope = gelu_and_slope(dot_tn(weight_ref[:, :part], x_ref[...]))
            act_ref[:, cols] = act
            slope_ref[:, cols] = slope.astype(low)
            term = dot_nn(weight_ref[:, part:], act)
            total = term if total is None else total + term
        part_ref[...] = total.astype(part_ref.dtype)


def hidden_back_body(
    own_ref,
    other_ref,
    mine_ref,
    copy_ref,
    slope_mine_ref,
    slope_copy_ref,
    pre_mine_ref,
    pre_copy_ref,
    part_own_ref,
    part_other_ref,
):
    part = slope_mine_ref.shape[0]
    for seq, (x_ref, part_ref) in enumerate(
        ((own_ref, part_own_ref), (other_ref, part_other_ref))
    ):
        cols = slice(seq * SPAN, (seq + 1) * SPAN)
        total = None
        for weight_ref, slope_ref, pre_ref in (
            (mine_ref, slope_mine_ref, pre_mine_ref),
            (copy_ref, slope_copy_ref, pre_copy_ref),
        ):
            grad_pre = (dot_tn(weight_ref[:, part:], x_ref[...]) * slope_ref[:, cols].astype(wide)).astype(low)
            pre_ref[:, cols] = grad_pre
            term = dot_nn(weight_ref[:, :part], grad_pre)
            total = term if total is None else total + term
        part_ref[...] = total.astype(part_ref.dtype)


def half_grads_body(own_ref, other_ref, mine_ref, copy_ref, kept_ref, sent_ref):
    for pre_ref, out_ref in ((copy_ref, sent_ref), (mine_ref, kept_ref)):
        out_ref[...] = (
            dot_nt(own_ref[...], pre_ref[:, :SPAN]) + dot_nt(other_ref[...], pre_ref[:, SPAN:])
        ).astype(low)


def quarters(flags_ref, refs):
    core, copy = flags_ref[CORE], flags_ref[COPY]
    for ref, other_core, other_copy in zip(refs, (0, 0, 1, 1), (0, 1, 0, 1)):
        core_place = 1 - core if other_core else core
        copy_place = 1 - copy if other_copy else copy
        yield core_place * 2 + copy_place, ref


def place_hidden_body(flags_ref, *refs):
    down_ref, up_ref, out_ref = refs[4:7]
    part = up_ref.shape[1] // 4
    for place, ref in quarters(flags_ref, refs[:4]):
        cols = pl.ds(pl.multiple_of(place * part, 128), part)
        down_ref[:, cols] = ref[:, :part].astype(wide)
        up_ref[:, cols] = ref[:, part : 2 * part].astype(wide)
    half = (WIDTH + SUM_LANES) // 2
    first_core, first_copy = flags_ref[CORE] == 0, flags_ref[COPY] == 0
    sums = []
    for own_ref, copy_ref in (refs[:2], refs[2:4]):
        own, copied = own_ref[:, 2 * part :].astype(wide), copy_ref[:, 2 * part :].astype(wide)
        sums.append((jnp.where(first_copy, own, copied), jnp.where(first_copy, copied, own)))
    first = [jnp.where(first_core, sums[0][i], sums[1][i]) for i in (0, 1)]
    second = [jnp.where(first_core, sums[1][i], sums[0][i]) for i in (0, 1)]
    for parts, start in ((first, 0), (second, WIDTH)):
        out_ref[:, start : start + half] = parts[0]
        out_ref[:, start + half : start + WIDTH] = parts[1][:, : WIDTH - half]
    vecs = first[1][:, WIDTH - half :] + second[1][:, WIDTH - half :]
    lines = lax.broadcasted_iota(jnp.int32, (8, SUM_LANES), 0)
    lanes = lax.broadcasted_iota(jnp.int32, (8, SUM_LANES), 1)
    picked = lax.dot_general(
        (lines == lanes).astype(wide),
        vecs,
        (((1,), (1,)), ((), ())),
        precision=highest,
        preferred_element_type=wide,
    )
    for line, ref in enumerate(refs[7:]):
        ref[...] = picked[line : line + 1]


def place_last_body(flags_ref, *refs):
    join_back_body(flags_ref, refs[4], refs[5], refs[6])
    outs = refs[7:]
    first_core = flags_ref[CORE] == 0
    part = refs[0].shape[0]
    for own_ref, other_ref, other_copy in ((refs[0], refs[2], 0), (refs[1], refs[3], 1)):
        copy = 1 - flags_ref[COPY] if other_copy else flags_ref[COPY]
        rows = pl.ds(pl.multiple_of(copy * part, 8), part)
        own, other = own_ref[...].astype(wide), other_ref[...].astype(wide)
        for place, out_ref in enumerate(outs):
            cols = slice(place * WIDTH, (place + 1) * WIDTH)
            out_ref[rows, :WIDTH] = jnp.where(first_core, own[:, cols], other[:, cols])
            out_ref[rows, WIDTH:] = jnp.where(first_core, other[:, cols], own[:, cols])


def gelu_and_slope(pre):
    cdf = 0.5 * (1.0 + lax.erf(pre * math.sqrt(0.5)))
    density = jnp.exp(-0.5 * pre * pre) * (1.0 / math.sqrt(2.0 * math.pi))
    return (pre * cdf).astype(low), (cdf + pre * density)


def all_quarters(own, direct=False):
    copied = swap_copies(own)
    if direct:
        pairs = [(i, i ^ 3) for i in range(lax.axis_size("dp"))]
        return own, copied, swap_pair(own), lax.ppermute(own, "dp", pairs)
    return own, copied, swap_pair(own), swap_pair(copied)


def on_device_paired(
    tokens,
    lengths,
    w_query,
    w_key,
    w_value,
    w_out,
    gain_one,
    bias_one,
    w_up,
    w_down,
    gain_two,
    bias_two,
    cotangent,
):
    rows = lax.axis_size("row")
    seq_len = SPAN * rows
    dp_idx = lax.axis_index("dp")
    feat_rows = tokens.shape[0]
    half_feats = feat_rows // 2
    flags = jnp.stack(
        [dp_idx % 2, dp_idx // 2, lax.axis_index("row"), lax.axis_index("col"), dp_idx]
    )
    trig, reweight = local_call(
        partial(turn_body, seq_len=seq_len),
        [((8, SPAN), wide), ((SPAN, SPAN), wide)],
        "turn",
        flags,
        lengths,
    )

    def passed_on(pieces):
        return [pieces[0]] + [
            rotate_rows(piece, step) for step, piece in enumerate(pieces) if step
        ]

    def cols_back(own, other, kind, name):
        return local_call(
            join_back_body,
            [((feat_rows, SPAN * rows // 2), kind)],
            name,
            flags,
            own,
            swap_cols(other),
        )[0]

    def column_parts(own_part, other_part, name):
        (half,) = local_call(add_body, low_outs(1, D, SPAN), name, own_part, swap_pair(other_part))
        return half, swap_cols(half)

    first_col = lax.axis_index("col") == 0

    def halved(block):
        top, bottom = block[:half_feats], block[half_feats:]
        return jnp.where(first_col, top, bottom), jnp.where(first_col, bottom, top)

    (token_own, token_sent), (cot_own, cot_sent) = halved(tokens), halved(cotangent)
    got = swap_cols(jnp.concatenate([token_sent, cot_sent], 0))

    part = w_up.shape[1] // 4
    first_core = dp_idx % 2 == 0

    def core_part(operand):
        return jnp.where(first_core, operand[:, :WIDTH], operand[:, WIDTH:])

    parts = [core_part(operand) for operand in (w_query, w_key, w_value, w_out.T)]
    first_packed = jnp.concatenate(parts, 1)
    first_mine = jnp.where(
        dp_idx < 2, jnp.concatenate(parts[:2], 1), jnp.concatenate(parts[2:], 1)
    )

    def row_blocks(block):
        return swap_rows(block, 1), swap_rows(block, 2)

    first_one, first_two = row_blocks(first_mine)
    first_one, got = lax.optimization_barrier((first_one, got))
    hidden_packed = local_call(
        pack_hidden_body,
        low_outs(2, feat_rows, 2 * part),
        "pack_hidden",
        flags,
        w_up,
        w_down.T,
        scratch=[pltpu.SemaphoreType.DMA((4,))],
        space=pltpu.HBM,
    )
    vecs = jnp.stack([gain_one, bias_one, gain_two, bias_two], 0)
    token_pieces = local_call(
        partial(pieces_body, rows=rows),
        low_outs(rows, feat_rows + 16, SPAN),
        "token_pieces",
        flags,
        token_own,
        cot_own,
        got,
        vecs,
    )
    def after(value, *others):
        return lax.optimization_barrier((value, others))[0]

    first_three = swap_rows(after(first_two, token_pieces[0]), 1)
    first_copies = [
        swap_copies(after(first_one, token_pieces[0])),
        swap_copies(first_two),
        swap_copies(first_three),
    ]
    token_pieces = passed_on(token_pieces)
    token_pieces, first_three, first_copies[0] = lax.optimization_barrier(
        (token_pieces, first_three, first_copies[0])
    )
    first_blocks = [first_one, first_two, first_three, *first_copies]
    x_half, norm_vecs = local_call(
        partial(place_tokens_body, rows=rows, part=half_feats),
        low_outs(1, D, SPAN) + [((D, 8), wide)],
        "token_place",
        flags,
        *token_pieces,
    )
    x_half, trig, reweight = lax.optimization_barrier((x_half, trig, reweight))
    hidden_one, hidden_two = row_blocks(hidden_packed[0])
    x_got, hidden_one = lax.optimization_barrier((swap_cols(x_half), hidden_one))
    x_own, cot = local_call(
        partial(join_halves_body, rows=rows),
        low_outs(2, D, SPAN),
        "token_join",
        flags,
        x_half,
        x_got,
    )
    x_own, first_blocks = lax.optimization_barrier((x_own, first_blocks))
    x_other = swap_pair(x_own)
    state_shape = ((STATE_ROWS + SUM_ROWS, 2 * HD), low)
    sets = 2 * HEADS
    block_low = ((D, SPAN), low)
    block_wide = ((D, SPAN), wide)
    weight, qkv, state = local_call(
        project_body,
        [((D, 4 * WIDTH), low), ((2, 3 * WIDTH, SPAN), low), state_shape],
        "project",
        flags,
        x_own,
        x_other,
        trig,
        first_packed,
        *first_blocks,
    )
    hidden_three = swap_rows(hidden_two, 1)
    copy_two = swap_copies(hidden_two)
    arrived = [shift_rows(state, step) for step in range(1, rows)]
    arrived, hidden_three, copy_two = lax.optimization_barrier(
        (arrived, hidden_three, copy_two)
    )
    weights, numer, denom = local_call(
        block_body,
        [((sets, SPAN, SPAN), low), ((sets, HD, SPAN), wide), ((SUM_ROWS, SPAN), wide)],
        "block",
        qkv,
        trig,
        reweight,
    )
    prior, attn_wide, branch_own, branch_other = local_call(
        attend_body,
        [
            state_shape,
            ((STATE_ROWS + SUM_ROWS, SPAN), wide),
            block_wide,
            block_low,
        ],
        "attend",
        qkv,
        trig,
        numer,
        denom,
        weight,
        *arrived,
        scratch=[((2, WIDTH, SPAN), low)],
    )
    copy_one = swap_copies(hidden_one)
    branch_own, branch_other, copy_one = lax.optimization_barrier(
        (branch_own, branch_other, copy_one)
    )
    branch = column_parts(branch_own, branch_other, "branch_half")
    copy_three = swap_copies(hidden_three)
    branch, copy_three = lax.optimization_barrier((branch, copy_three))
    hidden_mine, hidden_copy = local_call(
        hidden_weights_body,
        low_outs(2, D, 2 * part),
        "hidden_weights",
        flags,
        hidden_packed[0],
        hidden_one,
        hidden_two,
        hidden_three,
        hidden_packed[1],
        copy_one,
        copy_two,
        copy_three,
    )
    branch, hidden_mine = lax.optimization_barrier((branch, hidden_mine))
    first, first_low, normed = local_call(
        norm_body,
        [block_wide, block_low, ((D + 8, SPAN), wide)],
        "norm",
        x_own,
        *branch,
        norm_vecs,
    )
    first_other = swap_pair(first_low)
    hidden_acts = [((part, 2 * SPAN), low)] * 4
    act_mine, act_copy, slope_mine, slope_copy, ffn_own, ffn_other = local_call(
        hidden_body,
        hidden_acts + [block_wide, block_low],
        "hidden",
        first_low,
        first_other,
        hidden_mine,
        hidden_copy,
    )
    ffn = column_parts(ffn_own, ffn_other, "ffn_half")
    result, grad_second, grad_ffn = local_call(
        second_norm_body,
        [block_low, ((D, SPAN + 2 * SUM_LANES), wide), block_low],
        "second_norm",
        first,
        *ffn,
        norm_vecs,
        cot,
        trig,
    )
    grad_ffn_other = swap_pair(grad_ffn)
    pair_low = ((D, part), low)
    down_held, down_sent = local_call(
        down_grad_body,
        low_outs(2, 2 * feat_rows, 2 * part),
        "down_grad",
        flags,
        grad_ffn,
        grad_ffn_other,
        act_mine,
        act_copy,
        scratch=[((D, 2 * part), low)],
    )
    down_got = swap_rows(down_sent, 1)
    grad_ffn, grad_ffn_other, down_held = lax.optimization_barrier(
        (grad_ffn, grad_ffn_other, down_held)
    )
    hidden_low = ((part, 2 * SPAN), low)
    pre_mine, pre_copy, first_own_part, first_other_part = local_call(
        hidden_back_body,
        [hidden_low, hidden_low, block_wide, block_low],
        "hidden_back",
        grad_ffn,
        grad_ffn_other,
        hidden_mine,
        hidden_copy,
        slope_mine,
        slope_copy,
    )
    first_sum = column_parts(first_own_part, first_other_part, "first_half")

    kept_up, sent_up = local_call(
        half_grads_body,
        [pair_low, pair_low],
        "up_grad",
        first_low,
        first_other,
        pre_mine,
        pre_copy,
    )
    got_up = swap_copies(sent_up)
    down_kept, down_pair = local_call(
        down_pairs_body,
        [((2 * feat_rows, part), wide), ((2 * feat_rows, part), low)],
        "down_pairs",
        down_held,
        down_got,
    )
    first_sum, kept_up, down_kept = lax.optimization_barrier((first_sum, kept_up, down_kept))
    grad_hidden, branch_grad, vec_sums = local_call(
        norm_back_body,
        [block_wide, block_low, ((D, 2 * SUM_LANES), low)],
        "norm_back",
        grad_second,
        *first_sum,
        normed,
        norm_vecs,
    )
    branch_grad_other = swap_pair(branch_grad)
    grad_num, grad_den, grad_state = local_call(
        grad_attend_body,
        [((sets, HD, SPAN), low), ((SUM_ROWS, SPAN), wide), state_shape],
        "grad_attend",
        branch_grad,
        branch_grad_other,
        weight,
        attn_wide,
        qkv,
        trig,
    )
    later = [shift_rows(grad_state, -step) for step in range(1, rows)]
    half_lanes = (WIDTH + SUM_LANES) // 2
    mix_kept, mix_sent = local_call(
        mix_body,
        [((D, half_lanes), low), ((2 * feat_rows, part + 2 * half_lanes), low)],
        "mix",
        flags,
        branch_grad,
        branch_grad_other,
        attn_wide,
        vec_sums,
        after(down_pair, grad_num),
        scratch=[((D, WIDTH + SUM_LANES), low)],
    )
    grad_query, grad_key, grad_value = local_call(
        grad_block_body,
        [
            ((2, WIDTH, SPAN), low),
            ((sets, HD, SPAN), wide),
            ((sets, HD, SPAN), wide),
        ],
        "grad_block",
        grad_num,
        grad_den,
        qkv,
        trig,
        reweight,
        weights,
        prior,
    )
    mix_got = swap_copies(after(mix_sent, got_up, grad_den))
    up_lanes = SPAN // 2 + part + half_lanes
    down_part, down_far = local_call(
        down_far_body,
        [((feat_rows, part), wide), ((feat_rows, part), low)],
        "down_far",
        down_kept,
        mix_got,
    )
    down_far = swap_rows(down_far, 2)
    up_held, up_sent = local_call(
        up_pieces_body,
        low_outs(2, 2 * feat_rows, up_lanes),
        "up_pieces",
        flags,
        result,
        kept_up,
        after(got_up, grad_query),
        mix_kept,
        mix_got,
        scratch=[((D, half_lanes), low)],
    )
    up_got = swap_rows(up_sent, 1)
    later, up_held = lax.optimization_barrier((later, up_held))
    half_rows = ((rows, half_feats, 3 * WIDTH), low)
    kept_w, sent_w, x_grad_own, x_grad_other = local_call(
        grad_project_body,
        [half_rows, half_rows, block_wide, block_low],
        "grad_project",
        grad_query,
        grad_key,
        grad_value,
        qkv,
        trig,
        x_own,
        x_other,
        weight,
        flags,
        *later,
        scratch=[state_shape, ((2, 3 * WIDTH, SPAN), low)],
    )
    got_w = swap_copies(sent_w)
    got_w = after(got_w, down_part)
    got_x = swap_pair(x_grad_other)
    x_half_grad, x_half_sent = local_call(
        partial(input_halves_body, rows=rows),
        [((D // 2, SPAN), wide), ((D // 2, SPAN), low)],
        "input_halves",
        flags,
        x_grad_own,
        got_x,
        scratch=[block_wide],
    )
    got_half = swap_cols(x_half_sent)
    last_lanes = 3 * WIDTH
    last_held, last_sent = local_call(
        last_pieces_body,
        low_outs(2, 2 * half_feats, last_lanes + SPAN),
        "last_pieces",
        flags,
        kept_w,
        got_w,
        x_half_grad,
        got_half,
        grad_hidden,
    )
    up_part, up_far = local_call(
        up_pairs_body,
        [((feat_rows, up_lanes - SPAN // 2), wide), ((feat_rows, up_lanes + SPAN // 2), low)],
        "up_pairs",
        up_held,
        up_got,
    )
    up_far = swap_rows(up_far, 2)
    last_got = swap_rows(last_sent, 1)
    last_part, last_far = local_call(
        last_pairs_body,
        [((half_feats, last_lanes), wide), ((half_feats, last_lanes + 2 * SPAN), low)],
        "last_pairs",
        last_held,
        last_got,
    )
    hidden_sum, *out_wide = local_call(
        hidden_sums_body,
        low_outs(1, feat_rows, 2 * part + half_lanes)
        + low_outs(2, half_feats, SPAN * rows // 2),
        "hidden_sums",
        flags,
        down_part,
        down_far,
        up_part,
        up_held,
        up_got,
        up_far,
        scratch=[((4, half_feats, SPAN), low)],
    )
    last_sum, *input_wide = local_call(
        last_sums_body,
        low_outs(1, half_feats, last_lanes) + low_outs(2, half_feats, SPAN * rows // 2),
        "last_sums",
        flags,
        last_part,
        last_held,
        last_got,
        swap_rows(last_far, 2),
    )
    output = cols_back(*out_wide, low, "out_join")
    down_t, up_grad, out_t, *vec_sums_all = local_call(
        place_hidden_body,
        [((feat_rows, 4 * part), wide)] * 2
        + [((feat_rows, 2 * WIDTH), wide)]
        + [((1, feat_rows), wide)] * 4,
        "place_hidden",
        flags,
        *all_quarters(hidden_sum, True),
    )
    last_parts = all_quarters(last_sum, True)
    last_parts = (after(last_parts[0], up_grad), *last_parts[1:])
    input_grad, query_grad, key_grad, value_grad = local_call(
        place_last_body,
        [((feat_rows, SPAN * rows // 2), wide)] + [((feat_rows, 2 * WIDTH), wide)] * 3,
        "place_last",
        flags,
        *last_parts,
        input_wide[0],
        swap_cols(input_wide[1]),
    )
    return (
        output,
        input_grad,
        query_grad,
        key_grad,
        value_grad,
        out_t.T,
        vec_sums_all[0].reshape(feat_rows),
        vec_sums_all[1].reshape(feat_rows),
        up_grad,
        down_t.T,
        vec_sums_all[2].reshape(feat_rows),
        vec_sums_all[3].reshape(feat_rows),
    )


def solution(mesh):
    placed = (
        P("row", ("dp", "col")),
        P(),
        P("row", "col"),
        P("row", "col"),
        P("row", "col"),
        P("col", "row"),
        P("row"),
        P("row"),
        P("row", "col"),
        P("col", "row"),
        P("row"),
        P("row"),
        P("row", ("dp", "col")),
    )
    return jax.shard_map(
        on_device_paired if paired_layout(mesh) else on_device,
        mesh=mesh,
        in_specs=placed,
        out_specs=(
            P("row", ("dp", "col")),
            P("row", ("dp", "col")),
            P("row", "col"),
            P("row", "col"),
            P("row", "col"),
            P("col", "row"),
            P("row"),
            P("row"),
            P("row", "col"),
            P("col", "row"),
            P("row"),
            P("row"),
        ),
        check_vma=False,
    )
```

```python
from functools import partial
import math

import jax
import jax.numpy as jnp
from jax import lax
from jax.experimental import pallas as pl
from jax.experimental.pallas import tpu as pltpu
from jax.sharding import PartitionSpec as P

D = 768
H = 12
HD = 64
SEQ_MAX = 4096
TOK_DEV = 128


norm_eps = 1e-05
highest = lax.Precision.HIGHEST


def carried_in(shard, axis, join, neutral, backward):
    count = lax.axis_size(axis)
    place = lax.axis_index(axis)
    ahead = count - 1 - place if backward else place
    gathered = jax.tree.map(
        lambda a, kind: lax.all_gather(a.astype(kind), axis),
        shard,
        jax.tree.map(lambda a: jnp.bfloat16 if a.dtype == jnp.float32 else a.dtype, shard),
    )
    state = jax.tree.map(lambda a, e: jnp.zeros_like(a) + jnp.asarray(e, a.dtype), shard, neutral)

    def one(turn, state):
        source = count - 1 - turn if backward else turn
        return join(
            state,
            jax.tree.map(
                lambda a, own: lax.dynamic_index_in_dim(a, source, 0, False).astype(own.dtype),
                gathered,
                shard,
            ),
        )

    return lax.fori_loop(0, ahead, one, state)


def gather_cols(operand):
    return lax.all_gather(operand, "col", axis=0, tiled=True)


def gather_rows(operand):
    return lax.all_gather(operand, "row", axis=0, tiled=True)


def summed_over_rows(gathered, matrix):
    out_rows = gathered.shape[0] // lax.axis_size("row")

    def term_rows(first_row, row_count):
        sliced = lax.dynamic_slice_in_dim(gathered, first_row, row_count, 0)
        return jnp.dot(sliced, matrix, preferred_element_type=jnp.float32)

    return lax.psum_scatter(
        term_rows(jnp.int32(0), out_rows * lax.axis_size("row")),
        "row",
        scatter_dimension=0,
        tiled=True,
    )


def summed_over_cols(gathered, matrix):
    out_rows = gathered.shape[0] // lax.axis_size("col")

    def term_rows(first_row, row_count):
        sliced = lax.dynamic_slice_in_dim(gathered, first_row, row_count, 0)
        return jnp.dot(sliced, matrix, preferred_element_type=jnp.float32)

    return lax.psum_scatter(
        term_rows(jnp.int32(0), out_rows * lax.axis_size("col")).astype(jnp.bfloat16),
        "col",
        scatter_dimension=0,
        tiled=True,
    ).astype(jnp.float32)


def to_heads(stacked):
    return lax.all_to_all(stacked, "col", split_axis=1, concat_axis=2, tiled=True)


def to_tokens(stacked):
    return lax.all_to_all(stacked, "col", split_axis=2, concat_axis=1, tiled=True)


def row_totals(first_part, second_part):
    return lax.psum((first_part, second_part), "row")


def norm_forward(hidden, scale_vec, shift_vec):
    sum_one, sum_two = row_totals(jnp.sum(hidden, 1), jnp.sum(hidden * hidden, 1))
    row_mean = sum_one / D
    variance = sum_two / D - row_mean * row_mean
    inv_std = lax.rsqrt(variance + norm_eps)
    normed = (hidden - row_mean[:, None]) * inv_std[:, None]
    return (normed * scale_vec + shift_vec, normed, inv_std)


def norm_backward(grad_in, normed, inv_std, scale_vec):
    grad_normed = grad_in * scale_vec
    total_one, total_two = row_totals(jnp.sum(grad_normed, 1), jnp.sum(grad_normed * normed, 1))
    grad_hidden = inv_std[:, None] * (
        grad_normed - total_one[:, None] / D - normed * (total_two[:, None] / D)
    )
    return (grad_hidden, jnp.sum(grad_in * normed, 0), jnp.sum(grad_in, 0))


def seq_lengths(lengths, seq_ids):
    matches = seq_ids[:, None] == jnp.arange(lengths.shape[0], dtype=jnp.int32)[None, :]
    return jnp.sum(jnp.where(matches, lengths[None, :], 0), 1)


def reset_combine(earlier, later):
    keep_prior = 1.0 - later[4]
    joined = tuple(
        (
            keep_prior * prior_part + next_part
            for prior_part, next_part in zip(earlier[:4], later[:4])
        )
    )
    return joined + (jnp.maximum(earlier[4], later[4]),)


def empty_state():
    return (
        jnp.zeros((H, HD, HD), jnp.float32),
        jnp.zeros((H, HD, HD), jnp.float32),
        jnp.zeros((H, HD), jnp.float32),
        jnp.zeros((H, HD), jnp.float32),
        jnp.zeros((), jnp.float32),
    )


def attend_forward(queries, keys_in, values_in, present, cos_flat, sin_flat, opens_seq):
    block_rows = queries.shape[0]
    cos_pos = cos_flat[:, None, None]
    sin_pos = sin_flat[:, None, None]
    q_pos = jnp.maximum(queries, 0)
    k_pos = jnp.maximum(keys_in, 0) * present[:, None, None].astype(jnp.bfloat16)
    q_cos = q_pos.astype(jnp.float32) * cos_pos
    q_sin = q_pos.astype(jnp.float32) * sin_pos
    k_cos = k_pos.astype(jnp.float32) * cos_pos
    k_sin = k_pos.astype(jnp.float32) * sin_pos
    values_wide = values_in.astype(jnp.float32)
    local_state = (
        jnp.einsum("jhd,jhe->hde", k_cos, values_wide, precision=highest),
        jnp.einsum("jhd,jhe->hde", k_sin, values_wide, precision=highest),
        jnp.sum(k_cos, 0),
        jnp.sum(k_sin, 0),
    )
    arrived = carried_in(
        local_state + (opens_seq,), ("row", "col"), reset_combine, empty_state(), False
    )
    s_cos, s_sin, z_cos, z_sin = tuple(
        (state_part * (1.0 - opens_seq) for state_part in arrived[:4])
    )
    row_ids = jnp.arange(block_rows, dtype=jnp.int32)
    causal = (row_ids[:, None] >= row_ids[None, :]).astype(jnp.float32)
    reweight = (
        cos_flat[:, None] * cos_flat[None, :] + sin_flat[:, None] * sin_flat[None, :]
    ) * causal
    scores = jnp.einsum("ihd,jhd->hij", q_pos, k_pos, preferred_element_type=jnp.float32)
    weights = scores * reweight[None]
    weights_low = weights.astype(jnp.bfloat16)
    numerator = jnp.einsum(
        "hij,jhe->ihe", weights_low, values_in, preferred_element_type=jnp.float32
    )
    numerator = numerator + jnp.einsum("ihd,hde->ihe", q_cos, s_cos, precision=highest)
    numerator = numerator + jnp.einsum("ihd,hde->ihe", q_sin, s_sin, precision=highest)
    denominator = 1.0 + jnp.sum(weights, 2).T
    denominator = denominator + jnp.einsum("ihd,hd->ih", q_cos, z_cos, precision=highest)
    denominator = denominator + jnp.einsum("ihd,hd->ih", q_sin, z_sin, precision=highest)
    mixed = (numerator / denominator[:, :, None]).astype(jnp.bfloat16).reshape(block_rows, D)
    kept = (
        queries,
        keys_in,
        values_in,
        q_pos,
        k_pos,
        q_cos,
        q_sin,
        k_cos,
        k_sin,
        values_wide,
        reweight,
        weights_low,
        numerator,
        denominator,
        s_cos,
        s_sin,
        z_cos,
        z_sin,
        present,
        cos_pos,
        sin_pos,
    )
    return (mixed, kept)


def attend_backward(grad_heads, kept, closes_seq):
    (
        queries,
        keys_in,
        values_in,
        q_pos,
        k_pos,
        q_cos,
        q_sin,
        k_cos,
        k_sin,
        values_wide,
        reweight,
        weights_low,
        numerator,
        denominator,
        s_cos,
        s_sin,
        z_cos,
        z_sin,
        present,
        cos_pos,
        sin_pos,
    ) = kept
    block_rows = queries.shape[0]
    grad_attn = grad_heads.astype(jnp.float32).reshape(block_rows, H, HD)
    grad_num_low = (grad_attn / denominator[:, :, None]).astype(jnp.bfloat16)
    grad_num = grad_num_low.astype(jnp.float32)
    grad_den = -jnp.sum(grad_attn * numerator, 2) / (denominator * denominator)
    grad_weights = jnp.einsum(
        "ihe,jhe->hij", grad_num_low, values_in, preferred_element_type=jnp.float32
    )
    grad_weights = grad_weights + grad_den.T[:, :, None]
    grad_scores = (grad_weights * reweight[None]).astype(jnp.bfloat16)
    local_grad = (
        jnp.einsum("ihd,ihe->hde", q_cos, grad_num, precision=highest),
        jnp.einsum("ihd,ihe->hde", q_sin, grad_num, precision=highest),
        jnp.einsum("ihd,ih->hd", q_cos, grad_den, precision=highest),
        jnp.einsum("ihd,ih->hd", q_sin, grad_den, precision=highest),
    )
    later_sum = carried_in(
        local_grad + (closes_seq,), ("row", "col"), reset_combine, empty_state(), True
    )
    g_cos, g_sin, gz_cos, gz_sin = tuple(
        (state_part * (1.0 - closes_seq) for state_part in later_sum[:4])
    )
    grad_qpos = jnp.einsum("hij,jhd->ihd", grad_scores, k_pos, preferred_element_type=jnp.float32)
    grad_qpos = grad_qpos + cos_pos * (
        jnp.einsum("ihe,hde->ihd", grad_num, s_cos, precision=highest)
        + grad_den[:, :, None] * z_cos[None]
    )
    grad_qpos = grad_qpos + sin_pos * (
        jnp.einsum("ihe,hde->ihd", grad_num, s_sin, precision=highest)
        + grad_den[:, :, None] * z_sin[None]
    )
    grad_kpos = jnp.einsum("hij,ihd->jhd", grad_scores, q_pos, preferred_element_type=jnp.float32)
    grad_kpos = grad_kpos + cos_pos * (
        jnp.einsum("jhe,hde->jhd", values_wide, g_cos, precision=highest) + gz_cos[None]
    )
    grad_kpos = grad_kpos + sin_pos * (
        jnp.einsum("jhe,hde->jhd", values_wide, g_sin, precision=highest) + gz_sin[None]
    )
    grad_values = jnp.einsum(
        "hij,ihe->jhe", weights_low, grad_num_low, preferred_element_type=jnp.float32
    )
    grad_values = grad_values + jnp.einsum("jhd,hde->jhe", k_cos, g_cos, precision=highest)
    grad_values = grad_values + jnp.einsum("jhd,hde->jhe", k_sin, g_sin, precision=highest)
    grad_q = (grad_qpos * (queries > 0).astype(jnp.float32)).astype(jnp.bfloat16)
    grad_k = (grad_kpos * (keys_in > 0).astype(jnp.float32) * present[:, None, None]).astype(
        jnp.bfloat16
    )
    grad_v = grad_values.astype(jnp.bfloat16)
    return (
        grad_q.reshape(block_rows, D),
        grad_k.reshape(block_rows, D),
        grad_v.reshape(block_rows, D),
    )


def on_device(
    tokens,
    lengths,
    w_query,
    w_key,
    w_value,
    w_out,
    gain_one,
    bias_one,
    w_up,
    w_down,
    gain_two,
    bias_two,
    cotangent,
):
    row_count = lax.axis_size("row")
    col_count = lax.axis_size("col")
    seq_len = min(SEQ_MAX, TOK_DEV * row_count * col_count)
    data_idx = lax.axis_index("dp")
    row_idx = lax.axis_index("row")
    col_idx = lax.axis_index("col")
    feat_rows = tokens.shape[0]
    group_idx = row_idx * col_count + col_idx
    global_idx = (data_idx * row_count * col_count + group_idx) * TOK_DEV + jnp.arange(
        TOK_DEV, dtype=jnp.int32
    )
    positions = global_idx % seq_len
    present = (positions < seq_lengths(lengths, global_idx // seq_len)).astype(jnp.float32)
    angles = math.pi * positions.astype(jnp.float32) / (2.0 * seq_len)
    cos_flat = jnp.cos(angles)
    sin_flat = jnp.sin(angles)
    opens_seq = (group_idx * TOK_DEV % seq_len == 0).astype(jnp.float32)
    closes_seq = ((group_idx + 1) * TOK_DEV % seq_len == 0).astype(jnp.float32)
    token_rows = tokens.T
    width_col = w_query.shape[1]
    w_cat = jnp.concatenate([w_query, w_key, w_value], 1)
    x_gathered = gather_cols(token_rows)
    qkv = summed_over_rows(x_gathered, w_cat).astype(jnp.bfloat16)
    stacked = jnp.stack(
        [qkv[:, :width_col], qkv[:, width_col : 2 * width_col], qkv[:, 2 * width_col :]], 0
    )
    head_rows = to_heads(stacked)
    mixed, kept = attend_forward(
        head_rows[0].reshape(TOK_DEV, H, HD),
        head_rows[1].reshape(TOK_DEV, H, HD),
        head_rows[2].reshape(TOK_DEV, H, HD),
        present,
        cos_flat,
        sin_flat,
        opens_seq,
    )
    mixed_two = to_tokens(mixed[None])[0]
    mixed_gathered = gather_rows(mixed_two)
    branch = summed_over_cols(mixed_gathered, w_out)
    first, normed_one, inv_one = norm_forward(
        token_rows.astype(jnp.float32) + branch, gain_one, bias_one
    )
    first_low = first.astype(jnp.bfloat16)
    first_gathered = gather_cols(first_low)
    pre = summed_over_rows(first_gathered, w_up)
    act, gelu_pull = jax.vjp(partial(jax.nn.gelu, approximate=False), pre)
    act_low = act.astype(jnp.bfloat16)
    act_gathered = gather_rows(act_low)
    ffn = summed_over_cols(act_gathered, w_down)
    result, normed_two, inv_two = norm_forward(first + ffn, gain_two, bias_two)
    rows_one = token_rows.shape[0]
    global_one = (data_idx * col_count + col_idx) * rows_one + jnp.arange(rows_one, dtype=jnp.int32)
    present_one = (global_one % seq_len < seq_lengths(lengths, global_one // seq_len)).astype(
        jnp.float32
    )
    grad_result = cotangent.T.astype(jnp.float32) * present_one[:, None]
    grad_second, grad_gain_two, grad_bias_two = norm_backward(
        grad_result, normed_two, inv_two, gain_two
    )
    grad_ffn_gathered = gather_cols(grad_second.astype(jnp.bfloat16))
    act_again = gather_rows(act_low)
    grad_down = jnp.einsum(
        "tf,td->fd", act_again, grad_ffn_gathered, preferred_element_type=jnp.float32
    )
    grad_act = summed_over_rows(grad_ffn_gathered, w_down.T)
    grad_pre = gelu_pull(grad_act)[0].astype(jnp.bfloat16)
    grad_pre_gathered = gather_rows(grad_pre)
    first_again = gather_cols(first_low)
    grad_up = jnp.einsum(
        "td,tf->df", first_again, grad_pre_gathered, preferred_element_type=jnp.float32
    )
    grad_first = summed_over_cols(grad_pre_gathered, w_up.T) + grad_second
    grad_hidden, grad_gain_one, grad_bias_one = norm_backward(
        grad_first, normed_one, inv_one, gain_one
    )
    branch_grad_gathered = gather_cols(grad_hidden.astype(jnp.bfloat16))
    mixed_again = gather_rows(mixed_two)
    grad_out = jnp.einsum(
        "tc,tr->cr", mixed_again, branch_grad_gathered, preferred_element_type=jnp.float32
    )
    grad_mixed = summed_over_rows(branch_grad_gathered, w_out.T).astype(jnp.bfloat16)
    grad_heads = to_heads(grad_mixed[None])[0]
    grad_q, grad_k, grad_v = attend_backward(grad_heads, kept, closes_seq)
    grad_rows = to_tokens(jnp.stack([grad_q, grad_k, grad_v], 0))
    grad_cat = jnp.concatenate([grad_rows[0], grad_rows[1], grad_rows[2]], 1)
    grad_cat_gathered = gather_rows(grad_cat)
    x_again = gather_cols(token_rows)
    grad_cat_w = jnp.einsum(
        "tr,tc->rc", x_again, grad_cat_gathered, preferred_element_type=jnp.float32
    )
    input_rows = summed_over_cols(grad_cat_gathered, w_cat.T) + grad_hidden
    gain_parts = jnp.stack([grad_gain_one, grad_bias_one, grad_gain_two, grad_bias_two], 0)
    gain_sums = lax.psum(gain_parts.reshape(4 * feat_rows), "col")
    grad_query = grad_cat_w[:, :width_col]
    grad_key = grad_cat_w[:, width_col : 2 * width_col]
    grad_value = grad_cat_w[:, 2 * width_col :]
    output = result.astype(jnp.bfloat16).T
    input_grad = input_rows.T
    sums = (
        lax.psum(grad_query.astype(jnp.bfloat16), "dp").astype(jnp.float32),
        lax.psum(grad_key.astype(jnp.bfloat16), "dp").astype(jnp.float32),
        lax.psum(grad_value.astype(jnp.bfloat16), "dp").astype(jnp.float32),
        lax.psum(grad_out.astype(jnp.bfloat16), "dp").astype(jnp.float32),
        lax.psum(grad_up.astype(jnp.bfloat16), "dp").astype(jnp.float32),
        lax.psum(grad_down.astype(jnp.bfloat16), "dp").astype(jnp.float32),
        lax.psum(gain_sums.astype(jnp.bfloat16), "dp").astype(jnp.float32),
    )
    gain_total = sums[6].reshape(4, feat_rows)
    return (
        output,
        input_grad,
        sums[0],
        sums[1],
        sums[2],
        sums[3],
        gain_total[0],
        gain_total[1],
        sums[4],
        sums[5],
        gain_total[2],
        gain_total[3],
    )


def paired_layout(mesh):
    rows, cols, dps = mesh.shape["row"], mesh.shape["col"], mesh.shape["dp"]
    return rows == 4 and cols == 2 and dps == 4 and H % 4 == 0 and 8 * TOK_DEV <= SEQ_MAX


low = jnp.bfloat16
wide = jnp.float32
SPAN = 2 * TOK_DEV
HEADS = H // 4
WIDTH = HEADS * HD
STATE_ROWS = 2 * HEADS * HD
SUM_ROWS = 16
SUM_LANES = 64


def swap_cols(operand):
    return lax.ppermute(operand, "col", [(0, 1), (1, 0)])


def swap_pair(operand):
    return lax.ppermute(operand, "dp", [(i, i ^ 1) for i in range(lax.axis_size("dp"))])


def swap_copies(operand):
    return lax.ppermute(operand, "dp", [(i, i ^ 2) for i in range(lax.axis_size("dp"))])


def shift_rows(operand, step):
    count = lax.axis_size("row")
    pairs = [(i, i + step) for i in range(count) if 0 <= i + step < count]
    return lax.ppermute(operand, "row", pairs)


def swap_rows(operand, mask):
    return lax.ppermute(operand, "row", [(i, i ^ mask) for i in range(4)])


def rotate_rows(operand, step):
    count = lax.axis_size("row")
    return lax.ppermute(operand, "row", [(i, (i + step) % count) for i in range(count)])


def dot_tn(left, right):
    return lax.dot_general(left, right, (((0,), (0,)), ((), ())), preferred_element_type=wide)


def dot_nt(left, right):
    return lax.dot_general(left, right, (((1,), (1,)), ((), ())), preferred_element_type=wide)


def dot_nn(left, right):
    return jnp.dot(left, right, preferred_element_type=wide)


def norm_columns(hidden, scale, shift):
    mean = jnp.mean(hidden, 0, keepdims=True)
    centered = hidden - mean
    variance = jnp.mean(centered * centered, 0, keepdims=True)
    inv_std = lax.rsqrt(variance + norm_eps)
    normed = centered * inv_std
    return (normed * scale + shift, normed, inv_std)


def norm_columns_back(grad_in, normed, inv_std, scale):
    grad_normed = grad_in * scale
    mean_one = jnp.mean(grad_normed, 0, keepdims=True)
    mean_two = jnp.mean(grad_normed * normed, 0, keepdims=True)
    return inv_std * (grad_normed - mean_one - normed * mean_two)


def local_call(body, outs, name, *operands, scratch=(), space=None):
    shapes = [jax.ShapeDtypeStruct(shape, kind) for shape, kind in outs]
    return pl.pallas_call(
        body,
        out_shape=shapes,
        in_specs=[
            pl.BlockSpec(
                memory_space=pltpu.SMEM
                if operand.dtype == jnp.int32
                else space or pltpu.VMEM
            )
            for operand in operands
        ],
        out_specs=[pl.BlockSpec(memory_space=pltpu.VMEM)] * len(outs),
        scratch_shapes=[
            pltpu.VMEM(*kind) if isinstance(kind, tuple) else kind for kind in scratch
        ],
        compiler_params=pltpu.CompilerParams(vmem_limit_bytes=24 * 2**20),
        name=name,
    )(*operands)


CORE, COPY, ROW, COL, SEQ = range(5)


def low_outs(count, *shape):
    return [(shape, low)] * count


def turn_body(flags_ref, lengths_ref, trig_ref, reweight_ref, *, seq_len):
    start = flags_ref[ROW] * SPAN
    positions = start + lax.broadcasted_iota(jnp.int32, (8, SPAN), 1)
    lines = lax.broadcasted_iota(jnp.int32, (8, SPAN), 0)
    angles = math.pi * positions.astype(wide) / (2.0 * seq_len)
    turns = jnp.where(lines == 0, jnp.cos(angles), jnp.where(lines == 1, jnp.sin(angles), 0.0))
    own = lengths_ref[flags_ref[SEQ]]
    other = lengths_ref[flags_ref[SEQ] + 1 - 2 * flags_ref[CORE]]
    limits = jnp.where(lines == 2, own, other)
    present = jnp.where(positions < limits, 1.0, 0.0)
    trig_ref[...] = turns + jnp.where(lines == 2, present, jnp.where(lines == 3, present, 0.0))
    rows = lax.broadcasted_iota(jnp.int32, (SPAN, SPAN), 0)
    cols = lax.broadcasted_iota(jnp.int32, (SPAN, SPAN), 1)
    both = lax.dot_general(
        turns, turns, (((0,), (0,)), ((), ())), precision=highest, preferred_element_type=wide
    )
    reweight_ref[...] = jnp.where(rows <= cols, both, 0.0)


def token_piece(flags_ref, own_ref, recv_ref, step, rows):
    place = lax.rem(flags_ref[ROW] + step, rows)
    half = lax.div(place, rows // 2)
    cols = pl.ds(pl.multiple_of(lax.rem(place, rows // 2) * SPAN, SPAN), SPAN)
    return jnp.where(half == flags_ref[COL], own_ref[:, cols], recv_ref[:, cols])


def pieces_body(flags_ref, own_ref, cot_ref, recv_ref, *refs, rows):
    vec_ref, piece_refs = refs[0], refs[1:]
    part = own_ref.shape[0]
    lines = []
    for line in range(4):
        vec = vec_ref[line : line + 1, :]
        vec = jnp.concatenate([vec, jnp.zeros((1, SPAN - vec.shape[1]), wide)], 1)
        high = vec.astype(low).astype(wide)
        lines = lines + [high, vec - high]
    for step, ref in enumerate(piece_refs):
        ref[:part] = token_piece(flags_ref, own_ref, recv_ref.at[:part], step, rows)
        ref[part : 2 * part] = token_piece(flags_ref, cot_ref, recv_ref.at[part:], step, rows)
        ref[2 * part :] = jnp.concatenate(lines + [jnp.zeros((8, SPAN), wide)], 0).astype(low)


def came_from(flags_ref, step, rows):
    return lax.rem(flags_ref[ROW] + rows - step, rows)


def place_tokens_body(flags_ref, *refs, rows, part):
    pieces, (half_ref, vec_ref) = refs[:rows], refs[rows:]
    below = half_ref.shape[0] // 2
    for step, ref in enumerate(pieces):
        row = came_from(flags_ref, step, rows)
        half_ref[pl.ds(pl.multiple_of(row * part, 16), part), :] = ref[:part]
        half_ref[pl.ds(pl.multiple_of(below + row * part, 16), part), :] = ref[part : 2 * part]
        extra = ref[2 * part :].astype(wide)
        sums = [extra[2 * i : 2 * i + 1] + extra[2 * i + 1 : 2 * i + 2] for i in range(4)]
        columns = jnp.concatenate(sums + [jnp.zeros((4, SPAN), wide)], 0).T
        vec_ref[pl.ds(pl.multiple_of(row * 2 * part, 8), 2 * part), :] = columns[: 2 * part]


def join_halves_body(flags_ref, half_ref, recv_ref, x_ref, cot_ref, *, rows):
    part = half_ref.shape[0] // (2 * rows)
    first_col = flags_ref[COL] == 0
    for place, full_ref in enumerate((x_ref, cot_ref)):
        for row in range(rows):
            source = (place * rows + row) * part
            own = half_ref[source : source + part]
            other = recv_ref[source : source + part]
            start = 2 * row * part
            full_ref[start : start + part] = jnp.where(first_col, own, other)
            full_ref[start + part : start + 2 * part] = jnp.where(first_col, other, own)


def add_body(own_ref, recv_ref, half_ref):
    half_ref[...] = (own_ref[...] + recv_ref[...].astype(wide)).astype(low)


def feature_piece(flags_ref, source, step, rows):
    part = source.shape[0] // (2 * rows)
    start = (lax.rem(flags_ref[ROW] + step, rows) * 2 + flags_ref[COL]) * part
    return source[pl.ds(pl.multiple_of(start, 16), part), :]


def place_back(flags_ref, pieces, rows, own_ref, other_ref):
    half = len(pieces) // 2
    for row, piece in zip(rows, pieces):
        cols = pl.ds(pl.multiple_of(lax.rem(row, half) * SPAN, SPAN), SPAN)
        mine = lax.div(row, half) == flags_ref[COL]

        @pl.when(mine)
        def _(piece=piece, cols=cols):
            own_ref[:, cols] = piece[...]

        @pl.when(jnp.logical_not(mine))
        def _(piece=piece, cols=cols):
            other_ref[:, cols] = piece[...]


def sum_of(refs):
    total = refs[0][...].astype(wide)
    for ref in refs[1:]:
        total = total + ref[...].astype(wide)
    return total


def join_back_body(flags_ref, own_ref, recv_ref, out_ref):
    part = own_ref.shape[0]
    first_col = flags_ref[COL] == 0
    out_ref[:part] = jnp.where(first_col, own_ref[...], recv_ref[...]).astype(out_ref.dtype)
    out_ref[part:] = jnp.where(first_col, recv_ref[...], own_ref[...]).astype(out_ref.dtype)


def input_halves_body(flags_ref, own_ref, recv_ref, half_ref, sent_ref, sum_ref, *, rows):
    part = own_ref.shape[0] // (2 * rows)
    sum_ref[...] = own_ref[...] + recv_ref[...].astype(wide)
    for row in range(rows):
        rows_out = slice(row * part, (row + 1) * part)
        mine = pl.multiple_of((2 * row + flags_ref[COL]) * part, 16)
        theirs = pl.multiple_of((2 * row + 1 - flags_ref[COL]) * part, 16)
        half_ref[rows_out] = sum_ref[pl.ds(mine, part), :]
        sent_ref[rows_out] = sum_ref[pl.ds(theirs, part), :].astype(low)


def last_pieces_body(
    flags_ref, kept_ref, got_ref, half_ref, recv_ref, hidden_ref, held_ref, sent_ref
):
    rows = kept_ref.shape[0]
    part = half_ref.shape[0] // rows
    lanes = kept_ref.shape[2]
    for mask in range(rows):
        ref = sent_ref if mask % 2 else held_ref
        out = slice(mask // 2 * part, (mask // 2 + 1) * part)
        place = partner(flags_ref[ROW], mask)
        ref[out, :lanes] = (kept_ref[place].astype(wide) + got_ref[place].astype(wide)).astype(low)
        rows_in = pl.ds(pl.multiple_of(place * part, 16), part)
        total = half_ref[rows_in, :] + recv_ref[rows_in, :].astype(wide)
        start = pl.multiple_of((place * 2 + flags_ref[COL]) * part, 16)
        ref[out, lanes:] = (total + hidden_ref[pl.ds(start, part), :]).astype(low)


def last_pairs_body(held_ref, got_ref, sum_ref, sent_ref):
    part, lanes = sum_ref.shape
    sum_ref[...] = held_ref[:part, :lanes].astype(wide) + got_ref[:part, :lanes].astype(wide)
    pair = held_ref[part:, :lanes].astype(wide) + got_ref[part:, :lanes].astype(wide)
    sent_ref[:, :lanes] = pair.astype(low)
    sent_ref[:, lanes : lanes + SPAN] = held_ref[part:, lanes:]
    sent_ref[:, lanes + SPAN :] = got_ref[part:, lanes:]


def last_sums_body(
    flags_ref, part_ref, held_ref, got_ref, far_ref, sum_ref, own_ref, other_ref
):
    part, lanes = part_ref.shape
    sum_ref[...] = (part_ref[...] + far_ref[:, :lanes].astype(wide)).astype(low)
    pieces = (
        held_ref.at[:part, lanes:],
        got_ref.at[:part, lanes:],
        far_ref.at[:, lanes : lanes + SPAN],
        far_ref.at[:, lanes + SPAN :],
    )
    rows = [partner(flags_ref[ROW], mask) for mask in range(4)]
    place_back(flags_ref, pieces, rows, own_ref, other_ref)


def down_grad_body(
    flags_ref, own_ref, other_ref, mine_ref, copy_ref, held_ref, sent_ref, grad_ref
):
    feats, part = held_ref.shape[0] // 2, mine_ref.shape[0]
    for act_ref, cols in ((mine_ref, slice(0, part)), (copy_ref, slice(part, 2 * part))):
        grad_ref[:, cols] = (
            dot_nt(own_ref[...], act_ref[:, :SPAN]) + dot_nt(other_ref[...], act_ref[:, SPAN:])
        ).astype(low)
    for mask in range(4):
        ref = sent_ref if mask % 2 else held_ref
        start = mask // 2 * feats
        place = partner(flags_ref[ROW], mask)
        rows_in = pl.ds(pl.multiple_of(place * feats, 16), feats)
        ref[start : start + feats, :] = grad_ref[rows_in, :]


def down_pairs_body(held_ref, got_ref, kept_ref, sent_ref):
    part = kept_ref.shape[1]
    kept_ref[...] = held_ref[:, :part].astype(wide) + got_ref[:, :part].astype(wide)
    sent_ref[...] = (held_ref[:, part:].astype(wide) + got_ref[:, part:].astype(wide)).astype(low)


def mix_body(
    flags_ref, own_ref, other_ref, attn_wide_ref, vec_ref, pair_ref, kept_ref, sent_ref, grad_ref
):
    grad_ref[:, :WIDTH] = (
        dot_nt(own_ref[...], attn_wide_ref[:WIDTH, :].astype(low))
        + dot_nt(other_ref[...], attn_wide_ref[WIDTH : 2 * WIDTH, :].astype(low))
    ).astype(low)
    grad_ref[:, WIDTH:] = vec_ref[:, :SUM_LANES]
    first_copy = flags_ref[COPY] == 0
    half = (WIDTH + SUM_LANES) // 2
    kept_ref[...] = jnp.where(first_copy, grad_ref[:, :half], grad_ref[:, half:])
    sent = jnp.where(first_copy, grad_ref[:, half:], grad_ref[:, :half])
    lines, part = pair_ref.shape
    sent_ref[:, :part] = pair_ref[...]
    sent_ref[:, part : part + half] = sent[:lines]
    sent_ref[:, part + half :] = sent[lines:]


def down_far_body(kept_ref, got_ref, sum_ref, sent_ref):
    feats, part = sum_ref.shape
    sum_ref[...] = kept_ref[:feats] + got_ref[:feats, :part].astype(wide)
    sent_ref[...] = (kept_ref[feats:] + got_ref[feats:, :part].astype(wide)).astype(low)


def up_pieces_body(
    flags_ref, result_ref, kept_ref, got_ref, mix_ref, mix_got_ref, held_ref, sent_ref, sum_ref
):
    feats, part = kept_ref.shape[0] // 4, kept_ref.shape[1]
    half, lanes = feats // 2, SPAN // 2
    lines, cols = mix_got_ref.shape[0], mix_ref.shape[1]
    sum_ref[:lines] = (
        mix_ref[:lines].astype(wide) + mix_got_ref[:, part : part + cols].astype(wide)
    ).astype(low)
    sum_ref[lines:] = (
        mix_ref[lines:].astype(wide) + mix_got_ref[:, part + cols :].astype(wide)
    ).astype(low)
    for mask in range(4):
        ref = sent_ref if mask % 2 else held_ref
        start = mask // 2 * feats
        out = slice(start, start + feats)
        place = partner(flags_ref[ROW], mask)
        rows_in = pl.ds(pl.multiple_of((place * 2 + flags_ref[COL]) * half, 16), half)
        ref[start : start + half, :lanes] = result_ref[rows_in, :lanes]
        ref[start + half : start + feats, :lanes] = result_ref[rows_in, lanes:]
        rows_in = pl.ds(pl.multiple_of(place * feats, 16), feats)
        ref[out, lanes : lanes + part] = (
            kept_ref[rows_in, :].astype(wide) + got_ref[rows_in, :].astype(wide)
        ).astype(low)
        ref[out, lanes + part :] = sum_ref[rows_in, :]


def up_pairs_body(held_ref, got_ref, sum_ref, sent_ref):
    feats, total = held_ref.shape[0] // 2, held_ref.shape[1]
    lanes = SPAN // 2
    sum_ref[...] = held_ref[:feats, lanes:].astype(wide) + got_ref[:feats, lanes:].astype(wide)
    pair = held_ref[feats:, lanes:].astype(wide) + got_ref[feats:, lanes:].astype(wide)
    sent_ref[:, :lanes] = held_ref[feats:, :lanes]
    sent_ref[:, lanes:total] = pair.astype(low)
    sent_ref[:, total:] = got_ref[feats:, :lanes]


def hidden_sums_body(
    flags_ref,
    down_ref,
    down_far_ref,
    up_ref,
    held_ref,
    got_ref,
    far_ref,
    sum_ref,
    own_ref,
    other_ref,
    piece_ref,
):
    feats, part = down_ref.shape
    lanes = SPAN // 2
    total = lanes + up_ref.shape[1]
    sum_ref[:, :part] = (down_ref[...] + down_far_ref[...].astype(wide)).astype(low)
    sum_ref[:, part:] = (up_ref[...] + far_ref[:, lanes:total].astype(wide)).astype(low)
    pieces = (
        held_ref[:feats, :lanes],
        got_ref[:feats, :lanes],
        far_ref[:, :lanes],
        far_ref[:, total:],
    )
    for place, piece in enumerate(pieces):
        piece_ref[place, :, :lanes] = piece[: feats // 2]
        piece_ref[place, :, lanes:] = piece[feats // 2 :]
    rows = [partner(flags_ref[ROW], mask) for mask in range(4)]
    place_back(flags_ref, [piece_ref.at[i] for i in range(4)], rows, own_ref, other_ref)


def head_sets():
    return [(seq, head, seq * HEADS + head) for seq in range(2) for head in range(HEADS)]


def set_row(place):
    ids = lax.broadcasted_iota(jnp.int32, (SUM_ROWS, SPAN), 0)
    return (ids == place).astype(wide)


def turned(parts, trig_ref):
    part_wide = parts.astype(wide)
    return jnp.concatenate(
        [(part_wide * trig_ref[0:1, :]).astype(low), (part_wide * trig_ref[1:2, :]).astype(low)], 0
    )


def unturned(pair, trig_ref):
    return pair[:HD] * trig_ref[0:1, :] + pair[HD:] * trig_ref[1:2, :]


def query_part(qkv_ref, seq, head):
    return qkv_ref[seq, head * HD : (head + 1) * HD, :]


def key_part(qkv_ref, seq, head):
    return qkv_ref[seq, WIDTH + head * HD : WIDTH + (head + 1) * HD, :]


def value_part(qkv_ref, seq, head):
    return qkv_ref[seq, 2 * WIDTH + head * HD : 2 * WIDTH + (head + 1) * HD, :]


def kept_keys(qkv_ref, trig_ref, seq, head):
    keys = jnp.maximum(key_part(qkv_ref, seq, head), 0)
    return (keys.astype(wide) * trig_ref[2 + seq : 3 + seq, :]).astype(low)


def state_slice(state, place):
    return state[place * HD : (place + 1) * HD]


def pack_hidden_body(flags_ref, up_ref, down_ref, mine_ref, copy_ref, sems):
    part = mine_ref.shape[1] // 2
    copies = []
    for half, packed_ref in enumerate((mine_ref, copy_ref)):
        copy = 1 - flags_ref[COPY] if half else flags_ref[COPY]
        start = pl.multiple_of((flags_ref[CORE] * 2 + copy) * part, 128)
        for place, ref in enumerate((up_ref, down_ref)):
            copies.append(
                pltpu.make_async_copy(
                    ref.at[:, pl.ds(start, part)],
                    packed_ref.at[:, pl.ds(place * part, part)],
                    sems.at[2 * half + place],
                )
            )
    for copy in copies:
        copy.start()
    for copy in copies:
        copy.wait()


def partner(row, mask):
    if mask == 0:
        return row
    if mask == 1:
        return row + 1 - 2 * lax.rem(row, 2)
    return lax.rem(row + 2, 4) if mask == 2 else 3 - row


def row_block(flags_ref, mask, feats):
    return pl.ds(pl.multiple_of(partner(flags_ref[ROW], mask) * feats, 16), feats)


def project_body(flags_ref, own_ref, other_ref, trig_ref, packed_ref, *refs):
    weight_ref, qkv_ref, state_ref = refs[-3:]
    blocks = refs[:-3]
    count = len(blocks) // 2
    first_copy = flags_ref[COPY] == 0
    feats = packed_ref.shape[0]
    part = packed_ref.shape[1] // 2

    def rows_of(mask):
        return row_block(flags_ref, mask, feats)

    weight_ref[rows_of(0), :] = packed_ref[...]
    for step in range(1, count + 1):
        mine, copied = blocks[step - 1][...], blocks[count + step - 1][...]
        weight_ref[rows_of(step), :part] = jnp.where(first_copy, mine, copied)
        weight_ref[rows_of(step), part:] = jnp.where(first_copy, copied, mine)
    matrix = weight_ref[:, : 3 * WIDTH]
    for seq, x_ref in enumerate((own_ref, other_ref)):
        qkv_ref[seq] = dot_tn(matrix, x_ref[...]).astype(low)
    sums = jnp.zeros((SUM_ROWS, 2 * HD), wide)
    for seq, head, place in head_sets():
        turned_keys = turned(kept_keys(qkv_ref, trig_ref, seq, head), trig_ref)
        values = value_part(qkv_ref, seq, head)
        state_ref[place * HD : (place + 1) * HD, :] = dot_nt(values, turned_keys).astype(low)
        sums = sums + dot_nt(set_row(place).astype(low), turned_keys)
    state_ref[STATE_ROWS:, :] = sums.astype(low)


def block_body(qkv_ref, trig_ref, reweight_ref, weights_ref, numer_ref, denom_ref):
    denoms = jnp.zeros((SUM_ROWS, SPAN), wide)
    for seq, head, place in head_sets():
        queries = jnp.maximum(query_part(qkv_ref, seq, head), 0)
        keys = kept_keys(qkv_ref, trig_ref, seq, head)
        weights = dot_tn(keys, queries) * reweight_ref[...]
        weights_low = weights.astype(low)
        weights_ref[place] = weights_low
        numer_ref[place] = dot_nn(value_part(qkv_ref, seq, head), weights_low)
        denoms = denoms + set_row(place) * jnp.sum(weights, 0, keepdims=True)
    denom_ref[...] = denoms


def attend_body(
    qkv_ref,
    trig_ref,
    numer_ref,
    denom_ref,
    weight_ref,
    *refs,
):
    arrived = refs[:-5]
    prior_ref, attn_wide_ref, own_ref, other_ref, attn_ref = refs[-5:]
    total = arrived[0][...].astype(wide)
    for ref in arrived[1:]:
        total = total + ref[...].astype(wide)
    prior_ref[...] = total.astype(low)
    matrix = weight_ref[:, 3 * WIDTH : 4 * WIDTH]
    prior_sums = prior_ref[STATE_ROWS:, :]
    inverses = jnp.zeros((SUM_ROWS, SPAN), wide)
    for seq, head, place in head_sets():
        queries = turned(jnp.maximum(query_part(qkv_ref, seq, head), 0), trig_ref)
        prior = prior_ref[place * HD : (place + 1) * HD, :]
        numer = numer_ref[place] + dot_nn(prior, queries)
        denoms = dot_nn(prior_sums, queries) + denom_ref[...]
        denom = 1.0 + jnp.sum(denoms * set_row(place), 0, keepdims=True)
        inverse = 1.0 / denom
        inverses = inverses + set_row(place) * inverse
        attended = numer * inverse
        attn_wide_ref[place * HD : (place + 1) * HD, :] = attended
        attn_ref[seq, head * HD : (head + 1) * HD, :] = attended.astype(low)
    attn_wide_ref[STATE_ROWS:, :] = inverses
    own_ref[...] = dot_nn(matrix, attn_ref[0])
    other_ref[...] = dot_nn(matrix, attn_ref[1]).astype(low)


def grad_attend_body(
    own_ref,
    other_ref,
    weight_ref,
    attn_wide_ref,
    qkv_ref,
    trig_ref,
    grad_num_ref,
    grad_den_ref,
    state_ref,
):
    matrix = weight_ref[:, 3 * WIDTH : 4 * WIDTH]
    sums = jnp.zeros((SUM_ROWS, 2 * HD), wide)
    dens = jnp.zeros((SUM_ROWS, SPAN), wide)
    for seq, grad_ref in enumerate((own_ref, other_ref)):
        grads = dot_tn(matrix, grad_ref[...]).astype(low).astype(wide)
        for head in range(HEADS):
            place = seq * HEADS + head
            inverse = jnp.sum(attn_wide_ref[STATE_ROWS:, :] * set_row(place), 0, keepdims=True)
            scaled = grads[head * HD : (head + 1) * HD] * inverse
            grad_num = scaled.astype(low)
            grad_num_ref[place] = grad_num
            grad_den = -jnp.sum(scaled * attn_wide_ref[place * HD : (place + 1) * HD, :], 0, keepdims=True)
            den_row = set_row(place) * grad_den
            dens = dens + den_row
            queries = turned(jnp.maximum(query_part(qkv_ref, seq, head), 0), trig_ref)
            state_ref[place * HD : (place + 1) * HD, :] = dot_nt(grad_num, queries).astype(low)
            sums = sums + dot_nt(den_row.astype(low), queries)
    state_ref[STATE_ROWS:, :] = sums.astype(low)
    grad_den_ref[...] = dens


def grad_block_body(
    grad_num_ref,
    grad_den_ref,
    qkv_ref,
    trig_ref,
    reweight_ref,
    weights_ref,
    prior_ref,
    grad_query_ref,
    grad_key_ref,
    grad_value_ref,
):
    prior_sums = prior_ref[STATE_ROWS:, :]
    for seq, head, place in head_sets():
        query = query_part(qkv_ref, seq, head)
        queries = jnp.maximum(query, 0)
        keys = kept_keys(qkv_ref, trig_ref, seq, head)
        grad_num = grad_num_ref[place]
        den_rows = grad_den_ref[...] * set_row(place)
        grad_den = jnp.sum(den_rows, 0, keepdims=True)
        grad_scores = (
            (dot_tn(value_part(qkv_ref, seq, head), grad_num) + grad_den) * reweight_ref[...]
        ).astype(low)
        prior = jnp.concatenate([prior_ref[place * HD : (place + 1) * HD, :], prior_sums], 0)
        grads = jnp.concatenate([grad_num, den_rows.astype(low)], 0)
        grad_query = dot_nn(keys, grad_scores) + unturned(dot_tn(prior, grads), trig_ref)
        grad_query_ref[seq, head * HD : (head + 1) * HD, :] = jnp.where(
            query.astype(wide) > 0, grad_query, 0.0
        ).astype(low)
        grad_key_ref[place] = dot_nt(queries, grad_scores)
        grad_value_ref[place] = dot_nt(grad_num, weights_ref[place])


def grad_project_body(
    grad_query_ref,
    grad_key_ref,
    grad_value_ref,
    qkv_ref,
    trig_ref,
    x_own_ref,
    x_other_ref,
    weight_ref,
    flags_ref,
    *refs,
):
    arrived = refs[:-6]
    kept_ref, sent_ref, own_ref, other_ref, after_ref, grad_ref = refs[-6:]
    total = arrived[0][...].astype(wide)
    for ref in arrived[1:]:
        total = total + ref[...].astype(wide)
    after_ref[...] = total.astype(low)
    after_sums = after_ref[STATE_ROWS:, :]
    for seq, head, place in head_sets():
        key = key_part(qkv_ref, seq, head)
        keys = turned(kept_keys(qkv_ref, trig_ref, seq, head), trig_ref)
        values = value_part(qkv_ref, seq, head)
        after = after_ref[place * HD : (place + 1) * HD, :]
        left = jnp.concatenate([after, after_sums], 0)
        right = jnp.concatenate([values, set_row(place).astype(low)], 0)
        grad_key = grad_key_ref[place] + unturned(dot_tn(left, right), trig_ref)
        grad_key = jnp.where(key.astype(wide) > 0, grad_key, 0.0) * trig_ref[2 + seq : 3 + seq, :]
        grad_value = grad_value_ref[place] + dot_nn(after, keys)
        rows = slice(head * HD, (head + 1) * HD)
        grad_ref[seq, rows, :] = grad_query_ref[seq, rows, :]
        rows = slice(WIDTH + head * HD, WIDTH + (head + 1) * HD)
        grad_ref[seq, rows, :] = grad_key.astype(low)
        rows = slice(2 * WIDTH + head * HD, 2 * WIDTH + (head + 1) * HD)
        grad_ref[seq, rows, :] = grad_value.astype(low)
    matrix = weight_ref[:, : 3 * WIDTH]
    grad_w = (
        dot_nt(x_own_ref[...], grad_ref[0]) + dot_nt(x_other_ref[...], grad_ref[1])
    ).astype(low)
    rows, part, _ = kept_ref.shape
    first_copy = flags_ref[COPY] == 0
    for row in range(rows):
        start = row * 2 * part
        first, second = grad_w[start : start + part], grad_w[start + part : start + 2 * part]
        kept_ref[row] = jnp.where(first_copy, first, second)
        sent_ref[row] = jnp.where(first_copy, second, first)
    own_ref[...] = dot_nn(matrix, grad_ref[0])
    other_ref[...] = dot_nn(matrix, grad_ref[1]).astype(low)


def norm_body(x_ref, half_ref, recv_ref, vec_ref, first_ref, low_ref, normed_ref):
    hidden = x_ref[...].astype(wide) + (half_ref[...].astype(wide) + recv_ref[...].astype(wide))
    first, normed, inv_std = norm_columns(hidden, vec_ref[:, 0:1], vec_ref[:, 1:2])
    first_ref[...] = first
    low_ref[...] = first.astype(low)
    normed_ref[:D, :] = normed
    normed_ref[D:, :] = jnp.broadcast_to(inv_std, (8, SPAN))


def lane_sums(columns, place):
    lanes = lax.broadcasted_iota(jnp.int32, (columns[0].shape[0], 2 * SUM_LANES), 1)
    total = jnp.zeros(lanes.shape, wide)
    for shift, column in enumerate(columns):
        total = jnp.where(lanes == place + shift, jnp.sum(column, 1, keepdims=True), total)
    return total


def second_norm_body(
    first_ref, half_ref, recv_ref, vec_ref, cot_ref, trig_ref, result_ref, grad_ref, low_ref
):
    hidden = first_ref[...] + (half_ref[...].astype(wide) + recv_ref[...].astype(wide))
    scale = vec_ref[:, 2:3]
    result, normed, inv_std = norm_columns(hidden, scale, vec_ref[:, 3:4])
    result_ref[...] = result.astype(low)
    grad_in = cot_ref[...].astype(wide) * trig_ref[2:3, :]
    grad = norm_columns_back(grad_in, normed, inv_std, scale)
    grad_ref[:, :SPAN] = grad
    low_ref[...] = grad.astype(low)
    grad_ref[:, SPAN:] = lane_sums((grad_in * normed, grad_in), 2)


def norm_back_body(
    grad_ref, half_ref, recv_ref, normed_ref, vec_ref, hidden_ref, low_ref, sum_ref
):
    grad_in = grad_ref[:, :SPAN] + (half_ref[...].astype(wide) + recv_ref[...].astype(wide))
    normed = normed_ref[:D, :]
    grad = norm_columns_back(grad_in, normed, normed_ref[D : D + 1, :], vec_ref[:, 0:1])
    hidden_ref[...] = grad
    low_ref[...] = grad.astype(low)
    sum_ref[...] = (lane_sums((grad_in * normed, grad_in), 0) + grad_ref[:, SPAN:]).astype(low)


def hidden_weights_body(flags_ref, *refs):
    blocks, outs = refs[:-2], refs[-2:]
    for half, weight_ref in enumerate(outs):
        for mask, ref in enumerate(blocks[4 * half : 4 * half + 4]):
            weight_ref[row_block(flags_ref, mask, ref.shape[0]), :] = ref[...]


def hidden_body(own_ref, other_ref, mine_ref, copy_ref, *refs):
    acts, slopes, parts = refs[:2], refs[2:4], refs[4:]
    part = acts[0].shape[0]
    for seq, (x_ref, part_ref) in enumerate(zip((own_ref, other_ref), parts)):
        cols = slice(seq * SPAN, (seq + 1) * SPAN)
        total = None
        for weight_ref, act_ref, slope_ref in zip((mine_ref, copy_ref), acts, slopes):
            act, slope = gelu_and_slope(dot_tn(weight_ref[:, :part], x_ref[...]))
            act_ref[:, cols] = act
            slope_ref[:, cols] = slope
            term = dot_nn(weight_ref[:, part:], act)
            total = term if total is None else total + term
        part_ref[...] = total.astype(part_ref.dtype)


def hidden_back_body(
    own_ref,
    other_ref,
    mine_ref,
    copy_ref,
    slope_mine_ref,
    slope_copy_ref,
    pre_mine_ref,
    pre_copy_ref,
    part_own_ref,
    part_other_ref,
):
    part = slope_mine_ref.shape[0]
    for seq, (x_ref, part_ref) in enumerate(
        ((own_ref, part_own_ref), (other_ref, part_other_ref))
    ):
        cols = slice(seq * SPAN, (seq + 1) * SPAN)
        total = None
        for weight_ref, slope_ref, pre_ref in (
            (mine_ref, slope_mine_ref, pre_mine_ref),
            (copy_ref, slope_copy_ref, pre_copy_ref),
        ):
            grad_pre = (dot_tn(weight_ref[:, part:], x_ref[...]) * slope_ref[:, cols]).astype(low)
            pre_ref[:, cols] = grad_pre
            term = dot_nn(weight_ref[:, :part], grad_pre)
            total = term if total is None else total + term
        part_ref[...] = total.astype(part_ref.dtype)


def half_grads_body(own_ref, other_ref, mine_ref, copy_ref, kept_ref, sent_ref):
    for pre_ref, out_ref in ((copy_ref, sent_ref), (mine_ref, kept_ref)):
        out_ref[...] = (
            dot_nt(own_ref[...], pre_ref[:, :SPAN]) + dot_nt(other_ref[...], pre_ref[:, SPAN:])
        ).astype(low)


def quarters(flags_ref, refs):
    core, copy = flags_ref[CORE], flags_ref[COPY]
    for ref, other_core, other_copy in zip(refs, (0, 0, 1, 1), (0, 1, 0, 1)):
        core_place = 1 - core if other_core else core
        copy_place = 1 - copy if other_copy else copy
        yield core_place * 2 + copy_place, ref


def place_hidden_body(flags_ref, *refs):
    down_ref, up_ref, out_ref, vec_ref = refs[4:]
    part = up_ref.shape[1] // 4
    for place, ref in quarters(flags_ref, refs[:4]):
        cols = pl.ds(pl.multiple_of(place * part, 128), part)
        down_ref[:, cols] = ref[:, :part].astype(wide)
        up_ref[:, cols] = ref[:, part : 2 * part].astype(wide)
    half = (WIDTH + SUM_LANES) // 2
    first_core, first_copy = flags_ref[CORE] == 0, flags_ref[COPY] == 0
    sums = []
    for own_ref, copy_ref in (refs[:2], refs[2:4]):
        own, copied = own_ref[:, 2 * part :].astype(wide), copy_ref[:, 2 * part :].astype(wide)
        sums.append((jnp.where(first_copy, own, copied), jnp.where(first_copy, copied, own)))
    first = [jnp.where(first_core, sums[0][i], sums[1][i]) for i in (0, 1)]
    second = [jnp.where(first_core, sums[1][i], sums[0][i]) for i in (0, 1)]
    for parts, start in ((first, 0), (second, WIDTH)):
        out_ref[:, start : start + half] = parts[0]
        out_ref[:, start + half : start + WIDTH] = parts[1][:, : WIDTH - half]
    vec_ref[...] = first[1][:, WIDTH - half :] + second[1][:, WIDTH - half :]


def place_last_body(flags_ref, *refs):
    join_back_body(flags_ref, refs[4], refs[5], refs[6])
    outs = refs[7:]
    first_core = flags_ref[CORE] == 0
    part = refs[0].shape[0]
    for own_ref, other_ref, other_copy in ((refs[0], refs[2], 0), (refs[1], refs[3], 1)):
        copy = 1 - flags_ref[COPY] if other_copy else flags_ref[COPY]
        rows = pl.ds(pl.multiple_of(copy * part, 8), part)
        own, other = own_ref[...].astype(wide), other_ref[...].astype(wide)
        for place, out_ref in enumerate(outs):
            cols = slice(place * WIDTH, (place + 1) * WIDTH)
            out_ref[rows, :WIDTH] = jnp.where(first_core, own[:, cols], other[:, cols])
            out_ref[rows, WIDTH:] = jnp.where(first_core, other[:, cols], own[:, cols])


def gelu_and_slope(pre):
    cdf = 0.5 * (1.0 + lax.erf(pre * math.sqrt(0.5)))
    density = jnp.exp(-0.5 * pre * pre) * (1.0 / math.sqrt(2.0 * math.pi))
    return (pre * cdf).astype(low), (cdf + pre * density)


def all_quarters(own, direct=False):
    copied = swap_copies(own)
    if direct:
        pairs = [(i, i ^ 3) for i in range(lax.axis_size("dp"))]
        return own, copied, swap_pair(own), lax.ppermute(own, "dp", pairs)
    return own, copied, swap_pair(own), swap_pair(copied)


def on_device_paired(
    tokens,
    lengths,
    w_query,
    w_key,
    w_value,
    w_out,
    gain_one,
    bias_one,
    w_up,
    w_down,
    gain_two,
    bias_two,
    cotangent,
):
    rows = lax.axis_size("row")
    seq_len = SPAN * rows
    dp_idx = lax.axis_index("dp")
    feat_rows = tokens.shape[0]
    half_feats = feat_rows // 2
    flags = jnp.stack(
        [dp_idx % 2, dp_idx // 2, lax.axis_index("row"), lax.axis_index("col"), dp_idx]
    )
    trig, reweight = local_call(
        partial(turn_body, seq_len=seq_len),
        [((8, SPAN), wide), ((SPAN, SPAN), wide)],
        "turn",
        flags,
        lengths,
    )

    def passed_on(pieces):
        return [pieces[0]] + [
            rotate_rows(piece, step) for step, piece in enumerate(pieces) if step
        ]

    def cols_back(own, other, kind, name):
        return local_call(
            join_back_body,
            [((feat_rows, SPAN * rows // 2), kind)],
            name,
            flags,
            own,
            swap_cols(other),
        )[0]

    def column_parts(own_part, other_part, name):
        (half,) = local_call(add_body, low_outs(1, D, SPAN), name, own_part, swap_pair(other_part))
        return half, swap_cols(half)

    first_col = lax.axis_index("col") == 0

    def halved(block):
        top, bottom = block[:half_feats], block[half_feats:]
        return jnp.where(first_col, top, bottom), jnp.where(first_col, bottom, top)

    (token_own, token_sent), (cot_own, cot_sent) = halved(tokens), halved(cotangent)
    got = swap_cols(jnp.concatenate([token_sent, cot_sent], 0))

    part = w_up.shape[1] // 4
    first_core = dp_idx % 2 == 0

    def core_part(operand):
        return jnp.where(first_core, operand[:, :WIDTH], operand[:, WIDTH:])

    parts = [core_part(operand) for operand in (w_query, w_key, w_value, w_out.T)]
    first_packed = jnp.concatenate(parts, 1)
    first_mine = jnp.where(
        dp_idx < 2, jnp.concatenate(parts[:2], 1), jnp.concatenate(parts[2:], 1)
    )

    def row_blocks(block):
        return swap_rows(block, 1), swap_rows(block, 2)

    first_one, first_two = row_blocks(first_mine)
    first_one, got = lax.optimization_barrier((first_one, got))
    hidden_packed = local_call(
        pack_hidden_body,
        low_outs(2, feat_rows, 2 * part),
        "pack_hidden",
        flags,
        w_up,
        w_down.T,
        scratch=[pltpu.SemaphoreType.DMA((4,))],
        space=pltpu.HBM,
    )
    vecs = jnp.stack([gain_one, bias_one, gain_two, bias_two], 0)
    token_pieces = local_call(
        partial(pieces_body, rows=rows),
        low_outs(rows, feat_rows + 16, SPAN),
        "token_pieces",
        flags,
        token_own,
        cot_own,
        got,
        vecs,
    )
    def after(value, *others):
        return lax.optimization_barrier((value, others))[0]

    first_three = swap_rows(after(first_two, token_pieces[0]), 1)
    first_copies = [
        swap_copies(after(first_one, token_pieces[0])),
        swap_copies(first_two),
        swap_copies(first_three),
    ]
    token_pieces = passed_on(token_pieces)
    token_pieces, first_three, first_copies[0] = lax.optimization_barrier(
        (token_pieces, first_three, first_copies[0])
    )
    first_blocks = [first_one, first_two, first_three, *first_copies]
    x_half, norm_vecs = local_call(
        partial(place_tokens_body, rows=rows, part=half_feats),
        low_outs(1, D, SPAN) + [((D, 8), wide)],
        "token_place",
        flags,
        *token_pieces,
    )
    x_half, trig, reweight, hidden_packed = lax.optimization_barrier(
        (x_half, trig, reweight, hidden_packed)
    )
    hidden_one, hidden_two = row_blocks(hidden_packed[0])
    x_got, hidden_one = lax.optimization_barrier((swap_cols(x_half), hidden_one))
    x_own, cot = local_call(
        partial(join_halves_body, rows=rows),
        low_outs(2, D, SPAN),
        "token_join",
        flags,
        x_half,
        x_got,
    )
    x_own, first_blocks = lax.optimization_barrier((x_own, first_blocks))
    x_other = swap_pair(x_own)
    state_shape = ((STATE_ROWS + SUM_ROWS, 2 * HD), low)
    sets = 2 * HEADS
    block_low = ((D, SPAN), low)
    block_wide = ((D, SPAN), wide)
    weight, qkv, state = local_call(
        project_body,
        [((D, 4 * WIDTH), low), ((2, 3 * WIDTH, SPAN), low), state_shape],
        "project",
        flags,
        x_own,
        x_other,
        trig,
        first_packed,
        *first_blocks,
    )
    hidden_three = swap_rows(hidden_two, 1)
    copy_two = swap_copies(hidden_two)
    arrived = [shift_rows(state, step) for step in range(1, rows)]
    arrived, hidden_three, copy_two = lax.optimization_barrier(
        (arrived, hidden_three, copy_two)
    )
    weights, numer, denom = local_call(
        block_body,
        [((sets, SPAN, SPAN), low), ((sets, HD, SPAN), wide), ((SUM_ROWS, SPAN), wide)],
        "block",
        qkv,
        trig,
        reweight,
    )
    prior, attn_wide, branch_own, branch_other = local_call(
        attend_body,
        [
            state_shape,
            ((STATE_ROWS + SUM_ROWS, SPAN), wide),
            block_wide,
            block_low,
        ],
        "attend",
        qkv,
        trig,
        numer,
        denom,
        weight,
        *arrived,
        scratch=[((2, WIDTH, SPAN), low)],
    )
    copy_one = swap_copies(hidden_one)
    branch_own, branch_other, copy_one = lax.optimization_barrier(
        (branch_own, branch_other, copy_one)
    )
    branch = column_parts(branch_own, branch_other, "branch_half")
    copy_three = swap_copies(hidden_three)
    branch, copy_three = lax.optimization_barrier((branch, copy_three))
    hidden_mine, hidden_copy = local_call(
        hidden_weights_body,
        low_outs(2, D, 2 * part),
        "hidden_weights",
        flags,
        hidden_packed[0],
        hidden_one,
        hidden_two,
        hidden_three,
        hidden_packed[1],
        copy_one,
        copy_two,
        copy_three,
    )
    branch, hidden_mine = lax.optimization_barrier((branch, hidden_mine))
    first, first_low, normed = local_call(
        norm_body,
        [block_wide, block_low, ((D + 8, SPAN), wide)],
        "norm",
        x_own,
        *branch,
        norm_vecs,
    )
    first_other = swap_pair(first_low)
    hidden_acts = [((part, 2 * SPAN), low)] * 2 + [((part, 2 * SPAN), wide)] * 2
    act_mine, act_copy, slope_mine, slope_copy, ffn_own, ffn_other = local_call(
        hidden_body,
        hidden_acts + [block_wide, block_low],
        "hidden",
        first_low,
        first_other,
        hidden_mine,
        hidden_copy,
    )
    ffn = column_parts(ffn_own, ffn_other, "ffn_half")
    result, grad_second, grad_ffn = local_call(
        second_norm_body,
        [block_low, ((D, SPAN + 2 * SUM_LANES), wide), block_low],
        "second_norm",
        first,
        *ffn,
        norm_vecs,
        cot,
        trig,
    )
    grad_ffn_other = swap_pair(grad_ffn)
    pair_low = ((D, part), low)
    down_held, down_sent = local_call(
        down_grad_body,
        low_outs(2, 2 * feat_rows, 2 * part),
        "down_grad",
        flags,
        grad_ffn,
        grad_ffn_other,
        act_mine,
        act_copy,
        scratch=[((D, 2 * part), low)],
    )
    down_got = swap_rows(down_sent, 1)
    grad_ffn, grad_ffn_other, down_held = lax.optimization_barrier(
        (grad_ffn, grad_ffn_other, down_held)
    )
    hidden_low = ((part, 2 * SPAN), low)
    pre_mine, pre_copy, first_own_part, first_other_part = local_call(
        hidden_back_body,
        [hidden_low, hidden_low, block_wide, block_low],
        "hidden_back",
        grad_ffn,
        grad_ffn_other,
        hidden_mine,
        hidden_copy,
        slope_mine,
        slope_copy,
    )
    first_sum = column_parts(first_own_part, first_other_part, "first_half")

    kept_up, sent_up = local_call(
        half_grads_body,
        [pair_low, pair_low],
        "up_grad",
        first_low,
        first_other,
        pre_mine,
        pre_copy,
    )
    got_up = swap_copies(sent_up)
    down_kept, down_pair = local_call(
        down_pairs_body,
        [((2 * feat_rows, part), wide), ((2 * feat_rows, part), low)],
        "down_pairs",
        down_held,
        down_got,
    )
    first_sum, kept_up, down_kept = lax.optimization_barrier((first_sum, kept_up, down_kept))
    grad_hidden, branch_grad, vec_sums = local_call(
        norm_back_body,
        [block_wide, block_low, ((D, 2 * SUM_LANES), low)],
        "norm_back",
        grad_second,
        *first_sum,
        normed,
        norm_vecs,
    )
    branch_grad_other = swap_pair(branch_grad)
    grad_num, grad_den, grad_state = local_call(
        grad_attend_body,
        [((sets, HD, SPAN), low), ((SUM_ROWS, SPAN), wide), state_shape],
        "grad_attend",
        branch_grad,
        branch_grad_other,
        weight,
        attn_wide,
        qkv,
        trig,
    )
    later = [shift_rows(grad_state, -step) for step in range(1, rows)]
    half_lanes = (WIDTH + SUM_LANES) // 2
    mix_kept, mix_sent = local_call(
        mix_body,
        [((D, half_lanes), low), ((2 * feat_rows, part + 2 * half_lanes), low)],
        "mix",
        flags,
        branch_grad,
        branch_grad_other,
        attn_wide,
        vec_sums,
        after(down_pair, grad_num),
        scratch=[((D, WIDTH + SUM_LANES), low)],
    )
    grad_query, grad_key, grad_value = local_call(
        grad_block_body,
        [
            ((2, WIDTH, SPAN), low),
            ((sets, HD, SPAN), wide),
            ((sets, HD, SPAN), wide),
        ],
        "grad_block",
        grad_num,
        grad_den,
        qkv,
        trig,
        reweight,
        weights,
        prior,
    )
    mix_got = swap_copies(after(mix_sent, got_up, grad_den))
    up_lanes = SPAN // 2 + part + half_lanes
    down_part, down_far = local_call(
        down_far_body,
        [((feat_rows, part), wide), ((feat_rows, part), low)],
        "down_far",
        down_kept,
        mix_got,
    )
    down_far = swap_rows(down_far, 2)
    up_held, up_sent = local_call(
        up_pieces_body,
        low_outs(2, 2 * feat_rows, up_lanes),
        "up_pieces",
        flags,
        result,
        kept_up,
        after(got_up, grad_query),
        mix_kept,
        mix_got,
        scratch=[((D, half_lanes), low)],
    )
    up_got = swap_rows(up_sent, 1)
    later, up_held = lax.optimization_barrier((later, up_held))
    half_rows = ((rows, half_feats, 3 * WIDTH), low)
    kept_w, sent_w, x_grad_own, x_grad_other = local_call(
        grad_project_body,
        [half_rows, half_rows, block_wide, block_low],
        "grad_project",
        grad_query,
        grad_key,
        grad_value,
        qkv,
        trig,
        x_own,
        x_other,
        weight,
        flags,
        *later,
        scratch=[state_shape, ((2, 3 * WIDTH, SPAN), low)],
    )
    got_w = swap_copies(sent_w)
    got_x = swap_pair(x_grad_other)
    x_half_grad, x_half_sent = local_call(
        partial(input_halves_body, rows=rows),
        [((D // 2, SPAN), wide), ((D // 2, SPAN), low)],
        "input_halves",
        flags,
        x_grad_own,
        got_x,
        scratch=[block_wide],
    )
    got_half = swap_cols(x_half_sent)
    last_lanes = 3 * WIDTH
    last_held, last_sent = local_call(
        last_pieces_body,
        low_outs(2, 2 * half_feats, last_lanes + SPAN),
        "last_pieces",
        flags,
        kept_w,
        got_w,
        x_half_grad,
        got_half,
        grad_hidden,
    )
    up_part, up_far = local_call(
        up_pairs_body,
        [((feat_rows, up_lanes - SPAN // 2), wide), ((feat_rows, up_lanes + SPAN // 2), low)],
        "up_pairs",
        up_held,
        after(up_got, kept_w),
    )
    up_far = swap_rows(up_far, 2)
    last_got = swap_rows(last_sent, 1)
    last_part, last_far = local_call(
        last_pairs_body,
        [((half_feats, last_lanes), wide), ((half_feats, last_lanes + 2 * SPAN), low)],
        "last_pairs",
        last_held,
        last_got,
    )
    hidden_sum, *out_wide = local_call(
        hidden_sums_body,
        low_outs(1, feat_rows, 2 * part + half_lanes)
        + low_outs(2, half_feats, SPAN * rows // 2),
        "hidden_sums",
        flags,
        down_part,
        down_far,
        up_part,
        up_held,
        up_got,
        up_far,
        scratch=[((4, half_feats, SPAN), low)],
    )
    last_sum, *input_wide = local_call(
        last_sums_body,
        low_outs(1, half_feats, last_lanes) + low_outs(2, half_feats, SPAN * rows // 2),
        "last_sums",
        flags,
        last_part,
        last_held,
        last_got,
        swap_rows(last_far, 2),
    )
    output = cols_back(*out_wide, low, "out_join")
    down_t, up_grad, out_t, vec_total = local_call(
        place_hidden_body,
        [((feat_rows, 4 * part), wide)] * 2
        + [((feat_rows, 2 * WIDTH), wide), ((feat_rows, SUM_LANES), wide)],
        "place_hidden",
        flags,
        *all_quarters(hidden_sum, True),
    )
    last_parts = all_quarters(last_sum, True)
    last_parts = (after(last_parts[0], up_grad), *last_parts[1:])
    input_grad, query_grad, key_grad, value_grad = local_call(
        place_last_body,
        [((feat_rows, SPAN * rows // 2), wide)] + [((feat_rows, 2 * WIDTH), wide)] * 3,
        "place_last",
        flags,
        *last_parts,
        input_wide[0],
        swap_cols(input_wide[1]),
    )
    return (
        output,
        input_grad,
        query_grad,
        key_grad,
        value_grad,
        out_t.T,
        vec_total[:, 0],
        vec_total[:, 1],
        up_grad,
        down_t.T,
        vec_total[:, 2],
        vec_total[:, 3],
    )


def solution(mesh):
    placed = (
        P("row", ("dp", "col")),
        P(),
        P("row", "col"),
        P("row", "col"),
        P("row", "col"),
        P("col", "row"),
        P("row"),
        P("row"),
        P("row", "col"),
        P("col", "row"),
        P("row"),
        P("row"),
        P("row", ("dp", "col")),
    )
    return jax.shard_map(
        on_device_paired if paired_layout(mesh) else on_device,
        mesh=mesh,
        in_specs=placed,
        out_specs=(
            P("row", ("dp", "col")),
            P("row", ("dp", "col")),
            P("row", "col"),
            P("row", "col"),
            P("row", "col"),
            P("col", "row"),
            P("row"),
            P("row"),
            P("row", "col"),
            P("col", "row"),
            P("row"),
            P("row"),
        ),
        check_vma=False,
    )
```
